32 devices in a mesh: ctx: 8 (over z, x), exp: 4 (over y, core).
Axes of the slice: x: 2, y: 2, z: 4, core: 2. Of those that a mesh axis runs over, the one named last changes fastest.
Arguments:
- grad_out: bfloat16 [4096, 2880], P(('ctx', 'exp')), may hold values from -6 to 6
- top_logits: float32 [4096, 4], P(('ctx', 'exp')), may hold values from -8 to 308
- expert_ids: int32 [4096, 4], P(('ctx', 'exp')), may hold values from 0 to 3, all different within a row; in each aligned block of 128 rows (0 to 127, 128 to 255, ...) at most 128 rows name the same one
- saved_hidden: bfloat16 [8, 4, 512, 1536], P('ctx', 'exp'), may hold values from -0.29882812 to 0.29882812
- w_down: bfloat16 [4, 1536, 2880], P('exp', 'ctx'), may hold values from -0.15625 to 0.15625
Outputs:
- logit_grad: float32 [4096, 4], P(('ctx', 'exp'))
- hidden_grad: bfloat16 [8, 4, 512, 1536], P('ctx', 'exp')
- down_grad: float32 [4, 1536, 2880], P('exp', 'ctx')
The draws below stay inside these ranges and needn't reach their ends.
Inputs may be any that keep to these rules, and one draw needn't show every extreme that they name: `expert_ids`: each row names 4 different experts; among the rows of one device no expert is named by more than 128 rows, a bound that some blocks reach.
All inputs are finite; a program needn't handle non-finite values.
Results may differ from the reference program's by a relative error of at most 0.0048.
Values may be sent and summed in bfloat16 or wider, within the bound.
No kernel may reach another device: no remote copies, remote signals or barrier semaphores. Data moves between devices by JAX's collectives and lax.ppermute only.
A program may use at most 128 MiB of HBM per device.

```python
import math
import jax
import jax.numpy as jnp
import numpy as np
from jax import lax

D = 2880
TOPK = 4
FF = 1536
TOK_DEV = 128
EXPERTS = 4
CAP = 128
SLOTS = 512
TOKENS = 4096
N_CTX = 8
N_EXP = 4


def draw_top_logits(key, part):
    base_key = jax.random.fold_in(jax.random.fold_in(key, 7), 0)
    values = jnp.clip(1.5 * jax.random.normal(base_key, (TOKENS, TOPK), jnp.float32), -8.0, 8.0)
    return values


def level_of(stream_key, extent, cuts, smallest, largest):
    def one(position, blocks):
        steps = jax.random.uniform(jax.random.fold_in(jax.random.fold_in(stream_key, 6), position), (blocks,), jnp.float32, smallest / len(cuts), largest / len(cuts))
        return jnp.repeat(jnp.exp(steps), extent[position] // blocks).reshape((-1,) + (1,) * (len(extent) - position - 1))

    loudness = one(*cuts[0])
    for cut in cuts[1:]:
        loudness = loudness * one(*cut)
    return loudness


def shared_out(stream_key, own, number, rows, number_of, top, most, skew):
    sequence = jax.random.permutation(stream_key, number_of)
    packed, ordinary = portions_of(number_of, rows * top, most, skew, True), portions_of(number_of, rows * top, most, skew, False)
    places = jnp.arange(number_of)

    def named(sizes, turn):
        used = int((sizes > 0).sum())
        fixed = max(1, used // 4)
        shifted = fixed + (places - fixed + turn * (used - fixed)) % max(1, number_of - fixed)
        return jnp.zeros((number_of,), jnp.int32).at[sequence[jnp.where(places < fixed, places, shifted)]].set(jnp.asarray(sizes, jnp.int32))

    sizes = jnp.where(number % 4 == 0, named(packed, number // 4), named(ordinary, number - number // 4 - 1))
    mixed = jax.random.permutation(jax.random.fold_in(own, 3), number_of)
    source_of, sink = mixed[0:number_of // 2 * 2:2], mixed[1:number_of // 2 * 2:2]
    room = jnp.minimum(sizes[source_of] - 1, most - sizes[sink]) // 2
    room = jnp.where((source_of == sequence[0]) | (sink == sequence[0]) | (sizes[sink] == 0), 0, jnp.maximum(room, 0))
    shifted = jax.random.randint(jax.random.fold_in(own, 4), (number_of // 2,), 0, 1 << 20) % (room + 1)
    sizes = sizes.at[source_of].add(-shifted).at[sink].add(shifted)
    labels = jnp.searchsorted(jnp.cumsum(sizes), jnp.arange(rows * top), side="right").astype(jnp.int32)
    listing = labels.reshape(top, rows).T
    listing = listing[jax.random.permutation(jax.random.fold_in(own, 1), rows)]
    turn = jax.random.randint(jax.random.fold_in(own, 2), (rows, 1), 0, top)
    return jnp.take_along_axis(listing, (jnp.arange(top)[None, :] + turn) % top, axis=1)


def portions_of(count, total, most, skew, full):
    loads = [(1 << 20) // math.isqrt(grade ** skew) + 1 for grade in range(1, count + 1)]
    largest = most if full else min(most, max(-(-total // count), total * loads[0] // sum(loads)))
    least = 1 if total - largest >= count - 1 else 0
    holding, rest = [largest] + [least] * (count - 1), total - largest - least * (count - 1)
    while rest > 0:
        candidates = [i for i in range(1, count) if holding[i] < largest] or [i for i in range(1, count) if holding[i] < most]
        whole, remaining = sum([loads[i] for i in candidates]), rest
        for i in candidates:
            more = min(most - holding[i], max(1, remaining * loads[i] // whole), rest)
            holding[i] = holding[i] + more
            rest = rest - more
    return np.array(holding)


def normal_values(stream_key, extent, scale, bound, pieces=(), held_as=jnp.bfloat16):
    array = jax.random.normal(stream_key, extent, jnp.float32) * scale
    if len(pieces) > 0:
        array = level_of(stream_key, extent, pieces, -0.22, 0.18) * array
    return jnp.clip(array, min=-bound, max=bound).astype(held_as)


def setup_inputs(seed: int = 0) -> dict:
    key_of = jax.random.split(jax.random.key(seed), 6)
    grad_out = normal_values(key_of[0], (TOKENS, D), 1.0, 6.0, ((0, 32),))
    top_logits = draw_top_logits(jax.random.fold_in(key_of[5], 71), 0)
    expert_ids_keys = jax.random.split(jax.random.fold_in(key_of[2], 1), TOKENS // TOK_DEV)
    expert_ids_turns = jax.random.permutation(jax.random.fold_in(key_of[2], 3), TOKENS // TOK_DEV)
    expert_ids = jax.vmap(lambda own, number: shared_out(jax.random.fold_in(key_of[2], 2), own, number, TOK_DEV, EXPERTS, TOPK, CAP, 2))(expert_ids_keys, expert_ids_turns).reshape((TOKENS, TOPK))
    saved_hidden = normal_values(key_of[3], (N_CTX, EXPERTS, SLOTS, FF), 0.05, 0.29882812, ((0, 8), (1, 4)))
    w_down = normal_values(key_of[4], (EXPERTS, FF, D), FF ** -0.5, 0.15625, ((0, 4), (1, 8)))
    return dict(grad_out=grad_out, top_logits=top_logits, expert_ids=expert_ids, saved_hidden=saved_hidden, w_down=w_down)


def reference(grad_out, top_logits, expert_ids, saved_hidden, w_down):
    highest = lax.Precision.HIGHEST
    gate_probs = jax.nn.softmax(top_logits, axis=-1)
    gate_sent = lax.optimization_barrier(gate_probs.astype(jnp.bfloat16)).astype(jnp.float32)
    id_blocks = expert_ids.reshape(N_CTX, N_EXP, TOK_DEV, TOPK)
    row_blocks = grad_out.reshape(N_CTX, N_EXP, TOK_DEV, D)
    gate_blocks = gate_sent.reshape(N_CTX, N_EXP, TOK_DEV, TOPK)
    weights_wide = w_down.astype(jnp.float32)
    columns = jnp.arange(EXPERTS, dtype=jnp.int32)
    slot_iota = jnp.arange(CAP, dtype=jnp.int32)

    def one_group(carry, inputs):
        ids_group, rows_group, gate_group, hidden_group = inputs
        matches = ids_group[..., None] == columns
        onehot = matches.astype(jnp.float32)
        per_token = jnp.sum(matches.astype(jnp.int32), axis=2)
        rank_table = jnp.cumsum(per_token, axis=1) - per_token
        select = ((per_token[..., None] == 1) & (rank_table[..., None] == slot_iota)).astype(jnp.float32)
        gate_by_expert = jnp.sum(onehot * gate_group[..., None], axis=2)
        rows_in = jnp.einsum("stec,std->escd", select, rows_group.astype(jnp.float32), precision=highest).reshape(EXPERTS, SLOTS, D)
        gate_in = jnp.einsum("stec,ste->esc", select, gate_by_expert, precision=highest).reshape(EXPERTS, SLOTS, 1)
        backprop = jnp.einsum("esd,efd->esf", rows_in, weights_wide)
        hidden_wide = hidden_group.astype(jnp.float32)
        hidden_grad = (gate_in * backprop).astype(jnp.bfloat16)
        slot_grad = jnp.sum(hidden_wide * backprop, axis=2).reshape(EXPERTS, N_EXP, CAP)
        scaled = lax.optimization_barrier((gate_in * rows_in).astype(jnp.bfloat16)).astype(jnp.float32)
        carry = carry + jnp.einsum("esf,esd->efd", hidden_wide, scaled)
        by_expert = jnp.einsum("stec,esc->ste", select, slot_grad, precision=highest)
        gate_grad = jnp.sum(onehot * by_expert[:, :, None, :], axis=3)
        return carry, (hidden_grad, gate_grad)

    zero_grad = jnp.zeros((EXPERTS, FF, D), jnp.float32)
    down_grad, (hidden_grad, gate_grad) = lax.scan(one_group, zero_grad, (id_blocks, row_blocks, gate_blocks, saved_hidden))
    gate_grad = gate_grad.reshape(TOKENS, TOPK)
    logit_grad = gate_probs * (gate_grad - jnp.sum(gate_probs * gate_grad, axis=1, keepdims=True))
    return logit_grad, hidden_grad, down_grad
```

```python
import functools

import jax
import jax.numpy as jnp
from jax import lax
from jax.experimental import pallas as pl
from jax.experimental.pallas import tpu as pltpu
from jax.sharding import PartitionSpec as P

LANES = 128
VMEM_BYTES = 56 * 1024 * 1024
NT = (((1,), (1,)), ((), ()))
NN = (((1,), (0,)), ((), ()))
f32 = jnp.float32
bf16 = jnp.bfloat16


def dot(a, b, dims):
    return lax.dot_general(a, b, dims, preferred_element_type=f32)


def whole():
    return pl.BlockSpec(memory_space=pltpu.VMEM)


def scalars():
    return pl.BlockSpec(memory_space=pltpu.SMEM)


def params():
    return pltpu.CompilerParams(vmem_limit_bytes=VMEM_BYTES)


def cost(flops, size):
    return pl.CostEstimate(flops=int(flops), bytes_accessed=int(size), transcendentals=0)


def rows_kernel(width, grad_ref, logits_ref, ids_ref, rows_ref, gates_ref):
    model, tokens = grad_ref.shape
    count = logits_ref.shape[0]
    logits = logits_ref[...]
    powers = jnp.exp(logits - jnp.max(logits, axis=0, keepdims=True))
    gates = powers / jnp.sum(powers, axis=0, keepdims=True)
    gates_ref[...] = gates
    sent = gates.astype(bf16).astype(f32)
    ids = ids_ref[...]
    tail = width - model
    row = lax.broadcasted_iota(jnp.int32, (tail, tokens), 0)
    extra = jnp.zeros((tail, tokens), f32)
    for expert in range(count):
        chosen = jnp.sum(jnp.where(ids == expert, sent, 0.0), axis=0, keepdims=True)
        extra = extra + jnp.where(row == expert, chosen, 0.0)
    for start in range(0, width, LANES):
        stop = start + LANES
        if stop <= model:
            block = grad_ref[start:stop, :].astype(f32)
        elif start >= model:
            block = extra[start - model : stop - model, :]
        else:
            block = jnp.concatenate(
                [grad_ref[start:model, :].astype(f32), extra[: stop - model, :]], axis=0
            )
        rows_ref[:, start:stop] = block.T.astype(bf16)


def make_rows(grad_out, top_logits, expert_ids, width):
    tokens, model = grad_out.shape
    count = top_logits.shape[1]
    return pl.pallas_call(
        functools.partial(rows_kernel, width),
        out_shape=(
            jax.ShapeDtypeStruct((tokens, width), bf16),
            jax.ShapeDtypeStruct((count, tokens), f32),
        ),
        in_specs=[whole()] * 3,
        out_specs=(whole(), whole()),
        compiler_params=params(),
        cost_estimate=cost(0, 4 * tokens * width),
        name="make_rows",
    )(grad_out.T, top_logits.T, expert_ids.T)


def split_kernel(where_ref, hidden_ref, own_ref, other_ref):
    parts, units, _ = own_ref.shape
    for part in range(parts):
        turned = hidden_ref[:, part * 2 * units : (part + 1) * 2 * units].astype(f32).T.astype(bf16)

        @pl.when(where_ref[1] == 0)
        def _():
            own_ref[part] = turned[:units]
            other_ref[part] = turned[units:]

        @pl.when(where_ref[1] != 0)
        def _():
            own_ref[part] = turned[units:]
            other_ref[part] = turned[:units]


def split_hidden(where, hidden, parts, units):
    slots = hidden.shape[0]
    half = jax.ShapeDtypeStruct((parts, units, slots), bf16)
    return pl.pallas_call(
        split_kernel,
        out_shape=(half, half),
        in_specs=[scalars(), whole()],
        out_specs=(whole(), whole()),
        compiler_params=params(),
        cost_estimate=cost(0, 4 * hidden.size),
        name="split_hidden",
    )(where, hidden)


def first_kernel(model, count, where_ref, *refs):
    number = 2 * count
    blocks, gate_tiles = refs[:number], refs[number : 2 * number]
    own_ref, other_ref = refs[2 * number : 2 * number + 2]
    sent_ref, rows_ref, scaled_ref, gate_rows_ref, column = refs[2 * number + 2 :]
    tokens = blocks[0].shape[0]
    me = where_ref[2]
    shift = model % LANES

    @pl.when(pl.program_id(0) == 0)
    def _():
        lane = lax.broadcasted_iota(jnp.int32, (tokens, LANES), 1)
        eight = lax.broadcasted_iota(jnp.int32, (8, LANES), 1)
        onehot = jnp.where(eight == shift + me, 1.0, 0.0).astype(bf16)
        for place in range(number):
            start = (place // count) * count * tokens + ((place % count) ^ me) * tokens
            here = pl.ds(pl.multiple_of(start, tokens), tokens)
            tile = gate_tiles[place][...]
            picked = jnp.where(lane == shift + me, tile.astype(f32), 0.0)
            total = jnp.sum(picked, axis=1, keepdims=True)
            column[here, :] = jnp.broadcast_to(total, (tokens, LANES))
            gate_rows_ref[:, here] = dot(onehot, tile, NT)

    for place in range(number):
        start = (place // count) * count * tokens + ((place % count) ^ me) * tokens
        here = pl.ds(pl.multiple_of(start, tokens), tokens)
        block = blocks[place][...]
        rows_ref[here, :] = block
        scaled_ref[here, :] = (block.astype(f32) * column[here, 0:1]).astype(bf16)
    slots = count * tokens
    index = where_ref[3]
    total = dot(own_ref[index], scaled_ref[:slots, :], NN)
    total = total + dot(other_ref[index], scaled_ref[slots:, :], NN)
    sent_ref[...] = total.astype(bf16)


def first_part(where, blocks, own, other, model, step):
    tokens, width = blocks[0].shape
    number = len(blocks)
    units = own.shape[1]
    grid = (pl.cdiv(width, step),)
    tile_spec = pl.BlockSpec((tokens, LANES), lambda j, s: (0, model // LANES))
    block_spec = pl.BlockSpec((tokens, step), lambda j, s: (0, j))
    return pl.pallas_call(
        functools.partial(first_kernel, model, number // 2),
        out_shape=(
            jax.ShapeDtypeStruct((units, model), bf16),
            jax.ShapeDtypeStruct((number * tokens, width), bf16),
            jax.ShapeDtypeStruct((number * tokens, width), bf16),
            jax.ShapeDtypeStruct((8, number * tokens), f32),
        ),
        grid_spec=pltpu.PrefetchScalarGridSpec(
            num_scalar_prefetch=1,
            grid=grid,
            in_specs=[block_spec] * number + [tile_spec] * number + [whole()] * 2,
            out_specs=(
                pl.BlockSpec((units, step), lambda j, s: (0, j)),
                pl.BlockSpec((number * tokens, step), lambda j, s: (0, j)),
                pl.BlockSpec((number * tokens, step), lambda j, s: (0, j)),
                pl.BlockSpec((8, number * tokens), lambda j, s: (0, 0)),
            ),
            scratch_shapes=[pltpu.VMEM((number * tokens, LANES), f32)],
        ),
        compiler_params=params(),
        cost_estimate=cost(2 * units * number * tokens * model, 6 * number * tokens * width),
        name="first_part",
    )(where, *blocks, *blocks, own, other)


def rest_kernel(where_ref, scaled_ref, own_ref, other_ref, *outs):
    slots = own_ref.shape[2]
    for place, out_ref in enumerate(outs):
        index = where_ref[4 + place]
        total = dot(own_ref[index], scaled_ref[:slots, :], NN)
        out_ref[...] = total + dot(other_ref[index], scaled_ref[slots:, :], NN)


def rest_parts(where, scaled, own, other, model, count, step):
    rows, width = scaled.shape
    units = own.shape[1]
    return pl.pallas_call(
        rest_kernel,
        out_shape=[jax.ShapeDtypeStruct((units, model), f32)] * count,
        grid_spec=pltpu.PrefetchScalarGridSpec(
            num_scalar_prefetch=1,
            grid=(pl.cdiv(width, step),),
            in_specs=[pl.BlockSpec((rows, step), lambda j, s: (0, j)), whole(), whole()],
            out_specs=[pl.BlockSpec((units, step), lambda j, s: (0, j))] * count,
        ),
        compiler_params=params(),
        cost_estimate=cost(2 * units * rows * model * count, 4 * count * units * model),
        name="rest_parts",
    )(where, scaled, own, other)


def back_kernel(distance, where_ref, rows_ref, gate_ref, own_ref, other_ref, before_ref, *refs):
    weights = refs[: len(refs) - 3]
    mine_ref, theirs_ref, sums_ref = refs[len(refs) - 3 :]
    model = weights[0].shape[1]
    slots = own_ref.shape[2]
    parts = own_ref.shape[0]
    sums_ref[...] = before_ref[...]
    for place, weight_ref in enumerate(weights):
        index = where_ref[0] + (distance if place == 1 else -distance)

        @pl.when(jnp.logical_and(index >= 0, index < parts))
        def _():
            for side, (hidden_ref, out_ref) in enumerate(((own_ref, mine_ref), (other_ref, theirs_ref))):
                here = slice(side * slots, (side + 1) * slots)
                product = dot(weight_ref[...], rows_ref[here, :model], NT)
                out_ref[place] = (product * gate_ref[0:1, here]).astype(bf16)
                sums_ref[0:1, here] += jnp.sum(
                    hidden_ref[index].astype(f32) * product, axis=0, keepdims=True
                )


def back_part(where, rows, gate_rows, own, other, before, weights, distance):
    units, slots = own.shape[1:]
    model = weights[0].shape[1]
    number = len(weights)
    half = jax.ShapeDtypeStruct((number, units, slots), bf16)
    return pl.pallas_call(
        functools.partial(back_kernel, distance),
        out_shape=(half, half, jax.ShapeDtypeStruct(before.shape, f32)),
        in_specs=[scalars()] + [whole()] * (5 + number),
        out_specs=(whole(),) * 3,
        compiler_params=params(),
        cost_estimate=cost(4 * units * slots * model, 2 * rows.size + 2 * number * units * model),
        name="back_part",
    )(where, rows, gate_rows, own, other, before, *weights)


def join_kernel(where_ref, *refs):
    out_ref = refs[-1]
    pairs = refs[:-1]
    units = pairs[0].shape[1]
    parts = out_ref.shape[1] // (2 * units)
    for distance in range(len(pairs) // 2):
        mine_ref, theirs_ref = pairs[2 * distance], pairs[2 * distance + 1]
        for place in range(mine_ref.shape[0]):
            index = where_ref[0] + (distance if place == 1 else -distance)

            @pl.when(jnp.logical_and(index >= 0, index < parts))
            def _():
                mine, theirs = mine_ref[place].astype(f32), theirs_ref[place].astype(f32)
                low = jnp.where(where_ref[1] == 0, mine, theirs)
                high = jnp.where(where_ref[1] == 0, theirs, mine)
                both = jnp.concatenate([low, high], axis=0)
                here = pl.ds(pl.multiple_of(index * 2 * units, LANES), 2 * units)
                out_ref[:, here] = both.T.astype(bf16)


def join_hidden(where, pairs, slots, hidden):
    flat = [array for pair in pairs for array in pair]
    return pl.pallas_call(
        join_kernel,
        out_shape=jax.ShapeDtypeStruct((slots, hidden), bf16),
        in_specs=[scalars()] + [whole()] * len(flat),
        out_specs=whole(),
        compiler_params=params(),
        cost_estimate=cost(0, 4 * slots * hidden),
        name="join_hidden",
    )(where, *flat)


def logits_kernel(gates_ref, ids_ref, grads_ref, out_ref):
    gates, ids, grads = gates_ref[...], ids_ref[...], grads_ref[...]
    picked = jnp.zeros_like(gates)
    for expert in range(grads.shape[0]):
        picked = picked + jnp.where(ids == expert, grads[expert : expert + 1, :], 0.0)
    out_ref[...] = gates * (picked - jnp.sum(gates * picked, axis=0, keepdims=True))


def logits_grad(gates, ids, grads):
    return pl.pallas_call(
        logits_kernel,
        out_shape=jax.ShapeDtypeStruct(gates.shape, f32),
        in_specs=[whole()] * 3,
        out_specs=whole(),
        name="logits_grad",
    )(gates, ids, grads)


def per_device_full(grad_out, top_logits, expert_ids, saved_hidden, w_down):
    experts = lax.axis_size("exp")
    groups = lax.axis_size("ctx")
    depth = groups // 2
    tokens, model = grad_out.shape
    slots, hidden = saved_hidden.shape[2:]
    units = w_down.shape[1]
    width = pl.cdiv(model + experts, LANES) * LANES
    step = 4 * LANES

    place = lax.axis_index("ctx")
    z, x = place // 2, place % 2
    me = lax.axis_index("exp")
    first = jnp.where(z < (depth + 1) // 2, depth - 1, 0)

    def swap_x(value):
        return lax.ppermute(value, "ctx", [(i, i ^ 1) for i in range(groups)])

    def swap_exp(value, bit):
        return lax.ppermute(value, "exp", [(i, i ^ bit) for i in range(experts)])

    def shift(value, way, sources):
        pairs = [(2 * s + i, 2 * (s + way) + i) for s in sources for i in range(2) if 0 <= s + way < depth]
        return lax.ppermute(value, "ctx", pairs)

    roles = []
    for turn in range(2, depth):
        roles.append(("right", turn, jnp.clip(z + depth - turn, 0, depth - 1)))
        roles.append(("left", turn, jnp.clip(z - depth + turn, 0, depth - 1)))
    roles.append(("own", depth, z))
    where = jnp.stack([z, x, me, first] + [role[2] for role in roles]).astype(jnp.int32)

    rows, gates = make_rows(grad_out, top_logits, expert_ids, width)
    own, other = split_hidden(where, saved_hidden[0, 0], depth, units)
    near, far = [rows], [swap_x(rows)]
    bit = experts // 2
    while bit:
        near = near + [swap_exp(block, bit) for block in near]
        far = far + [swap_exp(block, bit) for block in far]
        bit //= 2
    order = [0]
    bit = experts // 2
    while bit:
        order = order + [k ^ bit for k in order]
        bit //= 2
    near = [near[order.index(k)] for k in range(experts)]
    far = [far[order.index(k)] for k in range(experts)]
    other = swap_x(other)

    weight = w_down[0]
    gathered = [(weight,)]
    right = left = weight
    for turn in range(1, depth):
        right = shift(right, 1, range(turn - 1, depth))
        left = shift(left, -1, range(0, depth - turn + 1))
        gathered.append((right, left))

    sent, rows_all, scaled, gate_rows = first_part(where, near + far, own, other, model, step)
    rest = rest_parts(where, scaled, own, other, model, len(roles), step)
    parts = {role[:2]: part for role, part in zip(roles, rest)}
    right = shift(sent, 1, range(0, 1))
    left = shift(sent, -1, range(depth - 1, depth))
    for turn in range(2, depth):
        right = (parts["right", turn] + right.astype(f32)).astype(bf16)
        left = (parts["left", turn] + left.astype(f32)).astype(bf16)
        right = shift(right, 1, range(0, turn))
        left = shift(left, -1, range(depth - turn, depth))
    weight_grad = parts["own", depth] + right.astype(f32) + left.astype(f32)

    sums = jnp.zeros((8, 2 * slots), f32)
    pairs = []
    for distance, weights in enumerate(gathered):
        mine, theirs, sums = back_part(
            where, rows_all, gate_rows, own, other, sums, weights, distance
        )
        pairs.append((mine, swap_x(theirs)))
    hidden_grad = join_hidden(where, pairs, slots, hidden)
    slot_grad = sums[0:1, :slots] + swap_x(sums[0:1, slots:])
    grads = lax.all_to_all(
        slot_grad.reshape(experts, tokens), "exp", split_axis=0, concat_axis=0, tiled=True
    )
    logit_grad = logits_grad(gates, expert_ids.T, grads).T
    return (logit_grad, hidden_grad[None, None], weight_grad[None])


def routing_tables(expert_ids, count_experts, capacity):
    columns = jnp.arange(count_experts, dtype=jnp.int32)
    matches = expert_ids[:, :, None] == columns[None, None, :]
    per_token = jnp.sum(matches.astype(jnp.int32), axis=1)
    rank_table = jnp.cumsum(per_token, axis=0) - per_token
    slot_iota = jnp.arange(capacity, dtype=jnp.int32)
    select = (per_token.T[:, None, :] == 1) & (rank_table.T[:, None, :] == slot_iota[None, :, None])
    return (matches.astype(jnp.float32), select)


def per_device_routed(grad_out, top_logits, expert_ids, saved_hidden, w_down):
    count_experts = lax.axis_size("exp")
    slot_count = saved_hidden.shape[2]
    capacity = slot_count // count_experts
    model_width = grad_out.shape[1]
    onehot, select = routing_tables(expert_ids, count_experts, capacity)
    select_wide = select.astype(jnp.float32)
    gate_probs = jax.nn.softmax(top_logits, axis=-1)
    gate_sent = gate_probs.astype(jnp.bfloat16)
    gate_by_expert = jnp.sum(onehot * gate_sent.astype(jnp.float32)[:, :, None], axis=1)
    send_rows = jnp.einsum(
        "ect,td->ecd", select.astype(jnp.bfloat16), grad_out, preferred_element_type=jnp.float32
    ).astype(jnp.bfloat16)
    send_gate = jnp.sum(select_wide * gate_by_expert.T[:, None, :], axis=2).astype(jnp.bfloat16)
    hidden = saved_hidden[0, 0]
    rows_in, gate_in = (
        lax.all_to_all(send_rows, "exp", split_axis=0, concat_axis=0, tiled=True),
        lax.all_to_all(send_gate, "exp", split_axis=0, concat_axis=0, tiled=True),
    )
    flat_rows = rows_in.reshape(slot_count, model_width)
    backprop = lax.dot_general(
        flat_rows,
        lax.all_gather(w_down[0], "ctx", axis=0, tiled=True),
        (((1,), (1,)), ((), ())),
        preferred_element_type=jnp.float32,
    )
    flat_gate = gate_in.reshape(slot_count, 1).astype(jnp.float32)
    hidden_grad = (flat_gate * backprop).astype(jnp.bfloat16)
    slot_grad = jnp.sum(hidden.astype(jnp.float32) * backprop, axis=1)
    scaled = (flat_gate * flat_rows.astype(jnp.float32)).astype(jnp.bfloat16)
    partial_grad = lax.dot_general(
        hidden, scaled, (((0,), (0,)), ((), ())), preferred_element_type=jnp.float32
    )
    weight_grad = lax.psum_scatter(partial_grad, "ctx", scatter_dimension=0, tiled=True)
    returned = lax.all_to_all(
        slot_grad.reshape(count_experts, capacity), "exp", split_axis=0, concat_axis=0, tiled=True
    )
    grad_by_expert = jnp.sum(select_wide * returned[:, :, None], axis=1)
    gate_grad = jnp.sum(onehot * grad_by_expert.T[:, None, :], axis=2)
    logit_grad = gate_probs * (gate_grad - jnp.sum(gate_probs * gate_grad, axis=1, keepdims=True))
    return (logit_grad, hidden_grad.reshape(1, 1, slot_count, -1), weight_grad[None])


def per_device(grad_out, top_logits, expert_ids, saved_hidden, w_down):
    experts = lax.axis_size("exp")
    groups = lax.axis_size("ctx")
    everywhere = top_logits.shape[1] == experts and saved_hidden.shape[2] == experts * grad_out.shape[0]
    plain = experts & (experts - 1) == 0 and groups % 2 == 0 and groups >= 4
    body = per_device_full if everywhere and plain else per_device_routed
    return body(grad_out, top_logits, expert_ids, saved_hidden, w_down)


def solution(mesh):
    return jax.shard_map(
        per_device,
        mesh=mesh,
        in_specs=(
            P(("ctx", "exp"), None),
            P(("ctx", "exp"), None),
            P(("ctx", "exp"), None),
            P("ctx", "exp", None, None),
            P("exp", "ctx", None),
        ),
        out_specs=(P(("ctx", "exp"), None), P("ctx", "exp", None, None), P("exp", "ctx", None)),
        check_vma=False,
    )
```

```python
import functools

import jax
import jax.numpy as jnp
import numpy as np
from jax import lax
from jax.experimental import pallas as pl
from jax.experimental.pallas import tpu as pltpu
from jax.sharding import PartitionSpec as P

LANES = 128
NT = (((1,), (1,)), ((), ()))
NN = (((1,), (0,)), ((), ()))
f32 = jnp.float32
bf16 = jnp.bfloat16


def dot(a, b, dims):
    return lax.dot_general(a, b, dims, preferred_element_type=f32)


def anywhere():
    return pl.BlockSpec(memory_space=pl.ANY)


def whole():
    return pl.BlockSpec(memory_space=pltpu.VMEM)


def scalars():
    return pl.BlockSpec(memory_space=pltpu.SMEM)


def params(mib):
    return pltpu.CompilerParams(vmem_limit_bytes=mib * 1024 * 1024)


def small():
    return pl.CostEstimate(flops=0, bytes_accessed=0, transcendentals=0)


def rows_kernel(width, grad_ref, logits_ref, ids_ref, rows_ref, gates_ref):
    model, tokens = grad_ref.shape
    count = logits_ref.shape[0]
    logits = logits_ref[...]
    powers = jnp.exp(logits - jnp.max(logits, axis=0, keepdims=True))
    gates = powers / jnp.sum(powers, axis=0, keepdims=True)
    gates_ref[...] = gates
    sent = gates.astype(bf16).astype(f32)
    ids = ids_ref[...]
    tail = width - model
    row = lax.broadcasted_iota(jnp.int32, (tail, tokens), 0)
    extra = jnp.zeros((tail, tokens), f32)
    for expert in range(count):
        chosen = jnp.sum(jnp.where(ids == expert, sent, 0.0), axis=0, keepdims=True)
        extra = extra + jnp.where(row == expert, chosen, 0.0)
    for start in range(0, width, LANES):
        stop = start + LANES
        if stop <= model:
            block = grad_ref[start:stop, :].astype(f32)
        elif start >= model:
            block = extra[start - model : stop - model, :]
        else:
            block = jnp.concatenate(
                [grad_ref[start:model, :].astype(f32), extra[: stop - model, :]], axis=0
            )
        rows_ref[:, start:stop] = block.T.astype(bf16)


def make_rows(grad_out, top_logits, expert_ids, width):
    tokens, model = grad_out.shape
    count = top_logits.shape[1]
    return pl.pallas_call(
        functools.partial(rows_kernel, width),
        out_shape=(
            jax.ShapeDtypeStruct((tokens, width), bf16),
            jax.ShapeDtypeStruct((count, tokens), f32),
        ),
        in_specs=[whole()] * 3,
        out_specs=(whole(), whole()),
        compiler_params=params(16),
        cost_estimate=small(),
        name="make_rows",
    )(grad_out.T, top_logits.T, expert_ids.T)


def chain_plan(depth):
    products, weights = [], []
    for z in range(depth):
        uses = []
        for turn in range(2, depth + 1):
            if z < depth - 1 and turn >= z + 2:
                uses.append((turn, "AB"[z % 2], depth + 1 + z - turn))
            if z > 0 and turn >= depth - z + 1:
                uses.append((turn, "BA"[z % 2], z + turn - depth - 1))
        products.append(sorted(uses) + [(depth + 1, "own", z)])
        brought = {}
        for turn in range(1, depth):
            for name in "AB":
                index = z + turn if (name == "A") == (z % 2 == 0) else z - turn
                brought[turn, name] = index if 0 <= index < depth else -1
        weights.append(brought)
    return products, weights


class Scalars:
    def __init__(self):
        self.columns = []
        self.names = {}

    def add(self, name, values):
        self.names[name] = len(self.columns)
        self.columns.append(values)

    def __getitem__(self, name):
        return self.names[name]

    def row(self, place, me):
        return jnp.asarray(np.stack(self.columns, axis=-1).astype(np.int32))[place, me]


def device_scalars(depth, experts):
    products, weights = chain_plan(depth)
    table = Scalars()
    along = np.arange(2 * depth)[:, None] + np.zeros((1, experts), np.int32)

    def by_z(values):
        return np.asarray(values)[along // 2]

    table.add("x", along % 2)
    table.add("me", np.zeros_like(along) + np.arange(experts)[None, :])
    table.add(("shard", 0, "own"), along // 2)
    slot_of = [{use[2]: slot for slot, use in enumerate(products[z])} for z in range(depth)]
    for part in range(depth):
        table.add(("slot of", part), by_z([slot_of[z][part] for z in range(depth)]))
    table.add(("slot", 0, "own"), by_z([slot_of[z][z] for z in range(depth)]))
    for turn in range(1, depth):
        for name in "AB":
            shard = [weights[z][turn, name] for z in range(depth)]
            table.add(("shard", turn, name), by_z(shard))
            table.add(("slot", turn, name), by_z([slot_of[z].get(k, 0) for z, k in enumerate(shard)]))
    uses = {}
    for turn in range(2, depth + 1):
        for name in "AB":
            slots = [-1] * depth
            for z in range(depth):
                for slot, use in enumerate(products[z]):
                    if use[:2] == (turn, name):
                        slots[z] = slot
            uses[turn, name] = slots
            table.add(("use", turn, name), by_z(slots))
            table.add(("block", turn, name), by_z([max(slot - 1, 0) for slot in slots]))
    return table, weights, uses


def hold_kernel(*refs):
    del refs


def hold(values, after):
    return pl.pallas_call(
        hold_kernel,
        out_shape=tuple(jax.ShapeDtypeStruct(value.shape, value.dtype) for value in values),
        in_specs=[anywhere()] * (len(values) + len(after)),
        out_specs=(anywhere(),) * len(values),
        input_output_aliases={place: place for place in range(len(values))},
        cost_estimate=small(),
        name="hold",
    )(*values, *after)


def split_kernel(table, where_ref, hidden_ref, *refs):
    own_ref, first_ref, rest_ref = refs[-3:]
    parts, units, _ = own_ref.shape
    row = lax.broadcasted_iota(jnp.int32, (2 * units, 2 * units), 0)
    column = lax.broadcasted_iota(jnp.int32, (2 * units, 2 * units), 1)
    unit = jnp.where(row == column, 1.0, 0.0).astype(bf16)
    low = where_ref[table["x"]] == 0
    for part in range(parts):
        block = hidden_ref[:, part * 2 * units : (part + 1) * 2 * units]
        turned = dot(unit, block, NT).astype(bf16)
        slot = where_ref[table["slot of", part]]
        other = jnp.where(low, turned[units:], turned[:units])
        own_ref[slot] = jnp.where(low, turned[:units], turned[units:])

        @pl.when(slot == 0)
        def _():
            first_ref[0] = other

        @pl.when(slot != 0)
        def _():
            rest_ref[slot - 1] = other


def split_hidden(table, where, hidden, parts, units, after):
    slots = hidden.shape[0]
    return pl.pallas_call(
        functools.partial(split_kernel, table),
        out_shape=tuple(
            jax.ShapeDtypeStruct((count, units, slots), bf16) for count in (parts, 1, parts - 1)
        ),
        in_specs=[scalars(), whole()] + [anywhere()] * len(after),
        out_specs=(whole(),) * 3,
        compiler_params=params(16),
        cost_estimate=small(),
        name="split_hidden",
    )(where, hidden, *after)


def place_of(place, count, me, tokens):
    start = (place // count) * count * tokens + ((place % count) ^ me) * tokens
    return pl.multiple_of(start, tokens)


def products_kernel(table, model, count, number, first, where_ref, *refs):
    blocks, gate_tiles = refs[:number], refs[number : 2 * number]
    own_ref, other_ref = refs[2 * number : 2 * number + 2]
    column, scaled, stacked = refs[-3:]
    tokens, step = blocks[0].shape
    slots = count * tokens
    me = where_ref[table["me"]]
    shift = model % LANES
    shards = other_ref.shape[0]
    units = other_ref.shape[1]
    offset = own_ref.shape[0] - shards if not first else 0

    @pl.when(pl.program_id(0) == 0)
    def _():
        lane = lax.broadcasted_iota(jnp.int32, (tokens, LANES), 1)
        for place in range(number):
            here = pl.ds(place_of(place, count, me, tokens), tokens)
            picked = jnp.where(lane == shift + me, gate_tiles[place][...].astype(f32), 0.0)
            total = jnp.sum(picked, axis=1, keepdims=True)
            column[here, :] = jnp.broadcast_to(total, (tokens, LANES))
        for shard in range(shards):
            stacked[shard * units : (shard + 1) * units, :slots] = own_ref[offset + shard]
            stacked[shard * units : (shard + 1) * units, slots:] = other_ref[shard]

    for place in range(number):
        here = pl.ds(place_of(place, count, me, tokens), tokens)
        scaled[here, :] = (blocks[place][...].astype(f32) * column[here, 0:1]).astype(bf16)
    total = dot(stacked[...], scaled[...], NN)
    if first:
        coming_ref = refs[2 * number + 2]
        sent_ref, kept_ref = refs[-5:-3]
        kept_ref[0] = total
        flag = where_ref[table["use", 2, "A"]] == 0
        sent_ref[...] = (coming_ref[...].astype(f32) + jnp.where(flag, total, 0.0)).astype(bf16)
    else:
        kept_ref = refs[-4]
        for shard in range(shards):
            kept_ref[shard] = total[shard * units : (shard + 1) * units]


def products(table, where, blocks, own, other, model, step, coming, after, name):
    tokens, width = blocks[0].shape
    number = len(blocks)
    shards, units, _ = other.shape
    first = coming is not None
    tile_spec = pl.BlockSpec((tokens, LANES), lambda j, s: (0, model // LANES))
    block_spec = pl.BlockSpec((tokens, step), lambda j, s: (0, j))
    flat_spec = pl.BlockSpec((units, step), lambda j, s: (0, j))
    kept_spec = pl.BlockSpec((shards, units, step), lambda j, s: (0, 0, j))
    kept = jax.ShapeDtypeStruct((shards, units, model), f32)
    return pl.pallas_call(
        functools.partial(products_kernel, table, model, number // 2, number, first),
        out_shape=(jax.ShapeDtypeStruct((units, model), bf16), kept) if first else kept,
        grid_spec=pltpu.PrefetchScalarGridSpec(
            num_scalar_prefetch=1,
            grid=(pl.cdiv(model, step),),
            in_specs=[block_spec] * number
            + [tile_spec] * number
            + [whole()] * 2
            + ([flat_spec] if first else [])
            + [anywhere()] * len(after),
            out_specs=(flat_spec, kept_spec) if first else kept_spec,
            scratch_shapes=[
                pltpu.VMEM((number * tokens, LANES), f32),
                pltpu.VMEM((number * tokens, step), bf16),
                pltpu.VMEM((shards * units, number * tokens), bf16),
            ],
        ),
        compiler_params=params(24),
        cost_estimate=small(),
        name=name,
    )(where, *blocks, *blocks, own, other, *([coming] if first else []), *after)


def combine_kernel(table, key, sides, where_ref, coming_ref, *refs):
    slot = where_ref[table[key]]
    out_ref = refs[-1]
    total = coming_ref[...].astype(f32)
    for ref, side in zip(refs, sides):
        flag = slot == 0 if side == "first" else slot > 0
        total = total + jnp.where(flag, ref[0], 0.0)
    out_ref[...] = total.astype(bf16)


def combine(table, where, coming, first, rest, turn, name, used, after):
    units, model = coming.shape
    step = pl.cdiv(pl.cdiv(model, 2), LANES) * LANES
    column = table["block", turn, name]
    flat = pl.BlockSpec((units, step), lambda j, s: (0, j))
    sides, operands, specs = [], [], []
    if any(slot == 0 for slot in used):
        sides, operands = ["first"], [first]
        specs = [pl.BlockSpec((1, units, step), lambda j, s: (0, 0, j))]
    if any(slot > 0 for slot in used):
        sides, operands = sides + ["rest"], operands + [rest]
        specs = specs + [pl.BlockSpec((1, units, step), lambda j, s: (s[column], 0, j))]
    return pl.pallas_call(
        functools.partial(combine_kernel, table, ("use", turn, name), sides),
        out_shape=jax.ShapeDtypeStruct((units, model), bf16),
        grid_spec=pltpu.PrefetchScalarGridSpec(
            num_scalar_prefetch=1,
            grid=(pl.cdiv(model, step),),
            in_specs=[flat] + specs + [anywhere()] * len(after),
            out_specs=flat,
        ),
        compiler_params=params(16),
        cost_estimate=small(),
        name="combine",
    )(where, coming, *operands, *after)


def total_kernel(a_ref, b_ref, kept_ref, out_ref):
    out_ref[0] = kept_ref[0] + a_ref[...].astype(f32) + b_ref[...].astype(f32)


def total_grad(a, b, rest):
    units, model = a.shape
    last = rest.shape[0] - 1
    step = pl.cdiv(pl.cdiv(model, 2), LANES) * LANES
    flat = pl.BlockSpec((units, step), lambda j: (0, j))
    return pl.pallas_call(
        total_kernel,
        out_shape=jax.ShapeDtypeStruct((1, units, model), f32),
        grid=(pl.cdiv(model, step),),
        in_specs=[flat, flat, pl.BlockSpec((1, units, step), lambda j: (last, 0, j))],
        out_specs=pl.BlockSpec((1, units, step), lambda j: (0, 0, j)),
        compiler_params=params(16),
        cost_estimate=small(),
        name="total_grad",
    )(a, b, rest)


def back_kernel(table, model, count, choices, guard, summed, where_ref, *refs):
    number = 2 * count
    keys = [key for choice in choices for key in choice]
    blocks = refs[:number]
    own_ref, first_ref, rest_ref = refs[number : number + 3]
    weight_refs = dict(zip(keys, refs[number + 3 : number + 3 + len(keys)]))
    before_ref = refs[number + 3 + len(keys)] if summed else None
    mine_ref, theirs_ref, sums_ref = refs[-3:]
    tokens = blocks[0].shape[0]
    units = own_ref.shape[1]
    me = where_ref[table["me"]]
    shift = model % LANES
    start = (model // LANES) * LANES
    eight = lax.broadcasted_iota(jnp.int32, (8, LANES), 1)
    onehot = jnp.where(eight == shift + me, 1.0, 0.0).astype(bf16)
    shards = {key: where_ref[table[("shard",) + key]] for key in keys}
    slots = {key: where_ref[table[("slot",) + key]] for key in keys}
    sums_ref[...] = before_ref[...] if summed else jnp.zeros(sums_ref.shape, f32)

    def work():
        stack, here_valid, here_slot = [], [], []
        for choice in choices:
            weight, valid, slot = weight_refs[choice[0]][...], shards[choice[0]] >= 0, slots[choice[0]]
            for key in choice[1:]:
                weight = jnp.where(valid, weight, weight_refs[key][...])
                slot = jnp.where(valid, slot, slots[key])
                valid = jnp.logical_or(valid, shards[key] >= 0)
            stack.append(weight)
            here_valid.append(valid)
            here_slot.append(slot)
        weight = jnp.concatenate(stack, axis=0) if len(stack) > 1 else stack[0]
        for pair in range(0, number, 2):
            both = jnp.concatenate([blocks[pair][:, :model], blocks[pair + 1][:, :model]], axis=0)
            product = dot(weight, both, NT)
            for half in range(2):
                place = pair + half
                block = product[:, half * tokens : (half + 1) * tokens]
                gate = dot(onehot, blocks[place][:, start : start + LANES], NT)[0:1]
                lanes = place_of(place % count, count, me, tokens)
                wide = place_of(place, count, me, tokens)
                out_ref = mine_ref if place < count else theirs_ref
                gated = (block * gate).astype(bf16)
                total = jnp.zeros((1, tokens), f32)
                for index, (valid, slot) in enumerate(zip(here_valid, here_slot)):
                    some = slice(index * units, (index + 1) * units)
                    out_ref[index, :, pl.ds(lanes, tokens)] = gated[some]
                    if place < count:
                        hidden = own_ref[slot, :, pl.ds(lanes, tokens)].astype(f32)
                    else:
                        hidden = jnp.where(
                            slot == 0,
                            first_ref[0, :, pl.ds(lanes, tokens)].astype(f32),
                            rest_ref[jnp.maximum(slot - 1, 0), :, pl.ds(lanes, tokens)].astype(f32),
                        )
                    part = jnp.sum(hidden * block[some], axis=0, keepdims=True)
                    total = total + jnp.where(valid, part, 0.0)
                sums_ref[0:1, pl.ds(wide, tokens)] += total

    if guard:
        some = functools.reduce(jnp.logical_or, [shards[key] >= 0 for key in keys])
        pl.when(some)(work)
    else:
        work()


def back_part(table, where, blocks, own, first, rest, choices, weights, before, guard, after, model):
    units, slots = own.shape[1:]
    keys = [key for choice in choices for key in choice]
    count = len(blocks) // 2
    half = jax.ShapeDtypeStruct((len(choices), units, slots), bf16)
    summed = before is not None
    operands = [*blocks, own, first, rest, *[weights[key] for key in keys]] + ([before] if summed else [])
    return pl.pallas_call(
        functools.partial(back_kernel, table, model, count, choices, guard, summed),
        out_shape=(half, half, jax.ShapeDtypeStruct((8, 2 * slots), f32)),
        in_specs=[scalars()] + [whole()] * len(operands) + [anywhere()] * len(after),
        out_specs=(whole(),) * 3,
        compiler_params=params(32),
        cost_estimate=small(),
        name="back_part",
    )(where, *operands, *after)


def join_kernel(table, groups, extends, where_ref, *refs):
    out_ref, turned, sem = refs[-3:]
    slots, _, width = turned.shape[1], turned.shape[0], turned.shape[2]
    units = width // 2
    row = lax.broadcasted_iota(jnp.int32, (slots, slots), 0)
    column = lax.broadcasted_iota(jnp.int32, (slots, slots), 1)
    unit = jnp.where(row == column, 1.0, 0.0).astype(bf16)
    low = where_ref[table["x"]] == 0
    copies = []
    total = 0
    for number, choices in enumerate(groups):
        mine_ref, theirs_ref = refs[2 * number], refs[2 * number + 1]
        for place, choice in enumerate(choices):
            index = where_ref[table[("shard",) + choice[0]]]
            for key in choice[1:]:
                index = jnp.where(index >= 0, index, where_ref[table[("shard",) + key]])
            mine, theirs = mine_ref[place], theirs_ref[place]
            both = jnp.concatenate(
                [jnp.where(low, mine, theirs), jnp.where(low, theirs, mine)], axis=0
            )
            turned[total] = dot(unit, both, NT).astype(bf16)
            here = pl.ds(pl.multiple_of(jnp.maximum(index, 0) * width, LANES), width)
            copy = pltpu.make_async_copy(turned.at[total], out_ref.at[:, here], sem.at[total])
            copies.append((index, copy))

            @pl.when(index >= 0)
            def _():
                copy.start()

            total += 1
    for index, copy in copies:
        pl.when(index >= 0)(copy.wait)


def join_hidden(table, where, groups, pairs, slots, hidden, before):
    flat = [array for pair in pairs for array in pair]
    units = flat[0].shape[1]
    total = sum(len(choices) for choices in groups)
    extends = before is not None
    return pl.pallas_call(
        functools.partial(join_kernel, table, groups, extends),
        out_shape=jax.ShapeDtypeStruct((slots, hidden), bf16),
        in_specs=[scalars()] + [whole()] * len(flat) + [anywhere()] * extends,
        out_specs=anywhere(),
        scratch_shapes=[
            pltpu.VMEM((total, slots, 2 * units), bf16),
            pltpu.SemaphoreType.DMA((total,)),
        ],
        input_output_aliases={1 + len(flat): 0} if extends else {},
        compiler_params=params(24),
        cost_estimate=small(),
        name="join_hidden",
    )(where, *flat, *([before] if extends else []))


def logits_kernel(gates_ref, ids_ref, grads_ref, out_ref):
    gates, ids, grads = gates_ref[...], ids_ref[...], grads_ref[...]
    picked = jnp.zeros_like(gates)
    for expert in range(grads.shape[0]):
        picked = picked + jnp.where(ids == expert, grads[expert : expert + 1, :], 0.0)
    out_ref[...] = gates * (picked - jnp.sum(gates * picked, axis=0, keepdims=True))


def logits_grad(gates, ids, grads):
    return pl.pallas_call(
        logits_kernel,
        out_shape=jax.ShapeDtypeStruct(gates.shape, f32),
        in_specs=[whole()] * 3,
        out_specs=whole(),
        cost_estimate=small(),
        name="logits_grad",
    )(gates, ids, grads)


def per_device_full(grad_out, top_logits, expert_ids, saved_hidden, w_down):
    experts = lax.axis_size("exp")
    groups = lax.axis_size("ctx")
    depth = groups // 2
    tokens, model = grad_out.shape
    slots, hidden = saved_hidden.shape[2:]
    units = w_down.shape[1]
    width = pl.cdiv(model + experts, LANES) * LANES
    step = 4 * LANES

    table, brought, uses = device_scalars(depth, experts)
    where = table.row(lax.axis_index("ctx"), lax.axis_index("exp"))

    def swap_x(value):
        return lax.ppermute(value, "ctx", [(i, i ^ 1) for i in range(groups)])

    def swap_exp(value, bit):
        return lax.ppermute(value, "exp", [(i, i ^ bit) for i in range(experts)])

    def swap_z(value, name):
        first = "AB".index(name)
        pairs = []
        for z in range(first, depth - 1, 2):
            for x in range(2):
                pairs += [(2 * z + x, 2 * z + 2 + x), (2 * z + 2 + x, 2 * z + x)]
        return lax.ppermute(value, "ctx", pairs)

    got = {(0, "own"): w_down[0]}
    for name in "AB":
        got[1, name] = swap_z(w_down[0], name)
    got[2, "B"] = swap_z(got[1, "A"], "B")

    rows, gates = make_rows(grad_out, top_logits, expert_ids, width)
    own, other_first, other_rest = split_hidden(table, where, saved_hidden[0, 0], depth, units, [rows])
    across, other_first, other_rest = hold((swap_x(rows), other_first, other_rest), [])
    other_first, other_rest = swap_x(other_first), swap_x(other_rest)
    near, far, order = [rows], [across], [0]
    bit = experts // 2
    while bit:
        fresh = [swap_exp(block, bit) for block in near]
        if len(near) == 1:
            fresh = list(hold(fresh, [got[1, "A"], got[1, "B"]]))
        near = near + fresh
        distant = [swap_exp(block, bit) for block in far]
        if len(far) == 1:
            distant = list(hold(distant, [other_first, other_rest]))
        far = far + distant
        order = order + [k ^ bit for k in order]
        bit //= 2
    blocks = [near[order.index(k)] for k in range(experts)]
    blocks += [far[order.index(k)] for k in range(experts)]

    sent, kept_first = products(
        table, where, blocks, own, other_first, model, step, got[1, "B"], [other_rest], "first_product"
    )
    got[2, "A"] = swap_z(sent, "A")
    kept_rest = products(
        table, where, blocks, own, other_rest, model, step, None, [sent], "other_products"
    )

    groups_of = [[[(0, "own")], [(1, "A")], [(1, "B")]]]
    pairs = []

    def backprop(choices, before, guard, after):
        mine, theirs, sums = back_part(
            table, where, blocks, own, other_first, other_rest, choices, got, before, guard, after, model
        )
        pairs.append((mine, swap_x(theirs)))
        return sums

    sums = backprop(groups_of[0], None, False, [kept_rest])
    marker = sums
    for turn in range(3, depth + 1):
        for name, back in (("A", "B"), ("B", "A")):
            used = uses[turn, name]
            value = combine(
                table, where, got[turn - 1, back], kept_first, kept_rest, turn, name, used, [marker]
            )
            marker = value
            got[turn, name] = swap_z(value, name)
        last = turn - 1
        both = any(b[last, "A"] >= 0 and b[last, "B"] >= 0 for b in brought)
        choices = [[(last, "A")], [(last, "B")]] if both else [[(last, "A"), (last, "B")]]
        groups_of.append(choices)
        sums = backprop(choices, sums, not both, [marker])
        marker = sums
    weight_grad = total_grad(got[depth, "A"], got[depth, "B"], kept_rest)

    hidden_grad = join_hidden(table, where, groups_of, pairs, slots, hidden, None)
    slot_grad = sums[0:1, :slots] + swap_x(sums[0:1, slots:])
    grads = lax.all_to_all(
        slot_grad.reshape(experts, tokens), "exp", split_axis=0, concat_axis=0, tiled=True
    )
    logit_grad = logits_grad(gates, expert_ids.T, grads).T
    return (logit_grad, hidden_grad[None, None], weight_grad)


def routing_tables(expert_ids, count_experts, capacity):
    columns = jnp.arange(count_experts, dtype=jnp.int32)
    matches = expert_ids[:, :, None] == columns[None, None, :]
    per_token = jnp.sum(matches.astype(jnp.int32), axis=1)
    rank_table = jnp.cumsum(per_token, axis=0) - per_token
    slot_iota = jnp.arange(capacity, dtype=jnp.int32)
    select = (per_token.T[:, None, :] == 1) & (rank_table.T[:, None, :] == slot_iota[None, :, None])
    return (matches.astype(jnp.float32), select)


def per_device_routed(grad_out, top_logits, expert_ids, saved_hidden, w_down):
    count_experts = lax.axis_size("exp")
    slot_count = saved_hidden.shape[2]
    capacity = slot_count // count_experts
    model_width = grad_out.shape[1]
    onehot, select = routing_tables(expert_ids, count_experts, capacity)
    select_wide = select.astype(jnp.float32)
    gate_probs = jax.nn.softmax(top_logits, axis=-1)
    gate_sent = gate_probs.astype(jnp.bfloat16)
    gate_by_expert = jnp.sum(onehot * gate_sent.astype(jnp.float32)[:, :, None], axis=1)
    send_rows = jnp.einsum(
        "ect,td->ecd", select.astype(jnp.bfloat16), grad_out, preferred_element_type=jnp.float32
    ).astype(jnp.bfloat16)
    send_gate = jnp.sum(select_wide * gate_by_expert.T[:, None, :], axis=2).astype(jnp.bfloat16)
    hidden = saved_hidden[0, 0]
    rows_in, gate_in = (
        lax.all_to_all(send_rows, "exp", split_axis=0, concat_axis=0, tiled=True),
        lax.all_to_all(send_gate, "exp", split_axis=0, concat_axis=0, tiled=True),
    )
    flat_rows = rows_in.reshape(slot_count, model_width)
    backprop = lax.dot_general(
        flat_rows,
        lax.all_gather(w_down[0], "ctx", axis=0, tiled=True),
        (((1,), (1,)), ((), ())),
        preferred_element_type=jnp.float32,
    )
    flat_gate = gate_in.reshape(slot_count, 1).astype(jnp.float32)
    hidden_grad = (flat_gate * backprop).astype(jnp.bfloat16)
    slot_grad = jnp.sum(hidden.astype(jnp.float32) * backprop, axis=1)
    scaled = (flat_gate * flat_rows.astype(jnp.float32)).astype(jnp.bfloat16)
    partial_grad = lax.dot_general(
        hidden, scaled, (((0,), (0,)), ((), ())), preferred_element_type=jnp.float32
    )
    weight_grad = lax.psum_scatter(partial_grad, "ctx", scatter_dimension=0, tiled=True)
    returned = lax.all_to_all(
        slot_grad.reshape(count_experts, capacity), "exp", split_axis=0, concat_axis=0, tiled=True
    )
    grad_by_expert = jnp.sum(select_wide * returned[:, :, None], axis=1)
    gate_grad = jnp.sum(onehot * grad_by_expert.T[:, None, :], axis=2)
    logit_grad = gate_probs * (gate_grad - jnp.sum(gate_probs * gate_grad, axis=1, keepdims=True))
    return (logit_grad, hidden_grad.reshape(1, 1, slot_count, -1), weight_grad[None])


def per_device(grad_out, top_logits, expert_ids, saved_hidden, w_down):
    experts = lax.axis_size("exp")
    groups = lax.axis_size("ctx")
    everywhere = top_logits.shape[1] == experts and saved_hidden.shape[2] == experts * grad_out.shape[0]
    plain = experts & (experts - 1) == 0 and groups % 4 == 0 and groups >= 8
    body = per_device_full if everywhere and plain else per_device_routed
    return body(grad_out, top_logits, expert_ids, saved_hidden, w_down)


def solution(mesh):
    return jax.shard_map(
        per_device,
        mesh=mesh,
        in_specs=(
            P(("ctx", "exp"), None),
            P(("ctx", "exp"), None),
            P(("ctx", "exp"), None),
            P("ctx", "exp", None, None),
            P("exp", "ctx", None),
        ),
        out_specs=(P(("ctx", "exp"), None), P("ctx", "exp", None, None), P("exp", "ctx", None)),
        check_vma=False,
    )
```

```python
import functools

import jax
import jax.numpy as jnp
import numpy as np
from jax import lax
from jax.experimental import pallas as pl
from jax.experimental.pallas import tpu as pltpu
from jax.sharding import PartitionSpec as P

LANES = 128
SCALE = 3_000_000
NT = (((1,), (1,)), ((), ()))
NN = (((1,), (0,)), ((), ()))
f32 = jnp.float32
bf16 = jnp.bfloat16


def dot(a, b, dims):
    return lax.dot_general(a, b, dims, preferred_element_type=f32)


def anywhere():
    return pl.BlockSpec(memory_space=pl.ANY)


def whole():
    return pl.BlockSpec(memory_space=pltpu.VMEM)


def scalars():
    return pl.BlockSpec(memory_space=pltpu.SMEM)


def params():
    return pltpu.CompilerParams(vmem_limit_bytes=24 * 1024 * 1024)


def taking(microseconds):
    return pl.CostEstimate(flops=0, bytes_accessed=int(microseconds * SCALE), transcendentals=0)


def chain_plan(depth):
    products, weights = [], []
    for z in range(depth):
        uses = []
        for turn in range(2, depth + 1):
            if z < depth - 1 and turn >= z + 2:
                uses.append((turn, "AB"[z % 2], depth + 1 + z - turn))
            if z > 0 and turn >= depth - z + 1:
                uses.append((turn, "BA"[z % 2], z + turn - depth - 1))
        products.append(sorted(uses) + [(depth + 1, "own", z)])
        brought = {}
        for turn in range(1, depth):
            for name in "AB":
                index = z + turn if (name == "A") == (z % 2 == 0) else z - turn
                brought[turn, name] = index if 0 <= index < depth else -1
        weights.append(brought)
    return products, weights


class Scalars:
    def __init__(self):
        self.columns = []
        self.names = {}

    def add(self, name, values):
        self.names[name] = len(self.columns)
        self.columns.append(values)

    def __getitem__(self, name):
        return self.names[name]

    def row(self, place, me):
        return jnp.asarray(np.stack(self.columns, axis=-1).astype(np.int32))[place, me]


def device_scalars(depth, experts):
    products, weights = chain_plan(depth)
    table = Scalars()
    along = np.arange(2 * depth)[:, None] + np.zeros((1, experts), np.int32)

    def by_z(values):
        return np.asarray(values)[along // 2]

    table.add("x", along % 2)
    table.add("me", np.zeros_like(along) + np.arange(experts)[None, :])
    table.add(("shard", 0, "own"), along // 2)
    slot_of = [{use[2]: slot for slot, use in enumerate(products[z])} for z in range(depth)]
    for part in range(depth):
        table.add(("slot of", part), by_z([slot_of[z][part] for z in range(depth)]))
    table.add(("slot", 0, "own"), by_z([slot_of[z][z] for z in range(depth)]))
    for turn in range(1, depth):
        for name in "AB":
            shard = [weights[z][turn, name] for z in range(depth)]
            table.add(("shard", turn, name), by_z(shard))
            table.add(("slot", turn, name), by_z([slot_of[z].get(k, 0) for z, k in enumerate(shard)]))
    uses = {}
    for turn in range(2, depth + 1):
        for name in "AB":
            slots = [-1] * depth
            for z in range(depth):
                for slot, use in enumerate(products[z]):
                    if use[:2] == (turn, name):
                        slots[z] = slot
            uses[turn, name] = slots
            table.add(("use", turn, name), by_z(slots))
            limit = max(depth - 3, 0)
            table.add(("block", turn, name), by_z([min(max(slot - 1, 0), limit) for slot in slots]))
    return table, weights, uses


def rows_kernel(cut, grad_ref, logits_ref, ids_ref, late_ref, early_ref, gates_ref):
    model, tokens = grad_ref.shape
    count = logits_ref.shape[0]
    width = cut + late_ref.shape[1]
    logits = logits_ref[...]
    powers = jnp.exp(logits - jnp.max(logits, axis=0, keepdims=True))
    gates = powers / jnp.sum(powers, axis=0, keepdims=True)
    gates_ref[...] = gates
    sent = gates.astype(bf16).astype(f32)
    ids = ids_ref[...]
    row = lax.broadcasted_iota(jnp.int32, (width - model, tokens), 0)
    extra = jnp.zeros((width - model, tokens), f32)
    for expert in range(count):
        chosen = jnp.sum(jnp.where(ids == expert, sent, 0.0), axis=0, keepdims=True)
        extra = extra + jnp.where(row == expert, chosen, 0.0)
    for start in range(0, width, LANES):
        stop = start + LANES
        if stop <= model:
            block = grad_ref[start:stop, :].astype(f32)
        elif start >= model:
            block = extra[start - model : stop - model, :]
        else:
            block = jnp.concatenate(
                [grad_ref[start:model, :].astype(f32), extra[: stop - model, :]], axis=0
            )
        turned = block.T.astype(bf16)
        if start < cut:
            early_ref[:, start:stop] = turned
        else:
            late_ref[:, start - cut : stop - cut] = turned


def make_rows(grad_out, top_logits, expert_ids, width, cut):
    tokens, model = grad_out.shape
    count = top_logits.shape[1]
    return pl.pallas_call(
        functools.partial(rows_kernel, cut),
        out_shape=(
            jax.ShapeDtypeStruct((tokens, width - cut), bf16),
            jax.ShapeDtypeStruct((tokens, cut), bf16),
            jax.ShapeDtypeStruct((count, tokens), f32),
        ),
        in_specs=[whole()] * 3,
        out_specs=(whole(),) * 3,
        compiler_params=params(),
        cost_estimate=taking(2),
        name="make_rows",
    )(grad_out.T, top_logits.T, expert_ids.T)


def pack_kernel(*refs):
    out_ref, sems = refs[-2:]
    copies = []
    for place in range(out_ref.shape[0]):
        copies.append(pltpu.make_async_copy(refs[place], out_ref.at[place], sems.at[place]))
        copies[-1].start()
    for copy in copies:
        copy.wait()


def pack(values, after):
    number = len(values)
    return pl.pallas_call(
        pack_kernel,
        out_shape=jax.ShapeDtypeStruct((number, *values[0].shape), values[0].dtype),
        in_specs=[anywhere()] * (number + len(after)),
        out_specs=anywhere(),
        scratch_shapes=[pltpu.SemaphoreType.DMA((number,))],
        compiler_params=params(),
        cost_estimate=taking(1),
        name="pack_rows",
    )(*values, *after)


def hold_kernel(*refs):
    del refs


def hold(values, after):
    return pl.pallas_call(
        hold_kernel,
        out_shape=tuple(jax.ShapeDtypeStruct(value.shape, value.dtype) for value in values),
        in_specs=[anywhere()] * (len(values) + len(after)),
        out_specs=(anywhere(),) * len(values),
        input_output_aliases={place: place for place in range(len(values))},
        compiler_params=params(),
        cost_estimate=taking(0),
        name="hold",
    )(*values, *after)


def split_kernel(table, where_ref, hidden_ref, *refs):
    own_ref, first_ref, rest_ref = refs[-3:]
    parts, units, _ = own_ref.shape
    row = lax.broadcasted_iota(jnp.int32, (2 * units, 2 * units), 0)
    column = lax.broadcasted_iota(jnp.int32, (2 * units, 2 * units), 1)
    unit = jnp.where(row == column, 1.0, 0.0).astype(bf16)
    low = where_ref[table["x"]] == 0
    for part in range(parts):
        block = hidden_ref[:, part * 2 * units : (part + 1) * 2 * units]
        turned = dot(unit, block, NT).astype(bf16)
        slot = where_ref[table["slot of", part]]
        other = jnp.where(low, turned[units:], turned[:units])
        own_ref[slot] = jnp.where(low, turned[:units], turned[units:])

        @pl.when(slot == 0)
        def _():
            first_ref[0] = other

        @pl.when(slot != 0)
        def _():
            rest_ref[slot - 1] = other


def split_hidden(table, where, hidden, parts, units, after):
    slots = hidden.shape[0]
    return pl.pallas_call(
        functools.partial(split_kernel, table),
        out_shape=tuple(
            jax.ShapeDtypeStruct((count, units, slots), bf16) for count in (parts, 1, parts - 1)
        ),
        in_specs=[scalars(), whole()] + [anywhere()] * len(after),
        out_specs=(whole(),) * 3,
        compiler_params=params(),
        cost_estimate=taking(2),
        name="split_hidden",
    )(where, hidden, *after)


def pair_lanes(step, steps, me, tokens):
    high = 2 * lax.rem(step, steps // 2)
    return pl.multiple_of(lax.div(me ^ high, 2) * 2 * tokens, 2 * tokens)


def half_of(me, tokens, other):
    return pl.multiple_of((lax.rem(me, 2) ^ other) * tokens, tokens)


def products_kernel(table, gate_lane, shards, cut, where_ref, *refs):
    first = len(refs) == 10
    rows = refs[:2]
    gate_tiles = refs[2:4]
    own_ref, other_ref = refs[4:6]
    scaled = refs[-1]
    kept_ref = refs[-2]
    tokens = rows[0].shape[1]
    slots = own_ref.shape[2]
    me = where_ref[table["me"]]
    step, steps = pl.program_id(0), pl.num_programs(0)
    lane = lax.broadcasted_iota(jnp.int32, (tokens, LANES), 1)
    for other in range(2):
        here = pl.ds(half_of(me, tokens, other), tokens)
        picked = jnp.where(lane == gate_lane + me, gate_tiles[other][0].astype(f32), 0.0)
        gate = jnp.sum(picked, axis=1, keepdims=True)
        scaled[here, :] = (rows[other][0].astype(f32) * gate).astype(bf16)
    lanes = pl.ds(pair_lanes(step, steps, me, tokens), 2 * tokens)
    skip = own_ref.shape[0] - len(shards)
    width = kept_ref.shape[2]

    def add(hidden):
        total = dot(hidden, scaled[...], NN)[:, :width]
        units = total.shape[0] // len(shards)

        @pl.when(step == 0)
        def _():
            for place in range(len(shards)):
                kept_ref[place] = total[place * units : (place + 1) * units]

        @pl.when(step != 0)
        def _():
            for place in range(len(shards)):
                kept_ref[place] += total[place * units : (place + 1) * units]

    def stacked(ref, offset):
        parts = [ref[offset + shard, :, lanes] for shard in range(len(shards))]
        return jnp.concatenate(parts, axis=0) if len(parts) > 1 else parts[0]

    @pl.when(step < steps // 2)
    def _():
        add(stacked(own_ref, skip))

    @pl.when(step >= steps // 2)
    def _():
        add(stacked(other_ref, 0))


def products(table, where, rows, gated, own, other, skip, model, cut, name, after):
    number, tokens, width = rows[0].shape
    shards, units, slots = other.shape
    late = cut > 0
    columns = model - cut if late else width
    gate_tile = (gated[0].shape[2] - LANES) // LANES
    row_spec = pl.BlockSpec((1, tokens, width), lambda j, s: (j, 0, 0))
    tile_spec = pl.BlockSpec((1, tokens, LANES), lambda j, s: (j, 0, gate_tile))
    own_shards = shards if skip == 0 else own.shape[0]
    own_spec = pl.BlockSpec((own_shards, units, slots), lambda j, s: (0, 0, 0))
    other_spec = pl.BlockSpec((shards, units, slots), lambda j, s: (0, 0, 0))
    return pl.pallas_call(
        functools.partial(products_kernel, table, model % LANES, list(range(shards)), cut),
        out_shape=jax.ShapeDtypeStruct((shards, units, columns), f32),
        grid_spec=pltpu.PrefetchScalarGridSpec(
            num_scalar_prefetch=1,
            grid=(number,),
            in_specs=[row_spec] * 2
            + [tile_spec] * 2
            + [own_spec, other_spec]
            + [anywhere()] * len(after),
            out_specs=pl.BlockSpec((shards, units, columns), lambda j, s: (0, 0, 0)),
            scratch_shapes=[pltpu.VMEM((2 * tokens, width), bf16)],
        ),
        compiler_params=params(),
        cost_estimate=taking(4),
        name=name,
    )(where, *rows, *gated, own, other, *after)


def rows_of(units):
    return units // 4 if units % 64 == 0 else units


def column_parts(arrays, cut):
    return [(0, arrays[0])] if len(arrays) == 1 else [(cut, arrays[0]), (0, arrays[1])]


def combine_kernel(table, key, cut, counts, sides, where_ref, *refs):
    slot = where_ref[table[key]]
    coming = refs[: counts[0]]
    outs = refs[len(refs) - counts[2] :]
    model = sum(ref.shape[1] for ref in coming)
    spans = [(cut, model), (0, cut)] if cut else [(0, model)]
    for chunk, (start, stop) in enumerate(spans):
        if counts[0] == 1:
            total = coming[0][:, start:stop]
        else:
            total = coming[chunk][...]
        total = total.astype(f32)
        for number, side in enumerate(sides):
            flag = slot == 0 if side == "first" else slot > 0
            total = total + jnp.where(flag, refs[counts[0] + len(spans) * number + chunk][0], 0.0)
        total = total.astype(bf16)
        if counts[2] == 1:
            outs[0][:, start:stop] = total
        else:
            outs[chunk][...] = total


def combine(table, where, coming, first, rest, turn, name, used, cut, after):
    units = coming[0].shape[0]
    model = sum(part.shape[1] for part in coming)
    block = rows_of(units)
    column = table["block", turn, name]
    sides, operands, specs = [], [], []
    if any(slot == 0 for slot in used):
        sides.append("first")
        operands += first
        specs += [pl.BlockSpec((1, block, part.shape[2]), lambda j, s: (0, j, 0)) for part in first]
    if any(slot > 0 for slot in used):
        sides.append("rest")
        operands += rest
        specs += [pl.BlockSpec((1, block, part.shape[2]), lambda j, s: (s[column], j, 0)) for part in rest]
    flat = pl.BlockSpec((block, model), lambda j, s: (j, 0))
    return pl.pallas_call(
        functools.partial(
            combine_kernel, table, ("use", turn, name), cut, (len(coming), len(operands), 1), sides
        ),
        out_shape=jax.ShapeDtypeStruct((units, model), bf16),
        grid_spec=pltpu.PrefetchScalarGridSpec(
            num_scalar_prefetch=1,
            grid=(units // block,),
            in_specs=[pl.BlockSpec((block, part.shape[1]), lambda j, s: (j, 0)) for part in coming]
            + specs
            + [anywhere()] * len(after),
            out_specs=flat,
        ),
        compiler_params=params(),
        cost_estimate=taking(1.5),
        name="combine",
    )(where, *coming, *operands, *after)


def begin_kernel(table, start, stop, where_ref, coming_ref, kept_ref, *refs):
    out_ref = refs[-1]
    flag = where_ref[table["use", 2, "A"]] == 0
    total = coming_ref[:, start:stop].astype(f32) + jnp.where(flag, kept_ref[0], 0.0)
    out_ref[...] = total.astype(bf16)


def begin(table, where, coming, kept, start, after):
    units, model = coming.shape
    width = kept.shape[2]
    block = rows_of(units)
    return pl.pallas_call(
        functools.partial(begin_kernel, table, start, start + width),
        out_shape=jax.ShapeDtypeStruct((units, width), bf16),
        grid_spec=pltpu.PrefetchScalarGridSpec(
            num_scalar_prefetch=1,
            grid=(units // block,),
            in_specs=[
                pl.BlockSpec((block, model), lambda j, s: (j, 0)),
                pl.BlockSpec((1, block, width), lambda j, s: (0, j, 0)),
            ]
            + [anywhere()] * len(after),
            out_specs=pl.BlockSpec((block, width), lambda j, s: (j, 0)),
        ),
        compiler_params=params(),
        cost_estimate=taking(1),
        name="begin",
    )(where, coming, kept, *after)


def total_kernel(cut, a_ref, b_ref, late_ref, early_ref, out_ref):
    for start, kept_ref in ((cut, late_ref), (0, early_ref)):
        here = slice(start, start + kept_ref.shape[2])
        out_ref[0, :, here] = kept_ref[0] + a_ref[:, here].astype(f32) + b_ref[:, here].astype(f32)


def total_grad(a, b, kept, cut):
    units, model = a.shape
    block = rows_of(units)
    flat = pl.BlockSpec((block, model), lambda j: (j, 0))
    return pl.pallas_call(
        functools.partial(total_kernel, cut),
        out_shape=jax.ShapeDtypeStruct((1, units, model), f32),
        grid=(units // block,),
        in_specs=[flat, flat]
        + [
            pl.BlockSpec((1, block, part.shape[2]), functools.partial(lambda last, j: (last, j, 0), part.shape[0] - 1))
            for part in kept
        ],
        out_specs=pl.BlockSpec((1, block, model), lambda j: (0, j, 0)),
        compiler_params=params(),
        cost_estimate=taking(2),
        name="total_grad",
    )(a, b, *kept)


def back_kernel(table, model, cut, choices, parts, guard, summed, where_ref, *refs):
    keys = [key for choice in choices for key in choice]
    late, early = refs[:2], refs[2:4]
    own_ref, first_ref, rest_ref = refs[4:7]
    weight_refs, used = {}, 7
    for key, count in zip(keys, parts):
        weight_refs[key] = refs[used : used + count]
        used += count
    before_ref = refs[used] if summed else None
    mine_ref, theirs_ref, sums_ref = refs[-3:]
    tokens = late[0].shape[1]
    units = own_ref.shape[1]
    slots_all = own_ref.shape[2]
    me = where_ref[table["me"]]
    step, steps = pl.program_id(0), pl.num_programs(0)
    start = late[0].shape[2] - LANES
    eight = lax.broadcasted_iota(jnp.int32, (8, LANES), 1)
    onehot = jnp.where(eight == model % LANES + me, 1.0, 0.0).astype(bf16)
    shards = {key: where_ref[table[("shard",) + key]] for key in keys}
    slots = {key: where_ref[table[("slot",) + key]] for key in keys}

    @pl.when(step == 0)
    def _():
        sums_ref[...] = before_ref[...] if summed else jnp.zeros(sums_ref.shape, f32)

    def whole_weight(key):
        got = weight_refs[key]
        return got[0][...] if len(got) == 1 else jnp.concatenate([got[1][...], got[0][...]], axis=1)

    def work(near):
        stack, here_valid, here_slot = [], [], []
        for choice in choices:
            weight, valid, slot = whole_weight(choice[0]), shards[choice[0]] >= 0, slots[choice[0]]
            for key in choice[1:]:
                weight = jnp.where(valid, weight, whole_weight(key))
                slot = jnp.where(valid, slot, slots[key])
                valid = jnp.logical_or(valid, shards[key] >= 0)
            stack.append(weight)
            here_valid.append(valid)
            here_slot.append(slot)
        weight = jnp.concatenate(stack, axis=0) if len(stack) > 1 else stack[0]
        both = jnp.concatenate(
            [jnp.concatenate([early[k][0], late[k][0][:, : model - cut]], axis=1) for k in range(2)],
            axis=0,
        )
        product = dot(weight, both, NT)
        lanes = pair_lanes(step, steps, me, tokens)
        out_ref = mine_ref if near else theirs_ref
        for half in range(2):
            block = product[:, half * tokens : (half + 1) * tokens]
            gate = dot(onehot, late[half][0][:, start:], NT)[0:1]
            here = pl.ds(pl.multiple_of(lanes + half_of(me, tokens, half), tokens), tokens)
            offset = 0 if near else slots_all
            wide = pl.ds(pl.multiple_of(offset + lanes + half_of(me, tokens, half), tokens), tokens)
            gated = (block * gate).astype(bf16)
            total = jnp.zeros((1, tokens), f32)
            for index, (valid, slot) in enumerate(zip(here_valid, here_slot)):
                some = slice(index * units, (index + 1) * units)
                out_ref[index, :, here] = gated[some]
                if near:
                    hidden = own_ref[slot, :, here].astype(f32)
                else:
                    hidden = jnp.where(
                        slot == 0,
                        first_ref[0, :, here].astype(f32),
                        rest_ref[jnp.maximum(slot - 1, 0), :, here].astype(f32),
                    )
                part = jnp.sum(hidden * block[some], axis=0, keepdims=True)
                total = total + jnp.where(valid, part, 0.0)
            sums_ref[0:1, wide] += total

    some = functools.reduce(jnp.logical_or, [shards[key] >= 0 for key in keys]) if guard else True
    pl.when(jnp.logical_and(some, step < steps // 2))(functools.partial(work, True))
    pl.when(jnp.logical_and(some, step >= steps // 2))(functools.partial(work, False))


def back_part(table, where, late, early, own, first, rest, choices, got, before, guard, after, model):
    units, slots = own.shape[1:]
    number, tokens, width = late[0].shape
    cut = early[0].shape[2]
    keys = [key for choice in choices for key in choice]
    weights = [got[key] for key in keys]
    flat = [part for weight in weights for part in weight]
    half = jax.ShapeDtypeStruct((len(choices), units, slots), bf16)
    summed = before is not None
    fixed = [own, first, rest, *flat] + ([before] if summed else [])
    sums = jax.ShapeDtypeStruct((8, 2 * slots), f32)

    def still(shape):
        zeros = (0,) * len(shape)
        return pl.BlockSpec(shape, lambda j, s: zeros)

    return pl.pallas_call(
        functools.partial(
            back_kernel, table, model, cut, choices, [len(weight) for weight in weights], guard, summed
        ),
        out_shape=(half, half, sums),
        grid_spec=pltpu.PrefetchScalarGridSpec(
            num_scalar_prefetch=1,
            grid=(number,),
            in_specs=[pl.BlockSpec((1, tokens, width), lambda j, s: (j, 0, 0))] * 2
            + [pl.BlockSpec((1, tokens, cut), lambda j, s: (j, 0, 0))] * 2
            + [still(value.shape) for value in fixed]
            + [anywhere()] * len(after),
            out_specs=(still(half.shape), still(half.shape), still(sums.shape)),
        ),
        compiler_params=params(),
        cost_estimate=taking(6),
        name="back_part",
    )(where, *late, *early, *fixed, *after)


def join_kernel(table, groups, where_ref, *refs):
    out_ref, turned, sem = refs[-3:]
    slots, width = turned.shape[1:]
    row = lax.broadcasted_iota(jnp.int32, (slots, slots), 0)
    column = lax.broadcasted_iota(jnp.int32, (slots, slots), 1)
    unit = jnp.where(row == column, 1.0, 0.0).astype(bf16)
    low = where_ref[table["x"]] == 0
    copies = []
    total = 0
    for number, choices in enumerate(groups):
        mine_ref, theirs_ref = refs[2 * number], refs[2 * number + 1]
        for place, choice in enumerate(choices):
            index = where_ref[table[("shard",) + choice[0]]]
            for key in choice[1:]:
                index = jnp.where(index >= 0, index, where_ref[table[("shard",) + key]])
            mine, theirs = mine_ref[place], theirs_ref[place]
            both = jnp.concatenate(
                [jnp.where(low, mine, theirs), jnp.where(low, theirs, mine)], axis=0
            )
            turned[total] = dot(unit, both, NT).astype(bf16)
            here = pl.ds(pl.multiple_of(jnp.maximum(index, 0) * width, LANES), width)
            copy = pltpu.make_async_copy(turned.at[total], out_ref.at[:, here], sem.at[total])
            copies.append((index, copy))
            pl.when(index >= 0)(copy.start)
            total += 1
    for index, copy in copies:
        pl.when(index >= 0)(copy.wait)


def join_hidden(table, where, groups, pairs, slots, hidden, before, after):
    flat = [array for pair in pairs for array in pair]
    units = flat[0].shape[1]
    total = sum(len(choices) for choices in groups)
    extends = before is not None
    return pl.pallas_call(
        functools.partial(join_kernel, table, groups),
        out_shape=jax.ShapeDtypeStruct((slots, hidden), bf16),
        in_specs=[scalars()] + [whole()] * len(flat) + [anywhere()] * (extends + len(after)),
        out_specs=anywhere(),
        scratch_shapes=[
            pltpu.VMEM((total, slots, 2 * units), bf16),
            pltpu.SemaphoreType.DMA((total,)),
        ],
        input_output_aliases={1 + len(flat): 0} if extends else {},
        compiler_params=params(),
        cost_estimate=taking(2),
        name="join_hidden",
    )(where, *flat, *([before] if extends else []), *after)


def logits_kernel(gates_ref, ids_ref, grads_ref, out_ref):
    gates, ids, grads = gates_ref[...], ids_ref[...], grads_ref[...]
    picked = jnp.zeros_like(gates)
    for expert in range(grads.shape[0]):
        picked = picked + jnp.where(ids == expert, grads[expert : expert + 1, :], 0.0)
    out_ref[...] = gates * (picked - jnp.sum(gates * picked, axis=0, keepdims=True))


def logits_grad(gates, ids, grads):
    return pl.pallas_call(
        logits_kernel,
        out_shape=jax.ShapeDtypeStruct(gates.shape, f32),
        in_specs=[whole()] * 3,
        out_specs=whole(),
        compiler_params=params(),
        cost_estimate=taking(1),
        name="logits_grad",
    )(gates, ids, grads)


def per_device_full(grad_out, top_logits, expert_ids, saved_hidden, w_down):
    experts = lax.axis_size("exp")
    groups = lax.axis_size("ctx")
    depth = groups // 2
    tokens, model = grad_out.shape
    slots, hidden = saved_hidden.shape[2:]
    width = pl.cdiv(model + experts, LANES) * LANES
    cut = width // LANES // 2 * LANES

    table, brought, uses = device_scalars(depth, experts)
    where = table.row(lax.axis_index("ctx"), lax.axis_index("exp"))

    def swap(value, x, exp):
        if not exp:
            return lax.ppermute(value, "ctx", [(i, i ^ x) for i in range(groups)])
        if not x:
            return lax.ppermute(value, "exp", [(i, i ^ exp) for i in range(experts)])
        pairs = [(c * experts + e, (c ^ x) * experts + (e ^ exp)) for c in range(groups) for e in range(experts)]
        return lax.ppermute(value, ("ctx", "exp"), pairs)

    def swap_z(value, name):
        first = "AB".index(name)
        pairs = []
        for z in range(first, depth - 1, 2):
            for x in range(2):
                pairs += [(2 * z + x, 2 * z + 2 + x), (2 * z + 2 + x, 2 * z + x)]
        return lax.ppermute(value, "ctx", pairs)

    got = {(0, "own"): [w_down[0]]}
    for name in "AB":
        got[1, name] = [swap_z(w_down[0], name)]

    late, early, gates = make_rows(grad_out, top_logits, expert_ids, width, cut)
    highs = list(range(2, experts, 2))
    late_near = [late] + [swap(late, 0, high) for high in highs]
    late_x = swap(late, 1, 0)
    late_far = [late_x] + [swap(late_x, 0, high) for high in highs]
    own, other_first, other_rest = split_hidden(
        table, where, saved_hidden[0, 0], depth, w_down.shape[1], [late]
    )
    other_first = swap(other_first, 1, 0)
    late_rows = pack(late_near + late_far, [other_first, got[1, "A"][0], got[1, "B"][0]])
    late_rows = (late_rows, swap(late_rows, 0, 1))

    (early,) = hold((early,), [late_rows[0]])
    early_x = swap(early, 1, 0)
    early_near = [early] + [swap(early, 0, high) for high in highs]
    early_x, other_rest = hold((early_x, other_rest), [])
    early_far = [early_x] + [swap(early_x, 0, high) for high in highs]
    other_rest = swap(other_rest, 1, 0)
    got[2, "B"] = [swap_z(got[1, "A"][0], "B")]

    first = [
        products(table, where, late_rows, late_rows, own, other_first, 0, model, cut, "first_late", [])
    ]
    sent = [begin(table, where, got[1, "B"][0], first[0], cut, [])]
    got[2, "A"] = [swap_z(sent[0], "A")]
    early_rows = pack(early_near + early_far, [sent[0]])
    early_rows = (early_rows, swap(early_rows, 0, 1))
    first.append(
        products(table, where, early_rows, late_rows, own, other_first, 0, model, 0, "first_early", [other_rest])
    )
    sent.append(begin(table, where, got[1, "B"][0], first[1], 0, [got[2, "A"][0]]))
    got[2, "A"].append(swap_z(sent[1], "A"))

    rest = []
    for rows, start, name in ((late_rows, cut, "rest_late"), (early_rows, 0, "rest_early")):
        rest.append(
            products(table, where, rows, late_rows, own, other_rest, 1, model, start, name, [sent[1]])
        )

    pairs, groups_of = [], []

    def backprop(choices, before, guard, after):
        mine, theirs, sums = back_part(
            table, where, late_rows, early_rows, own, other_first, other_rest, choices, got, before, guard, after, model
        )
        pairs.append((mine, swap(theirs, 1, 0)))
        groups_of.append(choices)
        return sums

    def pass_on(turn, name, after):
        back = "B" if name == "A" else "A"
        used = uses[turn, name]
        coming = got[turn - 1, back]
        if turn == 3 and name == "B":
            values = []
            for k in range(2):
                value = combine(table, where, [coming[k]], [first[k]], [rest[k]], turn, name, used, 0, after)
                values.append(value)
                after = [value]
        else:
            values = [combine(table, where, coming, first, rest, turn, name, used, cut, after)]
        got[turn, name] = [swap_z(value, name) for value in values]
        return values[-1]

    def choices_of(turn):
        both = any(b[turn, "A"] >= 0 and b[turn, "B"] >= 0 for b in brought)
        return [[(turn, "A")], [(turn, "B")]] if both else [[(turn, "A"), (turn, "B")]]

    marker = pass_on(3, "A", [*rest, got[2, "A"][0]])
    marker = pass_on(3, "B", [marker])
    sums = backprop([[(0, "own")], [(1, "A")], [(1, "B")]], None, False, [marker])
    marker = sums
    hidden_grad = None
    for turn in range(2, depth):
        choices = choices_of(turn)
        if turn > 2:
            marker = pass_on(turn + 1, "A", [marker])
            marker = pass_on(turn + 1, "B", [marker])
        sums = backprop(choices, sums, len(choices) == 1, [marker])
        marker = sums
        if turn == 2:
            hidden_grad = join_hidden(
                table, where, groups_of[:1], pairs[:1], slots, hidden, None, [marker]
            )
            marker = hidden_grad
    slot_grad = sums[0:1, :slots] + swap(sums[0:1, slots:], 1, 0)
    grads = lax.all_to_all(
        slot_grad.reshape(experts, tokens), "exp", split_axis=0, concat_axis=0, tiled=True
    )
    logit_grad = logits_grad(gates, expert_ids.T, grads).T
    hidden_grad = join_hidden(
        table, where, groups_of[1:], pairs[1:], slots, hidden, hidden_grad, [logit_grad]
    )
    weight_grad = total_grad(got[depth, "A"][0], got[depth, "B"][0], rest, cut)
    return (logit_grad, hidden_grad[None, None], weight_grad)


def routing_tables(expert_ids, count_experts, capacity):
    columns = jnp.arange(count_experts, dtype=jnp.int32)
    matches = expert_ids[:, :, None] == columns[None, None, :]
    per_token = jnp.sum(matches.astype(jnp.int32), axis=1)
    rank_table = jnp.cumsum(per_token, axis=0) - per_token
    slot_iota = jnp.arange(capacity, dtype=jnp.int32)
    select = (per_token.T[:, None, :] == 1) & (rank_table.T[:, None, :] == slot_iota[None, :, None])
    return (matches.astype(jnp.float32), select)


def per_device_routed(grad_out, top_logits, expert_ids, saved_hidden, w_down):
    count_experts = lax.axis_size("exp")
    slot_count = saved_hidden.shape[2]
    capacity = slot_count // count_experts
    model_width = grad_out.shape[1]
    onehot, select = routing_tables(expert_ids, count_experts, capacity)
    select_wide = select.astype(jnp.float32)
    gate_probs = jax.nn.softmax(top_logits, axis=-1)
    gate_sent = gate_probs.astype(jnp.bfloat16)
    gate_by_expert = jnp.sum(onehot * gate_sent.astype(jnp.float32)[:, :, None], axis=1)
    send_rows = jnp.einsum(
        "ect,td->ecd", select.astype(jnp.bfloat16), grad_out, preferred_element_type=jnp.float32
    ).astype(jnp.bfloat16)
    send_gate = jnp.sum(select_wide * gate_by_expert.T[:, None, :], axis=2).astype(jnp.bfloat16)
    hidden = saved_hidden[0, 0]
    rows_in, gate_in = (
        lax.all_to_all(send_rows, "exp", split_axis=0, concat_axis=0, tiled=True),
        lax.all_to_all(send_gate, "exp", split_axis=0, concat_axis=0, tiled=True),
    )
    flat_rows = rows_in.reshape(slot_count, model_width)
    backprop = lax.dot_general(
        flat_rows,
        lax.all_gather(w_down[0], "ctx", axis=0, tiled=True),
        (((1,), (1,)), ((), ())),
        preferred_element_type=jnp.float32,
    )
    flat_gate = gate_in.reshape(slot_count, 1).astype(jnp.float32)
    hidden_grad = (flat_gate * backprop).astype(jnp.bfloat16)
    slot_grad = jnp.sum(hidden.astype(jnp.float32) * backprop, axis=1)
    scaled = (flat_gate * flat_rows.astype(jnp.float32)).astype(jnp.bfloat16)
    partial_grad = lax.dot_general(
        hidden, scaled, (((0,), (0,)), ((), ())), preferred_element_type=jnp.float32
    )
    weight_grad = lax.psum_scatter(partial_grad, "ctx", scatter_dimension=0, tiled=True)
    returned = lax.all_to_all(
        slot_grad.reshape(count_experts, capacity), "exp", split_axis=0, concat_axis=0, tiled=True
    )
    grad_by_expert = jnp.sum(select_wide * returned[:, :, None], axis=1)
    gate_grad = jnp.sum(onehot * grad_by_expert.T[:, None, :], axis=2)
    logit_grad = gate_probs * (gate_grad - jnp.sum(gate_probs * gate_grad, axis=1, keepdims=True))
    return (logit_grad, hidden_grad.reshape(1, 1, slot_count, -1), weight_grad[None])


def per_device(grad_out, top_logits, expert_ids, saved_hidden, w_down):
    experts = lax.axis_size("exp")
    groups = lax.axis_size("ctx")
    everywhere = top_logits.shape[1] == experts and saved_hidden.shape[2] == experts * grad_out.shape[0]
    plain = experts & (experts - 1) == 0 and groups % 4 == 0 and groups >= 8
    body = per_device_full if everywhere and plain else per_device_routed
    return body(grad_out, top_logits, expert_ids, saved_hidden, w_down)


def solution(mesh):
    return jax.shard_map(
        per_device,
        mesh=mesh,
        in_specs=(
            P(("ctx", "exp"), None),
            P(("ctx", "exp"), None),
            P(("ctx", "exp"), None),
            P("ctx", "exp", None, None),
            P("exp", "ctx", None),
        ),
        out_specs=(P(("ctx", "exp"), None), P("ctx", "exp", None, None), P("exp", "ctx", None)),
        check_vma=False,
    )
```

```python
import functools

import jax
import jax.numpy as jnp
import numpy as np
from jax import lax
from jax.experimental import pallas as pl
from jax.experimental.pallas import tpu as pltpu
from jax.sharding import PartitionSpec as P

LANES = 128
SCALE = 1_000_000
NT = (((1,), (1,)), ((), ()))
NN = (((1,), (0,)), ((), ()))
f32 = jnp.float32
bf16 = jnp.bfloat16


def dot(a, b, dims):
    return lax.dot_general(a, b, dims, preferred_element_type=f32)


def anywhere():
    return pl.BlockSpec(memory_space=pl.ANY)


def whole():
    return pl.BlockSpec(memory_space=pltpu.VMEM)


def scalars():
    return pl.BlockSpec(memory_space=pltpu.SMEM)


def params():
    return pltpu.CompilerParams(vmem_limit_bytes=24 * 1024 * 1024)


def taking(microseconds):
    return pl.CostEstimate(flops=int(microseconds * SCALE), bytes_accessed=int(microseconds * 3e6), transcendentals=0)


def chain_plan(depth):
    products, weights = [], []
    for z in range(depth):
        uses = []
        for turn in range(2, depth + 1):
            if z < depth - 1 and turn >= z + 2:
                uses.append((turn, "AB"[z % 2], depth + 1 + z - turn))
            if z > 0 and turn >= depth - z + 1:
                uses.append((turn, "BA"[z % 2], z + turn - depth - 1))
        products.append(sorted(uses) + [(depth + 1, "own", z)])
        brought = {}
        for turn in range(1, depth):
            for name in "AB":
                index = z + turn if (name == "A") == (z % 2 == 0) else z - turn
                brought[turn, name] = index if 0 <= index < depth else -1
        weights.append(brought)
    return products, weights


class Scalars:
    def __init__(self):
        self.columns = []
        self.names = {}

    def add(self, name, values):
        self.names[name] = len(self.columns)
        self.columns.append(values)

    def __getitem__(self, name):
        return self.names[name]

    def row(self, place, me):
        return jnp.asarray(np.stack(self.columns, axis=-1).astype(np.int32))[place, me]


def device_scalars(depth, experts):
    products, weights = chain_plan(depth)
    table = Scalars()
    along = np.arange(2 * depth)[:, None] + np.zeros((1, experts), np.int32)

    def by_z(values):
        return np.asarray(values)[along // 2]

    table.add("x", along % 2)
    table.add("me", np.zeros_like(along) + np.arange(experts)[None, :])
    table.add(("shard", 0, "own"), along // 2)
    slot_of = [{use[2]: slot for slot, use in enumerate(products[z])} for z in range(depth)]
    for part in range(depth):
        table.add(("slot of", part), by_z([slot_of[z][part] for z in range(depth)]))
    table.add(("slot", 0, "own"), by_z([slot_of[z][z] for z in range(depth)]))
    for turn in range(1, depth):
        for name in "AB":
            shard = [weights[z][turn, name] for z in range(depth)]
            table.add(("shard", turn, name), by_z(shard))
            table.add(("slot", turn, name), by_z([slot_of[z].get(k, 0) for z, k in enumerate(shard)]))
    uses = {}
    for turn in range(2, depth + 1):
        for name in "AB":
            slots = [-1] * depth
            for z in range(depth):
                for slot, use in enumerate(products[z]):
                    if use[:2] == (turn, name):
                        slots[z] = slot
            uses[turn, name] = slots
            table.add(("use", turn, name), by_z(slots))
            limit = max(depth - 3, 0)
            table.add(("block", turn, name), by_z([min(max(slot - 1, 0), limit) for slot in slots]))
    return table, weights, uses


def rows_kernel(cut, grad_hbm, logits_hbm, ids_hbm, late_ref, early_ref, gates_ref, *scratch):
    grad_ref, logits_ref, ids_ref, sems = scratch
    model, tokens = grad_ref.shape
    copies = [
        pltpu.make_async_copy(source, target, sems.at[place])
        for place, (source, target) in enumerate(
            ((grad_hbm, grad_ref), (logits_hbm, logits_ref), (ids_hbm, ids_ref))
        )
    ]
    for copy in copies:
        copy.start()
    for copy in copies:
        copy.wait()
    count = logits_ref.shape[0]
    width = cut + late_ref.shape[1]
    logits = logits_ref[...]
    powers = jnp.exp(logits - jnp.max(logits, axis=0, keepdims=True))
    gates = powers / jnp.sum(powers, axis=0, keepdims=True)
    gates_ref[...] = gates
    sent = gates.astype(bf16).astype(f32)
    ids = ids_ref[...]
    row = lax.broadcasted_iota(jnp.int32, (width - model, tokens), 0)
    extra = jnp.zeros((width - model, tokens), f32)
    for expert in range(count):
        chosen = jnp.sum(jnp.where(ids == expert, sent, 0.0), axis=0, keepdims=True)
        extra = extra + jnp.where(row == expert, chosen, 0.0)
    for start in range(0, width, LANES):
        stop = start + LANES
        if stop <= model:
            block = grad_ref[start:stop, :].astype(f32)
        elif start >= model:
            block = extra[start - model : stop - model, :]
        else:
            block = jnp.concatenate(
                [grad_ref[start:model, :].astype(f32), extra[: stop - model, :]], axis=0
            )
        turned = block.T.astype(bf16)
        if start < cut:
            early_ref[:, start:stop] = turned
        else:
            late_ref[:, start - cut : stop - cut] = turned


def make_rows(grad_out, top_logits, expert_ids, width, cut):
    tokens, model = grad_out.shape
    count = top_logits.shape[1]
    return pl.pallas_call(
        functools.partial(rows_kernel, cut),
        out_shape=(
            jax.ShapeDtypeStruct((tokens, width - cut), bf16),
            jax.ShapeDtypeStruct((tokens, cut), bf16),
            jax.ShapeDtypeStruct((count, tokens), f32),
        ),
        in_specs=[anywhere()] * 3,
        out_specs=(whole(),) * 3,
        scratch_shapes=[
            pltpu.VMEM((model, tokens), bf16),
            pltpu.VMEM((count, tokens), f32),
            pltpu.VMEM((count, tokens), jnp.int32),
            pltpu.SemaphoreType.DMA((3,)),
        ],
        compiler_params=params(),
        cost_estimate=taking(2),
        name="make_rows",
    )(grad_out.T, top_logits.T, expert_ids.T)


def pack_kernel(*refs):
    out_ref, sems = refs[-2:]
    copies = []
    for place in range(out_ref.shape[0]):
        copies.append(pltpu.make_async_copy(refs[place], out_ref.at[place], sems.at[place]))
        copies[-1].start()
    for copy in copies:
        copy.wait()


def pack(values, after):
    number = len(values)
    return pl.pallas_call(
        pack_kernel,
        out_shape=jax.ShapeDtypeStruct((number, *values[0].shape), values[0].dtype),
        in_specs=[anywhere()] * (number + len(after)),
        out_specs=anywhere(),
        scratch_shapes=[pltpu.SemaphoreType.DMA((number,))],
        compiler_params=params(),
        cost_estimate=taking(1),
        name="pack_rows",
    )(*values, *after)


def blocks_of(refs, places):
    return [refs[array] if place is None else refs[array].at[place] for array, place in places]


def hold_kernel(*refs):
    del refs


def hold(values, after):
    return pl.pallas_call(
        hold_kernel,
        out_shape=tuple(jax.ShapeDtypeStruct(value.shape, value.dtype) for value in values),
        in_specs=[anywhere()] * (len(values) + len(after)),
        out_specs=(anywhere(),) * len(values),
        input_output_aliases={place: place for place in range(len(values))},
        compiler_params=params(),
        cost_estimate=taking(0),
        name="hold",
    )(*values, *after)


def split_kernel(table, where_ref, hidden_ref, *refs):
    own_ref, first_ref, rest_ref = refs[-3:]
    parts, units, _ = own_ref.shape
    row = lax.broadcasted_iota(jnp.int32, (2 * units, 2 * units), 0)
    column = lax.broadcasted_iota(jnp.int32, (2 * units, 2 * units), 1)
    unit = jnp.where(row == column, 1.0, 0.0).astype(bf16)
    low = where_ref[table["x"]] == 0
    for part in range(parts):
        block = hidden_ref[:, part * 2 * units : (part + 1) * 2 * units]
        turned = dot(unit, block, NT).astype(bf16)
        slot = where_ref[table["slot of", part]]
        other = jnp.where(low, turned[units:], turned[:units])
        own_ref[slot] = jnp.where(low, turned[:units], turned[units:])

        @pl.when(slot == 0)
        def _():
            first_ref[0] = other

        @pl.when(slot != 0)
        def _():
            rest_ref[slot - 1] = other


def split_hidden(table, where, hidden, parts, units, after):
    slots = hidden.shape[0]
    return pl.pallas_call(
        functools.partial(split_kernel, table),
        out_shape=tuple(
            jax.ShapeDtypeStruct((count, units, slots), bf16) for count in (parts, 1, parts - 1)
        ),
        in_specs=[scalars(), whole()] + [anywhere()] * len(after),
        out_specs=(whole(),) * 3,
        compiler_params=params(),
        cost_estimate=taking(2),
        name="split_hidden",
    )(where, hidden, *after)


def place_of(place, count, me, tokens):
    start = (place // count) * count * tokens + ((place % count) ^ me) * tokens
    return pl.multiple_of(start, tokens)


def products_kernel(table, model, counts, places, shards, skip, where_ref, *refs):
    used = sum(counts)
    rows = blocks_of(refs[: counts[0]], places[0])
    gated = blocks_of(refs[counts[0] : used], places[1])
    number = len(rows)
    own_ref, other_ref = refs[used : used + 2]
    kept_ref, scaled = refs[-2:]
    tokens = rows[0].shape[0]
    units, slots = own_ref.shape[1:]
    width = kept_ref.shape[2]
    me = where_ref[table["me"]]
    lane = lax.broadcasted_iota(jnp.int32, (tokens, LANES), 1)
    for place in range(number):
        here = pl.ds(place_of(place, number // 2, me, tokens), tokens)
        tile = gated[place][:, gated[place].shape[1] - LANES :]
        picked = jnp.where(lane == model % LANES + me, tile.astype(f32), 0.0)
        gate = jnp.sum(picked, axis=1, keepdims=True)
        scaled[here, :] = (rows[place][:, :width].astype(f32) * gate).astype(bf16)

    def stacked(ref, offset):
        parts = [ref[offset + shard] for shard in range(shards)]
        return jnp.concatenate(parts, axis=0) if len(parts) > 1 else parts[0]

    total = dot(stacked(own_ref, skip), scaled[:slots, :], NN)
    total = total + dot(stacked(other_ref, 0), scaled[slots:, :], NN)
    for shard in range(shards):
        kept_ref[shard] = total[shard * units : (shard + 1) * units]


def products(table, where, rows, gated, own, other, skip, model, width, name, after):
    arrays, places = zip(rows, gated)
    tokens = arrays[0][0].shape[-2]
    counts = [len(part) for part in arrays]
    number = 2 * (own.shape[2] // tokens)
    shards, units, slots = other.shape
    return pl.pallas_call(
        functools.partial(products_kernel, table, model, counts, places, shards, skip),
        out_shape=jax.ShapeDtypeStruct((shards, units, width), f32),
        in_specs=[scalars()] + [whole()] * (sum(counts) + 2) + [anywhere()] * len(after),
        out_specs=whole(),
        scratch_shapes=[pltpu.VMEM((number * tokens, width), bf16)],
        compiler_params=params(),
        cost_estimate=taking(4),
        name=name,
    )(where, *arrays[0], *arrays[1], own, other, *after)


def rows_of(units):
    return units // 2 if units % 32 == 0 else units


def column_parts(arrays, cut):
    return [(0, arrays[0])] if len(arrays) == 1 else [(cut, arrays[0]), (0, arrays[1])]


def combine_kernel(table, key, cut, counts, sides, where_ref, *refs):
    slot = where_ref[table[key]]
    coming = refs[: counts[0]]
    outs = refs[len(refs) - counts[2] :]
    model = sum(ref.shape[1] for ref in coming)
    spans = [(cut, model), (0, cut)] if cut else [(0, model)]
    for chunk, (start, stop) in enumerate(spans):
        if counts[0] == 1:
            total = coming[0][:, start:stop]
        else:
            total = coming[chunk][...]
        total = total.astype(f32)
        for number, side in enumerate(sides):
            flag = slot == 0 if side == "first" else slot > 0
            total = total + jnp.where(flag, refs[counts[0] + len(spans) * number + chunk][0], 0.0)
        total = total.astype(bf16)
        if counts[2] == 1:
            outs[0][:, start:stop] = total
        else:
            outs[chunk][...] = total


def combine(table, where, coming, first, rest, turn, name, used, cut, after, chunked=False):
    units = coming[0].shape[0]
    model = sum(part.shape[1] for part in coming)
    block = rows_of(units)
    column = table["block", turn, name]
    sides, operands, specs = [], [], []
    if any(slot == 0 for slot in used):
        sides.append("first")
        operands += first
        specs += [pl.BlockSpec((1, block, part.shape[2]), lambda j, s: (0, j, 0)) for part in first]
    if any(slot > 0 for slot in used):
        sides.append("rest")
        operands += rest
        specs += [pl.BlockSpec((1, block, part.shape[2]), lambda j, s: (s[column], j, 0)) for part in rest]
    widths = [model - cut, cut] if chunked else [model]
    return pl.pallas_call(
        functools.partial(
            combine_kernel, table, ("use", turn, name), cut, (len(coming), len(operands), len(widths)), sides
        ),
        out_shape=[jax.ShapeDtypeStruct((units, count), bf16) for count in widths],
        grid_spec=pltpu.PrefetchScalarGridSpec(
            num_scalar_prefetch=1,
            grid=(units // block,),
            in_specs=[pl.BlockSpec((block, part.shape[1]), lambda j, s: (j, 0)) for part in coming]
            + specs
            + [anywhere()] * len(after),
            out_specs=[pl.BlockSpec((block, count), lambda j, s: (j, 0)) for count in widths],
        ),
        compiler_params=params(),
        cost_estimate=taking(1.5),
        name="combine",
    )(where, *coming, *operands, *after)


def begin_kernel(table, start, stop, where_ref, coming_ref, kept_ref, *refs):
    out_ref = refs[-1]
    flag = where_ref[table["use", 2, "A"]] == 0
    total = coming_ref[:, start:stop].astype(f32) + jnp.where(flag, kept_ref[0], 0.0)
    out_ref[...] = total.astype(bf16)


def begin(table, where, coming, kept, start, after):
    units, model = coming.shape
    width = kept.shape[2]
    block = rows_of(units)
    return pl.pallas_call(
        functools.partial(begin_kernel, table, start, start + width),
        out_shape=jax.ShapeDtypeStruct((units, width), bf16),
        grid_spec=pltpu.PrefetchScalarGridSpec(
            num_scalar_prefetch=1,
            grid=(units // block,),
            in_specs=[
                pl.BlockSpec((block, model), lambda j, s: (j, 0)),
                pl.BlockSpec((1, block, width), lambda j, s: (0, j, 0)),
            ]
            + [anywhere()] * len(after),
            out_specs=pl.BlockSpec((block, width), lambda j, s: (j, 0)),
        ),
        compiler_params=params(),
        cost_estimate=taking(1),
        name="begin",
    )(where, coming, kept, *after)


def total_kernel(cut, counts, *refs):
    coming = [refs[: counts[0]], refs[counts[0] : sum(counts)]]
    out_ref = refs[-1]
    for chunk, start in enumerate((cut, 0)):
        kept_ref = refs[sum(counts) + chunk]
        here = slice(start, start + kept_ref.shape[2])
        total = kept_ref[0]
        for parts in coming:
            total = total + (parts[0][:, here] if len(parts) == 1 else parts[chunk][...]).astype(f32)
        out_ref[0, :, here] = total


def total_grad(a, b, kept, cut):
    units = a[0].shape[0]
    model = sum(part.shape[1] for part in a)
    block = rows_of(units)
    return pl.pallas_call(
        functools.partial(total_kernel, cut, (len(a), len(b))),
        out_shape=jax.ShapeDtypeStruct((1, units, model), f32),
        grid=(units // block,),
        in_specs=[pl.BlockSpec((block, part.shape[1]), lambda j: (j, 0)) for part in (*a, *b)]
        + [
            pl.BlockSpec((1, block, part.shape[2]), functools.partial(lambda last, j: (last, j, 0), part.shape[0] - 1))
            for part in kept
        ],
        out_specs=pl.BlockSpec((1, block, model), lambda j: (0, j, 0)),
        compiler_params=params(),
        cost_estimate=taking(2),
        name="total_grad",
    )(*a, *b, *kept)


def back_kernel(table, model, cut, counts, places, choices, parts, guard, summed, where_ref, *refs):
    keys = [key for choice in choices for key in choice]
    used = sum(counts)
    late = blocks_of(refs[: counts[0]], places[0])
    early = blocks_of(refs[counts[0] : used], places[1])
    number = len(late)
    own_ref, first_ref, rest_ref = refs[used : used + 3]
    weight_refs, used = {}, used + 3
    for key, count in zip(keys, parts):
        weight_refs[key] = refs[used : used + count]
        used += count
    before_ref = refs[used] if summed else None
    outs = refs[len(refs) - 2 * len(choices) - 1 : -1]
    sums_ref = refs[-1]
    tokens = late[0].shape[0]
    units = own_ref.shape[1]
    me = where_ref[table["me"]]
    start = late[0].shape[1] - LANES
    eight = lax.broadcasted_iota(jnp.int32, (8, LANES), 1)
    onehot = jnp.where(eight == model % LANES + me, 1.0, 0.0).astype(bf16)
    shards = {key: where_ref[table[("shard",) + key]] for key in keys}
    slots = {key: where_ref[table[("slot",) + key]] for key in keys}
    sums_ref[...] = before_ref[...] if summed else jnp.zeros(sums_ref.shape, f32)

    def whole_weight(key):
        got = weight_refs[key]
        return got[0][...] if len(got) == 1 else jnp.concatenate([got[1][...], got[0][...]], axis=1)

    def work():
        stack, here_valid, here_slot = [], [], []
        for choice in choices:
            weight, valid, slot = whole_weight(choice[0]), shards[choice[0]] >= 0, slots[choice[0]]
            for key in choice[1:]:
                weight = jnp.where(valid, weight, whole_weight(key))
                slot = jnp.where(valid, slot, slots[key])
                valid = jnp.logical_or(valid, shards[key] >= 0)
            stack.append(weight)
            here_valid.append(valid)
            here_slot.append(slot)
        weight = jnp.concatenate(stack, axis=0) if len(stack) > 1 else stack[0]
        for pair in range(0, number, 2):
            both = jnp.concatenate(
                [
                    jnp.concatenate([early[k][...], late[k][:, : model - cut]], axis=1)
                    for k in (pair, pair + 1)
                ],
                axis=0,
            )
            product = dot(weight, both, NT)
            for place in (pair, pair + 1):
                near = place < number // 2
                block = product[:, (place - pair) * tokens : (place - pair + 1) * tokens]
                gate = dot(onehot, late[place][:, start:], NT)[0:1]
                here = pl.ds(place_of(place % (number // 2), number // 2, me, tokens), tokens)
                wide = pl.ds(place_of(place, number // 2, me, tokens), tokens)
                gated = (block * gate).astype(bf16)
                total = jnp.zeros((1, tokens), f32)
                for index, (valid, slot) in enumerate(zip(here_valid, here_slot)):
                    some = slice(index * units, (index + 1) * units)
                    outs[2 * index + (0 if near else 1)][:, here] = gated[some]
                    if near:
                        hidden = own_ref[slot, :, here].astype(f32)
                    else:
                        hidden = jnp.where(
                            slot == 0,
                            first_ref[0, :, here].astype(f32),
                            rest_ref[jnp.maximum(slot - 1, 0), :, here].astype(f32),
                        )
                    part = jnp.sum(hidden * block[some], axis=0, keepdims=True)
                    total = total + jnp.where(valid, part, 0.0)
                sums_ref[0:1, wide] += total

    if guard:
        pl.when(functools.reduce(jnp.logical_or, [shards[key] >= 0 for key in keys]))(work)
    else:
        work()


def back_part(table, where, late, early, own, first, rest, choices, got, before, guard, after, model):
    units, slots = own.shape[1:]
    arrays, places = zip(late, early)
    counts = [len(part) for part in arrays]
    cut = arrays[1][0].shape[-1]
    keys = [key for choice in choices for key in choice]
    weights = [got[key] for key in keys]
    flat = [part for weight in weights for part in weight]
    half = jax.ShapeDtypeStruct((units, slots), bf16)
    summed = before is not None
    operands = [*arrays[0], *arrays[1], own, first, rest, *flat] + ([before] if summed else [])
    outs = [half] * (2 * len(choices)) + [jax.ShapeDtypeStruct((8, 2 * slots), f32)]
    parts = [len(weight) for weight in weights]
    return pl.pallas_call(
        functools.partial(
            back_kernel, table, model, cut, counts, places, choices, parts, guard, summed
        ),
        out_shape=outs,
        in_specs=[scalars()] + [whole()] * len(operands) + [anywhere()] * len(after),
        out_specs=[whole()] * len(outs),
        compiler_params=params(),
        cost_estimate=taking(6),
        name="back_part",
    )(where, *operands, *after)


def join_kernel(table, choices, where_ref, *refs):
    out_ref, turned, sem = refs[-3:]
    slots, width = turned.shape[1:]
    row = lax.broadcasted_iota(jnp.int32, (slots, slots), 0)
    column = lax.broadcasted_iota(jnp.int32, (slots, slots), 1)
    unit = jnp.where(row == column, 1.0, 0.0).astype(bf16)
    low = where_ref[table["x"]] == 0
    copies = []
    for place, choice in enumerate(choices):
        mine, theirs = refs[2 * place][...], refs[2 * place + 1][...]
        index = where_ref[table[("shard",) + choice[0]]]
        for key in choice[1:]:
            index = jnp.where(index >= 0, index, where_ref[table[("shard",) + key]])
        both = jnp.concatenate([jnp.where(low, mine, theirs), jnp.where(low, theirs, mine)], axis=0)
        turned[place] = dot(unit, both, NT).astype(bf16)
        here = pl.ds(pl.multiple_of(jnp.maximum(index, 0) * width, LANES), width)
        copy = pltpu.make_async_copy(turned.at[place], out_ref.at[:, here], sem.at[place])
        copies.append((index, copy))
        pl.when(index >= 0)(copy.start)
    for index, copy in copies:
        pl.when(index >= 0)(copy.wait)


def join_hidden(table, where, choices, halves, slots, hidden, before, after):
    units = halves[0].shape[0]
    extends = before is not None
    return pl.pallas_call(
        functools.partial(join_kernel, table, choices),
        out_shape=jax.ShapeDtypeStruct((slots, hidden), bf16),
        in_specs=[scalars()] + [whole()] * len(halves) + [anywhere()] * (extends + len(after)),
        out_specs=anywhere(),
        scratch_shapes=[
            pltpu.VMEM((len(choices), slots, 2 * units), bf16),
            pltpu.SemaphoreType.DMA((len(choices),)),
        ],
        input_output_aliases={1 + len(halves): 0} if extends else {},
        compiler_params=params(),
        cost_estimate=taking(2),
        name="join_hidden",
    )(where, *halves, *([before] if extends else []), *after)


def logits_kernel(gates_ref, ids_ref, grads_ref, out_ref):
    gates, ids, grads = gates_ref[...], ids_ref[...], grads_ref[...]
    picked = jnp.zeros_like(gates)
    for expert in range(grads.shape[0]):
        picked = picked + jnp.where(ids == expert, grads[expert : expert + 1, :], 0.0)
    out_ref[...] = gates * (picked - jnp.sum(gates * picked, axis=0, keepdims=True))


def logits_grad(gates, ids, grads):
    return pl.pallas_call(
        logits_kernel,
        out_shape=jax.ShapeDtypeStruct(gates.shape, f32),
        in_specs=[whole()] * 3,
        out_specs=whole(),
        compiler_params=params(),
        cost_estimate=taking(1),
        name="logits_grad",
    )(gates, ids, grads)


def per_device_full(grad_out, top_logits, expert_ids, saved_hidden, w_down):
    experts = lax.axis_size("exp")
    groups = lax.axis_size("ctx")
    depth = groups // 2
    tokens, model = grad_out.shape
    slots, hidden = saved_hidden.shape[2:]
    width = pl.cdiv(model + experts, LANES) * LANES
    cut = width // LANES // 2 * LANES

    table, brought, uses = device_scalars(depth, experts)
    where = table.row(lax.axis_index("ctx"), lax.axis_index("exp"))

    def swap(value, x, exp):
        if not exp:
            return lax.ppermute(value, "ctx", [(i, i ^ x) for i in range(groups)])
        if not x:
            return lax.ppermute(value, "exp", [(i, i ^ exp) for i in range(experts)])
        pairs = [(c * experts + e, (c ^ x) * experts + (e ^ exp)) for c in range(groups) for e in range(experts)]
        return lax.ppermute(value, ("ctx", "exp"), pairs)

    def swap_z(value, name):
        first = "AB".index(name)
        pairs = []
        for z in range(first, depth - 1, 2):
            for x in range(2):
                pairs += [(2 * z + x, 2 * z + 2 + x), (2 * z + 2 + x, 2 * z + x)]
        return lax.ppermute(value, "ctx", pairs)

    got = {(0, "own"): [w_down[0]]}
    for name in "AB":
        got[1, name] = [swap_z(w_down[0], name)]

    late, early, gates = make_rows(grad_out, top_logits, expert_ids, width, cut)
    highs = list(range(2, experts, 2))

    def sides(mine):
        return [mine, swap(mine, 0, 1)]

    late_x = swap(late, 1, 0)
    late_mine = [late] + [swap(late, 0, high) for high in highs]
    late_mine += [late_x] + [swap(late_x, 0, high) for high in highs]
    (early,) = hold((early,), [late_x])
    own, other_first, other_rest = split_hidden(
        table, where, saved_hidden[0, 0], depth, w_down.shape[1], [early]
    )
    other_first = swap(other_first, 1, 0)
    early_x = swap(early, 1, 0)
    late_rows = sides(pack(late_mine, [other_first, got[1, "A"][0], got[1, "B"][0], early_x]))
    late_rows = (late_rows, [(side, place) for place in range(experts) for side in range(2)])
    early_rows = sides(pack([early, early_x], []))
    places = [(0, 0), (1, 0)]
    for block, base in ((early, 0), (early_x, 1)):
        if base:
            places += [(0, 1), (1, 1)]
        for high in highs:
            places += [(len(early_rows), None), (len(early_rows) + 1, None)]
            early_rows += sides(swap(block, 0, high))
    early_rows = (early_rows, places)
    other_rest = swap(other_rest, 1, 0)

    first = [products(table, where, late_rows, late_rows, own, other_first, 0, model, model - cut, "first_late", [])]
    sent = [begin(table, where, got[1, "B"][0], first[0], cut, [early_rows[0][1]])]
    got[2, "A"] = [swap_z(sent[0], "A")]
    got[2, "B"] = [swap_z(got[1, "A"][0], "B")]
    first.append(
        products(table, where, early_rows, late_rows, own, other_first, 0, model, cut, "first_early", [other_rest])
    )
    sent.append(begin(table, where, got[1, "B"][0], first[1], 0, [got[2, "A"][0]]))
    got[2, "A"].append(swap_z(sent[1], "A"))

    halves, all_choices = [], []
    only_first = max(uses[3, "B"]) <= 0

    def backprop(choices, before, guard, after):
        *outs, sums = back_part(
            table, where, late_rows, early_rows, own, other_first, other_rest, choices, got, before, guard, after, model
        )
        for mine, theirs in zip(outs[::2], outs[1::2]):
            halves.extend([mine, swap(theirs, 1, 0)])
        all_choices.extend(choices)
        return sums

    def pass_on(turn, name, after, chunk=None):
        coming = got[turn - 1, "B" if name == "A" else "A"]
        parts, start, chunked = (first, rest), cut, turn == depth and name == "B"
        if chunk is not None:
            coming, parts, start = [coming[chunk]], (first[chunk:][:1], rest[chunk:][:1]), 0
        values = combine(table, where, coming, *parts, turn, name, uses[turn, name], start, after, chunked)
        got.setdefault((turn, name), []).extend(swap_z(value, name) for value in values)
        return values[-1]

    def choices_of(turn):
        both = any(b[turn, "A"] >= 0 and b[turn, "B"] >= 0 for b in brought)
        return [[(turn, "A")], [(turn, "B")]] if both else [[(turn, "A"), (turn, "B")]]

    rest = []
    marker = pass_on(3, "B", [sent[1]], 0) if only_first else sent[1]
    for rows, columns, name in ((late_rows, model - cut, "rest_late"), (early_rows, cut, "rest_early")):
        rest.append(
            products(table, where, rows, late_rows, own, other_rest, 1, model, columns, name, [marker])
        )
    marker = pass_on(3, "A", rest)
    for chunk in range(2)[only_first:]:
        marker = pass_on(3, "B", [marker], chunk)
    sums = backprop([[(0, "own")], [(1, "A")], [(1, "B")]], None, False, [marker])
    early_halves = halves[1::2]
    for turn in range(2, depth):
        choices = choices_of(turn)
        if turn > 2:
            pass_on(turn + 1, "B", [sums, *early_halves])
            marker = pass_on(turn + 1, "A", [sums, *early_halves])
        sums = backprop(choices, sums, len(choices) == 1, [marker])
    slot_grad = sums[0:1, :slots] + swap(sums[0:1, slots:], 1, 0)
    grads = lax.all_to_all(
        slot_grad.reshape(experts, tokens), "exp", split_axis=0, concat_axis=0, tiled=True
    )
    logit_grad = logits_grad(gates, expert_ids.T, grads)
    hidden_grad = join_hidden(table, where, all_choices, halves, slots, hidden, None, [])
    weight_grad = total_grad(got[depth, "A"], got[depth, "B"], rest, cut)
    return (logit_grad.T, hidden_grad[None, None], weight_grad)


def routing_tables(expert_ids, count_experts, capacity):
    columns = jnp.arange(count_experts, dtype=jnp.int32)
    matches = expert_ids[:, :, None] == columns[None, None, :]
    per_token = jnp.sum(matches.astype(jnp.int32), axis=1)
    rank_table = jnp.cumsum(per_token, axis=0) - per_token
    slot_iota = jnp.arange(capacity, dtype=jnp.int32)
    select = (per_token.T[:, None, :] == 1) & (rank_table.T[:, None, :] == slot_iota[None, :, None])
    return (matches.astype(jnp.float32), select)


def per_device_routed(grad_out, top_logits, expert_ids, saved_hidden, w_down):
    count_experts = lax.axis_size("exp")
    slot_count = saved_hidden.shape[2]
    capacity = slot_count // count_experts
    model_width = grad_out.shape[1]
    onehot, select = routing_tables(expert_ids, count_experts, capacity)
    select_wide = select.astype(jnp.float32)
    gate_probs = jax.nn.softmax(top_logits, axis=-1)
    gate_sent = gate_probs.astype(jnp.bfloat16)
    gate_by_expert = jnp.sum(onehot * gate_sent.astype(jnp.float32)[:, :, None], axis=1)
    send_rows = jnp.einsum(
        "ect,td->ecd", select.astype(jnp.bfloat16), grad_out, preferred_element_type=jnp.float32
    ).astype(jnp.bfloat16)
    send_gate = jnp.sum(select_wide * gate_by_expert.T[:, None, :], axis=2).astype(jnp.bfloat16)
    hidden = saved_hidden[0, 0]
    rows_in, gate_in = (
        lax.all_to_all(send_rows, "exp", split_axis=0, concat_axis=0, tiled=True),
        lax.all_to_all(send_gate, "exp", split_axis=0, concat_axis=0, tiled=True),
    )
    flat_rows = rows_in.reshape(slot_count, model_width)
    backprop = lax.dot_general(
        flat_rows,
        lax.all_gather(w_down[0], "ctx", axis=0, tiled=True),
        (((1,), (1,)), ((), ())),
        preferred_element_type=jnp.float32,
    )
    flat_gate = gate_in.reshape(slot_count, 1).astype(jnp.float32)
    hidden_grad = (flat_gate * backprop).astype(jnp.bfloat16)
    slot_grad = jnp.sum(hidden.astype(jnp.float32) * backprop, axis=1)
    scaled = (flat_gate * flat_rows.astype(jnp.float32)).astype(jnp.bfloat16)
    partial_grad = lax.dot_general(
        hidden, scaled, (((0,), (0,)), ((), ())), preferred_element_type=jnp.float32
    )
    weight_grad = lax.psum_scatter(partial_grad, "ctx", scatter_dimension=0, tiled=True)
    returned = lax.all_to_all(
        slot_grad.reshape(count_experts, capacity), "exp", split_axis=0, concat_axis=0, tiled=True
    )
    grad_by_expert = jnp.sum(select_wide * returned[:, :, None], axis=1)
    gate_grad = jnp.sum(onehot * grad_by_expert.T[:, None, :], axis=2)
    logit_grad = gate_probs * (gate_grad - jnp.sum(gate_probs * gate_grad, axis=1, keepdims=True))
    return (logit_grad, hidden_grad.reshape(1, 1, slot_count, -1), weight_grad[None])


def per_device(grad_out, top_logits, expert_ids, saved_hidden, w_down):
    experts = lax.axis_size("exp")
    groups = lax.axis_size("ctx")
    everywhere = top_logits.shape[1] == experts and saved_hidden.shape[2] == experts * grad_out.shape[0]
    plain = experts & (experts - 1) == 0 and groups % 4 == 0 and groups >= 8
    body = per_device_full if everywhere and plain else per_device_routed
    return body(grad_out, top_logits, expert_ids, saved_hidden, w_down)


def solution(mesh):
    return jax.shard_map(
        per_device,
        mesh=mesh,
        in_specs=(
            P(("ctx", "exp"), None),
            P(("ctx", "exp"), None),
            P(("ctx", "exp"), None),
            P("ctx", "exp", None, None),
            P("exp", "ctx", None),
        ),
        out_specs=(P(("ctx", "exp"), None), P("ctx", "exp", None, None), P("exp", "ctx", None)),
        check_vma=False,
    )
```

```python
import functools

import jax
import jax.numpy as jnp
import numpy as np
from jax import lax
from jax.experimental import pallas as pl
from jax.experimental.pallas import tpu as pltpu
from jax.sharding import PartitionSpec as P

LANES = 128
SCALE = 1_000_000
NT = (((1,), (1,)), ((), ()))
NN = (((1,), (0,)), ((), ()))
f32 = jnp.float32
bf16 = jnp.bfloat16


def dot(a, b, dims):
    return lax.dot_general(a, b, dims, preferred_element_type=f32)


def anywhere():
    return pl.BlockSpec(memory_space=pl.ANY)


def whole():
    return pl.BlockSpec(memory_space=pltpu.VMEM)


def scalars():
    return pl.BlockSpec(memory_space=pltpu.SMEM)


def params(mib=24):
    return pltpu.CompilerParams(vmem_limit_bytes=mib * 1024 * 1024)


def taking(microseconds):
    return pl.CostEstimate(flops=int(microseconds * SCALE), bytes_accessed=int(microseconds * 3e6), transcendentals=0)


def chain_plan(depth):
    products, weights = [], []
    for z in range(depth):
        uses = []
        for turn in range(2, depth + 1):
            if z < depth - 1 and turn >= z + 2:
                uses.append((turn, "AB"[z % 2], depth + 1 + z - turn))
            if z > 0 and turn >= depth - z + 1:
                uses.append((turn, "BA"[z % 2], z + turn - depth - 1))
        products.append(sorted(uses) + [(depth + 1, "own", z)])
        brought = {}
        for turn in range(1, depth):
            for name in "AB":
                index = z + turn if (name == "A") == (z % 2 == 0) else z - turn
                brought[turn, name] = index if 0 <= index < depth else -1
        weights.append(brought)
    return products, weights


class Scalars:
    def __init__(self):
        self.columns = []
        self.names = {}

    def add(self, name, values):
        self.names[name] = len(self.columns)
        self.columns.append(values)

    def __getitem__(self, name):
        return self.names[name]

    def row(self, place, me):
        return jnp.asarray(np.stack(self.columns, axis=-1).astype(np.int32))[place, me]


def device_scalars(depth, experts):
    products, weights = chain_plan(depth)
    table = Scalars()
    along = np.arange(2 * depth)[:, None] + np.zeros((1, experts), np.int32)

    def by_z(values):
        return np.asarray(values)[along // 2]

    table.add("x", along % 2)
    table.add("me", np.zeros_like(along) + np.arange(experts)[None, :])
    table.add(("shard", 0, "own"), along // 2)
    slot_of = [{use[2]: slot for slot, use in enumerate(products[z])} for z in range(depth)]
    for part in range(depth):
        table.add(("slot of", part), by_z([slot_of[z][part] for z in range(depth)]))
    table.add(("slot", 0, "own"), by_z([slot_of[z][z] for z in range(depth)]))
    for turn in range(1, depth):
        for name in "AB":
            shard = [weights[z][turn, name] for z in range(depth)]
            table.add(("shard", turn, name), by_z(shard))
            table.add(("slot", turn, name), by_z([slot_of[z].get(k, 0) for z, k in enumerate(shard)]))
    uses = {}
    for turn in range(2, depth + 1):
        for name in "AB":
            slots = [-1] * depth
            for z in range(depth):
                for slot, use in enumerate(products[z]):
                    if use[:2] == (turn, name):
                        slots[z] = slot
            uses[turn, name] = slots
            table.add(("use", turn, name), by_z(slots))
            limit = max(depth - 3, 0)
            table.add(("block", turn, name), by_z([min(max(slot - 1, 0), limit) for slot in slots]))
    return table, weights, uses


def rows_kernel(cut, grad_hbm, logits_hbm, ids_hbm, late_ref, early_ref, gates_ref, *scratch):
    grad_ref, logits_ref, ids_ref, sems = scratch
    model, tokens = grad_ref.shape
    copies = [
        pltpu.make_async_copy(source, target, sems.at[place])
        for place, (source, target) in enumerate(
            ((grad_hbm, grad_ref), (logits_hbm, logits_ref), (ids_hbm, ids_ref))
        )
    ]
    for copy in copies:
        copy.start()
    for copy in copies:
        copy.wait()
    count = logits_ref.shape[0]
    width = cut + late_ref.shape[1]
    logits = logits_ref[...]
    powers = jnp.exp(logits - jnp.max(logits, axis=0, keepdims=True))
    gates = powers / jnp.sum(powers, axis=0, keepdims=True)
    gates_ref[...] = gates
    sent = gates.astype(bf16).astype(f32)
    ids = ids_ref[...]
    row = lax.broadcasted_iota(jnp.int32, (width - model, tokens), 0)
    extra = jnp.zeros((width - model, tokens), f32)
    for expert in range(count):
        chosen = jnp.sum(jnp.where(ids == expert, sent, 0.0), axis=0, keepdims=True)
        extra = extra + jnp.where(row == expert, chosen, 0.0)
    for start in range(0, width, LANES):
        stop = start + LANES
        if stop <= model:
            block = grad_ref[start:stop, :].astype(f32)
        elif start >= model:
            block = extra[start - model : stop - model, :]
        else:
            block = jnp.concatenate(
                [grad_ref[start:model, :].astype(f32), extra[: stop - model, :]], axis=0
            )
        turned = block.T.astype(bf16)
        if start < cut:
            early_ref[:, start:stop] = turned
        else:
            late_ref[:, start - cut : stop - cut] = turned


def make_rows(grad_out, top_logits, expert_ids, width, cut):
    tokens, model = grad_out.shape
    count = top_logits.shape[1]
    return pl.pallas_call(
        functools.partial(rows_kernel, cut),
        out_shape=(
            jax.ShapeDtypeStruct((tokens, width - cut), bf16),
            jax.ShapeDtypeStruct((tokens, cut), bf16),
            jax.ShapeDtypeStruct((count, tokens), f32),
        ),
        in_specs=[pl.BlockSpec(memory_space=pltpu.HBM)] * 3,
        out_specs=(whole(),) * 3,
        scratch_shapes=[
            pltpu.VMEM((model, tokens), bf16),
            pltpu.VMEM((count, tokens), f32),
            pltpu.VMEM((count, tokens), jnp.int32),
            pltpu.SemaphoreType.DMA((3,)),
        ],
        compiler_params=params(58),
        cost_estimate=taking(2),
        name="make_rows",
    )(grad_out.T, top_logits.T, expert_ids.T)


def pack_kernel(*refs):
    out_ref, sems = refs[-2:]
    copies = []
    for place in range(out_ref.shape[0]):
        copies.append(pltpu.make_async_copy(refs[place], out_ref.at[place], sems.at[place]))
        copies[-1].start()
    for copy in copies:
        copy.wait()


def pack(values, after):
    number = len(values)
    return pl.pallas_call(
        pack_kernel,
        out_shape=jax.ShapeDtypeStruct((number, *values[0].shape), values[0].dtype),
        in_specs=[anywhere()] * (number + len(after)),
        out_specs=anywhere(),
        scratch_shapes=[pltpu.SemaphoreType.DMA((number,))],
        compiler_params=params(),
        cost_estimate=taking(1),
        name="pack_rows",
    )(*values, *after)


def blocks_of(refs, places):
    return [refs[array] if place is None else refs[array].at[place] for array, place in places]


def hold_kernel(*refs):
    del refs


def hold(values, after):
    return pl.pallas_call(
        hold_kernel,
        out_shape=tuple(jax.ShapeDtypeStruct(value.shape, value.dtype) for value in values),
        in_specs=[anywhere()] * (len(values) + len(after)),
        out_specs=(anywhere(),) * len(values),
        input_output_aliases={place: place for place in range(len(values))},
        compiler_params=params(),
        cost_estimate=taking(0),
        name="hold",
    )(*values, *after)


def split_kernel(table, where_ref, hidden_ref, *refs):
    own_ref, first_ref, rest_ref = refs[-3:]
    parts, units, _ = own_ref.shape
    row = lax.broadcasted_iota(jnp.int32, (2 * units, 2 * units), 0)
    column = lax.broadcasted_iota(jnp.int32, (2 * units, 2 * units), 1)
    unit = jnp.where(row == column, 1.0, 0.0).astype(bf16)
    low = where_ref[table["x"]] == 0
    for part in range(parts):
        block = hidden_ref[:, part * 2 * units : (part + 1) * 2 * units]
        turned = dot(unit, block, NT).astype(bf16)
        slot = where_ref[table["slot of", part]]
        other = jnp.where(low, turned[units:], turned[:units])
        own_ref[slot] = jnp.where(low, turned[:units], turned[units:])

        @pl.when(slot == 0)
        def _():
            first_ref[0] = other

        @pl.when(slot != 0)
        def _():
            rest_ref[slot - 1] = other


def split_hidden(table, where, hidden, parts, units, after):
    slots = hidden.shape[0]
    return pl.pallas_call(
        functools.partial(split_kernel, table),
        out_shape=tuple(
            jax.ShapeDtypeStruct((count, units, slots), bf16) for count in (parts, 1, parts - 1)
        ),
        in_specs=[scalars(), whole()] + [anywhere()] * len(after),
        out_specs=(whole(),) * 3,
        compiler_params=params(),
        cost_estimate=taking(2),
        name="split_hidden",
    )(where, hidden, *after)


def place_of(place, count, me, tokens):
    start = (place // count) * count * tokens + ((place % count) ^ me) * tokens
    return pl.multiple_of(start, tokens)


def products_kernel(table, model, counts, places, shards, skip, where_ref, *refs):
    used = sum(counts)
    rows = blocks_of(refs[: counts[0]], places[0])
    gated = blocks_of(refs[counts[0] : used], places[1])
    number = len(rows)
    own_ref, other_ref = refs[used : used + 2]
    kept_ref, scaled = refs[-2:]
    tokens = rows[0].shape[0]
    units, slots = own_ref.shape[1:]
    width = kept_ref.shape[2]
    me = where_ref[table["me"]]
    lane = lax.broadcasted_iota(jnp.int32, (tokens, LANES), 1)
    for place in range(number):
        here = pl.ds(place_of(place, number // 2, me, tokens), tokens)
        tile = gated[place][:, gated[place].shape[1] - LANES :]
        picked = jnp.where(lane == model % LANES + me, tile.astype(f32), 0.0)
        gate = jnp.sum(picked, axis=1, keepdims=True)
        scaled[here, :] = (rows[place][:, :width].astype(f32) * gate).astype(bf16)

    def stacked(ref, offset):
        parts = [ref[offset + shard] for shard in range(shards)]
        return jnp.concatenate(parts, axis=0) if len(parts) > 1 else parts[0]

    total = dot(stacked(own_ref, skip), scaled[:slots, :], NN)
    total = total + dot(stacked(other_ref, 0), scaled[slots:, :], NN)
    for shard in range(shards):
        kept_ref[shard] = total[shard * units : (shard + 1) * units]


def products(table, where, rows, gated, own, other, skip, model, width, name, after):
    arrays, places = zip(rows, gated)
    tokens = arrays[0][0].shape[-2]
    counts = [len(part) for part in arrays]
    number = 2 * (own.shape[2] // tokens)
    shards, units, slots = other.shape
    return pl.pallas_call(
        functools.partial(products_kernel, table, model, counts, places, shards, skip),
        out_shape=jax.ShapeDtypeStruct((shards, units, width), f32),
        in_specs=[scalars()] + [whole()] * (sum(counts) + 2) + [anywhere()] * len(after),
        out_specs=whole(),
        scratch_shapes=[pltpu.VMEM((number * tokens, width), bf16)],
        compiler_params=params(),
        cost_estimate=taking(4),
        name=name,
    )(where, *arrays[0], *arrays[1], own, other, *after)


def rows_of(units):
    return units // 2 if units % 32 == 0 else units


def column_parts(arrays, cut):
    return [(0, arrays[0])] if len(arrays) == 1 else [(cut, arrays[0]), (0, arrays[1])]


def combine_kernel(table, key, cut, counts, sides, where_ref, *refs):
    slot = where_ref[table[key]]
    coming = refs[: counts[0]]
    outs = refs[len(refs) - counts[2] :]
    model = sum(ref.shape[1] for ref in coming)
    spans = [(cut, model), (0, cut)] if cut else [(0, model)]
    for chunk, (start, stop) in enumerate(spans):
        if counts[0] == 1:
            total = coming[0][:, start:stop]
        else:
            total = coming[chunk][...]
        total = total.astype(f32)
        for number, side in enumerate(sides):
            flag = slot == 0 if side == "first" else slot > 0
            total = total + jnp.where(flag, refs[counts[0] + len(spans) * number + chunk][0], 0.0)
        total = total.astype(bf16)
        if counts[2] == 1:
            outs[0][:, start:stop] = total
        else:
            outs[chunk][...] = total


def combine(table, where, coming, first, rest, turn, name, used, cut, after, chunked=False):
    units = coming[0].shape[0]
    model = sum(part.shape[1] for part in coming)
    block = rows_of(units)
    column = table["block", turn, name]
    sides, operands, specs = [], [], []
    if any(slot == 0 for slot in used):
        sides.append("first")
        operands += first
        specs += [pl.BlockSpec((1, block, part.shape[2]), lambda j, s: (0, j, 0)) for part in first]
    if any(slot > 0 for slot in used):
        sides.append("rest")
        operands += rest
        specs += [pl.BlockSpec((1, block, part.shape[2]), lambda j, s: (s[column], j, 0)) for part in rest]
    widths = [model - cut, cut] if chunked else [model]
    return pl.pallas_call(
        functools.partial(
            combine_kernel, table, ("use", turn, name), cut, (len(coming), len(operands), len(widths)), sides
        ),
        out_shape=[jax.ShapeDtypeStruct((units, count), bf16) for count in widths],
        grid_spec=pltpu.PrefetchScalarGridSpec(
            num_scalar_prefetch=1,
            grid=(units // block,),
            in_specs=[pl.BlockSpec((block, part.shape[1]), lambda j, s: (j, 0)) for part in coming]
            + specs
            + [anywhere()] * len(after),
            out_specs=[pl.BlockSpec((block, count), lambda j, s: (j, 0)) for count in widths],
        ),
        compiler_params=params(),
        cost_estimate=taking(1.5),
        name="combine",
    )(where, *coming, *operands, *after)


def begin_kernel(table, start, stop, where_ref, coming_ref, kept_ref, *refs):
    out_ref = refs[-1]
    flag = where_ref[table["use", 2, "A"]] == 0
    total = coming_ref[:, start:stop].astype(f32) + jnp.where(flag, kept_ref[0], 0.0)
    out_ref[...] = total.astype(bf16)


def begin(table, where, coming, kept, start, after):
    units, model = coming.shape
    width = kept.shape[2]
    block = rows_of(units)
    return pl.pallas_call(
        functools.partial(begin_kernel, table, start, start + width),
        out_shape=jax.ShapeDtypeStruct((units, width), bf16),
        grid_spec=pltpu.PrefetchScalarGridSpec(
            num_scalar_prefetch=1,
            grid=(units // block,),
            in_specs=[
                pl.BlockSpec((block, model), lambda j, s: (j, 0)),
                pl.BlockSpec((1, block, width), lambda j, s: (0, j, 0)),
            ]
            + [anywhere()] * len(after),
            out_specs=pl.BlockSpec((block, width), lambda j, s: (j, 0)),
        ),
        compiler_params=params(),
        cost_estimate=taking(1),
        name="begin",
    )(where, coming, kept, *after)


def total_kernel(cut, counts, *refs):
    coming = [refs[: counts[0]], refs[counts[0] : sum(counts)]]
    out_ref = refs[-1]
    for chunk, start in enumerate((cut, 0)):
        kept_ref = refs[sum(counts) + chunk]
        here = slice(start, start + kept_ref.shape[2])
        total = kept_ref[0]
        for parts in coming:
            total = total + (parts[0][:, here] if len(parts) == 1 else parts[chunk][...]).astype(f32)
        out_ref[0, :, here] = total


def total_grad(a, b, kept, cut):
    units = a[0].shape[0]
    model = sum(part.shape[1] for part in a)
    block = rows_of(units)
    return pl.pallas_call(
        functools.partial(total_kernel, cut, (len(a), len(b))),
        out_shape=jax.ShapeDtypeStruct((1, units, model), f32),
        grid=(units // block,),
        in_specs=[pl.BlockSpec((block, part.shape[1]), lambda j: (j, 0)) for part in (*a, *b)]
        + [
            pl.BlockSpec((1, block, part.shape[2]), functools.partial(lambda last, j: (last, j, 0), part.shape[0] - 1))
            for part in kept
        ],
        out_specs=pl.BlockSpec((1, block, model), lambda j: (0, j, 0)),
        compiler_params=params(),
        cost_estimate=taking(2),
        name="total_grad",
    )(*a, *b, *kept)


def back_kernel(table, model, cut, counts, places, choices, parts, guard, summed, where_ref, *refs):
    keys = [key for choice in choices for key in choice]
    used = sum(counts)
    late = blocks_of(refs[: counts[0]], places[0])
    early = blocks_of(refs[counts[0] : used], places[1])
    number = len(late)
    own_ref, first_ref, rest_ref = refs[used : used + 3]
    weight_refs, used = {}, used + 3
    for key, count in zip(keys, parts):
        weight_refs[key] = refs[used : used + count]
        used += count
    before_ref = refs[used] if summed else None
    outs = refs[len(refs) - 2 * len(choices) - 1 : -1]
    sums_ref = refs[-1]
    tokens = late[0].shape[0]
    units = own_ref.shape[1]
    me = where_ref[table["me"]]
    start = late[0].shape[1] - LANES
    eight = lax.broadcasted_iota(jnp.int32, (8, LANES), 1)
    onehot = jnp.where(eight == model % LANES + me, 1.0, 0.0).astype(bf16)
    shards = {key: where_ref[table[("shard",) + key]] for key in keys}
    slots = {key: where_ref[table[("slot",) + key]] for key in keys}
    sums_ref[...] = before_ref[...] if summed else jnp.zeros(sums_ref.shape, f32)

    def whole_weight(key):
        got = weight_refs[key]
        return got[0][...] if len(got) == 1 else jnp.concatenate([got[1][...], got[0][...]], axis=1)

    def work():
        stack, here_valid, here_slot = [], [], []
        for choice in choices:
            weight, valid, slot = whole_weight(choice[0]), shards[choice[0]] >= 0, slots[choice[0]]
            for key in choice[1:]:
                weight = jnp.where(valid, weight, whole_weight(key))
                slot = jnp.where(valid, slot, slots[key])
                valid = jnp.logical_or(valid, shards[key] >= 0)
            stack.append(weight)
            here_valid.append(valid)
            here_slot.append(slot)
        weight = jnp.concatenate(stack, axis=0) if len(stack) > 1 else stack[0]
        for pair in range(0, number, 2):
            both = jnp.concatenate(
                [
                    jnp.concatenate([early[k][...], late[k][:, : model - cut]], axis=1)
                    for k in (pair, pair + 1)
                ],
                axis=0,
            )
            product = dot(weight, both, NT)
            for place in (pair, pair + 1):
                near = place < number // 2
                block = product[:, (place - pair) * tokens : (place - pair + 1) * tokens]
                gate = dot(onehot, late[place][:, start:], NT)[0:1]
                here = pl.ds(place_of(place % (number // 2), number // 2, me, tokens), tokens)
                wide = pl.ds(place_of(place, number // 2, me, tokens), tokens)
                gated = (block * gate).astype(bf16)
                total = jnp.zeros((1, tokens), f32)
                for index, (valid, slot) in enumerate(zip(here_valid, here_slot)):
                    some = slice(index * units, (index + 1) * units)
                    outs[2 * index + (0 if near else 1)][:, here] = gated[some]
                    if near:
                        hidden = own_ref[slot, :, here].astype(f32)
                    else:
                        hidden = jnp.where(
                            slot == 0,
                            first_ref[0, :, here].astype(f32),
                            rest_ref[jnp.maximum(slot - 1, 0), :, here].astype(f32),
                        )
                    part = jnp.sum(hidden * block[some], axis=0, keepdims=True)
                    total = total + jnp.where(valid, part, 0.0)
                sums_ref[0:1, wide] += total

    if guard:
        pl.when(functools.reduce(jnp.logical_or, [shards[key] >= 0 for key in keys]))(work)
    else:
        work()


def back_part(table, where, late, early, own, first, rest, choices, got, before, guard, after, model):
    units, slots = own.shape[1:]
    arrays, places = zip(late, early)
    counts = [len(part) for part in arrays]
    cut = arrays[1][0].shape[-1]
    keys = [key for choice in choices for key in choice]
    weights = [got[key] for key in keys]
    flat = [part for weight in weights for part in weight]
    half = jax.ShapeDtypeStruct((units, slots), bf16)
    summed = before is not None
    operands = [*arrays[0], *arrays[1], own, first, rest, *flat] + ([before] if summed else [])
    outs = [half] * (2 * len(choices)) + [jax.ShapeDtypeStruct((8, 2 * slots), f32)]
    parts = [len(weight) for weight in weights]
    return pl.pallas_call(
        functools.partial(
            back_kernel, table, model, cut, counts, places, choices, parts, guard, summed
        ),
        out_shape=outs,
        in_specs=[scalars()] + [whole()] * len(operands) + [anywhere()] * len(after),
        out_specs=[whole()] * len(outs),
        compiler_params=params(),
        cost_estimate=taking(6),
        name="back_part",
    )(where, *operands, *after)


def join_kernel(table, choices, where_ref, *refs):
    out_ref, turned, sem = refs[-3:]
    slots, width = turned.shape[1:]
    row = lax.broadcasted_iota(jnp.int32, (slots, slots), 0)
    column = lax.broadcasted_iota(jnp.int32, (slots, slots), 1)
    unit = jnp.where(row == column, 1.0, 0.0).astype(bf16)
    low = where_ref[table["x"]] == 0
    copies = []
    for place, choice in enumerate(choices):
        mine, theirs = refs[2 * place][...], refs[2 * place + 1][...]
        index = where_ref[table[("shard",) + choice[0]]]
        for key in choice[1:]:
            index = jnp.where(index >= 0, index, where_ref[table[("shard",) + key]])
        both = jnp.concatenate([jnp.where(low, mine, theirs), jnp.where(low, theirs, mine)], axis=0)
        turned[place] = dot(unit, both, NT).astype(bf16)
        here = pl.ds(pl.multiple_of(jnp.maximum(index, 0) * width, LANES), width)
        copy = pltpu.make_async_copy(turned.at[place], out_ref.at[:, here], sem.at[place])
        copies.append((index, copy))
        pl.when(index >= 0)(copy.start)
    for index, copy in copies:
        pl.when(index >= 0)(copy.wait)


def join_hidden(table, where, choices, halves, slots, hidden, before, after):
    units = halves[0].shape[0]
    extends = before is not None
    return pl.pallas_call(
        functools.partial(join_kernel, table, choices),
        out_shape=jax.ShapeDtypeStruct((slots, hidden), bf16),
        in_specs=[scalars()] + [whole()] * len(halves) + [anywhere()] * (extends + len(after)),
        out_specs=anywhere(),
        scratch_shapes=[
            pltpu.VMEM((len(choices), slots, 2 * units), bf16),
            pltpu.SemaphoreType.DMA((len(choices),)),
        ],
        input_output_aliases={1 + len(halves): 0} if extends else {},
        compiler_params=params(),
        cost_estimate=taking(2),
        name="join_hidden",
    )(where, *halves, *([before] if extends else []), *after)


def logits_kernel(gates_ref, ids_ref, grads_ref, out_ref):
    gates, ids, grads = gates_ref[...], ids_ref[...], grads_ref[...]
    picked = jnp.zeros_like(gates)
    for expert in range(grads.shape[0]):
        picked = picked + jnp.where(ids == expert, grads[expert : expert + 1, :], 0.0)
    out_ref[...] = gates * (picked - jnp.sum(gates * picked, axis=0, keepdims=True))


def logits_grad(gates, ids, grads):
    return pl.pallas_call(
        logits_kernel,
        out_shape=jax.ShapeDtypeStruct(gates.shape, f32),
        in_specs=[whole()] * 3,
        out_specs=whole(),
        compiler_params=params(),
        cost_estimate=taking(1),
        name="logits_grad",
    )(gates, ids, grads)


def per_device_full(grad_out, top_logits, expert_ids, saved_hidden, w_down):
    experts = lax.axis_size("exp")
    groups = lax.axis_size("ctx")
    depth = groups // 2
    tokens, model = grad_out.shape
    slots, hidden = saved_hidden.shape[2:]
    width = pl.cdiv(model + experts, LANES) * LANES
    cut = width // LANES // 2 * LANES

    table, brought, uses = device_scalars(depth, experts)
    where = table.row(lax.axis_index("ctx"), lax.axis_index("exp"))

    def swap(value, x, exp):
        if not exp:
            return lax.ppermute(value, "ctx", [(i, i ^ x) for i in range(groups)])
        if not x:
            return lax.ppermute(value, "exp", [(i, i ^ exp) for i in range(experts)])
        pairs = [(c * experts + e, (c ^ x) * experts + (e ^ exp)) for c in range(groups) for e in range(experts)]
        return lax.ppermute(value, ("ctx", "exp"), pairs)

    def swap_z(value, name):
        first = "AB".index(name)
        pairs = []
        for z in range(first, depth - 1, 2):
            for x in range(2):
                pairs += [(2 * z + x, 2 * z + 2 + x), (2 * z + 2 + x, 2 * z + x)]
        return lax.ppermute(value, "ctx", pairs)

    got = {(0, "own"): [w_down[0]]}
    for name in "BA":
        got[1, name] = [swap_z(w_down[0], name)]

    late, early, gates = make_rows(grad_out, top_logits, expert_ids, width, cut)
    highs = list(range(2, experts, 2))

    def sides(mine):
        return [mine, swap(mine, 0, 1)]

    late_x = swap(late, 1, 0)
    late_mine = [late] + [swap(late, 0, high) for high in highs]
    late_mine += [late_x] + [swap(late_x, 0, high) for high in highs]
    own, other_first, other_rest = split_hidden(
        table, where, saved_hidden[0, 0], depth, w_down.shape[1], [late]
    )
    (early,) = hold((early,), [late_x, own])
    other_first = swap(other_first, 1, 0)
    early_x = swap(early, 1, 0)
    late_rows = sides(pack(late_mine, [got[1, "B"][0], got[1, "A"][0], early_x]))
    late_rows = (late_rows, [(side, place) for place in range(experts) for side in range(2)])
    early_rows = sides(pack([early, early_x], []))
    places = [(0, 0), (1, 0)]
    for block, base in ((early, 0), (early_x, 1)):
        if base:
            places += [(0, 1), (1, 1)]
        for high in highs:
            places += [(len(early_rows), None), (len(early_rows) + 1, None)]
            early_rows += sides(swap(block, 0, high))
    early_rows = (early_rows, places)
    (other_rest,) = hold((other_rest,), [other_first])
    other_rest = swap(other_rest, 1, 0)

    first = [products(table, where, late_rows, late_rows, own, other_first, 0, model, model - cut, "first_late", [])]
    sent = [begin(table, where, got[1, "B"][0], first[0], cut, [early_rows[0][1]])]
    got[2, "A"] = [swap_z(sent[0], "A")]
    got[2, "B"] = [swap_z(got[1, "A"][0], "B")]
    first.append(
        products(table, where, early_rows, late_rows, own, other_first, 0, model, cut, "first_early", [other_rest])
    )
    sent.append(begin(table, where, got[1, "B"][0], first[1], 0, [got[2, "A"][0]]))
    got[2, "A"].append(swap_z(sent[1], "A"))

    halves, all_choices = [], []
    only_first = max(uses[3, "B"]) <= 0

    def backprop(choices, before, guard, after):
        *outs, sums = back_part(
            table, where, late_rows, early_rows, own, other_first, other_rest, choices, got, before, guard, after, model
        )
        for mine, theirs in zip(outs[::2], outs[1::2]):
            halves.extend([mine, swap(theirs, 1, 0)])
        all_choices.extend(choices)
        return sums

    def pass_on(turn, name, after, chunk=None):
        coming = got[turn - 1, "B" if name == "A" else "A"]
        parts, start, chunked = (first, rest), cut, turn == depth and name == "B"
        if chunk is not None:
            coming, parts, start = [coming[chunk]], (first[chunk:][:1], rest[chunk:][:1]), 0
        values = combine(table, where, coming, *parts, turn, name, uses[turn, name], start, after, chunked)
        got.setdefault((turn, name), []).extend(swap_z(value, name) for value in values)
        return values[-1]

    def choices_of(turn):
        both = any(b[turn, "A"] >= 0 and b[turn, "B"] >= 0 for b in brought)
        return [[(turn, "A")], [(turn, "B")]] if both else [[(turn, "A"), (turn, "B")]]

    rest = []
    marker = pass_on(3, "B", [sent[1]], 0) if only_first else sent[1]
    for rows, columns, name in ((late_rows, model - cut, "rest_late"), (early_rows, cut, "rest_early")):
        rest.append(
            products(table, where, rows, late_rows, own, other_rest, 1, model, columns, name, [marker])
        )
    marker = pass_on(3, "A", rest)
    for chunk in range(2)[only_first:]:
        marker = pass_on(3, "B", [marker], chunk)
    sums = backprop([[(0, "own")], [(1, "A")], [(1, "B")]], None, False, [marker])
    for turn in range(2, depth):
        choices = choices_of(turn)
        if turn > 2:
            pass_on(turn + 1, "B", [sums])
            marker = pass_on(turn + 1, "A", [sums])
        sums = backprop(choices, sums, len(choices) == 1, [marker])
    slot_grad = sums[0:1, :slots] + swap(sums[0:1, slots:], 1, 0)
    grads = lax.all_to_all(
        slot_grad.reshape(experts, tokens), "exp", split_axis=0, concat_axis=0, tiled=True
    )
    logit_grad = logits_grad(gates, expert_ids.T, grads)
    hidden_grad = join_hidden(table, where, all_choices, halves, slots, hidden, None, [])
    weight_grad = total_grad(got[depth, "A"], got[depth, "B"], rest, cut)
    return (logit_grad.T, hidden_grad[None, None], weight_grad)


def routing_tables(expert_ids, count_experts, capacity):
    columns = jnp.arange(count_experts, dtype=jnp.int32)
    matches = expert_ids[:, :, None] == columns[None, None, :]
    per_token = jnp.sum(matches.astype(jnp.int32), axis=1)
    rank_table = jnp.cumsum(per_token, axis=0) - per_token
    slot_iota = jnp.arange(capacity, dtype=jnp.int32)
    select = (per_token.T[:, None, :] == 1) & (rank_table.T[:, None, :] == slot_iota[None, :, None])
    return (matches.astype(jnp.float32), select)


def per_device_routed(grad_out, top_logits, expert_ids, saved_hidden, w_down):
    count_experts = lax.axis_size("exp")
    slot_count = saved_hidden.shape[2]
    capacity = slot_count // count_experts
    model_width = grad_out.shape[1]
    onehot, select = routing_tables(expert_ids, count_experts, capacity)
    select_wide = select.astype(jnp.float32)
    gate_probs = jax.nn.softmax(top_logits, axis=-1)
    gate_sent = gate_probs.astype(jnp.bfloat16)
    gate_by_expert = jnp.sum(onehot * gate_sent.astype(jnp.float32)[:, :, None], axis=1)
    send_rows = jnp.einsum(
        "ect,td->ecd", select.astype(jnp.bfloat16), grad_out, preferred_element_type=jnp.float32
    ).astype(jnp.bfloat16)
    send_gate = jnp.sum(select_wide * gate_by_expert.T[:, None, :], axis=2).astype(jnp.bfloat16)
    hidden = saved_hidden[0, 0]
    rows_in, gate_in = (
        lax.all_to_all(send_rows, "exp", split_axis=0, concat_axis=0, tiled=True),
        lax.all_to_all(send_gate, "exp", split_axis=0, concat_axis=0, tiled=True),
    )
    flat_rows = rows_in.reshape(slot_count, model_width)
    backprop = lax.dot_general(
        flat_rows,
        lax.all_gather(w_down[0], "ctx", axis=0, tiled=True),
        (((1,), (1,)), ((), ())),
        preferred_element_type=jnp.float32,
    )
    flat_gate = gate_in.reshape(slot_count, 1).astype(jnp.float32)
    hidden_grad = (flat_gate * backprop).astype(jnp.bfloat16)
    slot_grad = jnp.sum(hidden.astype(jnp.float32) * backprop, axis=1)
    scaled = (flat_gate * flat_rows.astype(jnp.float32)).astype(jnp.bfloat16)
    partial_grad = lax.dot_general(
        hidden, scaled, (((0,), (0,)), ((), ())), preferred_element_type=jnp.float32
    )
    weight_grad = lax.psum_scatter(partial_grad, "ctx", scatter_dimension=0, tiled=True)
    returned = lax.all_to_all(
        slot_grad.reshape(count_experts, capacity), "exp", split_axis=0, concat_axis=0, tiled=True
    )
    grad_by_expert = jnp.sum(select_wide * returned[:, :, None], axis=1)
    gate_grad = jnp.sum(onehot * grad_by_expert.T[:, None, :], axis=2)
    logit_grad = gate_probs * (gate_grad - jnp.sum(gate_probs * gate_grad, axis=1, keepdims=True))
    return (logit_grad, hidden_grad.reshape(1, 1, slot_count, -1), weight_grad[None])


def per_device(grad_out, top_logits, expert_ids, saved_hidden, w_down):
    experts = lax.axis_size("exp")
    groups = lax.axis_size("ctx")
    everywhere = top_logits.shape[1] == experts and saved_hidden.shape[2] == experts * grad_out.shape[0]
    plain = experts & (experts - 1) == 0 and groups % 4 == 0 and groups >= 8
    body = per_device_full if everywhere and plain else per_device_routed
    return body(grad_out, top_logits, expert_ids, saved_hidden, w_down)


def solution(mesh):
    return jax.shard_map(
        per_device,
        mesh=mesh,
        in_specs=(
            P(("ctx", "exp"), None),
            P(("ctx", "exp"), None),
            P(("ctx", "exp"), None),
            P("ctx", "exp", None, None),
            P("exp", "ctx", None),
        ),
        out_specs=(P(("ctx", "exp"), None), P("ctx", "exp", None, None), P("exp", "ctx", None)),
        check_vma=False,
    )
```

```python
import functools

import jax
import jax.numpy as jnp
import numpy as np
from jax import lax
from jax.experimental import pallas as pl
from jax.experimental.pallas import tpu as pltpu
from jax.sharding import PartitionSpec as P

LANES = 128
SCALE = 1_000_000
BEGIN_WEIGHT = 600
NT = (((1,), (1,)), ((), ()))
NN = (((1,), (0,)), ((), ()))
f32 = jnp.float32
bf16 = jnp.bfloat16


def dot(a, b, dims):
    return lax.dot_general(a, b, dims, preferred_element_type=f32)


def anywhere():
    return pl.BlockSpec(memory_space=pl.ANY)


def whole():
    return pl.BlockSpec(memory_space=pltpu.VMEM)


def scalars():
    return pl.BlockSpec(memory_space=pltpu.SMEM)


def params(mib=24):
    return pltpu.CompilerParams(vmem_limit_bytes=mib * 1024 * 1024)


def taking(microseconds):
    return pl.CostEstimate(flops=int(microseconds * SCALE), bytes_accessed=int(microseconds * 3e6), transcendentals=0)


def chain_plan(depth):
    products, weights = [], []
    for z in range(depth):
        uses = []
        for turn in range(2, depth + 1):
            if z < depth - 1 and turn >= z + 2:
                uses.append((turn, "AB"[z % 2], depth + 1 + z - turn))
            if z > 0 and turn >= depth - z + 1:
                uses.append((turn, "BA"[z % 2], z + turn - depth - 1))
        products.append(sorted(uses) + [(depth + 1, "own", z)])
        brought = {}
        for turn in range(1, depth):
            for name in "AB":
                index = z + turn if (name == "A") == (z % 2 == 0) else z - turn
                brought[turn, name] = index if 0 <= index < depth else -1
        weights.append(brought)
    return products, weights


class Scalars:
    def __init__(self):
        self.columns = []
        self.names = {}

    def add(self, name, values):
        self.names[name] = len(self.columns)
        self.columns.append(values)

    def __getitem__(self, name):
        return self.names[name]

    def row(self, place, me):
        return jnp.asarray(np.stack(self.columns, axis=-1).astype(np.int32))[place, me]


def device_scalars(depth, experts):
    products, weights = chain_plan(depth)
    table = Scalars()
    along = np.arange(2 * depth)[:, None] + np.zeros((1, experts), np.int32)

    def by_z(values):
        return np.asarray(values)[along // 2]

    table.add("x", along % 2)
    table.add("me", np.zeros_like(along) + np.arange(experts)[None, :])
    table.add(("shard", 0, "own"), along // 2)
    slot_of = [{use[2]: slot for slot, use in enumerate(products[z])} for z in range(depth)]
    for part in range(depth):
        table.add(("slot of", part), by_z([slot_of[z][part] for z in range(depth)]))
    table.add(("slot", 0, "own"), by_z([slot_of[z][z] for z in range(depth)]))
    for turn in range(1, depth):
        for name in "AB":
            shard = [weights[z][turn, name] for z in range(depth)]
            table.add(("shard", turn, name), by_z(shard))
            table.add(("slot", turn, name), by_z([slot_of[z].get(k, 0) for z, k in enumerate(shard)]))
    uses = {}
    for turn in range(2, depth + 1):
        for name in "AB":
            slots = [-1] * depth
            for z in range(depth):
                for slot, use in enumerate(products[z]):
                    if use[:2] == (turn, name):
                        slots[z] = slot
            uses[turn, name] = slots
            table.add(("use", turn, name), by_z(slots))
            limit = max(depth - 3, 0)
            table.add(("block", turn, name), by_z([min(max(slot - 1, 0), limit) for slot in slots]))
    return table, weights, uses


def rows_kernel(cut, grad_hbm, logits_hbm, ids_hbm, late_ref, early_ref, gates_ref, *scratch):
    grad_ref, logits_ref, ids_ref, sems = scratch
    model, tokens = grad_ref.shape
    copies = [
        pltpu.make_async_copy(source, target, sems.at[place])
        for place, (source, target) in enumerate(
            ((grad_hbm, grad_ref), (logits_hbm, logits_ref), (ids_hbm, ids_ref))
        )
    ]
    for copy in copies:
        copy.start()
    for copy in copies:
        copy.wait()
    count = logits_ref.shape[0]
    width = cut + late_ref.shape[1]
    logits = logits_ref[...]
    powers = jnp.exp(logits - jnp.max(logits, axis=0, keepdims=True))
    gates = powers / jnp.sum(powers, axis=0, keepdims=True)
    gates_ref[...] = gates
    sent = gates.astype(bf16).astype(f32)
    ids = ids_ref[...]
    row = lax.broadcasted_iota(jnp.int32, (width - model, tokens), 0)
    extra = jnp.zeros((width - model, tokens), f32)
    for expert in range(count):
        chosen = jnp.sum(jnp.where(ids == expert, sent, 0.0), axis=0, keepdims=True)
        extra = extra + jnp.where(row == expert, chosen, 0.0)
    for start in range(0, width, LANES):
        stop = start + LANES
        if stop <= model:
            block = grad_ref[start:stop, :].astype(f32)
        elif start >= model:
            block = extra[start - model : stop - model, :]
        else:
            block = jnp.concatenate(
                [grad_ref[start:model, :].astype(f32), extra[: stop - model, :]], axis=0
            )
        turned = block.T.astype(bf16)
        if start < cut:
            early_ref[:, start:stop] = turned
        else:
            late_ref[:, start - cut : stop - cut] = turned


def make_rows(grad_out, top_logits, expert_ids, width, cut):
    tokens, model = grad_out.shape
    count = top_logits.shape[1]
    return pl.pallas_call(
        functools.partial(rows_kernel, cut),
        out_shape=(
            jax.ShapeDtypeStruct((tokens, width - cut), bf16),
            jax.ShapeDtypeStruct((tokens, cut), bf16),
            jax.ShapeDtypeStruct((count, tokens), f32),
        ),
        in_specs=[pl.BlockSpec(memory_space=pltpu.HBM)] * 3,
        out_specs=(whole(),) * 3,
        scratch_shapes=[
            pltpu.VMEM((model, tokens), bf16),
            pltpu.VMEM((count, tokens), f32),
            pltpu.VMEM((count, tokens), jnp.int32),
            pltpu.SemaphoreType.DMA((3,)),
        ],
        compiler_params=params(58),
        cost_estimate=taking(2),
        name="make_rows",
    )(grad_out.T, top_logits.T, expert_ids.T)


def pack_kernel(*refs):
    out_ref, sems = refs[-2:]
    copies = []
    for place in range(out_ref.shape[0]):
        copies.append(pltpu.make_async_copy(refs[place], out_ref.at[place], sems.at[place]))
        copies[-1].start()
    for copy in copies:
        copy.wait()


def pack(values, after):
    number = len(values)
    return pl.pallas_call(
        pack_kernel,
        out_shape=jax.ShapeDtypeStruct((number, *values[0].shape), values[0].dtype),
        in_specs=[anywhere()] * (number + len(after)),
        out_specs=anywhere(),
        scratch_shapes=[pltpu.SemaphoreType.DMA((number,))],
        compiler_params=params(),
        cost_estimate=taking(1),
        name="pack_rows",
    )(*values, *after)


def blocks_of(refs, places):
    return [refs[array] if place is None else refs[array].at[place] for array, place in places]


def hold_kernel(*refs):
    del refs


def hold(values, after):
    return pl.pallas_call(
        hold_kernel,
        out_shape=tuple(jax.ShapeDtypeStruct(value.shape, value.dtype) for value in values),
        in_specs=[anywhere()] * (len(values) + len(after)),
        out_specs=(anywhere(),) * len(values),
        input_output_aliases={place: place for place in range(len(values))},
        compiler_params=params(),
        cost_estimate=taking(0),
        name="hold",
    )(*values, *after)


def split_kernel(table, where_ref, hidden_ref, *refs):
    own_ref, first_ref, rest_ref = refs[-3:]
    parts, units, _ = own_ref.shape
    row = lax.broadcasted_iota(jnp.int32, (2 * units, 2 * units), 0)
    column = lax.broadcasted_iota(jnp.int32, (2 * units, 2 * units), 1)
    unit = jnp.where(row == column, 1.0, 0.0).astype(bf16)
    low = where_ref[table["x"]] == 0
    for part in range(parts):
        block = hidden_ref[:, part * 2 * units : (part + 1) * 2 * units]
        turned = dot(unit, block, NT).astype(bf16)
        slot = where_ref[table["slot of", part]]
        other = jnp.where(low, turned[units:], turned[:units])
        own_ref[slot] = jnp.where(low, turned[:units], turned[units:])

        @pl.when(slot == 0)
        def _():
            first_ref[0] = other

        @pl.when(slot != 0)
        def _():
            rest_ref[slot - 1] = other


def split_hidden(table, where, hidden, parts, units, after):
    slots = hidden.shape[0]
    return pl.pallas_call(
        functools.partial(split_kernel, table),
        out_shape=tuple(
            jax.ShapeDtypeStruct((count, units, slots), bf16) for count in (parts, 1, parts - 1)
        ),
        in_specs=[scalars(), whole()] + [anywhere()] * len(after),
        out_specs=(whole(),) * 3,
        compiler_params=params(),
        cost_estimate=taking(2),
        name="split_hidden",
    )(where, hidden, *after)


def place_of(place, count, me, tokens):
    start = (place // count) * count * tokens + ((place % count) ^ me) * tokens
    return pl.multiple_of(start, tokens)


def products_kernel(table, model, counts, places, shards, skip, where_ref, *refs):
    used = sum(counts)
    rows = blocks_of(refs[: counts[0]], places[0])
    gated = blocks_of(refs[counts[0] : used], places[1])
    number = len(rows)
    own_ref, other_ref = refs[used : used + 2]
    kept_ref, scaled = refs[-2:]
    tokens = rows[0].shape[0]
    units, slots = own_ref.shape[1:]
    width = kept_ref.shape[2]
    me = where_ref[table["me"]]
    lane = lax.broadcasted_iota(jnp.int32, (tokens, LANES), 1)
    for place in range(number):
        here = pl.ds(place_of(place, number // 2, me, tokens), tokens)
        tile = gated[place][:, gated[place].shape[1] - LANES :]
        picked = jnp.where(lane == model % LANES + me, tile.astype(f32), 0.0)
        gate = jnp.sum(picked, axis=1, keepdims=True)
        scaled[here, :] = (rows[place][:, :width].astype(f32) * gate).astype(bf16)

    def stacked(ref, offset):
        parts = [ref[offset + shard] for shard in range(shards)]
        return jnp.concatenate(parts, axis=0) if len(parts) > 1 else parts[0]

    total = dot(stacked(own_ref, skip), scaled[:slots, :], NN)
    total = total + dot(stacked(other_ref, 0), scaled[slots:, :], NN)
    for shard in range(shards):
        kept_ref[shard] = total[shard * units : (shard + 1) * units]


def products(table, where, rows, gated, own, other, skip, model, width, name, after):
    arrays, places = zip(rows, gated)
    tokens = arrays[0][0].shape[-2]
    counts = [len(part) for part in arrays]
    number = 2 * (own.shape[2] // tokens)
    shards, units, slots = other.shape
    return pl.pallas_call(
        functools.partial(products_kernel, table, model, counts, places, shards, skip),
        out_shape=jax.ShapeDtypeStruct((shards, units, width), f32),
        in_specs=[scalars()] + [whole()] * (sum(counts) + 2) + [anywhere()] * len(after),
        out_specs=whole(),
        scratch_shapes=[pltpu.VMEM((number * tokens, width), bf16)],
        compiler_params=params(),
        cost_estimate=taking(4),
        name=name,
    )(where, *arrays[0], *arrays[1], own, other, *after)


def rows_of(units):
    return units // 2 if units % 32 == 0 else units


def column_parts(arrays, cut):
    return [(0, arrays[0])] if len(arrays) == 1 else [(cut, arrays[0]), (0, arrays[1])]


def combine_kernel(table, key, cut, counts, sides, where_ref, *refs):
    slot = where_ref[table[key]]
    coming = refs[: counts[0]]
    outs = refs[len(refs) - counts[2] :]
    model = sum(ref.shape[1] for ref in coming)
    spans = [(cut, model), (0, cut)] if cut else [(0, model)]
    for chunk, (start, stop) in enumerate(spans):
        if counts[0] == 1:
            total = coming[0][:, start:stop]
        else:
            total = coming[chunk][...]
        total = total.astype(f32)
        for number, side in enumerate(sides):
            flag = slot == 0 if side == "first" else slot > 0
            total = total + jnp.where(flag, refs[counts[0] + len(spans) * number + chunk][0], 0.0)
        total = total.astype(bf16)
        if counts[2] == 1:
            outs[0][:, start:stop] = total
        else:
            outs[chunk][...] = total


def combine(table, where, coming, first, rest, turn, name, used, cut, after, chunked=False):
    units = coming[0].shape[0]
    model = sum(part.shape[1] for part in coming)
    block = rows_of(units)
    column = table["block", turn, name]
    sides, operands, specs = [], [], []
    if any(slot == 0 for slot in used):
        sides.append("first")
        operands += first
        specs += [pl.BlockSpec((1, block, part.shape[2]), lambda j, s: (0, j, 0)) for part in first]
    if any(slot > 0 for slot in used):
        sides.append("rest")
        operands += rest
        specs += [pl.BlockSpec((1, block, part.shape[2]), lambda j, s: (s[column], j, 0)) for part in rest]
    widths = [model - cut, cut] if chunked else [model]
    return pl.pallas_call(
        functools.partial(
            combine_kernel, table, ("use", turn, name), cut, (len(coming), len(operands), len(widths)), sides
        ),
        out_shape=[jax.ShapeDtypeStruct((units, count), bf16) for count in widths],
        grid_spec=pltpu.PrefetchScalarGridSpec(
            num_scalar_prefetch=1,
            grid=(units // block,),
            in_specs=[pl.BlockSpec((block, part.shape[1]), lambda j, s: (j, 0)) for part in coming]
            + specs
            + [anywhere()] * len(after),
            out_specs=[pl.BlockSpec((block, count), lambda j, s: (j, 0)) for count in widths],
        ),
        compiler_params=params(),
        cost_estimate=taking(1.5),
        name="combine",
    )(where, *coming, *operands, *after)


def begin_kernel(table, start, stop, where_ref, coming_ref, kept_ref, *refs):
    out_ref = refs[-1]
    flag = where_ref[table["use", 2, "A"]] == 0
    total = coming_ref[:, start:stop].astype(f32) + jnp.where(flag, kept_ref[0], 0.0)
    out_ref[...] = total.astype(bf16)


def begin(table, where, coming, kept, start, after):
    units, model = coming.shape
    width = kept.shape[2]
    block = rows_of(units)
    return pl.pallas_call(
        functools.partial(begin_kernel, table, start, start + width),
        out_shape=jax.ShapeDtypeStruct((units, width), bf16),
        grid_spec=pltpu.PrefetchScalarGridSpec(
            num_scalar_prefetch=1,
            grid=(units // block,),
            in_specs=[
                pl.BlockSpec((block, model), lambda j, s: (j, 0)),
                pl.BlockSpec((1, block, width), lambda j, s: (0, j, 0)),
            ]
            + [anywhere()] * len(after),
            out_specs=pl.BlockSpec((block, width), lambda j, s: (j, 0)),
        ),
        compiler_params=params(),
        cost_estimate=taking(BEGIN_WEIGHT),
        name="begin",
    )(where, coming, kept, *after)


def total_kernel(cut, counts, *refs):
    coming = [refs[: counts[0]], refs[counts[0] : sum(counts)]]
    out_ref = refs[-1]
    for chunk, start in enumerate((cut, 0)):
        kept_ref = refs[sum(counts) + chunk]
        here = slice(start, start + kept_ref.shape[2])
        total = kept_ref[0]
        for parts in coming:
            total = total + (parts[0][:, here] if len(parts) == 1 else parts[chunk][...]).astype(f32)
        out_ref[0, :, here] = total


def total_grad(a, b, kept, cut):
    units = a[0].shape[0]
    model = sum(part.shape[1] for part in a)
    block = rows_of(units)
    return pl.pallas_call(
        functools.partial(total_kernel, cut, (len(a), len(b))),
        out_shape=jax.ShapeDtypeStruct((1, units, model), f32),
        grid=(units // block,),
        in_specs=[pl.BlockSpec((block, part.shape[1]), lambda j: (j, 0)) for part in (*a, *b)]
        + [
            pl.BlockSpec((1, block, part.shape[2]), functools.partial(lambda last, j: (last, j, 0), part.shape[0] - 1))
            for part in kept
        ],
        out_specs=pl.BlockSpec((1, block, model), lambda j: (0, j, 0)),
        compiler_params=params(),
        cost_estimate=taking(2),
        name="total_grad",
    )(*a, *b, *kept)


def back_kernel(table, model, cut, counts, places, choices, parts, guard, summed, where_ref, *refs):
    keys = [key for choice in choices for key in choice]
    used = sum(counts)
    late = blocks_of(refs[: counts[0]], places[0])
    early = blocks_of(refs[counts[0] : used], places[1])
    number = len(late)
    own_ref, first_ref, rest_ref = refs[used : used + 3]
    weight_refs, used = {}, used + 3
    for key, count in zip(keys, parts):
        weight_refs[key] = refs[used : used + count]
        used += count
    before_ref = refs[used] if summed else None
    outs = refs[len(refs) - 2 * len(choices) - 1 : -1]
    sums_ref = refs[-1]
    tokens = late[0].shape[0]
    units = own_ref.shape[1]
    me = where_ref[table["me"]]
    start = late[0].shape[1] - LANES
    eight = lax.broadcasted_iota(jnp.int32, (8, LANES), 1)
    onehot = jnp.where(eight == model % LANES + me, 1.0, 0.0).astype(bf16)
    shards = {key: where_ref[table[("shard",) + key]] for key in keys}
    slots = {key: where_ref[table[("slot",) + key]] for key in keys}
    sums_ref[...] = before_ref[...] if summed else jnp.zeros(sums_ref.shape, f32)

    def whole_weight(key):
        got = weight_refs[key]
        return got[0][...] if len(got) == 1 else jnp.concatenate([got[1][...], got[0][...]], axis=1)

    def work():
        stack, here_valid, here_slot = [], [], []
        for choice in choices:
            weight, valid, slot = whole_weight(choice[0]), shards[choice[0]] >= 0, slots[choice[0]]
            for key in choice[1:]:
                weight = jnp.where(valid, weight, whole_weight(key))
                slot = jnp.where(valid, slot, slots[key])
                valid = jnp.logical_or(valid, shards[key] >= 0)
            stack.append(weight)
            here_valid.append(valid)
            here_slot.append(slot)
        weight = jnp.concatenate(stack, axis=0) if len(stack) > 1 else stack[0]
        for pair in range(0, number, 2):
            both = jnp.concatenate(
                [
                    jnp.concatenate([early[k][...], late[k][:, : model - cut]], axis=1)
                    for k in (pair, pair + 1)
                ],
                axis=0,
            )
            product = dot(weight, both, NT)
            for place in (pair, pair + 1):
                near = place < number // 2
                block = product[:, (place - pair) * tokens : (place - pair + 1) * tokens]
                gate = dot(onehot, late[place][:, start:], NT)[0:1]
                here = pl.ds(place_of(place % (number // 2), number // 2, me, tokens), tokens)
                wide = pl.ds(place_of(place, number // 2, me, tokens), tokens)
                gated = (block * gate).astype(bf16)
                total = jnp.zeros((1, tokens), f32)
                for index, (valid, slot) in enumerate(zip(here_valid, here_slot)):
                    some = slice(index * units, (index + 1) * units)
                    outs[2 * index + (0 if near else 1)][:, here] = gated[some]
                    if near:
                        hidden = own_ref[slot, :, here].astype(f32)
                    else:
                        hidden = jnp.where(
                            slot == 0,
                            first_ref[0, :, here].astype(f32),
                            rest_ref[jnp.maximum(slot - 1, 0), :, here].astype(f32),
                        )
                    part = jnp.sum(hidden * block[some], axis=0, keepdims=True)
                    total = total + jnp.where(valid, part, 0.0)
                sums_ref[0:1, wide] += total

    if guard:
        pl.when(functools.reduce(jnp.logical_or, [shards[key] >= 0 for key in keys]))(work)
    else:
        work()


def back_part(table, where, late, early, own, first, rest, choices, got, before, guard, after, model):
    units, slots = own.shape[1:]
    arrays, places = zip(late, early)
    counts = [len(part) for part in arrays]
    cut = arrays[1][0].shape[-1]
    keys = [key for choice in choices for key in choice]
    weights = [got[key] for key in keys]
    flat = [part for weight in weights for part in weight]
    half = jax.ShapeDtypeStruct((units, slots), bf16)
    summed = before is not None
    operands = [*arrays[0], *arrays[1], own, first, rest, *flat] + ([before] if summed else [])
    outs = [half] * (2 * len(choices)) + [jax.ShapeDtypeStruct((8, 2 * slots), f32)]
    parts = [len(weight) for weight in weights]
    return pl.pallas_call(
        functools.partial(
            back_kernel, table, model, cut, counts, places, choices, parts, guard, summed
        ),
        out_shape=outs,
        in_specs=[scalars()] + [whole()] * len(operands) + [anywhere()] * len(after),
        out_specs=[whole()] * len(outs),
        compiler_params=params(),
        cost_estimate=taking(6),
        name="back_part",
    )(where, *operands, *after)


def join_kernel(table, choices, where_ref, *refs):
    out_ref, turned, sem = refs[-3:]
    slots, width = turned.shape[1:]
    row = lax.broadcasted_iota(jnp.int32, (slots, slots), 0)
    column = lax.broadcasted_iota(jnp.int32, (slots, slots), 1)
    unit = jnp.where(row == column, 1.0, 0.0).astype(bf16)
    low = where_ref[table["x"]] == 0
    copies = []
    for place, choice in enumerate(choices):
        mine, theirs = refs[2 * place][...], refs[2 * place + 1][...]
        index = where_ref[table[("shard",) + choice[0]]]
        for key in choice[1:]:
            index = jnp.where(index >= 0, index, where_ref[table[("shard",) + key]])
        both = jnp.concatenate([jnp.where(low, mine, theirs), jnp.where(low, theirs, mine)], axis=0)
        turned[place] = dot(unit, both, NT).astype(bf16)
        here = pl.ds(pl.multiple_of(jnp.maximum(index, 0) * width, LANES), width)
        copy = pltpu.make_async_copy(turned.at[place], out_ref.at[:, here], sem.at[place])
        copies.append((index, copy))
        pl.when(index >= 0)(copy.start)
    for index, copy in copies:
        pl.when(index >= 0)(copy.wait)


def join_hidden(table, where, choices, halves, slots, hidden, before, after):
    units = halves[0].shape[0]
    extends = before is not None
    return pl.pallas_call(
        functools.partial(join_kernel, table, choices),
        out_shape=jax.ShapeDtypeStruct((slots, hidden), bf16),
        in_specs=[scalars()] + [whole()] * len(halves) + [anywhere()] * (extends + len(after)),
        out_specs=anywhere(),
        scratch_shapes=[
            pltpu.VMEM((len(choices), slots, 2 * units), bf16),
            pltpu.SemaphoreType.DMA((len(choices),)),
        ],
        input_output_aliases={1 + len(halves): 0} if extends else {},
        compiler_params=params(),
        cost_estimate=taking(2),
        name="join_hidden",
    )(where, *halves, *([before] if extends else []), *after)


def logits_kernel(gates_ref, ids_ref, grads_ref, out_ref):
    gates, ids, grads = gates_ref[...], ids_ref[...], grads_ref[...]
    picked = jnp.zeros_like(gates)
    for expert in range(grads.shape[0]):
        picked = picked + jnp.where(ids == expert, grads[expert : expert + 1, :], 0.0)
    out_ref[...] = gates * (picked - jnp.sum(gates * picked, axis=0, keepdims=True))


def logits_grad(gates, ids, grads):
    return pl.pallas_call(
        logits_kernel,
        out_shape=jax.ShapeDtypeStruct(gates.shape, f32),
        in_specs=[whole()] * 3,
        out_specs=whole(),
        compiler_params=params(),
        cost_estimate=taking(1),
        name="logits_grad",
    )(gates, ids, grads)


def per_device_full(grad_out, top_logits, expert_ids, saved_hidden, w_down):
    experts = lax.axis_size("exp")
    groups = lax.axis_size("ctx")
    depth = groups // 2
    tokens, model = grad_out.shape
    slots, hidden = saved_hidden.shape[2:]
    width = pl.cdiv(model + experts, LANES) * LANES
    cut = width // LANES // 2 * LANES

    table, brought, uses = device_scalars(depth, experts)
    where = table.row(lax.axis_index("ctx"), lax.axis_index("exp"))

    def swap(value, x, exp):
        if not exp:
            return lax.ppermute(value, "ctx", [(i, i ^ x) for i in range(groups)])
        if not x:
            return lax.ppermute(value, "exp", [(i, i ^ exp) for i in range(experts)])
        pairs = [(c * experts + e, (c ^ x) * experts + (e ^ exp)) for c in range(groups) for e in range(experts)]
        return lax.ppermute(value, ("ctx", "exp"), pairs)

    def swap_z(value, name):
        first = "AB".index(name)
        pairs = []
        for z in range(first, depth - 1, 2):
            for x in range(2):
                pairs += [(2 * z + x, 2 * z + 2 + x), (2 * z + 2 + x, 2 * z + x)]
        return lax.ppermute(value, "ctx", pairs)

    got = {(0, "own"): [w_down[0]]}
    for name in "BA":
        got[1, name] = [swap_z(w_down[0], name)]

    late, early, gates = make_rows(grad_out, top_logits, expert_ids, width, cut)
    highs = list(range(2, experts, 2))

    def sides(mine):
        return [mine, swap(mine, 0, 1)]

    late_x = swap(late, 1, 0)
    late_near = [late] + [swap(late, 0, high) for high in highs]
    own, other_first, other_rest = split_hidden(
        table, where, saved_hidden[0, 0], depth, w_down.shape[1], [late]
    )
    other_first = swap(other_first, 1, 0)
    (late_x,) = hold((late_x,), late_near[1:])
    late_mine = late_near + [late_x] + [swap(late_x, 0, high) for high in highs]
    (early,) = hold((early,), [late_x, other_first])
    early_x = swap(early, 1, 0)
    late_rows = sides(pack(late_mine, [got[1, "B"][0], got[1, "A"][0], early_x]))
    late_rows = (late_rows, [(side, place) for place in range(experts) for side in range(2)])
    early_rows = sides(pack([early, early_x], []))
    places = [(0, 0), (1, 0)]
    for block, base in ((early, 0), (early_x, 1)):
        if base:
            places += [(0, 1), (1, 1)]
        for high in highs:
            places += [(len(early_rows), None), (len(early_rows) + 1, None)]
            early_rows += sides(swap(block, 0, high))
    early_rows = (early_rows, places)
    other_rest = swap(other_rest, 1, 0)

    first = [products(table, where, late_rows, late_rows, own, other_first, 0, model, model - cut, "first_late", [])]
    sent = [begin(table, where, got[1, "B"][0], first[0], cut, [early_rows[0][1]])]
    got[2, "A"] = [swap_z(sent[0], "A")]
    got[2, "B"] = [swap_z(got[1, "A"][0], "B")]
    first.append(
        products(table, where, early_rows, late_rows, own, other_first, 0, model, cut, "first_early", [])
    )
    sent.append(begin(table, where, got[1, "B"][0], first[1], 0, [got[2, "A"][0]]))
    got[2, "A"].append(swap_z(hold((sent[1],), [other_rest])[0], "A"))

    halves, all_choices = [], []
    only_first = max(uses[3, "B"]) <= 0

    def backprop(choices, before, guard, after):
        *outs, sums = back_part(
            table, where, late_rows, early_rows, own, other_first, other_rest, choices, got, before, guard, after, model
        )
        for mine, theirs in zip(outs[::2], outs[1::2]):
            halves.extend([mine, swap(theirs, 1, 0)])
        all_choices.extend(choices)
        return sums

    def pass_on(turn, name, after, chunk=None):
        coming = got[turn - 1, "B" if name == "A" else "A"]
        parts, start, chunked = (first, rest), cut, turn == depth and name == "B"
        if chunk is not None:
            coming, parts, start = [coming[chunk]], (first[chunk:][:1], rest[chunk:][:1]), 0
        values = combine(table, where, coming, *parts, turn, name, uses[turn, name], start, after, chunked)
        got.setdefault((turn, name), []).extend(swap_z(value, name) for value in values)
        return values[-1]

    def choices_of(turn):
        both = any(b[turn, "A"] >= 0 and b[turn, "B"] >= 0 for b in brought)
        return [[(turn, "A")], [(turn, "B")]] if both else [[(turn, "A"), (turn, "B")]]

    rest = []
    marker = pass_on(3, "B", [sent[1]], 0) if only_first else sent[1]
    for rows, columns, name in ((late_rows, model - cut, "rest_late"), (early_rows, cut, "rest_early")):
        rest.append(
            products(table, where, rows, late_rows, own, other_rest, 1, model, columns, name, [marker])
        )
    marker = pass_on(3, "A", rest)
    for chunk in range(2)[only_first:]:
        marker = pass_on(3, "B", [marker], chunk)
    sums = backprop([[(0, "own")], [(1, "A")], [(1, "B")]], None, False, [marker])
    sooner = halves[1::2]
    for turn in range(2, depth):
        choices = choices_of(turn)
        if turn > 2:
            pass_on(turn + 1, "B", [sums, *sooner])
            marker = pass_on(turn + 1, "A", [sums, *sooner])
        sums = backprop(choices, sums, len(choices) == 1, [marker])
    slot_grad = sums[0:1, :slots] + swap(sums[0:1, slots:], 1, 0)
    grads = lax.all_to_all(
        slot_grad.reshape(experts, tokens), "exp", split_axis=0, concat_axis=0, tiled=True
    )
    logit_grad = logits_grad(gates, expert_ids.T, grads)
    hidden_grad = join_hidden(table, where, all_choices, halves, slots, hidden, None, [])
    weight_grad = total_grad(got[depth, "A"], got[depth, "B"], rest, cut)
    return (logit_grad.T, hidden_grad[None, None], weight_grad)


def routing_tables(expert_ids, count_experts, capacity):
    columns = jnp.arange(count_experts, dtype=jnp.int32)
    matches = expert_ids[:, :, None] == columns[None, None, :]
    per_token = jnp.sum(matches.astype(jnp.int32), axis=1)
    rank_table = jnp.cumsum(per_token, axis=0) - per_token
    slot_iota = jnp.arange(capacity, dtype=jnp.int32)
    select = (per_token.T[:, None, :] == 1) & (rank_table.T[:, None, :] == slot_iota[None, :, None])
    return (matches.astype(jnp.float32), select)


def per_device_routed(grad_out, top_logits, expert_ids, saved_hidden, w_down):
    count_experts = lax.axis_size("exp")
    slot_count = saved_hidden.shape[2]
    capacity = slot_count // count_experts
    model_width = grad_out.shape[1]
    onehot, select = routing_tables(expert_ids, count_experts, capacity)
    select_wide = select.astype(jnp.float32)
    gate_probs = jax.nn.softmax(top_logits, axis=-1)
    gate_sent = gate_probs.astype(jnp.bfloat16)
    gate_by_expert = jnp.sum(onehot * gate_sent.astype(jnp.float32)[:, :, None], axis=1)
    send_rows = jnp.einsum(
        "ect,td->ecd", select.astype(jnp.bfloat16), grad_out, preferred_element_type=jnp.float32
    ).astype(jnp.bfloat16)
    send_gate = jnp.sum(select_wide * gate_by_expert.T[:, None, :], axis=2).astype(jnp.bfloat16)
    hidden = saved_hidden[0, 0]
    rows_in, gate_in = (
        lax.all_to_all(send_rows, "exp", split_axis=0, concat_axis=0, tiled=True),
        lax.all_to_all(send_gate, "exp", split_axis=0, concat_axis=0, tiled=True),
    )
    flat_rows = rows_in.reshape(slot_count, model_width)
    backprop = lax.dot_general(
        flat_rows,
        lax.all_gather(w_down[0], "ctx", axis=0, tiled=True),
        (((1,), (1,)), ((), ())),
        preferred_element_type=jnp.float32,
    )
    flat_gate = gate_in.reshape(slot_count, 1).astype(jnp.float32)
    hidden_grad = (flat_gate * backprop).astype(jnp.bfloat16)
    slot_grad = jnp.sum(hidden.astype(jnp.float32) * backprop, axis=1)
    scaled = (flat_gate * flat_rows.astype(jnp.float32)).astype(jnp.bfloat16)
    partial_grad = lax.dot_general(
        hidden, scaled, (((0,), (0,)), ((), ())), preferred_element_type=jnp.float32
    )
    weight_grad = lax.psum_scatter(partial_grad, "ctx", scatter_dimension=0, tiled=True)
    returned = lax.all_to_all(
        slot_grad.reshape(count_experts, capacity), "exp", split_axis=0, concat_axis=0, tiled=True
    )
    grad_by_expert = jnp.sum(select_wide * returned[:, :, None], axis=1)
    gate_grad = jnp.sum(onehot * grad_by_expert.T[:, None, :], axis=2)
    logit_grad = gate_probs * (gate_grad - jnp.sum(gate_probs * gate_grad, axis=1, keepdims=True))
    return (logit_grad, hidden_grad.reshape(1, 1, slot_count, -1), weight_grad[None])


def per_device(grad_out, top_logits, expert_ids, saved_hidden, w_down):
    experts = lax.axis_size("exp")
    groups = lax.axis_size("ctx")
    everywhere = top_logits.shape[1] == experts and saved_hidden.shape[2] == experts * grad_out.shape[0]
    plain = experts & (experts - 1) == 0 and groups % 4 == 0 and groups >= 8
    body = per_device_full if everywhere and plain else per_device_routed
    return body(grad_out, top_logits, expert_ids, saved_hidden, w_down)


def solution(mesh):
    return jax.shard_map(
        per_device,
        mesh=mesh,
        in_specs=(
            P(("ctx", "exp"), None),
            P(("ctx", "exp"), None),
            P(("ctx", "exp"), None),
            P("ctx", "exp", None, None),
            P("exp", "ctx", None),
        ),
        out_specs=(P(("ctx", "exp"), None), P("ctx", "exp", None, None), P("exp", "ctx", None)),
        check_vma=False,
    )
```

```python
import functools

import jax
import jax.numpy as jnp
import numpy as np
from jax import lax
from jax.experimental import pallas as pl
from jax.experimental.pallas import tpu as pltpu
from jax.sharding import PartitionSpec as P

LANES = 128
SCALE = 1_000_000
BEGIN_WEIGHT = 600
NT = (((1,), (1,)), ((), ()))
NN = (((1,), (0,)), ((), ()))
f32 = jnp.float32
bf16 = jnp.bfloat16


def dot(a, b, dims):
    return lax.dot_general(a, b, dims, preferred_element_type=f32)


def anywhere():
    return pl.BlockSpec(memory_space=pl.ANY)


def whole():
    return pl.BlockSpec(memory_space=pltpu.VMEM)


def scalars():
    return pl.BlockSpec(memory_space=pltpu.SMEM)


def params(mib=24):
    return pltpu.CompilerParams(vmem_limit_bytes=mib * 1024 * 1024)


def taking(microseconds):
    return pl.CostEstimate(flops=int(microseconds * SCALE), bytes_accessed=int(microseconds * 3e6), transcendentals=0)


def chain_plan(depth):
    products, weights = [], []
    for z in range(depth):
        uses = []
        for turn in range(2, depth + 1):
            if z < depth - 1 and turn >= z + 2:
                uses.append((turn, "AB"[z % 2], depth + 1 + z - turn))
            if z > 0 and turn >= depth - z + 1:
                uses.append((turn, "BA"[z % 2], z + turn - depth - 1))
        products.append(sorted(uses) + [(depth + 1, "own", z)])
        brought = {}
        for turn in range(1, depth):
            for name in "AB":
                index = z + turn if (name == "A") == (z % 2 == 0) else z - turn
                brought[turn, name] = index if 0 <= index < depth else -1
        weights.append(brought)
    return products, weights


class Scalars:
    def __init__(self):
        self.columns = []
        self.names = {}

    def add(self, name, values):
        self.names[name] = len(self.columns)
        self.columns.append(values)

    def __getitem__(self, name):
        return self.names[name]

    def row(self, place, me):
        return jnp.asarray(np.stack(self.columns, axis=-1).astype(np.int32))[place, me]


def device_scalars(depth, experts):
    products, weights = chain_plan(depth)
    table = Scalars()
    along = np.arange(2 * depth)[:, None] + np.zeros((1, experts), np.int32)

    def by_z(values):
        return np.asarray(values)[along // 2]

    table.add("x", along % 2)
    table.add("me", np.zeros_like(along) + np.arange(experts)[None, :])
    table.add(("shard", 0, "own"), along // 2)
    slot_of = [{use[2]: slot for slot, use in enumerate(products[z])} for z in range(depth)]
    for part in range(depth):
        table.add(("slot of", part), by_z([slot_of[z][part] for z in range(depth)]))
    table.add(("slot", 0, "own"), by_z([slot_of[z][z] for z in range(depth)]))
    for turn in range(1, depth):
        for name in "AB":
            shard = [weights[z][turn, name] for z in range(depth)]
            table.add(("shard", turn, name), by_z(shard))
            table.add(("slot", turn, name), by_z([slot_of[z].get(k, 0) for z, k in enumerate(shard)]))
    uses = {}
    for turn in range(2, depth + 1):
        for name in "AB":
            slots = [-1] * depth
            for z in range(depth):
                for slot, use in enumerate(products[z]):
                    if use[:2] == (turn, name):
                        slots[z] = slot
            uses[turn, name] = slots
            table.add(("use", turn, name), by_z(slots))
            limit = max(depth - 3, 0)
            table.add(("block", turn, name), by_z([min(max(slot - 1, 0), limit) for slot in slots]))
    return table, weights, uses


def rows_kernel(cut, grad_hbm, logits_hbm, ids_hbm, late_ref, early_ref, gates_ref, *scratch):
    grad_ref, logits_ref, ids_ref, sems = scratch
    model, tokens = grad_ref.shape
    copies = [
        pltpu.make_async_copy(source, target, sems.at[place])
        for place, (source, target) in enumerate(
            ((grad_hbm, grad_ref), (logits_hbm, logits_ref), (ids_hbm, ids_ref))
        )
    ]
    for copy in copies:
        copy.start()
    for copy in copies:
        copy.wait()
    count = logits_ref.shape[0]
    width = cut + late_ref.shape[1]
    logits = logits_ref[...]
    powers = jnp.exp(logits - jnp.max(logits, axis=0, keepdims=True))
    gates = powers / jnp.sum(powers, axis=0, keepdims=True)
    gates_ref[...] = gates
    sent = gates.astype(bf16).astype(f32)
    ids = ids_ref[...]
    row = lax.broadcasted_iota(jnp.int32, (width - model, tokens), 0)
    extra = jnp.zeros((width - model, tokens), f32)
    for expert in range(count):
        chosen = jnp.sum(jnp.where(ids == expert, sent, 0.0), axis=0, keepdims=True)
        extra = extra + jnp.where(row == expert, chosen, 0.0)
    for start in range(0, width, LANES):
        stop = start + LANES
        if stop <= model:
            block = grad_ref[start:stop, :].astype(f32)
        elif start >= model:
            block = extra[start - model : stop - model, :]
        else:
            block = jnp.concatenate(
                [grad_ref[start:model, :].astype(f32), extra[: stop - model, :]], axis=0
            )
        turned = block.T.astype(bf16)
        if start < cut:
            early_ref[:, start:stop] = turned
        else:
            late_ref[:, start - cut : stop - cut] = turned


def make_rows(grad_out, top_logits, expert_ids, width, cut):
    tokens, model = grad_out.shape
    count = top_logits.shape[1]
    return pl.pallas_call(
        functools.partial(rows_kernel, cut),
        out_shape=(
            jax.ShapeDtypeStruct((tokens, width - cut), bf16),
            jax.ShapeDtypeStruct((tokens, cut), bf16),
            jax.ShapeDtypeStruct((count, tokens), f32),
        ),
        in_specs=[pl.BlockSpec(memory_space=pltpu.HBM)] * 3,
        out_specs=(whole(),) * 3,
        scratch_shapes=[
            pltpu.VMEM((model, tokens), bf16),
            pltpu.VMEM((count, tokens), f32),
            pltpu.VMEM((count, tokens), jnp.int32),
            pltpu.SemaphoreType.DMA((3,)),
        ],
        compiler_params=params(58),
        cost_estimate=taking(2),
        name="make_rows",
    )(grad_out.T, top_logits.T, expert_ids.T)


def pack_kernel(*refs):
    out_ref, sems = refs[-2:]
    copies = []
    for place in range(out_ref.shape[0]):
        copies.append(pltpu.make_async_copy(refs[place], out_ref.at[place], sems.at[place]))
        copies[-1].start()
    for copy in copies:
        copy.wait()


def pack(values, after):
    number = len(values)
    return pl.pallas_call(
        pack_kernel,
        out_shape=jax.ShapeDtypeStruct((number, *values[0].shape), values[0].dtype),
        in_specs=[anywhere()] * (number + len(after)),
        out_specs=anywhere(),
        scratch_shapes=[pltpu.SemaphoreType.DMA((number,))],
        compiler_params=params(),
        cost_estimate=taking(1),
        name="pack_rows",
    )(*values, *after)


def blocks_of(refs, places):
    return [refs[array] if place is None else refs[array].at[place] for array, place in places]


def hold_kernel(*refs):
    del refs


def hold(values, after):
    return pl.pallas_call(
        hold_kernel,
        out_shape=tuple(jax.ShapeDtypeStruct(value.shape, value.dtype) for value in values),
        in_specs=[anywhere()] * (len(values) + len(after)),
        out_specs=(anywhere(),) * len(values),
        input_output_aliases={place: place for place in range(len(values))},
        compiler_params=params(),
        cost_estimate=taking(0),
        name="hold",
    )(*values, *after)


def split_kernel(table, where_ref, hidden_ref, *refs):
    own_ref, first_ref, rest_ref = refs[-3:]
    parts, units, _ = own_ref.shape
    row = lax.broadcasted_iota(jnp.int32, (2 * units, 2 * units), 0)
    column = lax.broadcasted_iota(jnp.int32, (2 * units, 2 * units), 1)
    unit = jnp.where(row == column, 1.0, 0.0).astype(bf16)
    low = where_ref[table["x"]] == 0
    for part in range(parts):
        block = hidden_ref[:, part * 2 * units : (part + 1) * 2 * units]
        turned = dot(unit, block, NT).astype(bf16)
        slot = where_ref[table["slot of", part]]
        other = jnp.where(low, turned[units:], turned[:units])
        own_ref[slot] = jnp.where(low, turned[:units], turned[units:])

        @pl.when(slot == 0)
        def _():
            first_ref[0] = other

        @pl.when(slot != 0)
        def _():
            rest_ref[slot - 1] = other


def split_hidden(table, where, hidden, parts, units, after):
    slots = hidden.shape[0]
    return pl.pallas_call(
        functools.partial(split_kernel, table),
        out_shape=tuple(
            jax.ShapeDtypeStruct((count, units, slots), bf16) for count in (parts, 1, parts - 1)
        ),
        in_specs=[scalars(), whole()] + [anywhere()] * len(after),
        out_specs=(whole(),) * 3,
        compiler_params=params(),
        cost_estimate=taking(2),
        name="split_hidden",
    )(where, hidden, *after)


def place_of(place, count, me, tokens):
    start = (place // count) * count * tokens + ((place % count) ^ me) * tokens
    return pl.multiple_of(start, tokens)


def products_kernel(table, model, counts, places, shards, skip, where_ref, *refs):
    used = sum(counts)
    rows = blocks_of(refs[: counts[0]], places[0])
    gated = blocks_of(refs[counts[0] : used], places[1])
    number = len(rows)
    own_ref, other_ref = refs[used : used + 2]
    kept_ref, scaled = refs[-2:]
    tokens = rows[0].shape[0]
    units, slots = own_ref.shape[1:]
    width = kept_ref.shape[2]
    me = where_ref[table["me"]]
    lane = lax.broadcasted_iota(jnp.int32, (tokens, LANES), 1)
    for place in range(number):
        here = pl.ds(place_of(place, number // 2, me, tokens), tokens)
        tile = gated[place][:, gated[place].shape[1] - LANES :]
        picked = jnp.where(lane == model % LANES + me, tile.astype(f32), 0.0)
        gate = jnp.sum(picked, axis=1, keepdims=True)
        scaled[here, :] = (rows[place][:, :width].astype(f32) * gate).astype(bf16)

    def stacked(ref, offset):
        parts = [ref[offset + shard] for shard in range(shards)]
        return jnp.concatenate(parts, axis=0) if len(parts) > 1 else parts[0]

    total = dot(stacked(own_ref, skip), scaled[:slots, :], NN)
    total = total + dot(stacked(other_ref, 0), scaled[slots:, :], NN)
    for shard in range(shards):
        kept_ref[shard] = total[shard * units : (shard + 1) * units]


def products(table, where, rows, gated, own, other, skip, model, width, name, after):
    arrays, places = zip(rows, gated)
    tokens = arrays[0][0].shape[-2]
    counts = [len(part) for part in arrays]
    number = 2 * (own.shape[2] // tokens)
    shards, units, slots = other.shape
    return pl.pallas_call(
        functools.partial(products_kernel, table, model, counts, places, shards, skip),
        out_shape=jax.ShapeDtypeStruct((shards, units, width), f32),
        in_specs=[scalars()] + [whole()] * (sum(counts) + 2) + [anywhere()] * len(after),
        out_specs=whole(),
        scratch_shapes=[pltpu.VMEM((number * tokens, width), bf16)],
        compiler_params=params(),
        cost_estimate=taking(4),
        name=name,
    )(where, *arrays[0], *arrays[1], own, other, *after)


def rows_of(units):
    return units // 2 if units % 32 == 0 else units


def column_parts(arrays, cut):
    return [(0, arrays[0])] if len(arrays) == 1 else [(cut, arrays[0]), (0, arrays[1])]


def combine_kernel(table, key, cut, counts, sides, where_ref, *refs):
    slot = where_ref[table[key]]
    coming = refs[: counts[0]]
    outs = refs[len(refs) - counts[2] :]
    model = sum(ref.shape[1] for ref in outs)
    spans = [(cut, model), (0, cut)] if cut else [(0, model)]
    for chunk, (start, stop) in enumerate(spans):
        if counts[0] == 0:
            total = jnp.zeros((outs[0].shape[0], stop - start), f32)
        elif counts[0] == 1:
            total = coming[0][:, start:stop].astype(f32)
        else:
            total = coming[chunk][...].astype(f32)
        for number, side in enumerate(sides):
            flag = slot == 0 if side == "first" else slot > 0
            total = total + jnp.where(flag, refs[counts[0] + len(spans) * number + chunk][0], 0.0)
        total = total.astype(bf16)
        if counts[2] == 1:
            outs[0][:, start:stop] = total
        else:
            outs[chunk][...] = total


def combine(table, where, coming, first, rest, turn, name, used, cut, after, chunked=False):
    units = first[0].shape[1]
    model = sum(part.shape[2] for part in first)
    block = rows_of(units)
    column = table["block", turn, name]
    sides, operands, specs = [], [], []
    if any(slot == 0 for slot in used):
        sides.append("first")
        operands += first
        specs += [pl.BlockSpec((1, block, part.shape[2]), lambda j, s: (0, j, 0)) for part in first]
    if any(slot > 0 for slot in used):
        sides.append("rest")
        operands += rest
        specs += [pl.BlockSpec((1, block, part.shape[2]), lambda j, s: (s[column], j, 0)) for part in rest]
    widths = [model - cut, cut] if chunked else [model]
    return pl.pallas_call(
        functools.partial(
            combine_kernel, table, ("use", turn, name), cut, (len(coming), len(operands), len(widths)), sides
        ),
        out_shape=[jax.ShapeDtypeStruct((units, count), bf16) for count in widths],
        grid_spec=pltpu.PrefetchScalarGridSpec(
            num_scalar_prefetch=1,
            grid=(units // block,),
            in_specs=[pl.BlockSpec((block, part.shape[1]), lambda j, s: (j, 0)) for part in coming]
            + specs
            + [anywhere()] * len(after),
            out_specs=[pl.BlockSpec((block, count), lambda j, s: (j, 0)) for count in widths],
        ),
        compiler_params=params(),
        cost_estimate=taking(1.5),
        name="combine",
    )(where, *coming, *operands, *after)


def begin_kernel(table, start, stop, where_ref, coming_ref, kept_ref, *refs):
    out_ref = refs[-1]
    flag = where_ref[table["use", 2, "A"]] == 0
    total = coming_ref[:, start:stop].astype(f32) + jnp.where(flag, kept_ref[0], 0.0)
    out_ref[...] = total.astype(bf16)


def begin(table, where, coming, kept, start, after):
    units, model = coming.shape
    width = kept.shape[2]
    block = rows_of(units)
    return pl.pallas_call(
        functools.partial(begin_kernel, table, start, start + width),
        out_shape=jax.ShapeDtypeStruct((units, width), bf16),
        grid_spec=pltpu.PrefetchScalarGridSpec(
            num_scalar_prefetch=1,
            grid=(units // block,),
            in_specs=[
                pl.BlockSpec((block, model), lambda j, s: (j, 0)),
                pl.BlockSpec((1, block, width), lambda j, s: (0, j, 0)),
            ]
            + [anywhere()] * len(after),
            out_specs=pl.BlockSpec((block, width), lambda j, s: (j, 0)),
        ),
        compiler_params=params(),
        cost_estimate=taking(BEGIN_WEIGHT),
        name="begin",
    )(where, coming, kept, *after)


def total_kernel(cut, counts, *refs):
    coming = [refs[: counts[0]], refs[counts[0] : sum(counts)]]
    out_ref = refs[-1]
    for chunk, start in enumerate((cut, 0)):
        kept_ref = refs[sum(counts) + chunk]
        here = slice(start, start + kept_ref.shape[2])
        total = kept_ref[0]
        for parts in coming:
            total = total + (parts[0][:, here] if len(parts) == 1 else parts[chunk][...]).astype(f32)
        out_ref[0, :, here] = total


def total_grad(a, b, kept, cut):
    units = a[0].shape[0]
    model = sum(part.shape[1] for part in a)
    block = rows_of(units)
    return pl.pallas_call(
        functools.partial(total_kernel, cut, (len(a), len(b))),
        out_shape=jax.ShapeDtypeStruct((1, units, model), f32),
        grid=(units // block,),
        in_specs=[pl.BlockSpec((block, part.shape[1]), lambda j: (j, 0)) for part in (*a, *b)]
        + [
            pl.BlockSpec((1, block, part.shape[2]), functools.partial(lambda last, j: (last, j, 0), part.shape[0] - 1))
            for part in kept
        ],
        out_specs=pl.BlockSpec((1, block, model), lambda j: (0, j, 0)),
        compiler_params=params(),
        cost_estimate=taking(2),
        name="total_grad",
    )(*a, *b, *kept)


def back_kernel(table, model, cut, counts, places, choices, parts, guard, summed, where_ref, *refs):
    keys = [key for choice in choices for key in choice]
    used = sum(counts)
    late = blocks_of(refs[: counts[0]], places[0])
    early = blocks_of(refs[counts[0] : used], places[1])
    number = len(late)
    own_ref, first_ref, rest_ref = refs[used : used + 3]
    weight_refs, used = {}, used + 3
    for key, count in zip(keys, parts):
        weight_refs[key] = refs[used : used + count]
        used += count
    before_ref = refs[used] if summed else None
    outs = refs[len(refs) - 2 * len(choices) - 1 : -1]
    sums_ref = refs[-1]
    tokens = late[0].shape[0]
    units = own_ref.shape[1]
    me = where_ref[table["me"]]
    start = late[0].shape[1] - LANES
    eight = lax.broadcasted_iota(jnp.int32, (8, LANES), 1)
    onehot = jnp.where(eight == model % LANES + me, 1.0, 0.0).astype(bf16)
    shards = {key: where_ref[table[("shard",) + key]] for key in keys}
    slots = {key: where_ref[table[("slot",) + key]] for key in keys}
    sums_ref[...] = before_ref[...] if summed else jnp.zeros(sums_ref.shape, f32)

    def whole_weight(key):
        got = weight_refs[key]
        return got[0][...] if len(got) == 1 else jnp.concatenate([got[1][...], got[0][...]], axis=1)

    def work():
        stack, here_valid, here_slot = [], [], []
        for choice in choices:
            weight, valid, slot = whole_weight(choice[0]), shards[choice[0]] >= 0, slots[choice[0]]
            for key in choice[1:]:
                weight = jnp.where(valid, weight, whole_weight(key))
                slot = jnp.where(valid, slot, slots[key])
                valid = jnp.logical_or(valid, shards[key] >= 0)
            stack.append(weight)
            here_valid.append(valid)
            here_slot.append(slot)
        weight = jnp.concatenate(stack, axis=0) if len(stack) > 1 else stack[0]
        for pair in range(0, number, 2):
            both = jnp.concatenate(
                [
                    jnp.concatenate([early[k][...], late[k][:, : model - cut]], axis=1)
                    for k in (pair, pair + 1)
                ],
                axis=0,
            )
            product = dot(weight, both, NT)
            for place in (pair, pair + 1):
                near = place < number // 2
                block = product[:, (place - pair) * tokens : (place - pair + 1) * tokens]
                gate = dot(onehot, late[place][:, start:], NT)[0:1]
                here = pl.ds(place_of(place % (number // 2), number // 2, me, tokens), tokens)
                wide = pl.ds(place_of(place, number // 2, me, tokens), tokens)
                gated = (block * gate).astype(bf16)
                total = jnp.zeros((1, tokens), f32)
                for index, (valid, slot) in enumerate(zip(here_valid, here_slot)):
                    some = slice(index * units, (index + 1) * units)
                    outs[2 * index + (0 if near else 1)][:, here] = gated[some]
                    if near:
                        hidden = own_ref[slot, :, here].astype(f32)
                    else:
                        hidden = jnp.where(
                            slot == 0,
                            first_ref[0, :, here].astype(f32),
                            rest_ref[jnp.maximum(slot - 1, 0), :, here].astype(f32),
                        )
                    part = jnp.sum(hidden * block[some], axis=0, keepdims=True)
                    total = total + jnp.where(valid, part, 0.0)
                sums_ref[0:1, wide] += total

    if guard:
        pl.when(functools.reduce(jnp.logical_or, [shards[key] >= 0 for key in keys]))(work)
    else:
        work()


def back_part(table, where, late, early, own, first, rest, choices, got, before, guard, after, model):
    units, slots = own.shape[1:]
    arrays, places = zip(late, early)
    counts = [len(part) for part in arrays]
    cut = arrays[1][0].shape[-1]
    keys = [key for choice in choices for key in choice]
    weights = [got[key] for key in keys]
    flat = [part for weight in weights for part in weight]
    half = jax.ShapeDtypeStruct((units, slots), bf16)
    summed = before is not None
    operands = [*arrays[0], *arrays[1], own, first, rest, *flat] + ([before] if summed else [])
    outs = [half] * (2 * len(choices)) + [jax.ShapeDtypeStruct((8, 2 * slots), f32)]
    parts = [len(weight) for weight in weights]
    return pl.pallas_call(
        functools.partial(
            back_kernel, table, model, cut, counts, places, choices, parts, guard, summed
        ),
        out_shape=outs,
        in_specs=[scalars()] + [whole()] * len(operands) + [anywhere()] * len(after),
        out_specs=[whole()] * len(outs),
        compiler_params=params(),
        cost_estimate=taking(6),
        name="back_part",
    )(where, *operands, *after)


def join_kernel(table, choices, where_ref, *refs):
    out_ref, turned, sem = refs[-3:]
    slots, width = turned.shape[1:]
    row = lax.broadcasted_iota(jnp.int32, (slots, slots), 0)
    column = lax.broadcasted_iota(jnp.int32, (slots, slots), 1)
    unit = jnp.where(row == column, 1.0, 0.0).astype(bf16)
    low = where_ref[table["x"]] == 0
    copies = []
    for place, choice in enumerate(choices):
        mine, theirs = refs[2 * place][...], refs[2 * place + 1][...]
        index = where_ref[table[("shard",) + choice[0]]]
        for key in choice[1:]:
            index = jnp.where(index >= 0, index, where_ref[table[("shard",) + key]])
        both = jnp.concatenate([jnp.where(low, mine, theirs), jnp.where(low, theirs, mine)], axis=0)
        turned[place] = dot(unit, both, NT).astype(bf16)
        here = pl.ds(pl.multiple_of(jnp.maximum(index, 0) * width, LANES), width)
        copy = pltpu.make_async_copy(turned.at[place], out_ref.at[:, here], sem.at[place])
        copies.append((index, copy))
        pl.when(index >= 0)(copy.start)
    for index, copy in copies:
        pl.when(index >= 0)(copy.wait)


def join_hidden(table, where, choices, halves, slots, hidden, before, after):
    units = halves[0].shape[0]
    extends = before is not None
    return pl.pallas_call(
        functools.partial(join_kernel, table, choices),
        out_shape=jax.ShapeDtypeStruct((slots, hidden), bf16),
        in_specs=[scalars()] + [whole()] * len(halves) + [anywhere()] * (extends + len(after)),
        out_specs=anywhere(),
        scratch_shapes=[
            pltpu.VMEM((len(choices), slots, 2 * units), bf16),
            pltpu.SemaphoreType.DMA((len(choices),)),
        ],
        input_output_aliases={1 + len(halves): 0} if extends else {},
        compiler_params=params(),
        cost_estimate=taking(2),
        name="join_hidden",
    )(where, *halves, *([before] if extends else []), *after)


def logits_kernel(gates_ref, ids_ref, grads_ref, out_ref):
    gates, ids, grads = gates_ref[...], ids_ref[...], grads_ref[...]
    picked = jnp.zeros_like(gates)
    for expert in range(grads.shape[0]):
        picked = picked + jnp.where(ids == expert, grads[expert : expert + 1, :], 0.0)
    out_ref[...] = gates * (picked - jnp.sum(gates * picked, axis=0, keepdims=True))


def logits_grad(gates, ids, grads):
    return pl.pallas_call(
        logits_kernel,
        out_shape=jax.ShapeDtypeStruct(gates.shape, f32),
        in_specs=[whole()] * 3,
        out_specs=whole(),
        compiler_params=params(),
        cost_estimate=taking(1),
        name="logits_grad",
    )(gates, ids, grads)


def per_device_full(grad_out, top_logits, expert_ids, saved_hidden, w_down):
    experts = lax.axis_size("exp")
    groups = lax.axis_size("ctx")
    depth = groups // 2
    tokens, model = grad_out.shape
    slots, hidden = saved_hidden.shape[2:]
    width = pl.cdiv(model + experts, LANES) * LANES
    cut = width // LANES // 2 * LANES

    table, brought, uses = device_scalars(depth, experts)
    where = table.row(lax.axis_index("ctx"), lax.axis_index("exp"))

    def swap(value, x, exp):
        if not exp:
            return lax.ppermute(value, "ctx", [(i, i ^ x) for i in range(groups)])
        if not x:
            return lax.ppermute(value, "exp", [(i, i ^ exp) for i in range(experts)])
        pairs = [(c * experts + e, (c ^ x) * experts + (e ^ exp)) for c in range(groups) for e in range(experts)]
        return lax.ppermute(value, ("ctx", "exp"), pairs)

    def swap_z(value, name, senders=range(depth)):
        first = "AB".index(name)
        pairs = []
        for low in range(first, depth - 1, 2):
            for z, other in ((low, low + 1), (low + 1, low)):
                pairs += [(2 * z + x, 2 * other + x) for x in range(2) if z in senders]
        return lax.ppermute(value, "ctx", pairs)

    got = {(0, "own"): [w_down[0]]}
    for name in "BA":
        got[1, name] = [swap_z(w_down[0], name)]

    late, early, gates = make_rows(grad_out, top_logits, expert_ids, width, cut)
    highs = list(range(2, experts, 2))

    def sides(mine):
        return [mine, swap(mine, 0, 1)]

    late_x = swap(late, 1, 0)
    late_near = [late] + [swap(late, 0, high) for high in highs]
    own, other_first, other_rest = split_hidden(
        table, where, saved_hidden[0, 0], depth, w_down.shape[1], [late]
    )
    other_first = swap(other_first, 1, 0)
    (late_x,) = hold((late_x,), late_near[1:])
    late_mine = late_near + [late_x] + [swap(late_x, 0, high) for high in highs]
    (early,) = hold((early,), [late_x, other_first])
    early_x = swap(early, 1, 0)
    late_rows = sides(pack(late_mine, [got[1, "B"][0], got[1, "A"][0], early_x]))
    late_rows = (late_rows, [(side, place) for place in range(experts) for side in range(2)])
    early_rows = sides(pack([early, early_x], []))
    places = [(0, 0), (1, 0)]
    for block, base in ((early, 0), (early_x, 1)):
        if base:
            places += [(0, 1), (1, 1)]
        for high in highs:
            places += [(len(early_rows), None), (len(early_rows) + 1, None)]
            early_rows += sides(swap(block, 0, high))
    early_rows = (early_rows, places)
    other_rest = swap(other_rest, 1, 0)

    first = [products(table, where, late_rows, late_rows, own, other_first, 0, model, model - cut, "first_late", [])]
    sent = [begin(table, where, got[1, "B"][0], first[0], cut, [early_rows[0][1]])]
    got[2, "A"] = [swap_z(sent[0], "A")]
    got[2, "B"] = [swap_z(got[1, "A"][0], "B")]
    first.append(
        products(table, where, early_rows, late_rows, own, other_first, 0, model, cut, "first_early", [])
    )
    sent.append(begin(table, where, got[1, "B"][0], first[1], 0, [got[2, "A"][0]]))
    sent[1:] = hold((sent[1],), [other_rest])
    got[2, "A"].append(swap_z(sent[1], "A"))

    halves, all_choices, weights_of = [], [], {}
    only_first = max(uses[3, "B"]) <= 0

    def backprop(choices, before, guard, after):
        *outs, sums = back_part(
            table, where, late_rows, early_rows, own, other_first, other_rest, choices,
            {**got, **weights_of}, before, guard, after, model,
        )
        for mine, theirs in zip(outs[::2], outs[1::2]):
            halves.extend([mine, swap(theirs, 1, 0)])
        all_choices.extend(choices)
        return sums

    def pass_on(turn, name, after, chunk=None, waited=()):
        coming = got[turn - 1, "B" if name == "A" else "A"]
        parts, start, chunked = (first, rest), cut, turn == depth and name == "B"
        used = uses[turn, name]
        senders = [z for z in range(depth) if used[z] >= 0] if turn == depth - 1 else range(depth)
        others = [z for z in range(depth) if z not in senders]
        if others and chunk is None and len(coming) == 1:
            weights_of[turn, name] = [swap_z(coming[0], name, others)]
            ends = {0, depth - 1} if name == "A" else set()
            coming = [] if set(senders) <= ends else coming
        if chunk is not None:
            coming, parts, start = [coming[chunk]], (first[chunk:][:1], rest[chunk:][:1]), 0
        values = list(combine(table, where, coming, *parts, turn, name, used, start, after, chunked))
        if waited:
            values[1:] = hold(values[1:], list(waited))
        got.setdefault((turn, name), []).extend(swap_z(value, name, senders) for value in values)
        return values[-1]

    def choices_of(turn):
        both = any(b[turn, "A"] >= 0 and b[turn, "B"] >= 0 for b in brought)
        return [[(turn, "A")], [(turn, "B")]] if both else [[(turn, "A"), (turn, "B")]]

    rest = []
    marker = pass_on(3, "B", [sent[1]], 0) if only_first else sent[1]
    for rows, columns, name in ((late_rows, model - cut, "rest_late"), (early_rows, cut, "rest_early")):
        rest.append(
            products(table, where, rows, late_rows, own, other_rest, 1, model, columns, name, [marker])
        )
    marker = pass_on(3, "A", rest)
    for chunk in range(2)[only_first:]:
        marker = pass_on(3, "B", [marker], chunk)
    sums = backprop([[(0, "own")], [(1, "A")], [(1, "B")]], None, False, [marker])
    sooner = halves[1::2]
    for turn in range(2, depth):
        choices = choices_of(turn)
        if turn > 2:
            waited = [array for key in ((turn, "A"), (turn, "B")) for array in weights_of.get(key, [])]
            pass_on(turn + 1, "B", [sums, *sooner], waited=waited)
            marker = pass_on(turn + 1, "A", [sums, *sooner])
        sums = backprop(choices, sums, len(choices) == 1, [marker])
    slot_grad = sums[0:1, :slots] + swap(sums[0:1, slots:], 1, 0)
    grads = lax.all_to_all(
        slot_grad.reshape(experts, tokens), "exp", split_axis=0, concat_axis=0, tiled=True
    )
    logit_grad = logits_grad(gates, expert_ids.T, grads)
    hidden_grad = join_hidden(table, where, all_choices, halves, slots, hidden, None, [])
    weight_grad = total_grad(got[depth, "A"], got[depth, "B"], rest, cut)
    return (logit_grad.T, hidden_grad[None, None], weight_grad)


def routing_tables(expert_ids, count_experts, capacity):
    columns = jnp.arange(count_experts, dtype=jnp.int32)
    matches = expert_ids[:, :, None] == columns[None, None, :]
    per_token = jnp.sum(matches.astype(jnp.int32), axis=1)
    rank_table = jnp.cumsum(per_token, axis=0) - per_token
    slot_iota = jnp.arange(capacity, dtype=jnp.int32)
    select = (per_token.T[:, None, :] == 1) & (rank_table.T[:, None, :] == slot_iota[None, :, None])
    return (matches.astype(jnp.float32), select)


def per_device_routed(grad_out, top_logits, expert_ids, saved_hidden, w_down):
    count_experts = lax.axis_size("exp")
    slot_count = saved_hidden.shape[2]
    capacity = slot_count // count_experts
    model_width = grad_out.shape[1]
    onehot, select = routing_tables(expert_ids, count_experts, capacity)
    select_wide = select.astype(jnp.float32)
    gate_probs = jax.nn.softmax(top_logits, axis=-1)
    gate_sent = gate_probs.astype(jnp.bfloat16)
    gate_by_expert = jnp.sum(onehot * gate_sent.astype(jnp.float32)[:, :, None], axis=1)
    send_rows = jnp.einsum(
        "ect,td->ecd", select.astype(jnp.bfloat16), grad_out, preferred_element_type=jnp.float32
    ).astype(jnp.bfloat16)
    send_gate = jnp.sum(select_wide * gate_by_expert.T[:, None, :], axis=2).astype(jnp.bfloat16)
    hidden = saved_hidden[0, 0]
    rows_in, gate_in = (
        lax.all_to_all(send_rows, "exp", split_axis=0, concat_axis=0, tiled=True),
        lax.all_to_all(send_gate, "exp", split_axis=0, concat_axis=0, tiled=True),
    )
    flat_rows = rows_in.reshape(slot_count, model_width)
    backprop = lax.dot_general(
        flat_rows,
        lax.all_gather(w_down[0], "ctx", axis=0, tiled=True),
        (((1,), (1,)), ((), ())),
        preferred_element_type=jnp.float32,
    )
    flat_gate = gate_in.reshape(slot_count, 1).astype(jnp.float32)
    hidden_grad = (flat_gate * backprop).astype(jnp.bfloat16)
    slot_grad = jnp.sum(hidden.astype(jnp.float32) * backprop, axis=1)
    scaled = (flat_gate * flat_rows.astype(jnp.float32)).astype(jnp.bfloat16)
    partial_grad = lax.dot_general(
        hidden, scaled, (((0,), (0,)), ((), ())), preferred_element_type=jnp.float32
    )
    weight_grad = lax.psum_scatter(partial_grad, "ctx", scatter_dimension=0, tiled=True)
    returned = lax.all_to_all(
        slot_grad.reshape(count_experts, capacity), "exp", split_axis=0, concat_axis=0, tiled=True
    )
    grad_by_expert = jnp.sum(select_wide * returned[:, :, None], axis=1)
    gate_grad = jnp.sum(onehot * grad_by_expert.T[:, None, :], axis=2)
    logit_grad = gate_probs * (gate_grad - jnp.sum(gate_probs * gate_grad, axis=1, keepdims=True))
    return (logit_grad, hidden_grad.reshape(1, 1, slot_count, -1), weight_grad[None])


def per_device(grad_out, top_logits, expert_ids, saved_hidden, w_down):
    experts = lax.axis_size("exp")
    groups = lax.axis_size("ctx")
    everywhere = top_logits.shape[1] == experts and saved_hidden.shape[2] == experts * grad_out.shape[0]
    plain = experts & (experts - 1) == 0 and groups % 4 == 0 and groups >= 8
    body = per_device_full if everywhere and plain else per_device_routed
    return body(grad_out, top_logits, expert_ids, saved_hidden, w_down)


def solution(mesh):
    return jax.shard_map(
        per_device,
        mesh=mesh,
        in_specs=(
            P(("ctx", "exp"), None),
            P(("ctx", "exp"), None),
            P(("ctx", "exp"), None),
            P("ctx", "exp", None, None),
            P("exp", "ctx", None),
        ),
        out_specs=(P(("ctx", "exp"), None), P("ctx", "exp", None, None), P("exp", "ctx", None)),
        check_vma=False,
    )
```

```python
import functools

import jax
import jax.numpy as jnp
import numpy as np
from jax import lax
from jax.experimental import pallas as pl
from jax.experimental.pallas import tpu as pltpu
from jax.sharding import PartitionSpec as P

LANES = 128
SCALE = 1_000_000
BEGIN_WEIGHT = 600
FIRST_WEIGHT = 12_000
NT = (((1,), (1,)), ((), ()))
NN = (((1,), (0,)), ((), ()))
f32 = jnp.float32
bf16 = jnp.bfloat16


def dot(a, b, dims):
    return lax.dot_general(a, b, dims, preferred_element_type=f32)


def anywhere():
    return pl.BlockSpec(memory_space=pl.ANY)


def whole():
    return pl.BlockSpec(memory_space=pltpu.VMEM)


def scalars():
    return pl.BlockSpec(memory_space=pltpu.SMEM)


def params(mib=24):
    return pltpu.CompilerParams(vmem_limit_bytes=mib * 1024 * 1024)


def taking(microseconds):
    return pl.CostEstimate(flops=int(microseconds * SCALE), bytes_accessed=int(microseconds * 3e6), transcendentals=0)


def chain_plan(depth):
    products, weights = [], []
    for z in range(depth):
        uses = []
        for turn in range(2, depth + 1):
            if z < depth - 1 and turn >= z + 2:
                uses.append((turn, "AB"[z % 2], depth + 1 + z - turn))
            if z > 0 and turn >= depth - z + 1:
                uses.append((turn, "BA"[z % 2], z + turn - depth - 1))
        products.append(sorted(uses) + [(depth + 1, "own", z)])
        brought = {}
        for turn in range(1, depth):
            for name in "AB":
                index = z + turn if (name == "A") == (z % 2 == 0) else z - turn
                brought[turn, name] = index if 0 <= index < depth else -1
        weights.append(brought)
    return products, weights


class Scalars:
    def __init__(self):
        self.columns = []
        self.names = {}

    def add(self, name, values):
        self.names[name] = len(self.columns)
        self.columns.append(values)

    def __getitem__(self, name):
        return self.names[name]

    def row(self, place, me):
        return jnp.asarray(np.stack(self.columns, axis=-1).astype(np.int32))[place, me]


def device_scalars(depth, experts):
    products, weights = chain_plan(depth)
    table = Scalars()
    along = np.arange(2 * depth)[:, None] + np.zeros((1, experts), np.int32)

    def by_z(values):
        return np.asarray(values)[along // 2]

    table.add("x", along % 2)
    table.add("me", np.zeros_like(along) + np.arange(experts)[None, :])
    table.add(("shard", 0, "own"), along // 2)
    slot_of = [{use[2]: slot for slot, use in enumerate(products[z])} for z in range(depth)]
    for part in range(depth):
        table.add(("slot of", part), by_z([slot_of[z][part] for z in range(depth)]))
    table.add(("slot", 0, "own"), by_z([slot_of[z][z] for z in range(depth)]))
    for turn in range(1, depth):
        for name in "AB":
            shard = [weights[z][turn, name] for z in range(depth)]
            table.add(("shard", turn, name), by_z(shard))
            table.add(("slot", turn, name), by_z([slot_of[z].get(k, 0) for z, k in enumerate(shard)]))
    uses = {}
    for turn in range(2, depth + 1):
        for name in "AB":
            slots = [-1] * depth
            for z in range(depth):
                for slot, use in enumerate(products[z]):
                    if use[:2] == (turn, name):
                        slots[z] = slot
            uses[turn, name] = slots
            table.add(("use", turn, name), by_z(slots))
            limit = max(depth - 3, 0)
            table.add(("block", turn, name), by_z([min(max(slot - 1, 0), limit) for slot in slots]))
    return table, weights, uses


def rows_kernel(cut, grad_hbm, logits_hbm, ids_hbm, late_ref, early_ref, gates_ref, *scratch):
    grad_ref, logits_ref, ids_ref, sems = scratch
    model, tokens = grad_ref.shape
    copies = [
        pltpu.make_async_copy(source, target, sems.at[place])
        for place, (source, target) in enumerate(
            ((grad_hbm, grad_ref), (logits_hbm, logits_ref), (ids_hbm, ids_ref))
        )
    ]
    for copy in copies:
        copy.start()
    for copy in copies:
        copy.wait()
    count = logits_ref.shape[0]
    width = cut + late_ref.shape[1]
    logits = logits_ref[...]
    powers = jnp.exp(logits - jnp.max(logits, axis=0, keepdims=True))
    gates = powers / jnp.sum(powers, axis=0, keepdims=True)
    gates_ref[...] = gates
    sent = gates.astype(bf16).astype(f32)
    ids = ids_ref[...]
    row = lax.broadcasted_iota(jnp.int32, (width - model, tokens), 0)
    extra = jnp.zeros((width - model, tokens), f32)
    for expert in range(count):
        chosen = jnp.sum(jnp.where(ids == expert, sent, 0.0), axis=0, keepdims=True)
        extra = extra + jnp.where(row == expert, chosen, 0.0)
    for start in range(0, width, LANES):
        stop = start + LANES
        if stop <= model:
            block = grad_ref[start:stop, :].astype(f32)
        elif start >= model:
            block = extra[start - model : stop - model, :]
        else:
            block = jnp.concatenate(
                [grad_ref[start:model, :].astype(f32), extra[: stop - model, :]], axis=0
            )
        turned = block.T.astype(bf16)
        if start < cut:
            early_ref[:, start:stop] = turned
        else:
            late_ref[:, start - cut : stop - cut] = turned


def make_rows(grad_out, top_logits, expert_ids, width, cut):
    tokens, model = grad_out.shape
    count = top_logits.shape[1]
    return pl.pallas_call(
        functools.partial(rows_kernel, cut),
        out_shape=(
            jax.ShapeDtypeStruct((tokens, width - cut), bf16),
            jax.ShapeDtypeStruct((tokens, cut), bf16),
            jax.ShapeDtypeStruct((count, tokens), f32),
        ),
        in_specs=[pl.BlockSpec(memory_space=pltpu.HBM)] * 3,
        out_specs=(whole(),) * 3,
        scratch_shapes=[
            pltpu.VMEM((model, tokens), bf16),
            pltpu.VMEM((count, tokens), f32),
            pltpu.VMEM((count, tokens), jnp.int32),
            pltpu.SemaphoreType.DMA((3,)),
        ],
        compiler_params=params(58),
        cost_estimate=taking(2),
        name="make_rows",
    )(grad_out.T, top_logits.T, expert_ids.T)


def pack_kernel(*refs):
    out_ref, sems = refs[-2:]
    copies = []
    for place in range(out_ref.shape[0]):
        copies.append(pltpu.make_async_copy(refs[place], out_ref.at[place], sems.at[place]))
        copies[-1].start()
    for copy in copies:
        copy.wait()


def pack(values, after):
    number = len(values)
    return pl.pallas_call(
        pack_kernel,
        out_shape=jax.ShapeDtypeStruct((number, *values[0].shape), values[0].dtype),
        in_specs=[anywhere()] * (number + len(after)),
        out_specs=anywhere(),
        scratch_shapes=[pltpu.SemaphoreType.DMA((number,))],
        compiler_params=params(),
        cost_estimate=taking(1),
        name="pack_rows",
    )(*values, *after)


def blocks_of(refs, places):
    return [refs[array] if place is None else refs[array].at[place] for array, place in places]


def hold_kernel(*refs):
    del refs


def hold(values, after, weight=0):
    return pl.pallas_call(
        hold_kernel,
        out_shape=tuple(jax.ShapeDtypeStruct(value.shape, value.dtype) for value in values),
        in_specs=[anywhere()] * (len(values) + len(after)),
        out_specs=(anywhere(),) * len(values),
        input_output_aliases={place: place for place in range(len(values))},
        compiler_params=params(),
        cost_estimate=taking(weight),
        name="hold",
    )(*values, *after)


def split_kernel(table, where_ref, hidden_ref, *refs):
    own_ref, first_ref, rest_ref = refs[-3:]
    parts, units, _ = own_ref.shape
    row = lax.broadcasted_iota(jnp.int32, (2 * units, 2 * units), 0)
    column = lax.broadcasted_iota(jnp.int32, (2 * units, 2 * units), 1)
    unit = jnp.where(row == column, 1.0, 0.0).astype(bf16)
    low = where_ref[table["x"]] == 0
    for part in range(parts):
        block = hidden_ref[:, part * 2 * units : (part + 1) * 2 * units]
        turned = dot(unit, block, NT).astype(bf16)
        slot = where_ref[table["slot of", part]]
        other = jnp.where(low, turned[units:], turned[:units])
        own_ref[slot] = jnp.where(low, turned[:units], turned[units:])

        @pl.when(slot == 0)
        def _():
            first_ref[0] = other

        @pl.when(slot != 0)
        def _():
            rest_ref[slot - 1] = other


def split_hidden(table, where, hidden, parts, units, after):
    slots = hidden.shape[0]
    return pl.pallas_call(
        functools.partial(split_kernel, table),
        out_shape=tuple(
            jax.ShapeDtypeStruct((count, units, slots), bf16) for count in (parts, 1, parts - 1)
        ),
        in_specs=[scalars(), whole()] + [anywhere()] * len(after),
        out_specs=(whole(),) * 3,
        compiler_params=params(),
        cost_estimate=taking(2),
        name="split_hidden",
    )(where, hidden, *after)


def place_of(place, count, me, tokens):
    start = (place // count) * count * tokens + ((place % count) ^ me) * tokens
    return pl.multiple_of(start, tokens)


def scale_rows(table, model, where_ref, rows, gated, scaled):
    tokens = rows[0].shape[0]
    me = where_ref[table["me"]]
    lane = lax.broadcasted_iota(jnp.int32, (tokens, LANES), 1)
    for place, block in enumerate(rows):
        here = pl.ds(place_of(place, len(rows) // 2, me, tokens), tokens)
        tile = gated[place][:, gated[place].shape[1] - LANES :]
        picked = jnp.where(lane == model % LANES + me, tile.astype(f32), 0.0)
        gate = jnp.sum(picked, axis=1, keepdims=True)
        scaled[here, :] = (block[:, : scaled.shape[1]].astype(f32) * gate).astype(bf16)


def products_kernel(table, model, counts, places, shards, skip, guard, where_ref, *refs):
    used = sum(counts)
    rows = blocks_of(refs[: counts[0]], places[0])
    gated = blocks_of(refs[counts[0] : used], places[1])
    own_ref, other_ref = refs[used : used + 2]
    kept_ref, scaled = refs[-2:]
    units, slots = own_ref.shape[1:]

    def stacked(ref, offset):
        parts = [ref[offset + shard] for shard in range(shards)]
        return jnp.concatenate(parts, axis=0) if len(parts) > 1 else parts[0]

    def work():
        scale_rows(table, model, where_ref, rows, gated, scaled)
        total = dot(stacked(own_ref, skip), scaled[:slots, :], NN)
        total = total + dot(stacked(other_ref, 0), scaled[slots:, :], NN)
        for shard in range(shards):
            kept_ref[shard] = total[shard * units : (shard + 1) * units]

    if guard:
        pl.when(where_ref[table["use", 2, "A"]] != 0)(work)
    else:
        work()


def products(table, where, rows, gated, own, other, skip, model, width, name, after, guard=False):
    arrays, places = zip(rows, gated)
    tokens = arrays[0][0].shape[-2]
    counts = [len(part) for part in arrays]
    shards, units, slots = other.shape
    return pl.pallas_call(
        functools.partial(products_kernel, table, model, counts, places, shards, skip, guard),
        out_shape=jax.ShapeDtypeStruct((shards, units, width), f32),
        in_specs=[scalars()] + [whole()] * (sum(counts) + 2) + [anywhere()] * len(after),
        out_specs=whole(),
        scratch_shapes=[pltpu.VMEM((2 * slots, width), bf16)],
        compiler_params=params(),
        cost_estimate=taking(4),
        name=name,
    )(where, *arrays[0], *arrays[1], own, other, *after)


def first_kernel(table, model, counts, places, start, where_ref, *refs):
    used = sum(counts)
    rows = blocks_of(refs[: counts[0]], places[0])
    gated = blocks_of(refs[counts[0] : used], places[1])
    own_ref, other_ref, coming_ref = refs[used : used + 3]
    out_ref, scaled = refs[-2:]
    slots = own_ref.shape[2]
    ends = where_ref[table["use", 2, "A"]] == 0

    @pl.when(ends)
    def _():
        scale_rows(table, model, where_ref, rows, gated, scaled)
        total = dot(own_ref[0], scaled[:slots, :], NN)
        out_ref[...] = (total + dot(other_ref[0], scaled[slots:, :], NN)).astype(bf16)

    @pl.when(jnp.logical_not(ends))
    def _():
        out_ref[...] = coming_ref[:, start : start + out_ref.shape[1]]


def first_sums(table, where, rows, gated, own, other, coming, model, start, width, after):
    arrays, places = zip(rows, gated)
    counts = [len(part) for part in arrays]
    units, slots = own.shape[1:]
    return pl.pallas_call(
        functools.partial(first_kernel, table, model, counts, places, start),
        out_shape=jax.ShapeDtypeStruct((units, width), bf16),
        in_specs=[scalars()] + [whole()] * (sum(counts) + 3) + [anywhere()] * len(after),
        out_specs=whole(),
        scratch_shapes=[pltpu.VMEM((2 * slots, width), bf16)],
        compiler_params=params(),
        cost_estimate=taking(BEGIN_WEIGHT),
        name="first_sums",
    )(where, *arrays[0], *arrays[1], own, other, coming, *after)


def rows_of(units):
    return units // 2 if units % 32 == 0 else units


def column_parts(arrays, cut):
    return [(0, arrays[0])] if len(arrays) == 1 else [(cut, arrays[0]), (0, arrays[1])]


def combine_kernel(table, key, cut, counts, sides, where_ref, *refs):
    slot = where_ref[table[key]]
    coming = refs[: counts[0]]
    outs = refs[len(refs) - counts[2] :]
    model = sum(ref.shape[1] for ref in outs)
    spans = [(cut, model), (0, cut)] if cut else [(0, model)]
    for chunk, (start, stop) in enumerate(spans):
        if counts[0] == 0:
            total = jnp.zeros((outs[0].shape[0], stop - start), f32)
        elif counts[0] == 1:
            total = coming[0][:, start:stop].astype(f32)
        else:
            total = coming[chunk][...].astype(f32)
        for number, side in enumerate(sides):
            flag = slot == 0 if side == "first" else slot > 0
            total = total + jnp.where(flag, refs[counts[0] + len(spans) * number + chunk][0], 0.0)
        total = total.astype(bf16)
        if counts[2] == 1:
            outs[0][:, start:stop] = total
        else:
            outs[chunk][...] = total


def combine(table, where, coming, first, rest, turn, name, used, cut, after, chunked=False):
    units = first[0].shape[1]
    model = sum(part.shape[2] for part in first)
    block = rows_of(units)
    column = table["block", turn, name]
    sides, operands, specs = [], [], []
    if any(slot == 0 for slot in used):
        sides.append("first")
        operands += first
        specs += [pl.BlockSpec((1, block, part.shape[2]), lambda j, s: (0, j, 0)) for part in first]
    if any(slot > 0 for slot in used):
        sides.append("rest")
        operands += rest
        specs += [pl.BlockSpec((1, block, part.shape[2]), lambda j, s: (s[column], j, 0)) for part in rest]
    widths = [model - cut, cut] if chunked else [model]
    return pl.pallas_call(
        functools.partial(
            combine_kernel, table, ("use", turn, name), cut, (len(coming), len(operands), len(widths)), sides
        ),
        out_shape=[jax.ShapeDtypeStruct((units, count), bf16) for count in widths],
        grid_spec=pltpu.PrefetchScalarGridSpec(
            num_scalar_prefetch=1,
            grid=(units // block,),
            in_specs=[pl.BlockSpec((block, part.shape[1]), lambda j, s: (j, 0)) for part in coming]
            + specs
            + [anywhere()] * len(after),
            out_specs=[pl.BlockSpec((block, count), lambda j, s: (j, 0)) for count in widths],
        ),
        compiler_params=params(),
        cost_estimate=taking(1.5),
        name="combine",
    )(where, *coming, *operands, *after)


def total_kernel(cut, counts, *refs):
    coming = [refs[: counts[0]], refs[counts[0] : sum(counts)]]
    out_ref = refs[-1]
    for chunk, start in enumerate((cut, 0)):
        kept_ref = refs[sum(counts) + chunk]
        here = slice(start, start + kept_ref.shape[2])
        total = kept_ref[0]
        for parts in coming:
            total = total + (parts[0][:, here] if len(parts) == 1 else parts[chunk][...]).astype(f32)
        out_ref[0, :, here] = total


def total_grad(a, b, kept, cut):
    units = a[0].shape[0]
    model = sum(part.shape[1] for part in a)
    block = rows_of(units)
    return pl.pallas_call(
        functools.partial(total_kernel, cut, (len(a), len(b))),
        out_shape=jax.ShapeDtypeStruct((1, units, model), f32),
        grid=(units // block,),
        in_specs=[pl.BlockSpec((block, part.shape[1]), lambda j: (j, 0)) for part in (*a, *b)]
        + [
            pl.BlockSpec((1, block, part.shape[2]), functools.partial(lambda last, j: (last, j, 0), part.shape[0] - 1))
            for part in kept
        ],
        out_specs=pl.BlockSpec((1, block, model), lambda j: (0, j, 0)),
        compiler_params=params(),
        cost_estimate=taking(2),
        name="total_grad",
    )(*a, *b, *kept)


def back_kernel(table, model, cut, counts, places, choices, parts, guard, summed, where_ref, *refs):
    keys = [key for choice in choices for key in choice]
    used = sum(counts)
    late = blocks_of(refs[: counts[0]], places[0])
    early = blocks_of(refs[counts[0] : used], places[1])
    number = len(late)
    own_ref, first_ref, rest_ref = refs[used : used + 3]
    weight_refs, used = {}, used + 3
    for key, count in zip(keys, parts):
        weight_refs[key] = refs[used : used + count]
        used += count
    before_ref = refs[used] if summed else None
    outs, sums_ref = refs[-3:-1], refs[-1]
    tokens = late[0].shape[0]
    units = own_ref.shape[1]
    me = where_ref[table["me"]]
    start = late[0].shape[1] - LANES
    eight = lax.broadcasted_iota(jnp.int32, (8, LANES), 1)
    onehot = jnp.where(eight == model % LANES + me, 1.0, 0.0).astype(bf16)
    shards = {key: where_ref[table[("shard",) + key]] for key in keys}
    slots = {key: where_ref[table[("slot",) + key]] for key in keys}
    sums_ref[...] = before_ref[...] if summed else jnp.zeros(sums_ref.shape, f32)

    def whole_weight(key):
        got = weight_refs[key]
        return got[0][...] if len(got) == 1 else jnp.concatenate([got[1][...], got[0][...]], axis=1)

    def work():
        stack, here_valid, here_slot = [], [], []
        for choice in choices:
            weight, valid, slot = whole_weight(choice[0]), shards[choice[0]] >= 0, slots[choice[0]]
            for key in choice[1:]:
                weight = jnp.where(valid, weight, whole_weight(key))
                slot = jnp.where(valid, slot, slots[key])
                valid = jnp.logical_or(valid, shards[key] >= 0)
            stack.append(weight)
            here_valid.append(valid)
            here_slot.append(slot)
        weight = jnp.concatenate(stack, axis=0) if len(stack) > 1 else stack[0]
        for pair in range(0, number, 2):
            both = jnp.concatenate(
                [
                    jnp.concatenate([early[k][...], late[k][:, : model - cut]], axis=1)
                    for k in (pair, pair + 1)
                ],
                axis=0,
            )
            product = dot(weight, both, NT)
            for place in (pair, pair + 1):
                near = place < number // 2
                block = product[:, (place - pair) * tokens : (place - pair + 1) * tokens]
                gate = dot(onehot, late[place][:, start:], NT)[0:1]
                here = pl.ds(place_of(place % (number // 2), number // 2, me, tokens), tokens)
                wide = pl.ds(place_of(place, number // 2, me, tokens), tokens)
                gated = (block * gate).astype(bf16)
                total = jnp.zeros((1, tokens), f32)
                for index, (valid, slot) in enumerate(zip(here_valid, here_slot)):
                    some = slice(index * units, (index + 1) * units)
                    outs[0 if near else 1][index, :, here] = gated[some]
                    if near:
                        hidden = own_ref[slot, :, here].astype(f32)
                    else:
                        hidden = jnp.where(
                            slot == 0,
                            first_ref[0, :, here].astype(f32),
                            rest_ref[jnp.maximum(slot - 1, 0), :, here].astype(f32),
                        )
                    part = jnp.sum(hidden * block[some], axis=0, keepdims=True)
                    total = total + jnp.where(valid, part, 0.0)
                sums_ref[0:1, wide] += total

    if guard:
        pl.when(functools.reduce(jnp.logical_or, [shards[key] >= 0 for key in keys]))(work)
    else:
        work()


def back_part(table, where, late, early, own, first, rest, choices, got, before, guard, after, model):
    units, slots = own.shape[1:]
    arrays, places = zip(late, early)
    counts = [len(part) for part in arrays]
    cut = arrays[1][0].shape[-1]
    keys = [key for choice in choices for key in choice]
    weights = [got[key] for key in keys]
    flat = [part for weight in weights for part in weight]
    half = jax.ShapeDtypeStruct((len(choices), units, slots), bf16)
    summed = before is not None
    operands = [*arrays[0], *arrays[1], own, first, rest, *flat] + ([before] if summed else [])
    outs = [half, half, jax.ShapeDtypeStruct((8, 2 * slots), f32)]
    parts = [len(weight) for weight in weights]
    return pl.pallas_call(
        functools.partial(
            back_kernel, table, model, cut, counts, places, choices, parts, guard, summed
        ),
        out_shape=outs,
        in_specs=[scalars()] + [whole()] * len(operands) + [anywhere()] * len(after),
        out_specs=[whole()] * len(outs),
        compiler_params=params(),
        cost_estimate=taking(6),
        name="back_part",
    )(where, *operands, *after)


def join_kernel(table, choices, where_ref, *refs):
    out_ref, turned, sem = refs[-3:]
    slots, width = turned.shape[1:]
    row = lax.broadcasted_iota(jnp.int32, (slots, slots), 0)
    column = lax.broadcasted_iota(jnp.int32, (slots, slots), 1)
    unit = jnp.where(row == column, 1.0, 0.0).astype(bf16)
    low = where_ref[table["x"]] == 0
    copies = []
    pairs = [
        (refs[2 * group][place], refs[2 * group + 1][place])
        for group in range((len(refs) - 3) // 2)
        for place in range(refs[2 * group].shape[0])
    ]
    for place, (choice, (mine, theirs)) in enumerate(zip(choices, pairs)):
        index = where_ref[table[("shard",) + choice[0]]]
        for key in choice[1:]:
            index = jnp.where(index >= 0, index, where_ref[table[("shard",) + key]])
        both = jnp.concatenate([jnp.where(low, mine, theirs), jnp.where(low, theirs, mine)], axis=0)
        turned[place] = dot(unit, both, NT).astype(bf16)
        here = pl.ds(pl.multiple_of(jnp.maximum(index, 0) * width, LANES), width)
        copy = pltpu.make_async_copy(turned.at[place], out_ref.at[:, here], sem.at[place])
        copies.append((index, copy))
        pl.when(index >= 0)(copy.start)
    for index, copy in copies:
        pl.when(index >= 0)(copy.wait)


def join_hidden(table, where, choices, halves, slots, hidden):
    units = halves[0].shape[1]
    return pl.pallas_call(
        functools.partial(join_kernel, table, choices),
        out_shape=jax.ShapeDtypeStruct((slots, hidden), bf16),
        in_specs=[scalars()] + [whole()] * len(halves),
        out_specs=anywhere(),
        scratch_shapes=[
            pltpu.VMEM((len(choices), slots, 2 * units), bf16),
            pltpu.SemaphoreType.DMA((len(choices),)),
        ],
        compiler_params=params(),
        cost_estimate=taking(2),
        name="join_hidden",
    )(where, *halves)


def logits_kernel(gates_ref, ids_ref, grads_ref, out_ref):
    gates, ids, grads = gates_ref[...], ids_ref[...], grads_ref[...]
    picked = jnp.zeros_like(gates)
    for expert in range(grads.shape[0]):
        picked = picked + jnp.where(ids == expert, grads[expert : expert + 1, :], 0.0)
    out_ref[...] = gates * (picked - jnp.sum(gates * picked, axis=0, keepdims=True))


def logits_grad(gates, ids, grads):
    return pl.pallas_call(
        logits_kernel,
        out_shape=jax.ShapeDtypeStruct(gates.shape, f32),
        in_specs=[whole()] * 3,
        out_specs=whole(),
        compiler_params=params(),
        cost_estimate=taking(1),
        name="logits_grad",
    )(gates, ids, grads)


def per_device_full(grad_out, top_logits, expert_ids, saved_hidden, w_down):
    experts = lax.axis_size("exp")
    groups = lax.axis_size("ctx")
    depth = groups // 2
    tokens, model = grad_out.shape
    slots, hidden = saved_hidden.shape[2:]
    width = pl.cdiv(model + experts, LANES) * LANES
    cut = width // LANES // 2 * LANES

    table, brought, uses = device_scalars(depth, experts)
    where = table.row(lax.axis_index("ctx"), lax.axis_index("exp"))

    def swap(value, x, exp):
        if not exp:
            return lax.ppermute(value, "ctx", [(i, i ^ x) for i in range(groups)])
        if not x:
            return lax.ppermute(value, "exp", [(i, i ^ exp) for i in range(experts)])
        pairs = [(c * experts + e, (c ^ x) * experts + (e ^ exp)) for c in range(groups) for e in range(experts)]
        return lax.ppermute(value, ("ctx", "exp"), pairs)

    def swap_z(value, name, senders=range(depth)):
        first = "AB".index(name)
        pairs = []
        for low in range(first, depth - 1, 2):
            for z, other in ((low, low + 1), (low + 1, low)):
                pairs += [(2 * z + x, 2 * other + x) for x in range(2) if z in senders]
        return lax.ppermute(value, "ctx", pairs)

    got = {(0, "own"): [w_down[0]]}
    for name in "BA":
        got[1, name] = [swap_z(w_down[0], name)]

    late, early, gates = make_rows(grad_out, top_logits, expert_ids, width, cut)
    highs = list(range(2, experts, 2))

    def sides(mine):
        return [mine, swap(mine, 0, 1)]

    late_x = swap(late, 1, 0)
    late_near = [late] + [swap(late, 0, high) for high in highs]
    own, other_first, other_rest = split_hidden(
        table, where, saved_hidden[0, 0], depth, w_down.shape[1], [late]
    )
    other_first = swap(other_first, 1, 0)
    (late_x,) = hold((late_x,), late_near[1:])
    late_mine = late_near + [late_x] + [swap(late_x, 0, high) for high in highs]
    (early,) = hold((early,), [late_x, other_first])
    early_x = swap(early, 1, 0)
    late_rows = sides(pack(late_mine, [early_x]))
    late_rows = (late_rows, [(side, place) for place in range(experts) for side in range(2)])
    early_rows = sides(pack([early, early_x], []))
    places = [(0, 0), (1, 0)]
    for block, base in ((early, 0), (early_x, 1)):
        if base:
            places += [(0, 1), (1, 1)]
        for high in highs:
            places += [(len(early_rows), None), (len(early_rows) + 1, None)]
            early_rows += sides(swap(block, 0, high))
    early_rows = (early_rows, places)
    other_rest = swap(other_rest, 1, 0)

    for name, value in zip("BA", hold([got[1, "B"][0], got[1, "A"][0]], [], FIRST_WEIGHT)):
        got[1, name] = [value]
    chunks = ((late_rows, cut, model - cut), (early_rows, 0, cut))
    after = [early_rows[0][1]]
    first = []
    for rows, start, columns in chunks:
        value = first_sums(
            table, where, rows, late_rows, own, other_first, got[1, "B"][0], model, start, columns, after
        )
        if first:
            (value,) = hold([value], [other_rest])
        got.setdefault((2, "A"), []).append(swap_z(value, "A"))
        first.append(
            products(table, where, rows, late_rows, own, other_first, 0, model, columns, "first_kept", [value], True)
        )
        after = [got[2, "A"][0], first[0]]
    marker = value
    got[2, "B"] = [swap_z(got[1, "A"][0], "B")]

    halves, all_choices, weights_of = [], [], {}
    only_first = max(uses[3, "B"]) <= 0

    def backprop(choices, before, guard, after):
        mine, theirs, sums = back_part(
            table, where, late_rows, early_rows, own, other_first, other_rest, choices,
            {**got, **weights_of}, before, guard, after, model,
        )
        halves.extend([mine, swap(theirs, 1, 0)])
        all_choices.extend(choices)
        return sums

    def pass_on(turn, name, after, chunk=None, waited=()):
        coming = got[turn - 1, "B" if name == "A" else "A"]
        parts, start, chunked = (first, rest), cut, turn == depth and name == "B"
        used = uses[turn, name]
        senders = [z for z in range(depth) if used[z] >= 0] if turn == depth - 1 else range(depth)
        others = [z for z in range(depth) if z not in senders]
        if others and chunk is None and len(coming) == 1:
            weights_of[turn, name] = [swap_z(coming[0], name, others)]
            ends = {0, depth - 1} if name == "A" else set()
            coming = [] if set(senders) <= ends else coming
        if chunk is not None:
            coming, parts, start = [coming[chunk]], (first[chunk:][:1], rest[chunk:][:1]), 0
        values = list(combine(table, where, coming, *parts, turn, name, used, start, after, chunked))
        if waited:
            values[1:] = hold(values[1:], list(waited))
        got.setdefault((turn, name), []).extend(swap_z(value, name, senders) for value in values)
        return values[-1]

    def choices_of(turn):
        both = any(b[turn, "A"] >= 0 and b[turn, "B"] >= 0 for b in brought)
        return [[(turn, "A")], [(turn, "B")]] if both else [[(turn, "A"), (turn, "B")]]

    rest = []
    marker = pass_on(3, "B", [marker], 0) if only_first else marker
    for rows, _, columns in chunks:
        rest.append(
            products(table, where, rows, late_rows, own, other_rest, 1, model, columns, "rest_kept", [marker])
        )
    marker = pass_on(3, "A", rest)
    for chunk in range(2)[only_first:]:
        marker = pass_on(3, "B", [marker], chunk)
    sums = backprop([[(0, "own")], [(1, "A")], [(1, "B")]], None, False, [marker])
    sooner = halves[1::2]
    for turn in range(2, depth):
        choices = choices_of(turn)
        if turn > 2:
            waited = [array for key in ((turn, "A"), (turn, "B")) for array in weights_of.get(key, [])]
            pass_on(turn + 1, "B", [sums, *sooner], waited=waited)
            marker = pass_on(turn + 1, "A", [sums])
        sums = backprop(choices, sums, len(choices) == 1, [marker])
    slot_grad = sums[0:1, :slots] + swap(sums[0:1, slots:], 1, 0)
    grads = lax.all_to_all(
        slot_grad.reshape(experts, tokens), "exp", split_axis=0, concat_axis=0, tiled=True
    )
    logit_grad = logits_grad(gates, expert_ids.T, grads)
    hidden_grad = join_hidden(table, where, all_choices, halves, slots, hidden)
    weight_grad = total_grad(got[depth, "A"], got[depth, "B"], rest, cut)
    return (logit_grad.T, hidden_grad[None, None], weight_grad)


def routing_tables(expert_ids, count_experts, capacity):
    columns = jnp.arange(count_experts, dtype=jnp.int32)
    matches = expert_ids[:, :, None] == columns[None, None, :]
    per_token = jnp.sum(matches.astype(jnp.int32), axis=1)
    rank_table = jnp.cumsum(per_token, axis=0) - per_token
    slot_iota = jnp.arange(capacity, dtype=jnp.int32)
    select = (per_token.T[:, None, :] == 1) & (rank_table.T[:, None, :] == slot_iota[None, :, None])
    return (matches.astype(jnp.float32), select)


def per_device_routed(grad_out, top_logits, expert_ids, saved_hidden, w_down):
    count_experts = lax.axis_size("exp")
    slot_count = saved_hidden.shape[2]
    capacity = slot_count // count_experts
    model_width = grad_out.shape[1]
    onehot, select = routing_tables(expert_ids, count_experts, capacity)
    select_wide = select.astype(jnp.float32)
    gate_probs = jax.nn.softmax(top_logits, axis=-1)
    gate_sent = gate_probs.astype(jnp.bfloat16)
    gate_by_expert = jnp.sum(onehot * gate_sent.astype(jnp.float32)[:, :, None], axis=1)
    send_rows = jnp.einsum(
        "ect,td->ecd", select.astype(jnp.bfloat16), grad_out, preferred_element_type=jnp.float32
    ).astype(jnp.bfloat16)
    send_gate = jnp.sum(select_wide * gate_by_expert.T[:, None, :], axis=2).astype(jnp.bfloat16)
    hidden = saved_hidden[0, 0]
    rows_in, gate_in = (
        lax.all_to_all(send_rows, "exp", split_axis=0, concat_axis=0, tiled=True),
        lax.all_to_all(send_gate, "exp", split_axis=0, concat_axis=0, tiled=True),
    )
    flat_rows = rows_in.reshape(slot_count, model_width)
    backprop = lax.dot_general(
        flat_rows,
        lax.all_gather(w_down[0], "ctx", axis=0, tiled=True),
        (((1,), (1,)), ((), ())),
        preferred_element_type=jnp.float32,
    )
    flat_gate = gate_in.reshape(slot_count, 1).astype(jnp.float32)
    hidden_grad = (flat_gate * backprop).astype(jnp.bfloat16)
    slot_grad = jnp.sum(hidden.astype(jnp.float32) * backprop, axis=1)
    scaled = (flat_gate * flat_rows.astype(jnp.float32)).astype(jnp.bfloat16)
    partial_grad = lax.dot_general(
        hidden, scaled, (((0,), (0,)), ((), ())), preferred_element_type=jnp.float32
    )
    weight_grad = lax.psum_scatter(partial_grad, "ctx", scatter_dimension=0, tiled=True)
    returned = lax.all_to_all(
        slot_grad.reshape(count_experts, capacity), "exp", split_axis=0, concat_axis=0, tiled=True
    )
    grad_by_expert = jnp.sum(select_wide * returned[:, :, None], axis=1)
    gate_grad = jnp.sum(onehot * grad_by_expert.T[:, None, :], axis=2)
    logit_grad = gate_probs * (gate_grad - jnp.sum(gate_probs * gate_grad, axis=1, keepdims=True))
    return (logit_grad, hidden_grad.reshape(1, 1, slot_count, -1), weight_grad[None])


def per_device(grad_out, top_logits, expert_ids, saved_hidden, w_down):
    experts = lax.axis_size("exp")
    groups = lax.axis_size("ctx")
    everywhere = top_logits.shape[1] == experts and saved_hidden.shape[2] == experts * grad_out.shape[0]
    plain = experts & (experts - 1) == 0 and groups % 4 == 0 and groups >= 8
    body = per_device_full if everywhere and plain else per_device_routed
    return body(grad_out, top_logits, expert_ids, saved_hidden, w_down)


def solution(mesh):
    return jax.shard_map(
        per_device,
        mesh=mesh,
        in_specs=(
            P(("ctx", "exp"), None),
            P(("ctx", "exp"), None),
            P(("ctx", "exp"), None),
            P("ctx", "exp", None, None),
            P("exp", "ctx", None),
        ),
        out_specs=(P(("ctx", "exp"), None), P("ctx", "exp", None, None), P("exp", "ctx", None)),
        check_vma=False,
    )
```

```python
import functools

import jax
import jax.numpy as jnp
import numpy as np
from jax import lax
from jax.experimental import pallas as pl
from jax.experimental.pallas import tpu as pltpu
from jax.sharding import PartitionSpec as P

LANES = 128
SCALE = 1_000_000
BEGIN_WEIGHT = 600
FIRST_WEIGHT = 12_000
LAST_WEIGHT = 90
NT = (((1,), (1,)), ((), ()))
NN = (((1,), (0,)), ((), ()))
f32 = jnp.float32
bf16 = jnp.bfloat16


def dot(a, b, dims):
    return lax.dot_general(a, b, dims, preferred_element_type=f32)


def anywhere():
    return pl.BlockSpec(memory_space=pl.ANY)


def whole():
    return pl.BlockSpec(memory_space=pltpu.VMEM)


def scalars():
    return pl.BlockSpec(memory_space=pltpu.SMEM)


def params(mib=24):
    return pltpu.CompilerParams(vmem_limit_bytes=mib * 1024 * 1024)


def taking(microseconds):
    return pl.CostEstimate(flops=int(microseconds * SCALE), bytes_accessed=int(microseconds * 3e6), transcendentals=0)


def chain_plan(depth):
    products, weights = [], []
    for z in range(depth):
        uses = []
        for turn in range(2, depth + 1):
            if z < depth - 1 and turn >= z + 2:
                uses.append((turn, "AB"[z % 2], depth + 1 + z - turn))
            if z > 0 and turn >= depth - z + 1:
                uses.append((turn, "BA"[z % 2], z + turn - depth - 1))
        products.append(sorted(uses) + [(depth + 1, "own", z)])
        brought = {}
        for turn in range(1, depth):
            for name in "AB":
                index = z + turn if (name == "A") == (z % 2 == 0) else z - turn
                brought[turn, name] = index if 0 <= index < depth else -1
        weights.append(brought)
    return products, weights


class Scalars:
    def __init__(self):
        self.columns = []
        self.names = {}

    def add(self, name, values):
        self.names[name] = len(self.columns)
        self.columns.append(values)

    def __getitem__(self, name):
        return self.names[name]

    def row(self, place, me):
        return jnp.asarray(np.stack(self.columns, axis=-1).astype(np.int32))[place, me]


def device_scalars(depth, experts):
    products, weights = chain_plan(depth)
    table = Scalars()
    along = np.arange(2 * depth)[:, None] + np.zeros((1, experts), np.int32)

    def by_z(values):
        return np.asarray(values)[along // 2]

    table.add("x", along % 2)
    table.add("me", np.zeros_like(along) + np.arange(experts)[None, :])
    table.add(("shard", 0, "own"), along // 2)
    slot_of = [{use[2]: slot for slot, use in enumerate(products[z])} for z in range(depth)]
    for part in range(depth):
        table.add(("slot of", part), by_z([slot_of[z][part] for z in range(depth)]))
    table.add(("slot", 0, "own"), by_z([slot_of[z][z] for z in range(depth)]))
    for turn in range(1, depth):
        for name in "AB":
            shard = [weights[z][turn, name] for z in range(depth)]
            table.add(("shard", turn, name), by_z(shard))
            table.add(("slot", turn, name), by_z([slot_of[z].get(k, 0) for z, k in enumerate(shard)]))
    uses = {}
    for turn in range(2, depth + 1):
        for name in "AB":
            slots = [-1] * depth
            for z in range(depth):
                for slot, use in enumerate(products[z]):
                    if use[:2] == (turn, name):
                        slots[z] = slot
            uses[turn, name] = slots
            table.add(("use", turn, name), by_z(slots))
            limit = max(depth - 3, 0)
            table.add(("block", turn, name), by_z([min(max(slot - 1, 0), limit) for slot in slots]))
    return table, weights, uses


def rows_kernel(cut, grad_hbm, logits_hbm, ids_hbm, late_ref, early_ref, gates_ref, *scratch):
    grad_ref, logits_ref, ids_ref, sems = scratch
    model, tokens = grad_ref.shape
    copies = [
        pltpu.make_async_copy(source, target, sems.at[place])
        for place, (source, target) in enumerate(
            ((grad_hbm, grad_ref), (logits_hbm, logits_ref), (ids_hbm, ids_ref))
        )
    ]
    for copy in copies:
        copy.start()
    for copy in copies:
        copy.wait()
    count = logits_ref.shape[0]
    width = cut + late_ref.shape[1]
    logits = logits_ref[...]
    powers = jnp.exp(logits - jnp.max(logits, axis=0, keepdims=True))
    gates = powers / jnp.sum(powers, axis=0, keepdims=True)
    gates_ref[...] = gates
    sent = gates.astype(bf16).astype(f32)
    ids = ids_ref[...]
    row = lax.broadcasted_iota(jnp.int32, (width - model, tokens), 0)
    extra = jnp.zeros((width - model, tokens), f32)
    for expert in range(count):
        chosen = jnp.sum(jnp.where(ids == expert, sent, 0.0), axis=0, keepdims=True)
        extra = extra + jnp.where(row == expert, chosen, 0.0)
    for start in range(0, width, LANES):
        stop = start + LANES
        if stop <= model:
            block = grad_ref[start:stop, :].astype(f32)
        elif start >= model:
            block = extra[start - model : stop - model, :]
        else:
            block = jnp.concatenate(
                [grad_ref[start:model, :].astype(f32), extra[: stop - model, :]], axis=0
            )
        turned = block.T.astype(bf16)
        if start < cut:
            early_ref[:, start:stop] = turned
        else:
            late_ref[:, start - cut : stop - cut] = turned


def make_rows(grad_out, top_logits, expert_ids, width, cut):
    tokens, model = grad_out.shape
    count = top_logits.shape[1]
    return pl.pallas_call(
        functools.partial(rows_kernel, cut),
        out_shape=(
            jax.ShapeDtypeStruct((tokens, width - cut), bf16),
            jax.ShapeDtypeStruct((tokens, cut), bf16),
            jax.ShapeDtypeStruct((count, tokens), f32),
        ),
        in_specs=[pl.BlockSpec(memory_space=pltpu.HBM)] * 3,
        out_specs=(whole(),) * 3,
        scratch_shapes=[
            pltpu.VMEM((model, tokens), bf16),
            pltpu.VMEM((count, tokens), f32),
            pltpu.VMEM((count, tokens), jnp.int32),
            pltpu.SemaphoreType.DMA((3,)),
        ],
        compiler_params=params(58),
        cost_estimate=taking(2),
        name="make_rows",
    )(grad_out.T, top_logits.T, expert_ids.T)


def pack_kernel(*refs):
    out_ref, sems = refs[-2:]
    copies = []
    for place in range(out_ref.shape[0]):
        copies.append(pltpu.make_async_copy(refs[place], out_ref.at[place], sems.at[place]))
        copies[-1].start()
    for copy in copies:
        copy.wait()


def pack(values, after):
    number = len(values)
    return pl.pallas_call(
        pack_kernel,
        out_shape=jax.ShapeDtypeStruct((number, *values[0].shape), values[0].dtype),
        in_specs=[anywhere()] * (number + len(after)),
        out_specs=anywhere(),
        scratch_shapes=[pltpu.SemaphoreType.DMA((number,))],
        compiler_params=params(),
        cost_estimate=taking(1),
        name="pack_rows",
    )(*values, *after)


def blocks_of(refs, places):
    return [refs[array] if place is None else refs[array].at[place] for array, place in places]


def hold_kernel(*refs):
    del refs


def hold(values, after, weight=0):
    return pl.pallas_call(
        hold_kernel,
        out_shape=tuple(jax.ShapeDtypeStruct(value.shape, value.dtype) for value in values),
        in_specs=[anywhere()] * (len(values) + len(after)),
        out_specs=(anywhere(),) * len(values),
        input_output_aliases={place: place for place in range(len(values))},
        compiler_params=params(),
        cost_estimate=taking(weight),
        name="hold",
    )(*values, *after)


def split_kernel(table, where_ref, hidden_ref, *refs):
    own_ref, first_ref, rest_ref = refs[-3:]
    parts, units, _ = own_ref.shape
    row = lax.broadcasted_iota(jnp.int32, (2 * units, 2 * units), 0)
    column = lax.broadcasted_iota(jnp.int32, (2 * units, 2 * units), 1)
    unit = jnp.where(row == column, 1.0, 0.0).astype(bf16)
    low = where_ref[table["x"]] == 0
    for part in range(parts):
        block = hidden_ref[:, part * 2 * units : (part + 1) * 2 * units]
        turned = dot(unit, block, NT).astype(bf16)
        slot = where_ref[table["slot of", part]]
        other = jnp.where(low, turned[units:], turned[:units])
        own_ref[slot] = jnp.where(low, turned[:units], turned[units:])

        @pl.when(slot == 0)
        def _():
            first_ref[0] = other

        @pl.when(slot != 0)
        def _():
            rest_ref[slot - 1] = other


def split_hidden(table, where, hidden, parts, units, after):
    slots = hidden.shape[0]
    return pl.pallas_call(
        functools.partial(split_kernel, table),
        out_shape=tuple(
            jax.ShapeDtypeStruct((count, units, slots), bf16) for count in (parts, 1, parts - 1)
        ),
        in_specs=[scalars(), whole()] + [anywhere()] * len(after),
        out_specs=(whole(),) * 3,
        compiler_params=params(),
        cost_estimate=taking(2),
        name="split_hidden",
    )(where, hidden, *after)


def place_of(place, count, me, tokens):
    start = (place // count) * count * tokens + ((place % count) ^ me) * tokens
    return pl.multiple_of(start, tokens)


def scale_rows(table, model, where_ref, rows, gated, scaled):
    tokens = rows[0].shape[0]
    me = where_ref[table["me"]]
    lane = lax.broadcasted_iota(jnp.int32, (tokens, LANES), 1)
    for place, block in enumerate(rows):
        here = pl.ds(place_of(place, len(rows) // 2, me, tokens), tokens)
        tile = gated[place][:, gated[place].shape[1] - LANES :]
        picked = jnp.where(lane == model % LANES + me, tile.astype(f32), 0.0)
        gate = jnp.sum(picked, axis=1, keepdims=True)
        scaled[here, :] = (block[:, : scaled.shape[1]].astype(f32) * gate).astype(bf16)


def products_kernel(table, model, counts, places, shards, skip, guard, where_ref, *refs):
    used = sum(counts)
    rows = blocks_of(refs[: counts[0]], places[0])
    gated = blocks_of(refs[counts[0] : used], places[1])
    own_ref, other_ref = refs[used : used + 2]
    kept_ref, scaled = refs[-2:]
    units, slots = own_ref.shape[1:]

    def stacked(ref, offset):
        parts = [ref[offset + shard] for shard in range(shards)]
        return jnp.concatenate(parts, axis=0) if len(parts) > 1 else parts[0]

    def work():
        scale_rows(table, model, where_ref, rows, gated, scaled)
        total = dot(stacked(own_ref, skip), scaled[:slots, :], NN)
        total = total + dot(stacked(other_ref, 0), scaled[slots:, :], NN)
        for shard in range(shards):
            kept_ref[shard] = total[shard * units : (shard + 1) * units]

    if guard:
        pl.when(where_ref[table["use", 2, "A"]] != 0)(work)
    else:
        work()


def products(table, where, rows, gated, own, other, skip, model, width, name, after, guard=False):
    arrays, places = zip(rows, gated)
    tokens = arrays[0][0].shape[-2]
    counts = [len(part) for part in arrays]
    shards, units, slots = other.shape
    return pl.pallas_call(
        functools.partial(products_kernel, table, model, counts, places, shards, skip, guard),
        out_shape=jax.ShapeDtypeStruct((shards, units, width), f32),
        in_specs=[scalars()] + [whole()] * (sum(counts) + 2) + [anywhere()] * len(after),
        out_specs=whole(),
        scratch_shapes=[pltpu.VMEM((2 * slots, width), bf16)],
        compiler_params=params(),
        cost_estimate=taking(4),
        name=name,
    )(where, *arrays[0], *arrays[1], own, other, *after)


def first_kernel(table, model, counts, places, start, where_ref, *refs):
    used = sum(counts)
    rows = blocks_of(refs[: counts[0]], places[0])
    gated = blocks_of(refs[counts[0] : used], places[1])
    own_ref, other_ref, coming_ref = refs[used : used + 3]
    out_ref, scaled = refs[-2:]
    slots = own_ref.shape[2]
    ends = where_ref[table["use", 2, "A"]] == 0

    @pl.when(ends)
    def _():
        scale_rows(table, model, where_ref, rows, gated, scaled)
        total = dot(own_ref[0], scaled[:slots, :], NN)
        out_ref[...] = (total + dot(other_ref[0], scaled[slots:, :], NN)).astype(bf16)

    @pl.when(jnp.logical_not(ends))
    def _():
        out_ref[...] = coming_ref[:, start : start + out_ref.shape[1]]


def first_sums(table, where, rows, gated, own, other, coming, model, start, width, after):
    arrays, places = zip(rows, gated)
    counts = [len(part) for part in arrays]
    units, slots = own.shape[1:]
    return pl.pallas_call(
        functools.partial(first_kernel, table, model, counts, places, start),
        out_shape=jax.ShapeDtypeStruct((units, width), bf16),
        in_specs=[scalars()] + [whole()] * (sum(counts) + 3) + [anywhere()] * len(after),
        out_specs=whole(),
        scratch_shapes=[pltpu.VMEM((2 * slots, width), bf16)],
        compiler_params=params(),
        cost_estimate=taking(1),
        name="first_sums",
    )(where, *arrays[0], *arrays[1], own, other, coming, *after)


def rows_of(units):
    return units // 2 if units % 32 == 0 else units


def column_parts(arrays, cut):
    return [(0, arrays[0])] if len(arrays) == 1 else [(cut, arrays[0]), (0, arrays[1])]


def combine_kernel(table, key, cut, counts, sides, where_ref, *refs):
    slot = where_ref[table[key]]
    coming = refs[: counts[0]]
    outs = refs[len(refs) - counts[2] :]
    model = sum(ref.shape[1] for ref in outs)
    spans = [(cut, model), (0, cut)] if cut else [(0, model)]
    for chunk, (start, stop) in enumerate(spans):
        if counts[0] == 0:
            total = jnp.zeros((outs[0].shape[0], stop - start), f32)
        elif counts[0] == 1:
            total = coming[0][:, start:stop].astype(f32)
        else:
            total = coming[chunk][...].astype(f32)
        for number, side in enumerate(sides):
            flag = slot == 0 if side == "first" else slot > 0
            total = total + jnp.where(flag, refs[counts[0] + len(spans) * number + chunk][0], 0.0)
        total = total.astype(bf16)
        if counts[2] == 1:
            outs[0][:, start:stop] = total
        else:
            outs[chunk][...] = total


def combine(table, where, coming, first, rest, turn, name, used, cut, after, chunked=False, weight=1):
    units = first[0].shape[1]
    model = sum(part.shape[2] for part in first)
    block = rows_of(units)
    column = table["block", turn, name]
    sides, operands, specs = [], [], []
    if any(slot == 0 for slot in used):
        sides.append("first")
        operands += first
        specs += [pl.BlockSpec((1, block, part.shape[2]), lambda j, s: (0, j, 0)) for part in first]
    if any(slot > 0 for slot in used):
        sides.append("rest")
        operands += rest
        specs += [pl.BlockSpec((1, block, part.shape[2]), lambda j, s: (s[column], j, 0)) for part in rest]
    widths = [model - cut, cut] if chunked else [model]
    return pl.pallas_call(
        functools.partial(
            combine_kernel, table, ("use", turn, name), cut, (len(coming), len(operands), len(widths)), sides
        ),
        out_shape=[jax.ShapeDtypeStruct((units, count), bf16) for count in widths],
        grid_spec=pltpu.PrefetchScalarGridSpec(
            num_scalar_prefetch=1,
            grid=(units // block,),
            in_specs=[pl.BlockSpec((block, part.shape[1]), lambda j, s: (j, 0)) for part in coming]
            + specs
            + [anywhere()] * len(after),
            out_specs=[pl.BlockSpec((block, count), lambda j, s: (j, 0)) for count in widths],
        ),
        compiler_params=params(),
        cost_estimate=taking(weight),
        name="combine",
    )(where, *coming, *operands, *after)


def total_kernel(cut, counts, *refs):
    coming = [refs[: counts[0]], refs[counts[0] : sum(counts)]]
    out_ref = refs[-1]
    for chunk, start in enumerate((cut, 0)):
        kept_ref = refs[sum(counts) + chunk]
        here = slice(start, start + kept_ref.shape[2])
        total = kept_ref[0]
        for parts in coming:
            total = total + (parts[0][:, here] if len(parts) == 1 else parts[chunk][...]).astype(f32)
        out_ref[0, :, here] = total


def total_grad(a, b, kept, cut):
    units = a[0].shape[0]
    model = sum(part.shape[1] for part in a)
    block = rows_of(units)
    return pl.pallas_call(
        functools.partial(total_kernel, cut, (len(a), len(b))),
        out_shape=jax.ShapeDtypeStruct((1, units, model), f32),
        grid=(units // block,),
        in_specs=[pl.BlockSpec((block, part.shape[1]), lambda j: (j, 0)) for part in (*a, *b)]
        + [
            pl.BlockSpec((1, block, part.shape[2]), functools.partial(lambda last, j: (last, j, 0), part.shape[0] - 1))
            for part in kept
        ],
        out_specs=pl.BlockSpec((1, block, model), lambda j: (0, j, 0)),
        compiler_params=params(),
        cost_estimate=taking(2),
        name="total_grad",
    )(*a, *b, *kept)


def back_kernel(table, model, cut, counts, places, choices, parts, guard, summed, where_ref, *refs):
    keys = [key for choice in choices for key in choice]
    used = sum(counts)
    late = blocks_of(refs[: counts[0]], places[0])
    early = blocks_of(refs[counts[0] : used], places[1])
    number = len(late)
    own_ref, first_ref, rest_ref = refs[used : used + 3]
    weight_refs, used = {}, used + 3
    for key, count in zip(keys, parts):
        weight_refs[key] = refs[used : used + count]
        used += count
    before_ref = refs[used] if summed else None
    outs, sums_ref = refs[-3:-1], refs[-1]
    tokens = late[0].shape[0]
    units = own_ref.shape[1]
    me = where_ref[table["me"]]
    start = late[0].shape[1] - LANES
    eight = lax.broadcasted_iota(jnp.int32, (8, LANES), 1)
    onehot = jnp.where(eight == model % LANES + me, 1.0, 0.0).astype(bf16)
    shards = {key: where_ref[table[("shard",) + key]] for key in keys}
    slots = {key: where_ref[table[("slot",) + key]] for key in keys}
    sums_ref[...] = before_ref[...] if summed else jnp.zeros(sums_ref.shape, f32)

    def whole_weight(key):
        got = weight_refs[key]
        return got[0][...] if len(got) == 1 else jnp.concatenate([got[1][...], got[0][...]], axis=1)

    def work():
        stack, here_valid, here_slot = [], [], []
        for choice in choices:
            weight, valid, slot = whole_weight(choice[0]), shards[choice[0]] >= 0, slots[choice[0]]
            for key in choice[1:]:
                weight = jnp.where(valid, weight, whole_weight(key))
                slot = jnp.where(valid, slot, slots[key])
                valid = jnp.logical_or(valid, shards[key] >= 0)
            stack.append(weight)
            here_valid.append(valid)
            here_slot.append(slot)
        weight = jnp.concatenate(stack, axis=0) if len(stack) > 1 else stack[0]
        for pair in range(0, number, 2):
            both = jnp.concatenate(
                [
                    jnp.concatenate([early[k][...], late[k][:, : model - cut]], axis=1)
                    for k in (pair, pair + 1)
                ],
                axis=0,
            )
            product = dot(weight, both, NT)
            for place in (pair, pair + 1):
                near = place < number // 2
                block = product[:, (place - pair) * tokens : (place - pair + 1) * tokens]
                gate = dot(onehot, late[place][:, start:], NT)[0:1]
                here = pl.ds(place_of(place % (number // 2), number // 2, me, tokens), tokens)
                wide = pl.ds(place_of(place, number // 2, me, tokens), tokens)
                gated = (block * gate).astype(bf16)
                total = jnp.zeros((1, tokens), f32)
                for index, (valid, slot) in enumerate(zip(here_valid, here_slot)):
                    some = slice(index * units, (index + 1) * units)
                    outs[0 if near else 1][index, :, here] = gated[some]
                    if near:
                        hidden = own_ref[slot, :, here].astype(f32)
                    else:
                        hidden = jnp.where(
                            slot == 0,
                            first_ref[0, :, here].astype(f32),
                            rest_ref[jnp.maximum(slot - 1, 0), :, here].astype(f32),
                        )
                    part = jnp.sum(hidden * block[some], axis=0, keepdims=True)
                    total = total + jnp.where(valid, part, 0.0)
                sums_ref[0:1, wide] += total

    if guard:
        pl.when(functools.reduce(jnp.logical_or, [shards[key] >= 0 for key in keys]))(work)
    else:
        work()


def back_part(table, where, late, early, own, first, rest, choices, got, before, guard, after, model):
    units, slots = own.shape[1:]
    arrays, places = zip(late, early)
    counts = [len(part) for part in arrays]
    cut = arrays[1][0].shape[-1]
    keys = [key for choice in choices for key in choice]
    weights = [got[key] for key in keys]
    flat = [part for weight in weights for part in weight]
    half = jax.ShapeDtypeStruct((len(choices), units, slots), bf16)
    summed = before is not None
    operands = [*arrays[0], *arrays[1], own, first, rest, *flat] + ([before] if summed else [])
    outs = [half, half, jax.ShapeDtypeStruct((8, 2 * slots), f32)]
    parts = [len(weight) for weight in weights]
    return pl.pallas_call(
        functools.partial(
            back_kernel, table, model, cut, counts, places, choices, parts, guard, summed
        ),
        out_shape=outs,
        in_specs=[scalars()] + [whole()] * len(operands) + [anywhere()] * len(after),
        out_specs=[whole()] * len(outs),
        compiler_params=params(),
        cost_estimate=taking(6),
        name="back_part",
    )(where, *operands, *after)


def join_kernel(table, choices, where_ref, *refs):
    out_ref, turned, sem = refs[-3:]
    slots, width = turned.shape[1:]
    row = lax.broadcasted_iota(jnp.int32, (slots, slots), 0)
    column = lax.broadcasted_iota(jnp.int32, (slots, slots), 1)
    unit = jnp.where(row == column, 1.0, 0.0).astype(bf16)
    low = where_ref[table["x"]] == 0
    copies = []
    pairs = [
        (refs[2 * group][place], refs[2 * group + 1][place])
        for group in range((len(refs) - 3) // 2)
        for place in range(refs[2 * group].shape[0])
    ]
    for place, (choice, (mine, theirs)) in enumerate(zip(choices, pairs)):
        index = where_ref[table[("shard",) + choice[0]]]
        for key in choice[1:]:
            index = jnp.where(index >= 0, index, where_ref[table[("shard",) + key]])
        both = jnp.concatenate([jnp.where(low, mine, theirs), jnp.where(low, theirs, mine)], axis=0)
        turned[place] = dot(unit, both, NT).astype(bf16)
        here = pl.ds(pl.multiple_of(jnp.maximum(index, 0) * width, LANES), width)
        copy = pltpu.make_async_copy(turned.at[place], out_ref.at[:, here], sem.at[place])
        copies.append((index, copy))
        pl.when(index >= 0)(copy.start)
    for index, copy in copies:
        pl.when(index >= 0)(copy.wait)


def join_hidden(table, where, choices, halves, slots, hidden):
    units = halves[0].shape[1]
    return pl.pallas_call(
        functools.partial(join_kernel, table, choices),
        out_shape=jax.ShapeDtypeStruct((slots, hidden), bf16),
        in_specs=[scalars()] + [whole()] * len(halves),
        out_specs=anywhere(),
        scratch_shapes=[
            pltpu.VMEM((len(choices), slots, 2 * units), bf16),
            pltpu.SemaphoreType.DMA((len(choices),)),
        ],
        compiler_params=params(),
        cost_estimate=taking(2),
        name="join_hidden",
    )(where, *halves)


def logits_kernel(gates_ref, ids_ref, grads_ref, out_ref):
    gates, ids, grads = gates_ref[...], ids_ref[...], grads_ref[...]
    picked = jnp.zeros_like(gates)
    for expert in range(grads.shape[0]):
        picked = picked + jnp.where(ids == expert, grads[expert : expert + 1, :], 0.0)
    out_ref[...] = gates * (picked - jnp.sum(gates * picked, axis=0, keepdims=True))


def logits_grad(gates, ids, grads):
    return pl.pallas_call(
        logits_kernel,
        out_shape=jax.ShapeDtypeStruct(gates.shape, f32),
        in_specs=[whole()] * 3,
        out_specs=whole(),
        compiler_params=params(),
        cost_estimate=taking(1),
        name="logits_grad",
    )(gates, ids, grads)


def per_device_full(grad_out, top_logits, expert_ids, saved_hidden, w_down):
    experts = lax.axis_size("exp")
    groups = lax.axis_size("ctx")
    depth = groups // 2
    tokens, model = grad_out.shape
    slots, hidden = saved_hidden.shape[2:]
    width = pl.cdiv(model + experts, LANES) * LANES
    cut = width // LANES // 2 * LANES

    table, brought, uses = device_scalars(depth, experts)
    where = table.row(lax.axis_index("ctx"), lax.axis_index("exp"))

    def swap(value, x, exp):
        if not exp:
            return lax.ppermute(value, "ctx", [(i, i ^ x) for i in range(groups)])
        if not x:
            return lax.ppermute(value, "exp", [(i, i ^ exp) for i in range(experts)])
        pairs = [(c * experts + e, (c ^ x) * experts + (e ^ exp)) for c in range(groups) for e in range(experts)]
        return lax.ppermute(value, ("ctx", "exp"), pairs)

    def swap_z(value, name, senders=range(depth)):
        first = "AB".index(name)
        pairs = []
        for low in range(first, depth - 1, 2):
            for z, other in ((low, low + 1), (low + 1, low)):
                pairs += [(2 * z + x, 2 * other + x) for x in range(2) if z in senders]
        return lax.ppermute(value, "ctx", pairs)

    got = {(0, "own"): [w_down[0]]}
    for name in "BA":
        got[1, name] = [swap_z(w_down[0], name)]

    late, early, gates = make_rows(grad_out, top_logits, expert_ids, width, cut)
    highs = list(range(2, experts, 2))

    def sides(mine):
        return [mine, swap(mine, 0, 1)]

    late_x = swap(late, 1, 0)
    late_near = [late] + [swap(late, 0, high) for high in highs]
    own, other_first, other_rest = split_hidden(
        table, where, saved_hidden[0, 0], depth, w_down.shape[1], [late]
    )
    other_first = swap(other_first, 1, 0)
    (late_x,) = hold((late_x,), late_near[1:])
    late_mine = late_near + [late_x] + [swap(late_x, 0, high) for high in highs]
    (early,) = hold((early,), [late_x, other_first])
    early_x = swap(early, 1, 0)
    late_rows = sides(pack(late_mine, [early_x]))
    late_rows = (late_rows, [(side, place) for place in range(experts) for side in range(2)])
    early_rows = sides(pack([early, early_x], []))
    places = [(0, 0), (1, 0)]
    for block, base in ((early, 0), (early_x, 1)):
        if base:
            places += [(0, 1), (1, 1)]
        for high in highs:
            places += [(len(early_rows), None), (len(early_rows) + 1, None)]
            early_rows += sides(swap(block, 0, high))
    early_rows = (early_rows, places)
    other_rest = swap(other_rest, 1, 0)

    for name, value in zip("BA", hold([got[1, "B"][0], got[1, "A"][0]], [], FIRST_WEIGHT)):
        got[1, name] = [value]
    chunks = ((late_rows, cut, model - cut), (early_rows, 0, cut))
    after = [early_rows[0][1]]
    first = []
    for rows, start, columns in chunks:
        value = first_sums(
            table, where, rows, late_rows, own, other_first, got[1, "B"][0], model, start, columns, after
        )
        if first:
            (value,) = hold([value], [got[2, "A"][0]], BEGIN_WEIGHT)
            (value,) = hold([value], [other_rest])
        got.setdefault((2, "A"), []).append(swap_z(value, "A"))
        first.append(
            products(table, where, rows, late_rows, own, other_first, 0, model, columns, "first_kept", [value], True)
        )
        after = [first[0]]
    marker = value
    got[2, "B"] = [swap_z(got[1, "A"][0], "B")]

    halves, all_choices, weights_of = [], [], {}
    only_first = max(uses[3, "B"]) <= 0

    def backprop(choices, before, guard, after):
        mine, theirs, sums = back_part(
            table, where, late_rows, early_rows, own, other_first, other_rest, choices,
            {**got, **weights_of}, before, guard, after, model,
        )
        halves.extend([mine, swap(theirs, 1, 0)])
        all_choices.extend(choices)
        return sums

    def pass_on(turn, name, after, chunk=None, waited=()):
        coming = got[turn - 1, "B" if name == "A" else "A"]
        parts, start, chunked = (first, rest), cut, turn == depth and name == "B"
        used = uses[turn, name]
        senders = [z for z in range(depth) if used[z] >= 0] if turn == depth - 1 else range(depth)
        others = [z for z in range(depth) if z not in senders]
        if others and chunk is None and len(coming) == 1:
            weights_of[turn, name] = [swap_z(coming[0], name, others)]
            ends = {0, depth - 1} if name == "A" else set()
            coming = [] if set(senders) <= ends else coming
        if chunk is not None:
            coming, parts, start = [coming[chunk]], (first[chunk:][:1], rest[chunk:][:1]), 0
        weight = LAST_WEIGHT if (turn, name) == (depth, "A") else 1
        values = list(combine(table, where, coming, *parts, turn, name, used, start, after, chunked, weight))
        if waited:
            values[1:] = hold(values[1:], list(waited), 2 * LAST_WEIGHT)
        got.setdefault((turn, name), []).extend(swap_z(value, name, senders) for value in values)
        return values[-1]

    def choices_of(turn):
        both = any(b[turn, "A"] >= 0 and b[turn, "B"] >= 0 for b in brought)
        return [[(turn, "A")], [(turn, "B")]] if both else [[(turn, "A"), (turn, "B")]]

    rest = []
    marker = pass_on(3, "B", [marker], 0) if only_first else marker
    for rows, _, columns in chunks:
        rest.append(
            products(table, where, rows, late_rows, own, other_rest, 1, model, columns, "rest_kept", [marker])
        )
    marker = pass_on(3, "A", rest)
    for chunk in range(2)[only_first:]:
        marker = pass_on(3, "B", [marker], chunk)
    sums = backprop([[(0, "own")], [(1, "A")], [(1, "B")]], None, False, [marker])
    sooner = halves[1::2]
    for turn in range(2, depth):
        choices = choices_of(turn)
        if turn > 2:
            waited = [array for key in ((turn, "A"), (turn, "B")) for array in weights_of.get(key, [])]
            pass_on(turn + 1, "B", [sums, *sooner], waited=waited)
            marker = pass_on(turn + 1, "A", [sums])
        sums = backprop(choices, sums, len(choices) == 1, [marker])
    slot_grad = sums[0:1, :slots] + swap(sums[0:1, slots:], 1, 0)
    grads = lax.all_to_all(
        slot_grad.reshape(experts, tokens), "exp", split_axis=0, concat_axis=0, tiled=True
    )
    logit_grad = logits_grad(gates, expert_ids.T, grads)
    hidden_grad = join_hidden(table, where, all_choices, halves, slots, hidden)
    weight_grad = total_grad(got[depth, "A"], got[depth, "B"], rest, cut)
    return (logit_grad.T, hidden_grad[None, None], weight_grad)


def routing_tables(expert_ids, count_experts, capacity):
    columns = jnp.arange(count_experts, dtype=jnp.int32)
    matches = expert_ids[:, :, None] == columns[None, None, :]
    per_token = jnp.sum(matches.astype(jnp.int32), axis=1)
    rank_table = jnp.cumsum(per_token, axis=0) - per_token
    slot_iota = jnp.arange(capacity, dtype=jnp.int32)
    select = (per_token.T[:, None, :] == 1) & (rank_table.T[:, None, :] == slot_iota[None, :, None])
    return (matches.astype(jnp.float32), select)


def per_device_routed(grad_out, top_logits, expert_ids, saved_hidden, w_down):
    count_experts = lax.axis_size("exp")
    slot_count = saved_hidden.shape[2]
    capacity = slot_count // count_experts
    model_width = grad_out.shape[1]
    onehot, select = routing_tables(expert_ids, count_experts, capacity)
    select_wide = select.astype(jnp.float32)
    gate_probs = jax.nn.softmax(top_logits, axis=-1)
    gate_sent = gate_probs.astype(jnp.bfloat16)
    gate_by_expert = jnp.sum(onehot * gate_sent.astype(jnp.float32)[:, :, None], axis=1)
    send_rows = jnp.einsum(
        "ect,td->ecd", select.astype(jnp.bfloat16), grad_out, preferred_element_type=jnp.float32
    ).astype(jnp.bfloat16)
    send_gate = jnp.sum(select_wide * gate_by_expert.T[:, None, :], axis=2).astype(jnp.bfloat16)
    hidden = saved_hidden[0, 0]
    rows_in, gate_in = (
        lax.all_to_all(send_rows, "exp", split_axis=0, concat_axis=0, tiled=True),
        lax.all_to_all(send_gate, "exp", split_axis=0, concat_axis=0, tiled=True),
    )
    flat_rows = rows_in.reshape(slot_count, model_width)
    backprop = lax.dot_general(
        flat_rows,
        lax.all_gather(w_down[0], "ctx", axis=0, tiled=True),
        (((1,), (1,)), ((), ())),
        preferred_element_type=jnp.float32,
    )
    flat_gate = gate_in.reshape(slot_count, 1).astype(jnp.float32)
    hidden_grad = (flat_gate * backprop).astype(jnp.bfloat16)
    slot_grad = jnp.sum(hidden.astype(jnp.float32) * backprop, axis=1)
    scaled = (flat_gate * flat_rows.astype(jnp.float32)).astype(jnp.bfloat16)
    partial_grad = lax.dot_general(
        hidden, scaled, (((0,), (0,)), ((), ())), preferred_element_type=jnp.float32
    )
    weight_grad = lax.psum_scatter(partial_grad, "ctx", scatter_dimension=0, tiled=True)
    returned = lax.all_to_all(
        slot_grad.reshape(count_experts, capacity), "exp", split_axis=0, concat_axis=0, tiled=True
    )
    grad_by_expert = jnp.sum(select_wide * returned[:, :, None], axis=1)
    gate_grad = jnp.sum(onehot * grad_by_expert.T[:, None, :], axis=2)
    logit_grad = gate_probs * (gate_grad - jnp.sum(gate_probs * gate_grad, axis=1, keepdims=True))
    return (logit_grad, hidden_grad.reshape(1, 1, slot_count, -1), weight_grad[None])


def per_device(grad_out, top_logits, expert_ids, saved_hidden, w_down):
    experts = lax.axis_size("exp")
    groups = lax.axis_size("ctx")
    everywhere = top_logits.shape[1] == experts and saved_hidden.shape[2] == experts * grad_out.shape[0]
    plain = experts & (experts - 1) == 0 and groups % 4 == 0 and groups >= 8
    body = per_device_full if everywhere and plain else per_device_routed
    return body(grad_out, top_logits, expert_ids, saved_hidden, w_down)


def solution(mesh):
    return jax.shard_map(
        per_device,
        mesh=mesh,
        in_specs=(
            P(("ctx", "exp"), None),
            P(("ctx", "exp"), None),
            P(("ctx", "exp"), None),
            P("ctx", "exp", None, None),
            P("exp", "ctx", None),
        ),
        out_specs=(P(("ctx", "exp"), None), P("ctx", "exp", None, None), P("exp", "ctx", None)),
        check_vma=False,
    )
```

```python
import functools

import jax
import jax.numpy as jnp
import numpy as np
from jax import lax
from jax.experimental import pallas as pl
from jax.experimental.pallas import tpu as pltpu
from jax.sharding import PartitionSpec as P

LANES = 128
SCALE = 1_000_000
FIRST_WEIGHT = 12_000
NEXT_WEIGHT = 600
HIDDEN_WEIGHT = 5_000
PASS_WEIGHT = 700
LAST_WEIGHT = 90
NT = (((1,), (1,)), ((), ()))
NN = (((1,), (0,)), ((), ()))
f32 = jnp.float32
bf16 = jnp.bfloat16


def dot(a, b, dims):
    return lax.dot_general(a, b, dims, preferred_element_type=f32)


def anywhere():
    return pl.BlockSpec(memory_space=pl.ANY)


def whole():
    return pl.BlockSpec(memory_space=pltpu.VMEM)


def scalars():
    return pl.BlockSpec(memory_space=pltpu.SMEM)


def params(mib=24):
    return pltpu.CompilerParams(vmem_limit_bytes=mib * 1024 * 1024)


def taking(microseconds):
    return pl.CostEstimate(flops=int(microseconds * SCALE), bytes_accessed=int(microseconds * 3e6), transcendentals=0)


def chain_plan(depth):
    products, weights = [], []
    for z in range(depth):
        uses = []
        for turn in range(2, depth + 1):
            if z < depth - 1 and turn >= z + 2:
                uses.append((turn, "AB"[z % 2], depth + 1 + z - turn))
            if z > 0 and turn >= depth - z + 1:
                uses.append((turn, "BA"[z % 2], z + turn - depth - 1))
        products.append(sorted(uses) + [(depth + 1, "own", z)])
        brought = {}
        for turn in range(1, depth):
            for name in "AB":
                index = z + turn if (name == "A") == (z % 2 == 0) else z - turn
                brought[turn, name] = index if 0 <= index < depth else -1
        weights.append(brought)
    return products, weights


class Scalars:
    def __init__(self):
        self.columns = []
        self.names = {}

    def add(self, name, values):
        self.names[name] = len(self.columns)
        self.columns.append(values)

    def __getitem__(self, name):
        return self.names[name]

    def row(self, place, me):
        return jnp.asarray(np.stack(self.columns, axis=-1).astype(np.int32))[place, me]


def device_scalars(depth, experts):
    products, weights = chain_plan(depth)
    table = Scalars()
    along = np.arange(2 * depth)[:, None] + np.zeros((1, experts), np.int32)

    def by_z(values):
        return np.asarray(values)[along // 2]

    table.add("x", along % 2)
    table.add("me", np.zeros_like(along) + np.arange(experts)[None, :])
    table.add(("shard", 0, "own"), along // 2)
    slot_of = [{use[2]: slot for slot, use in enumerate(products[z])} for z in range(depth)]
    for part in range(depth):
        table.add(("slot of", part), by_z([slot_of[z][part] for z in range(depth)]))
    table.add(("slot", 0, "own"), by_z([slot_of[z][z] for z in range(depth)]))
    for turn in range(1, depth):
        for name in "AB":
            shard = [weights[z][turn, name] for z in range(depth)]
            table.add(("shard", turn, name), by_z(shard))
            table.add(("slot", turn, name), by_z([slot_of[z].get(k, 0) for z, k in enumerate(shard)]))
    uses = {}
    for turn in range(2, depth + 1):
        for name in "AB":
            slots = [-1] * depth
            for z in range(depth):
                for slot, use in enumerate(products[z]):
                    if use[:2] == (turn, name):
                        slots[z] = slot
            uses[turn, name] = slots
            table.add(("use", turn, name), by_z(slots))
            limit = max(depth - 3, 0)
            table.add(("block", turn, name), by_z([min(max(slot - 1, 0), limit) for slot in slots]))
    return table, weights, uses


def rows_kernel(cut, grad_hbm, logits_hbm, ids_hbm, late_ref, early_ref, gates_ref, *scratch):
    grad_ref, logits_ref, ids_ref, sems = scratch
    model, tokens = grad_ref.shape
    copies = [
        pltpu.make_async_copy(source, target, sems.at[place])
        for place, (source, target) in enumerate(
            ((grad_hbm, grad_ref), (logits_hbm, logits_ref), (ids_hbm, ids_ref))
        )
    ]
    for copy in copies:
        copy.start()
    for copy in copies:
        copy.wait()
    count = logits_ref.shape[0]
    width = cut + late_ref.shape[1]
    logits = logits_ref[...]
    powers = jnp.exp(logits - jnp.max(logits, axis=0, keepdims=True))
    gates = powers / jnp.sum(powers, axis=0, keepdims=True)
    gates_ref[...] = gates
    sent = gates.astype(bf16).astype(f32)
    ids = ids_ref[...]
    row = lax.broadcasted_iota(jnp.int32, (width - model, tokens), 0)
    extra = jnp.zeros((width - model, tokens), f32)
    for expert in range(count):
        chosen = jnp.sum(jnp.where(ids == expert, sent, 0.0), axis=0, keepdims=True)
        extra = extra + jnp.where(row == expert, chosen, 0.0)
    for start in range(0, width, LANES):
        stop = start + LANES
        if stop <= model:
            block = grad_ref[start:stop, :].astype(f32)
        elif start >= model:
            block = extra[start - model : stop - model, :]
        else:
            block = jnp.concatenate(
                [grad_ref[start:model, :].astype(f32), extra[: stop - model, :]], axis=0
            )
        turned = block.T.astype(bf16)
        if start < cut:
            early_ref[:, start:stop] = turned
        else:
            late_ref[:, start - cut : stop - cut] = turned


def make_rows(grad_out, top_logits, expert_ids, width, cut):
    tokens, model = grad_out.shape
    count = top_logits.shape[1]
    return pl.pallas_call(
        functools.partial(rows_kernel, cut),
        out_shape=(
            jax.ShapeDtypeStruct((tokens, width - cut), bf16),
            jax.ShapeDtypeStruct((tokens, cut), bf16),
            jax.ShapeDtypeStruct((count, tokens), f32),
        ),
        in_specs=[pl.BlockSpec(memory_space=pltpu.HBM)] * 3,
        out_specs=(whole(),) * 3,
        scratch_shapes=[
            pltpu.VMEM((model, tokens), bf16),
            pltpu.VMEM((count, tokens), f32),
            pltpu.VMEM((count, tokens), jnp.int32),
            pltpu.SemaphoreType.DMA((3,)),
        ],
        compiler_params=params(58),
        cost_estimate=taking(2),
        name="make_rows",
    )(grad_out.T, top_logits.T, expert_ids.T)


def pack_kernel(*refs):
    out_ref, sems = refs[-2:]
    copies = []
    for place in range(out_ref.shape[0]):
        copies.append(pltpu.make_async_copy(refs[place], out_ref.at[place], sems.at[place]))
        copies[-1].start()
    for copy in copies:
        copy.wait()


def pack(values, after):
    number = len(values)
    return pl.pallas_call(
        pack_kernel,
        out_shape=jax.ShapeDtypeStruct((number, *values[0].shape), values[0].dtype),
        in_specs=[anywhere()] * (number + len(after)),
        out_specs=anywhere(),
        scratch_shapes=[pltpu.SemaphoreType.DMA((number,))],
        compiler_params=params(),
        cost_estimate=taking(1),
        name="pack_rows",
    )(*values, *after)


def blocks_of(refs, places):
    return [refs[array] if place is None else refs[array].at[place] for array, place in places]


def hold_kernel(*refs):
    del refs


def hold(values, after, weight=0):
    return pl.pallas_call(
        hold_kernel,
        out_shape=tuple(jax.ShapeDtypeStruct(value.shape, value.dtype) for value in values),
        in_specs=[anywhere()] * (len(values) + len(after)),
        out_specs=(anywhere(),) * len(values),
        input_output_aliases={place: place for place in range(len(values))},
        compiler_params=params(),
        cost_estimate=taking(weight),
        name="hold",
    )(*values, *after)


def split_kernel(table, where_ref, hidden_ref, *refs):
    own_ref, first_ref, rest_ref = refs[-3:]
    parts, units, _ = own_ref.shape
    row = lax.broadcasted_iota(jnp.int32, (2 * units, 2 * units), 0)
    column = lax.broadcasted_iota(jnp.int32, (2 * units, 2 * units), 1)
    unit = jnp.where(row == column, 1.0, 0.0).astype(bf16)
    low = where_ref[table["x"]] == 0
    for part in range(parts):
        block = hidden_ref[:, part * 2 * units : (part + 1) * 2 * units]
        turned = dot(unit, block, NT).astype(bf16)
        slot = where_ref[table["slot of", part]]
        other = jnp.where(low, turned[units:], turned[:units])
        own_ref[slot] = jnp.where(low, turned[:units], turned[units:])

        @pl.when(slot == 0)
        def _():
            first_ref[0] = other

        @pl.when(slot != 0)
        def _():
            rest_ref[slot - 1] = other


def split_hidden(table, where, hidden, parts, units, after):
    slots = hidden.shape[0]
    return pl.pallas_call(
        functools.partial(split_kernel, table),
        out_shape=tuple(
            jax.ShapeDtypeStruct((count, units, slots), bf16) for count in (parts, 1, parts - 1)
        ),
        in_specs=[scalars(), whole()] + [anywhere()] * len(after),
        out_specs=(whole(),) * 3,
        compiler_params=params(),
        cost_estimate=taking(2),
        name="split_hidden",
    )(where, hidden, *after)


def place_of(place, count, me, tokens):
    start = (place // count) * count * tokens + ((place % count) ^ me) * tokens
    return pl.multiple_of(start, tokens)


def scale_rows(table, model, where_ref, rows, gated, scaled):
    tokens = rows[0].shape[0]
    me = where_ref[table["me"]]
    lane = lax.broadcasted_iota(jnp.int32, (tokens, LANES), 1)
    for place, block in enumerate(rows):
        here = pl.ds(place_of(place, len(rows) // 2, me, tokens), tokens)
        tile = gated[place][:, gated[place].shape[1] - LANES :]
        picked = jnp.where(lane == model % LANES + me, tile.astype(f32), 0.0)
        gate = jnp.sum(picked, axis=1, keepdims=True)
        scaled[here, :] = (block[:, : scaled.shape[1]].astype(f32) * gate).astype(bf16)


def products_kernel(table, model, counts, places, shards, skip, ends, where_ref, *refs):
    used = sum(counts)
    rows = blocks_of(refs[: counts[0]], places[0])
    gated = blocks_of(refs[counts[0] : used], places[1])
    own_ref, other_ref = refs[used : used + 2]
    kept_ref, scaled, total_ref, sem = refs[-4:]
    units, slots = own_ref.shape[1:]

    def stacked(ref, offset):
        parts = [ref[offset + shard] for shard in range(shards)]
        return jnp.concatenate(parts, axis=0) if len(parts) > 1 else parts[0]

    @pl.when((where_ref[table["use", 2, "A"]] == 0) == ends)
    def _():
        scale_rows(table, model, where_ref, rows, gated, scaled)
        total = dot(stacked(own_ref, skip), scaled[:slots, :], NN)
        total = total + dot(stacked(other_ref, 0), scaled[slots:, :], NN)
        for shard in range(shards):
            total_ref[shard] = total[shard * units : (shard + 1) * units]
        copy = pltpu.make_async_copy(total_ref, kept_ref, sem)
        copy.start()
        copy.wait()


def products(table, where, rows, gated, own, other, skip, model, width, name, after, ends, before=None):
    arrays, places = zip(rows, gated)
    counts = [len(part) for part in arrays]
    shards, units, slots = other.shape
    kept = jax.ShapeDtypeStruct((shards, units, width), f32)
    operands = [*arrays[0], *arrays[1], own, other]
    extra = ([] if before is None else [before]) + list(after)
    return pl.pallas_call(
        functools.partial(products_kernel, table, model, counts, places, shards, skip, ends),
        out_shape=kept,
        in_specs=[scalars()] + [whole()] * len(operands) + [anywhere()] * len(extra),
        out_specs=anywhere(),
        scratch_shapes=[
            pltpu.VMEM((2 * slots, width), bf16),
            pltpu.VMEM(kept.shape, f32),
            pltpu.SemaphoreType.DMA,
        ],
        input_output_aliases={} if before is None else {1 + len(operands): 0},
        compiler_params=params(),
        cost_estimate=taking(1),
        name=name,
    )(where, *operands, *extra)


def first_kernel(table, model, counts, places, start, where_ref, *refs):
    used = sum(counts)
    rows = blocks_of(refs[: counts[0]], places[0])
    gated = blocks_of(refs[counts[0] : used], places[1])
    own_ref, other_ref, coming_ref = refs[used : used + 3]
    out_ref, scaled = refs[-2:]
    slots = own_ref.shape[2]
    ends = where_ref[table["use", 2, "A"]] == 0

    @pl.when(ends)
    def _():
        scale_rows(table, model, where_ref, rows, gated, scaled)
        total = dot(own_ref[0], scaled[:slots, :], NN)
        out_ref[...] = (total + dot(other_ref[0], scaled[slots:, :], NN)).astype(bf16)

    @pl.when(jnp.logical_not(ends))
    def _():
        out_ref[...] = coming_ref[:, start : start + out_ref.shape[1]]


def first_sums(table, where, rows, gated, own, other, coming, model, start, width, after):
    arrays, places = zip(rows, gated)
    counts = [len(part) for part in arrays]
    units, slots = own.shape[1:]
    return pl.pallas_call(
        functools.partial(first_kernel, table, model, counts, places, start),
        out_shape=jax.ShapeDtypeStruct((units, width), bf16),
        in_specs=[scalars()] + [whole()] * (sum(counts) + 3) + [anywhere()] * len(after),
        out_specs=whole(),
        scratch_shapes=[pltpu.VMEM((2 * slots, width), bf16)],
        compiler_params=params(),
        cost_estimate=taking(1),
        name="first_sums",
    )(where, *arrays[0], *arrays[1], own, other, coming, *after)


def rows_of(units):
    return units // 2 if units % 32 == 0 else units


def column_parts(arrays, cut):
    return [(0, arrays[0])] if len(arrays) == 1 else [(cut, arrays[0]), (0, arrays[1])]


def combine_kernel(table, key, cut, counts, sides, where_ref, *refs):
    slot = where_ref[table[key]]
    coming = refs[: counts[0]]
    outs = refs[len(refs) - counts[2] :]
    model = sum(ref.shape[1] for ref in outs)
    spans = [(cut, model), (0, cut)] if cut else [(0, model)]
    for chunk, (start, stop) in enumerate(spans):
        if counts[0] == 0:
            total = jnp.zeros((outs[0].shape[0], stop - start), f32)
        elif counts[0] == 1:
            total = coming[0][:, start:stop].astype(f32)
        else:
            total = coming[chunk][...].astype(f32)
        for number, side in enumerate(sides):
            flag = slot == 0 if side == "first" else slot > 0
            total = total + jnp.where(flag, refs[counts[0] + len(spans) * number + chunk][0], 0.0)
        total = total.astype(bf16)
        if counts[2] == 1:
            outs[0][:, start:stop] = total
        else:
            outs[chunk][...] = total


def combine(table, where, coming, first, rest, turn, name, used, cut, after, chunked=False, weight=1):
    units = first[0].shape[1]
    model = sum(part.shape[2] for part in first)
    block = rows_of(units)
    column = table["block", turn, name]
    sides, operands, specs = [], [], []
    if any(slot == 0 for slot in used):
        sides.append("first")
        operands += first
        specs += [pl.BlockSpec((1, block, part.shape[2]), lambda j, s: (0, j, 0)) for part in first]
    if any(slot > 0 for slot in used):
        sides.append("rest")
        operands += rest
        specs += [pl.BlockSpec((1, block, part.shape[2]), lambda j, s: (s[column], j, 0)) for part in rest]
    widths = [model - cut, cut] if chunked else [model]
    return pl.pallas_call(
        functools.partial(
            combine_kernel, table, ("use", turn, name), cut, (len(coming), len(operands), len(widths)), sides
        ),
        out_shape=[jax.ShapeDtypeStruct((units, count), bf16) for count in widths],
        grid_spec=pltpu.PrefetchScalarGridSpec(
            num_scalar_prefetch=1,
            grid=(units // block,),
            in_specs=[pl.BlockSpec((block, part.shape[1]), lambda j, s: (j, 0)) for part in coming]
            + specs
            + [anywhere()] * len(after),
            out_specs=[pl.BlockSpec((block, count), lambda j, s: (j, 0)) for count in widths],
        ),
        compiler_params=params(),
        cost_estimate=taking(weight),
        name="combine",
    )(where, *coming, *operands, *after)


def total_kernel(cut, counts, *refs):
    coming = [refs[: counts[0]], refs[counts[0] : sum(counts)]]
    out_ref = refs[-1]
    for chunk, start in enumerate((cut, 0)):
        kept_ref = refs[sum(counts) + chunk]
        here = slice(start, start + kept_ref.shape[2])
        total = kept_ref[0]
        for parts in coming:
            total = total + (parts[0][:, here] if len(parts) == 1 else parts[chunk][...]).astype(f32)
        out_ref[0, :, here] = total


def total_grad(a, b, kept, cut):
    units = a[0].shape[0]
    model = sum(part.shape[1] for part in a)
    block = rows_of(units)
    return pl.pallas_call(
        functools.partial(total_kernel, cut, (len(a), len(b))),
        out_shape=jax.ShapeDtypeStruct((1, units, model), f32),
        grid=(units // block,),
        in_specs=[pl.BlockSpec((block, part.shape[1]), lambda j: (j, 0)) for part in (*a, *b)]
        + [
            pl.BlockSpec((1, block, part.shape[2]), functools.partial(lambda last, j: (last, j, 0), part.shape[0] - 1))
            for part in kept
        ],
        out_specs=pl.BlockSpec((1, block, model), lambda j: (0, j, 0)),
        compiler_params=params(),
        cost_estimate=taking(2),
        name="total_grad",
    )(*a, *b, *kept)


def back_kernel(table, model, cut, counts, places, choices, parts, guard, summed, where_ref, *refs):
    keys = [key for choice in choices for key in choice]
    used = sum(counts)
    late = blocks_of(refs[: counts[0]], places[0])
    early = blocks_of(refs[counts[0] : used], places[1])
    number = len(late)
    own_ref, first_ref, rest_ref = refs[used : used + 3]
    weight_refs, used = {}, used + 3
    for key, count in zip(keys, parts):
        weight_refs[key] = refs[used : used + count]
        used += count
    before_ref = refs[used] if summed else None
    outs, sums_ref = refs[-3:-1], refs[-1]
    tokens = late[0].shape[0]
    units = own_ref.shape[1]
    me = where_ref[table["me"]]
    start = late[0].shape[1] - LANES
    eight = lax.broadcasted_iota(jnp.int32, (8, LANES), 1)
    onehot = jnp.where(eight == model % LANES + me, 1.0, 0.0).astype(bf16)
    shards = {key: where_ref[table[("shard",) + key]] for key in keys}
    slots = {key: where_ref[table[("slot",) + key]] for key in keys}
    sums_ref[...] = before_ref[...] if summed else jnp.zeros(sums_ref.shape, f32)

    def whole_weight(key):
        got = weight_refs[key]
        return got[0][...] if len(got) == 1 else jnp.concatenate([got[1][...], got[0][...]], axis=1)

    def work():
        stack, here_valid, here_slot = [], [], []
        for choice in choices:
            weight, valid, slot = whole_weight(choice[0]), shards[choice[0]] >= 0, slots[choice[0]]
            for key in choice[1:]:
                weight = jnp.where(valid, weight, whole_weight(key))
                slot = jnp.where(valid, slot, slots[key])
                valid = jnp.logical_or(valid, shards[key] >= 0)
            stack.append(weight)
            here_valid.append(valid)
            here_slot.append(slot)
        weight = jnp.concatenate(stack, axis=0) if len(stack) > 1 else stack[0]
        for pair in range(0, number, 2):
            both = jnp.concatenate(
                [
                    jnp.concatenate([early[k][...], late[k][:, : model - cut]], axis=1)
                    for k in (pair, pair + 1)
                ],
                axis=0,
            )
            product = dot(weight, both, NT)
            for place in (pair, pair + 1):
                near = place < number // 2
                block = product[:, (place - pair) * tokens : (place - pair + 1) * tokens]
                gate = dot(onehot, late[place][:, start:], NT)[0:1]
                here = pl.ds(place_of(place % (number // 2), number // 2, me, tokens), tokens)
                wide = pl.ds(place_of(place, number // 2, me, tokens), tokens)
                gated = (block * gate).astype(bf16)
                total = jnp.zeros((1, tokens), f32)
                for index, (valid, slot) in enumerate(zip(here_valid, here_slot)):
                    some = slice(index * units, (index + 1) * units)
                    outs[0 if near else 1][index, :, here] = gated[some]
                    if near:
                        hidden = own_ref[slot, :, here].astype(f32)
                    else:
                        hidden = jnp.where(
                            slot == 0,
                            first_ref[0, :, here].astype(f32),
                            rest_ref[jnp.maximum(slot - 1, 0), :, here].astype(f32),
                        )
                    part = jnp.sum(hidden * block[some], axis=0, keepdims=True)
                    total = total + jnp.where(valid, part, 0.0)
                sums_ref[0:1, wide] += total

    if guard:
        pl.when(functools.reduce(jnp.logical_or, [shards[key] >= 0 for key in keys]))(work)
    else:
        work()


def back_part(table, where, late, early, own, first, rest, choices, got, before, guard, after, model):
    units, slots = own.shape[1:]
    arrays, places = zip(late, early)
    counts = [len(part) for part in arrays]
    cut = arrays[1][0].shape[-1]
    keys = [key for choice in choices for key in choice]
    weights = [got[key] for key in keys]
    flat = [part for weight in weights for part in weight]
    half = jax.ShapeDtypeStruct((len(choices), units, slots), bf16)
    summed = before is not None
    operands = [*arrays[0], *arrays[1], own, first, rest, *flat] + ([before] if summed else [])
    outs = [half, half, jax.ShapeDtypeStruct((8, 2 * slots), f32)]
    parts = [len(weight) for weight in weights]
    return pl.pallas_call(
        functools.partial(
            back_kernel, table, model, cut, counts, places, choices, parts, guard, summed
        ),
        out_shape=outs,
        in_specs=[scalars()] + [whole()] * len(operands) + [anywhere()] * len(after),
        out_specs=[whole()] * len(outs),
        compiler_params=params(),
        cost_estimate=taking(6),
        name="back_part",
    )(where, *operands, *after)


def join_kernel(table, choices, where_ref, *refs):
    out_ref, turned, sem = refs[-3:]
    slots, width = turned.shape[1:]
    row = lax.broadcasted_iota(jnp.int32, (slots, slots), 0)
    column = lax.broadcasted_iota(jnp.int32, (slots, slots), 1)
    unit = jnp.where(row == column, 1.0, 0.0).astype(bf16)
    low = where_ref[table["x"]] == 0
    copies = []
    pairs = [
        (refs[2 * group][place], refs[2 * group + 1][place])
        for group in range((len(refs) - 3) // 2)
        for place in range(refs[2 * group].shape[0])
    ]
    for place, (choice, (mine, theirs)) in enumerate(zip(choices, pairs)):
        index = where_ref[table[("shard",) + choice[0]]]
        for key in choice[1:]:
            index = jnp.where(index >= 0, index, where_ref[table[("shard",) + key]])
        both = jnp.concatenate([jnp.where(low, mine, theirs), jnp.where(low, theirs, mine)], axis=0)
        turned[place] = dot(unit, both, NT).astype(bf16)
        here = pl.ds(pl.multiple_of(jnp.maximum(index, 0) * width, LANES), width)
        copy = pltpu.make_async_copy(turned.at[place], out_ref.at[:, here], sem.at[place])
        copies.append((index, copy))
        pl.when(index >= 0)(copy.start)
    for index, copy in copies:
        pl.when(index >= 0)(copy.wait)


def join_hidden(table, where, choices, halves, slots, hidden):
    units = halves[0].shape[1]
    return pl.pallas_call(
        functools.partial(join_kernel, table, choices),
        out_shape=jax.ShapeDtypeStruct((slots, hidden), bf16),
        in_specs=[scalars()] + [whole()] * len(halves),
        out_specs=anywhere(),
        scratch_shapes=[
            pltpu.VMEM((len(choices), slots, 2 * units), bf16),
            pltpu.SemaphoreType.DMA((len(choices),)),
        ],
        compiler_params=params(),
        cost_estimate=taking(2),
        name="join_hidden",
    )(where, *halves)


def logits_kernel(gates_ref, ids_ref, grads_ref, out_ref):
    gates, ids, grads = gates_ref[...], ids_ref[...], grads_ref[...]
    picked = jnp.zeros_like(gates)
    for expert in range(grads.shape[0]):
        picked = picked + jnp.where(ids == expert, grads[expert : expert + 1, :], 0.0)
    out_ref[...] = gates * (picked - jnp.sum(gates * picked, axis=0, keepdims=True))


def logits_grad(gates, ids, grads):
    return pl.pallas_call(
        logits_kernel,
        out_shape=jax.ShapeDtypeStruct(gates.shape, f32),
        in_specs=[whole()] * 3,
        out_specs=whole(),
        compiler_params=params(),
        cost_estimate=taking(1),
        name="logits_grad",
    )(gates, ids, grads)


def per_device_full(grad_out, top_logits, expert_ids, saved_hidden, w_down):
    experts = lax.axis_size("exp")
    groups = lax.axis_size("ctx")
    depth = groups // 2
    tokens, model = grad_out.shape
    slots, hidden = saved_hidden.shape[2:]
    width = pl.cdiv(model + experts, LANES) * LANES
    cut = width // LANES // 2 * LANES

    table, brought, uses = device_scalars(depth, experts)
    where = table.row(lax.axis_index("ctx"), lax.axis_index("exp"))

    def swap(value, x, exp):
        if not exp:
            return lax.ppermute(value, "ctx", [(i, i ^ x) for i in range(groups)])
        if not x:
            return lax.ppermute(value, "exp", [(i, i ^ exp) for i in range(experts)])
        pairs = [(c * experts + e, (c ^ x) * experts + (e ^ exp)) for c in range(groups) for e in range(experts)]
        return lax.ppermute(value, ("ctx", "exp"), pairs)

    def swap_z(value, name, senders=range(depth)):
        first = "AB".index(name)
        pairs = []
        for low in range(first, depth - 1, 2):
            for z, other in ((low, low + 1), (low + 1, low)):
                pairs += [(2 * z + x, 2 * other + x) for x in range(2) if z in senders]
        return lax.ppermute(value, "ctx", pairs)

    got = {(0, "own"): [w_down[0]]}
    for name in "BA":
        got[1, name] = [swap_z(w_down[0], name)]

    late, early, gates = make_rows(grad_out, top_logits, expert_ids, width, cut)
    highs = list(range(2, experts, 2))

    def sides(mine):
        return [mine, swap(mine, 0, 1)]

    late_x = swap(late, 1, 0)
    late_near = [late] + [swap(late, 0, high) for high in highs]
    own, other_first, other_rest = split_hidden(
        table, where, saved_hidden[0, 0], depth, w_down.shape[1], [late]
    )
    other_first = swap(other_first, 1, 0)
    (late_x,) = hold((late_x,), late_near[1:])
    late_mine = late_near + [late_x] + [swap(late_x, 0, high) for high in highs]
    (early,) = hold((early,), [late_x, other_first])
    early_x = swap(early, 1, 0)
    late_rows = sides(pack(late_mine, [early_x]))
    late_rows = (late_rows, [(side, place) for place in range(experts) for side in range(2)])
    early_rows = sides(pack([early, early_x], []))
    places = [(0, 0), (1, 0)]
    for block, base in ((early, 0), (early_x, 1)):
        if base:
            places += [(0, 1), (1, 1)]
        for high in highs:
            places += [(len(early_rows), None), (len(early_rows) + 1, None)]
            early_rows += sides(swap(block, 0, high))
    early_rows = (early_rows, places)
    other_rest = swap(other_rest, 1, 0)

    got[1, "B"] = list(hold(got[1, "B"], got[1, "A"], FIRST_WEIGHT))
    chunks = ((late_rows, cut, model - cut), (early_rows, 0, cut))
    after = [early_rows[0][1]]
    first = []
    for rows, start, columns in chunks:
        value = first_sums(
            table, where, rows, late_rows, own, other_first, got[1, "B"][0], model, start, columns, after
        )
        if first:
            (value,) = hold([value], got[2, "A"], NEXT_WEIGHT)
        got.setdefault((2, "A"), []).append(swap_z(value, "A"))
        first.append(
            products(
                table, where, rows, late_rows, own, other_first, 0, model, columns, "first_kept", [value], False
            )
        )
        after = [first[0]]
    marker = value
    got[2, "B"] = [swap_z(got[1, "A"][0], "B")]
    (other_rest,) = hold([other_rest], [], HIDDEN_WEIGHT)

    halves, all_choices, weights_of = [], [], {}
    only_first = max(uses[3, "B"]) <= 0

    def backprop(choices, before, guard, after):
        mine, theirs, sums = back_part(
            table, where, late_rows, early_rows, own, other_first, other_rest, choices,
            {**got, **weights_of}, before, guard, after, model,
        )
        halves.extend([mine, swap(theirs, 1, 0)])
        all_choices.extend(choices)
        return sums

    def pass_on(turn, name, after, chunk=None, waited=()):
        coming = got[turn - 1, "B" if name == "A" else "A"]
        parts, start, chunked = (first, rest), cut, turn == depth and name == "B"
        used = uses[turn, name]
        senders = [z for z in range(depth) if used[z] >= 0] if turn == depth - 1 else range(depth)
        others = [z for z in range(depth) if z not in senders]
        if others and chunk is None and len(coming) == 1:
            coming[:] = hold(coming, [], PASS_WEIGHT)
            weights_of[turn, name] = [swap_z(coming[0], name, others)]
            ends = {0, depth - 1} if name == "A" else set()
            coming = [] if set(senders) <= ends else coming
        if chunk is not None:
            coming, parts, start = [coming[chunk]], (first[chunk:][:1], rest[chunk:][:1]), 0
        weight = LAST_WEIGHT if (turn, name) == (depth, "A") else 1
        values = list(combine(table, where, coming, *parts, turn, name, used, start, after, chunked, weight))
        if waited:
            values[1:] = hold(values[1:], list(waited), 2 * LAST_WEIGHT)
        got.setdefault((turn, name), []).extend(swap_z(value, name, senders) for value in values)
        return values[-1]

    def choices_of(turn):
        both = any(b[turn, "A"] >= 0 and b[turn, "B"] >= 0 for b in brought)
        return [[(turn, "A")], [(turn, "B")]] if both else [[(turn, "A"), (turn, "B")]]

    rest = []
    marker = pass_on(3, "B", [marker], 0) if only_first else marker
    for rows, _, columns in chunks:
        rest.append(
            products(
                table, where, rows, late_rows, own, other_rest, 1, model, columns, "rest_kept", [marker], True
            )
        )
    marker = pass_on(3, "A", rest)
    for chunk in range(2)[only_first:]:
        marker = pass_on(3, "B", [marker], chunk)
    rest[:] = [
        products(
            table, where, rows, late_rows, own, other_rest, 1, model, columns, "rest_kept", [marker], False, before
        )
        for (rows, _, columns), before in zip(chunks, rest)
    ]
    marker = rest[1]
    sums = backprop([[(0, "own")], [(1, "A")], [(1, "B")]], None, False, [marker])
    sooner = halves[1::2]
    for turn in range(2, depth):
        choices = choices_of(turn)
        if turn > 2:
            waited = [array for key in ((turn, "A"), (turn, "B")) for array in weights_of.get(key, [])]
            pass_on(turn + 1, "B", [sums, *sooner], waited=waited)
            marker = pass_on(turn + 1, "A", [sums])
        sums = backprop(choices, sums, len(choices) == 1, [marker])
    slot_grad = sums[0:1, :slots] + swap(sums[0:1, slots:], 1, 0)
    grads = lax.all_to_all(
        slot_grad.reshape(experts, tokens), "exp", split_axis=0, concat_axis=0, tiled=True
    )
    logit_grad = logits_grad(gates, expert_ids.T, grads)
    hidden_grad = join_hidden(table, where, all_choices, halves, slots, hidden)
    weight_grad = total_grad(got[depth, "A"], got[depth, "B"], rest, cut)
    return (logit_grad.T, hidden_grad[None, None], weight_grad)


def routing_tables(expert_ids, count_experts, capacity):
    columns = jnp.arange(count_experts, dtype=jnp.int32)
    matches = expert_ids[:, :, None] == columns[None, None, :]
    per_token = jnp.sum(matches.astype(jnp.int32), axis=1)
    rank_table = jnp.cumsum(per_token, axis=0) - per_token
    slot_iota = jnp.arange(capacity, dtype=jnp.int32)
    select = (per_token.T[:, None, :] == 1) & (rank_table.T[:, None, :] == slot_iota[None, :, None])
    return (matches.astype(jnp.float32), select)


def per_device_routed(grad_out, top_logits, expert_ids, saved_hidden, w_down):
    count_experts = lax.axis_size("exp")
    slot_count = saved_hidden.shape[2]
    capacity = slot_count // count_experts
    model_width = grad_out.shape[1]
    onehot, select = routing_tables(expert_ids, count_experts, capacity)
    select_wide = select.astype(jnp.float32)
    gate_probs = jax.nn.softmax(top_logits, axis=-1)
    gate_sent = gate_probs.astype(jnp.bfloat16)
    gate_by_expert = jnp.sum(onehot * gate_sent.astype(jnp.float32)[:, :, None], axis=1)
    send_rows = jnp.einsum(
        "ect,td->ecd", select.astype(jnp.bfloat16), grad_out, preferred_element_type=jnp.float32
    ).astype(jnp.bfloat16)
    send_gate = jnp.sum(select_wide * gate_by_expert.T[:, None, :], axis=2).astype(jnp.bfloat16)
    hidden = saved_hidden[0, 0]
    rows_in, gate_in = (
        lax.all_to_all(send_rows, "exp", split_axis=0, concat_axis=0, tiled=True),
        lax.all_to_all(send_gate, "exp", split_axis=0, concat_axis=0, tiled=True),
    )
    flat_rows = rows_in.reshape(slot_count, model_width)
    backprop = lax.dot_general(
        flat_rows,
        lax.all_gather(w_down[0], "ctx", axis=0, tiled=True),
        (((1,), (1,)), ((), ())),
        preferred_element_type=jnp.float32,
    )
    flat_gate = gate_in.reshape(slot_count, 1).astype(jnp.float32)
    hidden_grad = (flat_gate * backprop).astype(jnp.bfloat16)
    slot_grad = jnp.sum(hidden.astype(jnp.float32) * backprop, axis=1)
    scaled = (flat_gate * flat_rows.astype(jnp.float32)).astype(jnp.bfloat16)
    partial_grad = lax.dot_general(
        hidden, scaled, (((0,), (0,)), ((), ())), preferred_element_type=jnp.float32
    )
    weight_grad = lax.psum_scatter(partial_grad, "ctx", scatter_dimension=0, tiled=True)
    returned = lax.all_to_all(
        slot_grad.reshape(count_experts, capacity), "exp", split_axis=0, concat_axis=0, tiled=True
    )
    grad_by_expert = jnp.sum(select_wide * returned[:, :, None], axis=1)
    gate_grad = jnp.sum(onehot * grad_by_expert.T[:, None, :], axis=2)
    logit_grad = gate_probs * (gate_grad - jnp.sum(gate_probs * gate_grad, axis=1, keepdims=True))
    return (logit_grad, hidden_grad.reshape(1, 1, slot_count, -1), weight_grad[None])


def per_device(grad_out, top_logits, expert_ids, saved_hidden, w_down):
    experts = lax.axis_size("exp")
    groups = lax.axis_size("ctx")
    everywhere = top_logits.shape[1] == experts and saved_hidden.shape[2] == experts * grad_out.shape[0]
    plain = experts & (experts - 1) == 0 and groups % 4 == 0 and groups >= 8
    body = per_device_full if everywhere and plain else per_device_routed
    return body(grad_out, top_logits, expert_ids, saved_hidden, w_down)


def solution(mesh):
    return jax.shard_map(
        per_device,
        mesh=mesh,
        in_specs=(
            P(("ctx", "exp"), None),
            P(("ctx", "exp"), None),
            P(("ctx", "exp"), None),
            P("ctx", "exp", None, None),
            P("exp", "ctx", None),
        ),
        out_specs=(P(("ctx", "exp"), None), P("ctx", "exp", None, None), P("exp", "ctx", None)),
        check_vma=False,
    )
```

```python
import functools

import jax
import jax.numpy as jnp
import numpy as np
from jax import lax
from jax.experimental import pallas as pl
from jax.experimental.pallas import tpu as pltpu
from jax.sharding import PartitionSpec as P

LANES = 128
SCALE = 1_000_000
FIRST_WEIGHT = 12_000
NEXT_WEIGHT = 600
HIDDEN_WEIGHT = 5_000
PASS_WEIGHT = 1
WAITED_WEIGHT = 210
ENTER_WEIGHT = 575
LEAVE_WEIGHT = 5_300
LAST_WEIGHT = 90
NT = (((1,), (1,)), ((), ()))
NN = (((1,), (0,)), ((), ()))
f32 = jnp.float32
bf16 = jnp.bfloat16


def dot(a, b, dims):
    return lax.dot_general(a, b, dims, preferred_element_type=f32)


def anywhere():
    return pl.BlockSpec(memory_space=pl.ANY)


def whole():
    return pl.BlockSpec(memory_space=pltpu.VMEM)


def scalars():
    return pl.BlockSpec(memory_space=pltpu.SMEM)


def params(mib=24):
    return pltpu.CompilerParams(vmem_limit_bytes=mib * 1024 * 1024)


def taking(microseconds):
    return pl.CostEstimate(flops=int(microseconds * SCALE), bytes_accessed=int(microseconds * 3e6), transcendentals=0)


def chain_plan(depth):
    products, weights = [], []
    for z in range(depth):
        uses = []
        for turn in range(2, depth + 1):
            if z < depth - 1 and turn >= z + 2:
                uses.append((turn, "AB"[z % 2], depth + 1 + z - turn))
            if z > 0 and turn >= depth - z + 1:
                uses.append((turn, "BA"[z % 2], z + turn - depth - 1))
        products.append(sorted(uses) + [(depth + 1, "own", z)])
        brought = {}
        for turn in range(1, depth):
            for name in "AB":
                index = z + turn if (name == "A") == (z % 2 == 0) else z - turn
                brought[turn, name] = index if 0 <= index < depth else -1
        weights.append(brought)
    return products, weights


class Scalars:
    def __init__(self):
        self.columns = []
        self.names = {}

    def add(self, name, values):
        self.names[name] = len(self.columns)
        self.columns.append(values)

    def __getitem__(self, name):
        return self.names[name]

    def row(self, place, me):
        return jnp.asarray(np.stack(self.columns, axis=-1).astype(np.int32))[place, me]


def device_scalars(depth, experts):
    products, weights = chain_plan(depth)
    table = Scalars()
    along = np.arange(2 * depth)[:, None] + np.zeros((1, experts), np.int32)

    def by_z(values):
        return np.asarray(values)[along // 2]

    table.add("x", along % 2)
    table.add("me", np.zeros_like(along) + np.arange(experts)[None, :])
    table.add(("shard", 0, "own"), along // 2)
    slot_of = [{use[2]: slot for slot, use in enumerate(products[z])} for z in range(depth)]
    for part in range(depth):
        table.add(("slot of", part), by_z([slot_of[z][part] for z in range(depth)]))
    table.add(("slot", 0, "own"), by_z([slot_of[z][z] for z in range(depth)]))
    for turn in range(1, depth):
        for name in "AB":
            shard = [weights[z][turn, name] for z in range(depth)]
            table.add(("shard", turn, name), by_z(shard))
            table.add(("slot", turn, name), by_z([slot_of[z].get(k, 0) for z, k in enumerate(shard)]))
    uses = {}
    for turn in range(2, depth + 1):
        for name in "AB":
            slots = [-1] * depth
            for z in range(depth):
                for slot, use in enumerate(products[z]):
                    if use[:2] == (turn, name):
                        slots[z] = slot
            uses[turn, name] = slots
            table.add(("use", turn, name), by_z(slots))
            limit = max(depth - 3, 0)
            table.add(("block", turn, name), by_z([min(max(slot - 1, 0), limit) for slot in slots]))
    return table, weights, uses


def rows_kernel(cut, grad_hbm, logits_hbm, ids_hbm, late_ref, early_ref, gates_ref, *scratch):
    grad_ref, logits_ref, ids_ref, sems = scratch
    model, tokens = grad_ref.shape
    copies = [
        pltpu.make_async_copy(source, target, sems.at[place])
        for place, (source, target) in enumerate(
            ((grad_hbm, grad_ref), (logits_hbm, logits_ref), (ids_hbm, ids_ref))
        )
    ]
    for copy in copies:
        copy.start()
    for copy in copies:
        copy.wait()
    count = logits_ref.shape[0]
    width = cut + late_ref.shape[1]
    logits = logits_ref[...]
    powers = jnp.exp(logits - jnp.max(logits, axis=0, keepdims=True))
    gates = powers / jnp.sum(powers, axis=0, keepdims=True)
    gates_ref[...] = gates
    sent = gates.astype(bf16).astype(f32)
    ids = ids_ref[...]
    row = lax.broadcasted_iota(jnp.int32, (width - model, tokens), 0)
    extra = jnp.zeros((width - model, tokens), f32)
    for expert in range(count):
        chosen = jnp.sum(jnp.where(ids == expert, sent, 0.0), axis=0, keepdims=True)
        extra = extra + jnp.where(row == expert, chosen, 0.0)
    for start in range(0, width, LANES):
        stop = start + LANES
        if stop <= model:
            block = grad_ref[start:stop, :].astype(f32)
        elif start >= model:
            block = extra[start - model : stop - model, :]
        else:
            block = jnp.concatenate(
                [grad_ref[start:model, :].astype(f32), extra[: stop - model, :]], axis=0
            )
        turned = block.T.astype(bf16)
        if start < cut:
            early_ref[:, start:stop] = turned
        else:
            late_ref[:, start - cut : stop - cut] = turned


def make_rows(grad_out, top_logits, expert_ids, width, cut):
    tokens, model = grad_out.shape
    count = top_logits.shape[1]
    return pl.pallas_call(
        functools.partial(rows_kernel, cut),
        out_shape=(
            jax.ShapeDtypeStruct((tokens, width - cut), bf16),
            jax.ShapeDtypeStruct((tokens, cut), bf16),
            jax.ShapeDtypeStruct((count, tokens), f32),
        ),
        in_specs=[pl.BlockSpec(memory_space=pltpu.HBM)] * 3,
        out_specs=(whole(),) * 3,
        scratch_shapes=[
            pltpu.VMEM((model, tokens), bf16),
            pltpu.VMEM((count, tokens), f32),
            pltpu.VMEM((count, tokens), jnp.int32),
            pltpu.SemaphoreType.DMA((3,)),
        ],
        compiler_params=params(58),
        cost_estimate=taking(2),
        name="make_rows",
    )(grad_out.T, top_logits.T, expert_ids.T)


def pack_kernel(*refs):
    out_ref, sems = refs[-2:]
    copies = []
    for place in range(out_ref.shape[0]):
        copies.append(pltpu.make_async_copy(refs[place], out_ref.at[place], sems.at[place]))
        copies[-1].start()
    for copy in copies:
        copy.wait()


def pack(values, after):
    number = len(values)
    return pl.pallas_call(
        pack_kernel,
        out_shape=jax.ShapeDtypeStruct((number, *values[0].shape), values[0].dtype),
        in_specs=[anywhere()] * (number + len(after)),
        out_specs=anywhere(),
        scratch_shapes=[pltpu.SemaphoreType.DMA((number,))],
        compiler_params=params(),
        cost_estimate=taking(1),
        name="pack_rows",
    )(*values, *after)


def blocks_of(refs, places):
    return [refs[array] if place is None else refs[array].at[place] for array, place in places]


def hold_kernel(*refs):
    del refs


def hold(values, after, weight=0):
    return pl.pallas_call(
        hold_kernel,
        out_shape=tuple(jax.ShapeDtypeStruct(value.shape, value.dtype) for value in values),
        in_specs=[anywhere()] * (len(values) + len(after)),
        out_specs=(anywhere(),) * len(values),
        input_output_aliases={place: place for place in range(len(values))},
        compiler_params=params(),
        cost_estimate=taking(weight),
        name="hold",
    )(*values, *after)


def split_kernel(table, where_ref, hidden_ref, *refs):
    own_ref, first_ref, rest_ref = refs[-3:]
    parts, units, _ = own_ref.shape
    row = lax.broadcasted_iota(jnp.int32, (2 * units, 2 * units), 0)
    column = lax.broadcasted_iota(jnp.int32, (2 * units, 2 * units), 1)
    unit = jnp.where(row == column, 1.0, 0.0).astype(bf16)
    low = where_ref[table["x"]] == 0
    for part in range(parts):
        block = hidden_ref[:, part * 2 * units : (part + 1) * 2 * units]
        turned = dot(unit, block, NT).astype(bf16)
        slot = where_ref[table["slot of", part]]
        other = jnp.where(low, turned[units:], turned[:units])
        own_ref[slot] = jnp.where(low, turned[:units], turned[units:])

        @pl.when(slot == 0)
        def _():
            first_ref[0] = other

        @pl.when(slot != 0)
        def _():
            rest_ref[slot - 1] = other


def split_hidden(table, where, hidden, parts, units, after):
    slots = hidden.shape[0]
    return pl.pallas_call(
        functools.partial(split_kernel, table),
        out_shape=tuple(
            jax.ShapeDtypeStruct((count, units, slots), bf16) for count in (parts, 1, parts - 1)
        ),
        in_specs=[scalars(), whole()] + [anywhere()] * len(after),
        out_specs=(whole(),) * 3,
        compiler_params=params(),
        cost_estimate=taking(2),
        name="split_hidden",
    )(where, hidden, *after)


def place_of(place, count, me, tokens):
    start = (place // count) * count * tokens + ((place % count) ^ me) * tokens
    return pl.multiple_of(start, tokens)


def scale_rows(table, model, where_ref, rows, gated, scaled):
    tokens = rows[0].shape[0]
    me = where_ref[table["me"]]
    lane = lax.broadcasted_iota(jnp.int32, (tokens, LANES), 1)
    for place, block in enumerate(rows):
        here = pl.ds(place_of(place, len(rows) // 2, me, tokens), tokens)
        tile = gated[place][:, gated[place].shape[1] - LANES :]
        picked = jnp.where(lane == model % LANES + me, tile.astype(f32), 0.0)
        gate = jnp.sum(picked, axis=1, keepdims=True)
        scaled[here, :] = (block[:, : scaled.shape[1]].astype(f32) * gate).astype(bf16)


def products_kernel(table, model, counts, places, shards, skip, middle, where_ref, *refs):
    used = sum(counts)
    rows = blocks_of(refs[: counts[0]], places[0])
    gated = blocks_of(refs[counts[0] : used], places[1])
    own_ref, other_ref = refs[used : used + 2]
    kept_ref, scaled = refs[-2:]
    units, slots = own_ref.shape[1:]

    def stacked(ref, offset):
        parts = [ref[offset + shard] for shard in range(shards)]
        return jnp.concatenate(parts, axis=0) if len(parts) > 1 else parts[0]

    def work():
        scale_rows(table, model, where_ref, rows, gated, scaled)
        total = dot(stacked(own_ref, skip), scaled[:slots, :], NN)
        total = total + dot(stacked(other_ref, 0), scaled[slots:, :], NN)
        for shard in range(shards):
            kept_ref[shard] = total[shard * units : (shard + 1) * units]

    if middle:
        pl.when(where_ref[table["use", 2, "A"]] != 0)(work)
    else:
        work()


def products(table, where, rows, gated, own, other, skip, model, width, name, after, middle=False):
    arrays, places = zip(rows, gated)
    counts = [len(part) for part in arrays]
    shards, units, slots = other.shape
    kept = jax.ShapeDtypeStruct((shards, units, width), f32)
    operands = [*arrays[0], *arrays[1], own, other]
    return pl.pallas_call(
        functools.partial(products_kernel, table, model, counts, places, shards, skip, middle),
        out_shape=kept,
        in_specs=[scalars()] + [whole()] * len(operands) + [anywhere()] * len(after),
        out_specs=whole(),
        scratch_shapes=[pltpu.VMEM((2 * slots, width), bf16)],
        compiler_params=params(),
        cost_estimate=taking(1),
        name=name,
    )(where, *operands, *after)


def first_kernel(table, model, counts, places, start, where_ref, *refs):
    used = sum(counts)
    rows = blocks_of(refs[: counts[0]], places[0])
    gated = blocks_of(refs[counts[0] : used], places[1])
    own_ref, other_ref, coming_ref = refs[used : used + 3]
    out_ref, scaled = refs[-2:]
    slots = own_ref.shape[2]
    ends = where_ref[table["use", 2, "A"]] == 0

    @pl.when(ends)
    def _():
        scale_rows(table, model, where_ref, rows, gated, scaled)
        total = dot(own_ref[0], scaled[:slots, :], NN)
        out_ref[...] = (total + dot(other_ref[0], scaled[slots:, :], NN)).astype(bf16)

    @pl.when(jnp.logical_not(ends))
    def _():
        out_ref[...] = coming_ref[:, start : start + out_ref.shape[1]]


def first_sums(table, where, rows, gated, own, other, coming, model, start, width, after):
    arrays, places = zip(rows, gated)
    counts = [len(part) for part in arrays]
    units, slots = own.shape[1:]
    return pl.pallas_call(
        functools.partial(first_kernel, table, model, counts, places, start),
        out_shape=jax.ShapeDtypeStruct((units, width), bf16),
        in_specs=[scalars()] + [whole()] * (sum(counts) + 3) + [anywhere()] * len(after),
        out_specs=whole(),
        scratch_shapes=[pltpu.VMEM((2 * slots, width), bf16)],
        compiler_params=params(),
        cost_estimate=taking(1),
        name="first_sums",
    )(where, *arrays[0], *arrays[1], own, other, coming, *after)


def rows_of(units):
    return units // 2 if units % 32 == 0 else units


def column_parts(arrays, cut):
    return [(0, arrays[0])] if len(arrays) == 1 else [(cut, arrays[0]), (0, arrays[1])]


def combine_kernel(table, key, cut, counts, sides, where_ref, *refs):
    slot = where_ref[table[key]]
    coming = refs[: counts[0]]
    outs = refs[len(refs) - counts[2] :]
    model = sum(ref.shape[1] for ref in outs)
    spans = [(cut, model), (0, cut)] if cut else [(0, model)]
    for chunk, (start, stop) in enumerate(spans):
        if counts[0] == 0:
            total = jnp.zeros((outs[0].shape[0], stop - start), f32)
        elif counts[0] == 1:
            total = coming[0][:, start:stop].astype(f32)
        else:
            total = coming[chunk][...].astype(f32)
        for number, side in enumerate(sides):
            flag = slot == 0 if side == "first" else slot > 0
            total = total + jnp.where(flag, refs[counts[0] + len(spans) * number + chunk][0], 0.0)
        total = total.astype(bf16)
        if counts[2] == 1:
            outs[0][:, start:stop] = total
        else:
            outs[chunk][...] = total


def combine(table, where, coming, first, rest, turn, name, used, cut, after, chunked=False, weight=1):
    units = first[0].shape[1]
    model = sum(part.shape[2] for part in first)
    block = rows_of(units)
    column = table["block", turn, name]
    sides, operands, specs = [], [], []
    if any(slot == 0 for slot in used):
        sides.append("first")
        operands += first
        specs += [pl.BlockSpec((1, block, part.shape[2]), lambda j, s: (0, j, 0)) for part in first]
    if any(slot > 0 for slot in used):
        sides.append("rest")
        operands += rest
        specs += [pl.BlockSpec((1, block, part.shape[2]), lambda j, s: (s[column], j, 0)) for part in rest]
    widths = [model - cut, cut] if chunked else [model]
    return pl.pallas_call(
        functools.partial(
            combine_kernel, table, ("use", turn, name), cut, (len(coming), len(operands), len(widths)), sides
        ),
        out_shape=[jax.ShapeDtypeStruct((units, count), bf16) for count in widths],
        grid_spec=pltpu.PrefetchScalarGridSpec(
            num_scalar_prefetch=1,
            grid=(units // block,),
            in_specs=[pl.BlockSpec((block, part.shape[1]), lambda j, s: (j, 0)) for part in coming]
            + specs
            + [anywhere()] * len(after),
            out_specs=[pl.BlockSpec((block, count), lambda j, s: (j, 0)) for count in widths],
        ),
        compiler_params=params(),
        cost_estimate=taking(weight),
        name="combine",
    )(where, *coming, *operands, *after)


def total_kernel(cut, counts, *refs):
    coming = [refs[: counts[0]], refs[counts[0] : sum(counts)]]
    out_ref = refs[-1]
    for chunk, start in enumerate((cut, 0)):
        kept_ref = refs[sum(counts) + chunk]
        here = slice(start, start + kept_ref.shape[2])
        total = kept_ref[0]
        for parts in coming:
            total = total + (parts[0][:, here] if len(parts) == 1 else parts[chunk][...]).astype(f32)
        out_ref[0, :, here] = total


def total_grad(a, b, kept, cut):
    units = a[0].shape[0]
    model = sum(part.shape[1] for part in a)
    block = rows_of(units)
    return pl.pallas_call(
        functools.partial(total_kernel, cut, (len(a), len(b))),
        out_shape=jax.ShapeDtypeStruct((1, units, model), f32),
        grid=(units // block,),
        in_specs=[pl.BlockSpec((block, part.shape[1]), lambda j: (j, 0)) for part in (*a, *b)]
        + [
            pl.BlockSpec((1, block, part.shape[2]), functools.partial(lambda last, j: (last, j, 0), part.shape[0] - 1))
            for part in kept
        ],
        out_specs=pl.BlockSpec((1, block, model), lambda j: (0, j, 0)),
        compiler_params=params(),
        cost_estimate=taking(2),
        name="total_grad",
    )(*a, *b, *kept)


def back_kernel(table, model, cut, counts, places, choices, parts, guard, summed, where_ref, *refs):
    keys = [key for choice in choices for key in choice]
    used = sum(counts)
    late = blocks_of(refs[: counts[0]], places[0])
    early = blocks_of(refs[counts[0] : used], places[1])
    number = len(late)
    own_ref, first_ref, rest_ref = refs[used : used + 3]
    weight_refs, used = {}, used + 3
    for key, count in zip(keys, parts):
        weight_refs[key] = refs[used : used + count]
        used += count
    before_ref = refs[used] if summed else None
    outs, sums_ref = refs[-3:-1], refs[-1]
    tokens = late[0].shape[0]
    units = own_ref.shape[1]
    me = where_ref[table["me"]]
    start = late[0].shape[1] - LANES
    eight = lax.broadcasted_iota(jnp.int32, (8, LANES), 1)
    onehot = jnp.where(eight == model % LANES + me, 1.0, 0.0).astype(bf16)
    shards = {key: where_ref[table[("shard",) + key]] for key in keys}
    slots = {key: where_ref[table[("slot",) + key]] for key in keys}
    sums_ref[...] = before_ref[...] if summed else jnp.zeros(sums_ref.shape, f32)

    def whole_weight(key):
        got = weight_refs[key]
        return got[0][...] if len(got) == 1 else jnp.concatenate([got[1][...], got[0][...]], axis=1)

    def work():
        stack, here_valid, here_slot = [], [], []
        for choice in choices:
            weight, valid, slot = whole_weight(choice[0]), shards[choice[0]] >= 0, slots[choice[0]]
            for key in choice[1:]:
                weight = jnp.where(valid, weight, whole_weight(key))
                slot = jnp.where(valid, slot, slots[key])
                valid = jnp.logical_or(valid, shards[key] >= 0)
            stack.append(weight)
            here_valid.append(valid)
            here_slot.append(slot)
        weight = jnp.concatenate(stack, axis=0) if len(stack) > 1 else stack[0]
        for pair in range(0, number, 2):
            both = jnp.concatenate(
                [
                    jnp.concatenate([early[k][...], late[k][:, : model - cut]], axis=1)
                    for k in (pair, pair + 1)
                ],
                axis=0,
            )
            product = dot(weight, both, NT)
            for place in (pair, pair + 1):
                near = place < number // 2
                block = product[:, (place - pair) * tokens : (place - pair + 1) * tokens]
                gate = dot(onehot, late[place][:, start:], NT)[0:1]
                here = pl.ds(place_of(place % (number // 2), number // 2, me, tokens), tokens)
                wide = pl.ds(place_of(place, number // 2, me, tokens), tokens)
                gated = (block * gate).astype(bf16)
                total = jnp.zeros((1, tokens), f32)
                for index, (valid, slot) in enumerate(zip(here_valid, here_slot)):
                    some = slice(index * units, (index + 1) * units)
                    outs[0 if near else 1][index, :, here] = gated[some]
                    if near:
                        hidden = own_ref[slot, :, here].astype(f32)
                    else:
                        hidden = jnp.where(
                            slot == 0,
                            first_ref[0, :, here].astype(f32),
                            rest_ref[jnp.maximum(slot - 1, 0), :, here].astype(f32),
                        )
                    part = jnp.sum(hidden * block[some], axis=0, keepdims=True)
                    total = total + jnp.where(valid, part, 0.0)
                sums_ref[0:1, wide] += total

    if guard:
        pl.when(functools.reduce(jnp.logical_or, [shards[key] >= 0 for key in keys]))(work)
    else:
        work()


def back_part(table, where, late, early, own, first, rest, choices, got, before, guard, after, model):
    units, slots = own.shape[1:]
    arrays, places = zip(late, early)
    counts = [len(part) for part in arrays]
    cut = arrays[1][0].shape[-1]
    keys = [key for choice in choices for key in choice]
    weights = [got[key] for key in keys]
    flat = [part for weight in weights for part in weight]
    half = jax.ShapeDtypeStruct((len(choices), units, slots), bf16)
    summed = before is not None
    operands = [*arrays[0], *arrays[1], own, first, rest, *flat] + ([before] if summed else [])
    outs = [half, half, jax.ShapeDtypeStruct((8, 2 * slots), f32)]
    parts = [len(weight) for weight in weights]
    return pl.pallas_call(
        functools.partial(
            back_kernel, table, model, cut, counts, places, choices, parts, guard, summed
        ),
        out_shape=outs,
        in_specs=[scalars()] + [whole()] * len(operands) + [anywhere()] * len(after),
        out_specs=[whole()] * len(outs),
        compiler_params=params(),
        cost_estimate=taking(6),
        name="back_part",
    )(where, *operands, *after)


def join_kernel(table, choices, where_ref, *refs):
    out_ref, turned, sem = refs[-3:]
    slots, width = turned.shape[1:]
    row = lax.broadcasted_iota(jnp.int32, (slots, slots), 0)
    column = lax.broadcasted_iota(jnp.int32, (slots, slots), 1)
    unit = jnp.where(row == column, 1.0, 0.0).astype(bf16)
    low = where_ref[table["x"]] == 0
    copies = []
    pairs = [
        (refs[2 * group][place], refs[2 * group + 1][place])
        for group in range((len(refs) - 3) // 2)
        for place in range(refs[2 * group].shape[0])
    ]
    for place, (choice, (mine, theirs)) in enumerate(zip(choices, pairs)):
        index = where_ref[table[("shard",) + choice[0]]]
        for key in choice[1:]:
            index = jnp.where(index >= 0, index, where_ref[table[("shard",) + key]])
        both = jnp.concatenate([jnp.where(low, mine, theirs), jnp.where(low, theirs, mine)], axis=0)
        turned[place] = dot(unit, both, NT).astype(bf16)
        here = pl.ds(pl.multiple_of(jnp.maximum(index, 0) * width, LANES), width)
        copy = pltpu.make_async_copy(turned.at[place], out_ref.at[:, here], sem.at[place])
        copies.append((index, copy))
        pl.when(index >= 0)(copy.start)
    for index, copy in copies:
        pl.when(index >= 0)(copy.wait)


def join_hidden(table, where, choices, halves, slots, hidden):
    units = halves[0].shape[1]
    return pl.pallas_call(
        functools.partial(join_kernel, table, choices),
        out_shape=jax.ShapeDtypeStruct((slots, hidden), bf16),
        in_specs=[scalars()] + [whole()] * len(halves),
        out_specs=anywhere(),
        scratch_shapes=[
            pltpu.VMEM((len(choices), slots, 2 * units), bf16),
            pltpu.SemaphoreType.DMA((len(choices),)),
        ],
        compiler_params=params(),
        cost_estimate=taking(2),
        name="join_hidden",
    )(where, *halves)


def logits_kernel(gates_ref, ids_ref, grads_ref, out_ref):
    gates, ids, grads = gates_ref[...], ids_ref[...], grads_ref[...]
    picked = jnp.zeros_like(gates)
    for expert in range(grads.shape[0]):
        picked = picked + jnp.where(ids == expert, grads[expert : expert + 1, :], 0.0)
    out_ref[...] = gates * (picked - jnp.sum(gates * picked, axis=0, keepdims=True))


def logits_grad(gates, ids, grads):
    return pl.pallas_call(
        logits_kernel,
        out_shape=jax.ShapeDtypeStruct(gates.shape, f32),
        in_specs=[whole()] * 3,
        out_specs=whole(),
        compiler_params=params(),
        cost_estimate=taking(1),
        name="logits_grad",
    )(gates, ids, grads)


def per_device_full(grad_out, top_logits, expert_ids, saved_hidden, w_down):
    experts = lax.axis_size("exp")
    groups = lax.axis_size("ctx")
    depth = groups // 2
    tokens, model = grad_out.shape
    slots, hidden = saved_hidden.shape[2:]
    width = pl.cdiv(model + experts, LANES) * LANES
    cut = width // LANES // 2 * LANES

    table, brought, uses = device_scalars(depth, experts)
    where = table.row(lax.axis_index("ctx"), lax.axis_index("exp"))

    def swap(value, x, exp):
        if not exp:
            return lax.ppermute(value, "ctx", [(i, i ^ x) for i in range(groups)])
        if not x:
            return lax.ppermute(value, "exp", [(i, i ^ exp) for i in range(experts)])
        pairs = [(c * experts + e, (c ^ x) * experts + (e ^ exp)) for c in range(groups) for e in range(experts)]
        return lax.ppermute(value, ("ctx", "exp"), pairs)

    def swap_z(value, name, senders=range(depth)):
        first = "AB".index(name)
        pairs = []
        for low in range(first, depth - 1, 2):
            for z, other in ((low, low + 1), (low + 1, low)):
                pairs += [(2 * z + x, 2 * other + x) for x in range(2) if z in senders]
        return lax.ppermute(value, "ctx", pairs)

    got = {(0, "own"): [w_down[0]]}
    for name in "BA":
        got[1, name] = [swap_z(w_down[0], name)]

    late, early, gates = make_rows(grad_out, top_logits, expert_ids, width, cut)
    highs = list(range(2, experts, 2))

    def sides(mine):
        return [mine, swap(mine, 0, 1)]

    late_x = swap(late, 1, 0)
    late_near = [late] + [swap(late, 0, high) for high in highs]
    own, other_first, other_rest = split_hidden(
        table, where, saved_hidden[0, 0], depth, w_down.shape[1], [late]
    )
    other_first = swap(other_first, 1, 0)
    (late_x,) = hold((late_x,), late_near[1:])
    late_mine = late_near + [late_x] + [swap(late_x, 0, high) for high in highs]
    (early,) = hold((early,), [late_x, other_first])
    early_x = swap(early, 1, 0)
    late_rows = sides(pack(late_mine, [early_x]))
    late_rows = (late_rows, [(side, place) for place in range(experts) for side in range(2)])
    early_rows = sides(pack([early, early_x], []))
    places = [(0, 0), (1, 0)]
    for block, base in ((early, 0), (early_x, 1)):
        if base:
            places += [(0, 1), (1, 1)]
        for high in highs:
            places += [(len(early_rows), None), (len(early_rows) + 1, None)]
            early_rows += sides(swap(block, 0, high))
    early_rows = (early_rows, places)
    other_rest = swap(other_rest, 1, 0)

    got[1, "B"] = list(hold(got[1, "B"], got[1, "A"], FIRST_WEIGHT))
    chunks = ((late_rows, cut, model - cut), (early_rows, 0, cut))
    after = [early_rows[0][1]]
    first = []
    for rows, start, columns in chunks:
        value = first_sums(
            table, where, rows, late_rows, own, other_first, got[1, "B"][0], model, start, columns, after
        )
        if first:
            (value,) = hold([value], got[2, "A"], NEXT_WEIGHT)
        got.setdefault((2, "A"), []).append(swap_z(value, "A"))
        first.append(
            products(
                table, where, rows, late_rows, own, other_first, 0, model, columns, "first_kept", [value], True
            )
        )
        after = [first[0]]
    marker = value
    got[2, "B"] = [swap_z(got[1, "A"][0], "B")]
    (other_rest,) = hold([other_rest], [], HIDDEN_WEIGHT)

    halves, all_choices, weights_of = [], [], {}
    only_first = max(uses[3, "B"]) <= 0

    def backprop(choices, before, guard, after):
        mine, theirs, sums = back_part(
            table, where, late_rows, early_rows, own, other_first, other_rest, choices,
            {**got, **weights_of}, before, guard, after, model,
        )
        halves.extend([mine, swap(theirs, 1, 0)])
        all_choices.extend(choices)
        return sums

    def pass_on(turn, name, after, chunk=None, waited=(), weight=1):
        coming = got[turn - 1, "B" if name == "A" else "A"]
        used = uses[turn, name]
        senders = range(depth)
        if turn == depth - 1 and min(used) < 0 and name == "A" and len(coming) == 1:
            senders = [z for z in range(depth) if used[z] >= 0]
            if (turn, name) not in weights_of:
                coming[:] = hold(coming, [], PASS_WEIGHT)
                others = [z for z in range(depth) if z not in senders]
                weights_of[turn, name] = [swap_z(coming[0], name, others)]
            if set(senders) <= {0, depth - 1}:
                coming = []
        parts, start = (first, rest), cut
        if chunk is not None:
            coming, parts, start = coming[chunk:][:1], (first[chunk:][:1], rest[chunk:][:1]), 0
        values = list(combine(table, where, coming, *parts, turn, name, used, start, after, False, weight))
        if waited:
            values = list(hold(values, list(waited), WAITED_WEIGHT))
        got.setdefault((turn, name), []).extend(swap_z(value, name, senders) for value in values)
        return values[-1]

    def choices_of(turn):
        both = any(b[turn, "A"] >= 0 and b[turn, "B"] >= 0 for b in brought)
        return [[(turn, "A")], [(turn, "B")]] if both else [[(turn, "A"), (turn, "B")]]

    rest = []

    def other_products(chunk, after):
        rows, _, columns = chunks[chunk]
        rest.append(
            products(table, where, rows, late_rows, own, other_rest, 1, model, columns, "rest_kept", after)
        )
        return rest[chunk]

    apart = max(uses[3, "B"]) <= 0 and depth == 4
    if apart:
        for chunk in range(2):
            marker = pass_on(3, "B", [marker], chunk)
            marker = other_products(chunk, [marker])
            marker = pass_on(3, "A", [marker], chunk)
    else:
        marker = other_products(1, [other_products(0, [marker])])
        marker = pass_on(3, "A", [marker])
        for chunk in range(2):
            marker = pass_on(3, "B", [marker], chunk)
    sums = backprop([[(0, "own")], [(1, "A")], [(1, "B")]], None, False, got[2, "A"][:1])
    sooner = halves[1::2]
    for turn in range(2, depth):
        choices = choices_of(turn)
        if turn > 2:
            waited = [array for key in ((turn, "A"), (turn, "B")) for array in weights_of.get(key, [])]
            if apart and turn + 1 == depth:
                pass_on(depth, "B", [sums], 0, (), ENTER_WEIGHT)
                pass_on(depth, "B", [sums, *sooner], 1, waited, LEAVE_WEIGHT)
                marker = pass_on(depth, "A", [sums], weight=LAST_WEIGHT)
            else:
                pass_on(turn + 1, "B", [sums, *sooner, *waited])
                marker = pass_on(turn + 1, "A", [sums])
        sums = backprop(choices, sums, len(choices) == 1, [marker])
    slot_grad = sums[0:1, :slots] + swap(sums[0:1, slots:], 1, 0)
    grads = lax.all_to_all(
        slot_grad.reshape(experts, tokens), "exp", split_axis=0, concat_axis=0, tiled=True
    )
    logit_grad = logits_grad(gates, expert_ids.T, grads)
    hidden_grad = join_hidden(table, where, all_choices, halves, slots, hidden)
    weight_grad = total_grad(got[depth, "A"], got[depth, "B"], rest, cut)
    return (logit_grad.T, hidden_grad[None, None], weight_grad)


def routing_tables(expert_ids, count_experts, capacity):
    columns = jnp.arange(count_experts, dtype=jnp.int32)
    matches = expert_ids[:, :, None] == columns[None, None, :]
    per_token = jnp.sum(matches.astype(jnp.int32), axis=1)
    rank_table = jnp.cumsum(per_token, axis=0) - per_token
    slot_iota = jnp.arange(capacity, dtype=jnp.int32)
    select = (per_token.T[:, None, :] == 1) & (rank_table.T[:, None, :] == slot_iota[None, :, None])
    return (matches.astype(jnp.float32), select)


def per_device_routed(grad_out, top_logits, expert_ids, saved_hidden, w_down):
    count_experts = lax.axis_size("exp")
    slot_count = saved_hidden.shape[2]
    capacity = slot_count // count_experts
    model_width = grad_out.shape[1]
    onehot, select = routing_tables(expert_ids, count_experts, capacity)
    select_wide = select.astype(jnp.float32)
    gate_probs = jax.nn.softmax(top_logits, axis=-1)
    gate_sent = gate_probs.astype(jnp.bfloat16)
    gate_by_expert = jnp.sum(onehot * gate_sent.astype(jnp.float32)[:, :, None], axis=1)
    send_rows = jnp.einsum(
        "ect,td->ecd", select.astype(jnp.bfloat16), grad_out, preferred_element_type=jnp.float32
    ).astype(jnp.bfloat16)
    send_gate = jnp.sum(select_wide * gate_by_expert.T[:, None, :], axis=2).astype(jnp.bfloat16)
    hidden = saved_hidden[0, 0]
    rows_in, gate_in = (
        lax.all_to_all(send_rows, "exp", split_axis=0, concat_axis=0, tiled=True),
        lax.all_to_all(send_gate, "exp", split_axis=0, concat_axis=0, tiled=True),
    )
    flat_rows = rows_in.reshape(slot_count, model_width)
    backprop = lax.dot_general(
        flat_rows,
        lax.all_gather(w_down[0], "ctx", axis=0, tiled=True),
        (((1,), (1,)), ((), ())),
        preferred_element_type=jnp.float32,
    )
    flat_gate = gate_in.reshape(slot_count, 1).astype(jnp.float32)
    hidden_grad = (flat_gate * backprop).astype(jnp.bfloat16)
    slot_grad = jnp.sum(hidden.astype(jnp.float32) * backprop, axis=1)
    scaled = (flat_gate * flat_rows.astype(jnp.float32)).astype(jnp.bfloat16)
    partial_grad = lax.dot_general(
        hidden, scaled, (((0,), (0,)), ((), ())), preferred_element_type=jnp.float32
    )
    weight_grad = lax.psum_scatter(partial_grad, "ctx", scatter_dimension=0, tiled=True)
    returned = lax.all_to_all(
        slot_grad.reshape(count_experts, capacity), "exp", split_axis=0, concat_axis=0, tiled=True
    )
    grad_by_expert = jnp.sum(select_wide * returned[:, :, None], axis=1)
    gate_grad = jnp.sum(onehot * grad_by_expert.T[:, None, :], axis=2)
    logit_grad = gate_probs * (gate_grad - jnp.sum(gate_probs * gate_grad, axis=1, keepdims=True))
    return (logit_grad, hidden_grad.reshape(1, 1, slot_count, -1), weight_grad[None])


def per_device(grad_out, top_logits, expert_ids, saved_hidden, w_down):
    experts = lax.axis_size("exp")
    groups = lax.axis_size("ctx")
    everywhere = top_logits.shape[1] == experts and saved_hidden.shape[2] == experts * grad_out.shape[0]
    plain = experts & (experts - 1) == 0 and groups % 4 == 0 and groups >= 8
    body = per_device_full if everywhere and plain else per_device_routed
    return body(grad_out, top_logits, expert_ids, saved_hidden, w_down)


def solution(mesh):
    return jax.shard_map(
        per_device,
        mesh=mesh,
        in_specs=(
            P(("ctx", "exp"), None),
            P(("ctx", "exp"), None),
            P(("ctx", "exp"), None),
            P("ctx", "exp", None, None),
            P("exp", "ctx", None),
        ),
        out_specs=(P(("ctx", "exp"), None), P("ctx", "exp", None, None), P("exp", "ctx", None)),
        check_vma=False,
    )
```

```python
import functools

import jax
import jax.numpy as jnp
import numpy as np
from jax import lax
from jax.experimental import pallas as pl
from jax.experimental.pallas import tpu as pltpu
from jax.sharding import PartitionSpec as P

LANES = 128
SCALE = 1_000_000
FIRST_WEIGHT = 12_000
NEXT_WEIGHT = 600
HIDDEN_WEIGHT = 5_000
PASS_WEIGHT = 1
WAITED_WEIGHT = 210
ENTER_WEIGHT = 575
LEAVE_WEIGHT = 5_250
LAST_WEIGHT = 90
NT = (((1,), (1,)), ((), ()))
NN = (((1,), (0,)), ((), ()))
f32 = jnp.float32
bf16 = jnp.bfloat16


def dot(a, b, dims):
    return lax.dot_general(a, b, dims, preferred_element_type=f32)


def anywhere():
    return pl.BlockSpec(memory_space=pl.ANY)


def whole():
    return pl.BlockSpec(memory_space=pltpu.VMEM)


def scalars():
    return pl.BlockSpec(memory_space=pltpu.SMEM)


def params(mib=24):
    return pltpu.CompilerParams(vmem_limit_bytes=mib * 1024 * 1024)


def taking(microseconds):
    return pl.CostEstimate(flops=int(microseconds * SCALE), bytes_accessed=int(microseconds * 3e6), transcendentals=0)


def chain_plan(depth):
    products, weights = [], []
    for z in range(depth):
        uses = []
        for turn in range(2, depth + 1):
            if z < depth - 1 and turn >= z + 2:
                uses.append((turn, "AB"[z % 2], depth + 1 + z - turn))
            if z > 0 and turn >= depth - z + 1:
                uses.append((turn, "BA"[z % 2], z + turn - depth - 1))
        products.append(sorted(uses) + [(depth + 1, "own", z)])
        brought = {}
        for turn in range(1, depth):
            for name in "AB":
                index = z + turn if (name == "A") == (z % 2 == 0) else z - turn
                brought[turn, name] = index if 0 <= index < depth else -1
        weights.append(brought)
    return products, weights


class Scalars:
    def __init__(self):
        self.columns = []
        self.names = {}

    def add(self, name, values):
        self.names[name] = len(self.columns)
        self.columns.append(values)

    def __getitem__(self, name):
        return self.names[name]

    def row(self, place, me):
        return jnp.asarray(np.stack(self.columns, axis=-1).astype(np.int32))[place, me]


def device_scalars(depth, experts):
    products, weights = chain_plan(depth)
    table = Scalars()
    along = np.arange(2 * depth)[:, None] + np.zeros((1, experts), np.int32)

    def by_z(values):
        return np.asarray(values)[along // 2]

    table.add("x", along % 2)
    table.add("me", np.zeros_like(along) + np.arange(experts)[None, :])
    table.add(("shard", 0, "own"), along // 2)
    slot_of = [{use[2]: slot for slot, use in enumerate(products[z])} for z in range(depth)]
    for part in range(depth):
        table.add(("slot of", part), by_z([slot_of[z][part] for z in range(depth)]))
    table.add(("slot", 0, "own"), by_z([slot_of[z][z] for z in range(depth)]))
    for turn in range(1, depth):
        for name in "AB":
            shard = [weights[z][turn, name] for z in range(depth)]
            table.add(("shard", turn, name), by_z(shard))
            table.add(("slot", turn, name), by_z([slot_of[z].get(k, 0) for z, k in enumerate(shard)]))
    uses = {}
    for turn in range(2, depth + 1):
        for name in "AB":
            slots = [-1] * depth
            for z in range(depth):
                for slot, use in enumerate(products[z]):
                    if use[:2] == (turn, name):
                        slots[z] = slot
            uses[turn, name] = slots
            table.add(("use", turn, name), by_z(slots))
            limit = max(depth - 3, 0)
            table.add(("block", turn, name), by_z([min(max(slot - 1, 0), limit) for slot in slots]))
    return table, weights, uses


def rows_kernel(cut, grad_hbm, logits_hbm, ids_hbm, late_ref, early_ref, gates_ref, *scratch):
    grad_ref, logits_ref, ids_ref, sems = scratch
    model, tokens = grad_ref.shape
    copies = [
        pltpu.make_async_copy(source, target, sems.at[place])
        for place, (source, target) in enumerate(
            ((grad_hbm, grad_ref), (logits_hbm, logits_ref), (ids_hbm, ids_ref))
        )
    ]
    for copy in copies:
        copy.start()
    for copy in copies:
        copy.wait()
    count = logits_ref.shape[0]
    width = cut + late_ref.shape[1]
    logits = logits_ref[...]
    powers = jnp.exp(logits - jnp.max(logits, axis=0, keepdims=True))
    gates = powers / jnp.sum(powers, axis=0, keepdims=True)
    gates_ref[...] = gates
    sent = gates.astype(bf16).astype(f32)
    ids = ids_ref[...]
    row = lax.broadcasted_iota(jnp.int32, (width - model, tokens), 0)
    extra = jnp.zeros((width - model, tokens), f32)
    for expert in range(count):
        chosen = jnp.sum(jnp.where(ids == expert, sent, 0.0), axis=0, keepdims=True)
        extra = extra + jnp.where(row == expert, chosen, 0.0)
    for start in range(0, width, LANES):
        stop = start + LANES
        if stop <= model:
            block = grad_ref[start:stop, :].astype(f32)
        elif start >= model:
            block = extra[start - model : stop - model, :]
        else:
            block = jnp.concatenate(
                [grad_ref[start:model, :].astype(f32), extra[: stop - model, :]], axis=0
            )
        turned = block.T.astype(bf16)
        if start < cut:
            early_ref[:, start:stop] = turned
        else:
            late_ref[:, start - cut : stop - cut] = turned


def make_rows(grad_out, top_logits, expert_ids, width, cut):
    tokens, model = grad_out.shape
    count = top_logits.shape[1]
    return pl.pallas_call(
        functools.partial(rows_kernel, cut),
        out_shape=(
            jax.ShapeDtypeStruct((tokens, width - cut), bf16),
            jax.ShapeDtypeStruct((tokens, cut), bf16),
            jax.ShapeDtypeStruct((count, tokens), f32),
        ),
        in_specs=[pl.BlockSpec(memory_space=pltpu.HBM)] * 3,
        out_specs=(whole(),) * 3,
        scratch_shapes=[
            pltpu.VMEM((model, tokens), bf16),
            pltpu.VMEM((count, tokens), f32),
            pltpu.VMEM((count, tokens), jnp.int32),
            pltpu.SemaphoreType.DMA((3,)),
        ],
        compiler_params=params(58),
        cost_estimate=taking(2),
        name="make_rows",
    )(grad_out.T, top_logits.T, expert_ids.T)


def pack_kernel(*refs):
    out_ref, sems = refs[-2:]
    copies = []
    for place in range(out_ref.shape[0]):
        copies.append(pltpu.make_async_copy(refs[place], out_ref.at[place], sems.at[place]))
        copies[-1].start()
    for copy in copies:
        copy.wait()


def pack(values, after):
    number = len(values)
    return pl.pallas_call(
        pack_kernel,
        out_shape=jax.ShapeDtypeStruct((number, *values[0].shape), values[0].dtype),
        in_specs=[anywhere()] * (number + len(after)),
        out_specs=anywhere(),
        scratch_shapes=[pltpu.SemaphoreType.DMA((number,))],
        compiler_params=params(),
        cost_estimate=taking(1),
        name="pack_rows",
    )(*values, *after)


def blocks_of(refs, places):
    return [refs[array] if place is None else refs[array].at[place] for array, place in places]


def hold_kernel(*refs):
    del refs


def hold(values, after, weight=0):
    return pl.pallas_call(
        hold_kernel,
        out_shape=tuple(jax.ShapeDtypeStruct(value.shape, value.dtype) for value in values),
        in_specs=[anywhere()] * (len(values) + len(after)),
        out_specs=(anywhere(),) * len(values),
        input_output_aliases={place: place for place in range(len(values))},
        compiler_params=params(),
        cost_estimate=taking(weight),
        name="hold",
    )(*values, *after)


def split_kernel(table, where_ref, hidden_ref, *refs):
    own_ref, first_ref, rest_ref = refs[-3:]
    parts, units, _ = own_ref.shape
    row = lax.broadcasted_iota(jnp.int32, (2 * units, 2 * units), 0)
    column = lax.broadcasted_iota(jnp.int32, (2 * units, 2 * units), 1)
    unit = jnp.where(row == column, 1.0, 0.0).astype(bf16)
    low = where_ref[table["x"]] == 0
    for part in range(parts):
        block = hidden_ref[:, part * 2 * units : (part + 1) * 2 * units]
        turned = dot(unit, block, NT).astype(bf16)
        slot = where_ref[table["slot of", part]]
        other = jnp.where(low, turned[units:], turned[:units])
        own_ref[slot] = jnp.where(low, turned[:units], turned[units:])

        @pl.when(slot == 0)
        def _():
            first_ref[0] = other

        @pl.when(slot != 0)
        def _():
            rest_ref[slot - 1] = other


def split_hidden(table, where, hidden, parts, units, after):
    slots = hidden.shape[0]
    return pl.pallas_call(
        functools.partial(split_kernel, table),
        out_shape=tuple(
            jax.ShapeDtypeStruct((count, units, slots), bf16) for count in (parts, 1, parts - 1)
        ),
        in_specs=[scalars(), whole()] + [anywhere()] * len(after),
        out_specs=(whole(),) * 3,
        compiler_params=params(),
        cost_estimate=taking(2),
        name="split_hidden",
    )(where, hidden, *after)


def place_of(place, count, me, tokens):
    start = (place // count) * count * tokens + ((place % count) ^ me) * tokens
    return pl.multiple_of(start, tokens)


def scale_rows(table, model, where_ref, rows, gated, scaled):
    tokens = rows[0].shape[0]
    me = where_ref[table["me"]]
    lane = lax.broadcasted_iota(jnp.int32, (tokens, LANES), 1)
    for place, block in enumerate(rows):
        here = pl.ds(place_of(place, len(rows) // 2, me, tokens), tokens)
        tile = gated[place][:, gated[place].shape[1] - LANES :]
        picked = jnp.where(lane == model % LANES + me, tile.astype(f32), 0.0)
        gate = jnp.sum(picked, axis=1, keepdims=True)
        scaled[here, :] = (block[:, : scaled.shape[1]].astype(f32) * gate).astype(bf16)


def products_kernel(table, model, counts, places, shards, skip, middle, where_ref, *refs):
    used = sum(counts)
    rows = blocks_of(refs[: counts[0]], places[0])
    gated = blocks_of(refs[counts[0] : used], places[1])
    own_ref, other_ref = refs[used : used + 2]
    kept_ref, scaled = refs[-2:]
    units, slots = own_ref.shape[1:]

    def stacked(ref, offset):
        parts = [ref[offset + shard] for shard in range(shards)]
        return jnp.concatenate(parts, axis=0) if len(parts) > 1 else parts[0]

    def work():
        scale_rows(table, model, where_ref, rows, gated, scaled)
        total = dot(stacked(own_ref, skip), scaled[:slots, :], NN)
        total = total + dot(stacked(other_ref, 0), scaled[slots:, :], NN)
        for shard in range(shards):
            kept_ref[shard] = total[shard * units : (shard + 1) * units]

    if middle:
        pl.when(where_ref[table["use", 2, "A"]] != 0)(work)
    else:
        work()


def products(table, where, rows, gated, own, other, skip, model, width, name, after, middle=False):
    arrays, places = zip(rows, gated)
    counts = [len(part) for part in arrays]
    shards, units, slots = other.shape
    kept = jax.ShapeDtypeStruct((shards, units, width), f32)
    operands = [*arrays[0], *arrays[1], own, other]
    return pl.pallas_call(
        functools.partial(products_kernel, table, model, counts, places, shards, skip, middle),
        out_shape=kept,
        in_specs=[scalars()] + [whole()] * len(operands) + [anywhere()] * len(after),
        out_specs=whole(),
        scratch_shapes=[pltpu.VMEM((2 * slots, width), bf16)],
        compiler_params=params(),
        cost_estimate=taking(1),
        name=name,
    )(where, *operands, *after)


def first_kernel(table, model, counts, places, start, where_ref, *refs):
    used = sum(counts)
    rows = blocks_of(refs[: counts[0]], places[0])
    gated = blocks_of(refs[counts[0] : used], places[1])
    own_ref, other_ref, coming_ref = refs[used : used + 3]
    out_ref, scaled = refs[-2:]
    slots = own_ref.shape[2]
    ends = where_ref[table["use", 2, "A"]] == 0

    @pl.when(ends)
    def _():
        scale_rows(table, model, where_ref, rows, gated, scaled)
        total = dot(own_ref[0], scaled[:slots, :], NN)
        out_ref[...] = (total + dot(other_ref[0], scaled[slots:, :], NN)).astype(bf16)

    @pl.when(jnp.logical_not(ends))
    def _():
        out_ref[...] = coming_ref[:, start : start + out_ref.shape[1]]


def first_sums(table, where, rows, gated, own, other, coming, model, start, width, after):
    arrays, places = zip(rows, gated)
    counts = [len(part) for part in arrays]
    units, slots = own.shape[1:]
    return pl.pallas_call(
        functools.partial(first_kernel, table, model, counts, places, start),
        out_shape=jax.ShapeDtypeStruct((units, width), bf16),
        in_specs=[scalars()] + [whole()] * (sum(counts) + 3) + [anywhere()] * len(after),
        out_specs=whole(),
        scratch_shapes=[pltpu.VMEM((2 * slots, width), bf16)],
        compiler_params=params(),
        cost_estimate=taking(1),
        name="first_sums",
    )(where, *arrays[0], *arrays[1], own, other, coming, *after)


def rows_of(units):
    return units // 2 if units % 32 == 0 else units


def column_parts(arrays, cut):
    return [(0, arrays[0])] if len(arrays) == 1 else [(cut, arrays[0]), (0, arrays[1])]


def combine_kernel(table, key, cut, counts, sides, where_ref, *refs):
    slot = where_ref[table[key]]
    coming = refs[: counts[0]]
    outs = refs[len(refs) - counts[2] :]
    model = sum(ref.shape[1] for ref in outs)
    spans = [(cut, model), (0, cut)] if cut else [(0, model)]
    for chunk, (start, stop) in enumerate(spans):
        if counts[0] == 0:
            total = jnp.zeros((outs[0].shape[0], stop - start), f32)
        elif counts[0] == 1:
            total = coming[0][:, start:stop].astype(f32)
        else:
            total = coming[chunk][...].astype(f32)
        for number, side in enumerate(sides):
            flag = slot == 0 if side == "first" else slot > 0
            total = total + jnp.where(flag, refs[counts[0] + len(spans) * number + chunk][0], 0.0)
        total = total.astype(bf16)
        if counts[2] == 1:
            outs[0][:, start:stop] = total
        else:
            outs[chunk][...] = total


def combine(table, where, coming, first, rest, turn, name, used, cut, after, chunked=False, weight=1):
    units = first[0].shape[1]
    model = sum(part.shape[2] for part in first)
    block = rows_of(units)
    column = table["block", turn, name]
    sides, operands, specs = [], [], []
    if any(slot == 0 for slot in used):
        sides.append("first")
        operands += first
        specs += [pl.BlockSpec((1, block, part.shape[2]), lambda j, s: (0, j, 0)) for part in first]
    if any(slot > 0 for slot in used):
        sides.append("rest")
        operands += rest
        specs += [pl.BlockSpec((1, block, part.shape[2]), lambda j, s: (s[column], j, 0)) for part in rest]
    widths = [model - cut, cut] if chunked else [model]
    return pl.pallas_call(
        functools.partial(
            combine_kernel, table, ("use", turn, name), cut, (len(coming), len(operands), len(widths)), sides
        ),
        out_shape=[jax.ShapeDtypeStruct((units, count), bf16) for count in widths],
        grid_spec=pltpu.PrefetchScalarGridSpec(
            num_scalar_prefetch=1,
            grid=(units // block,),
            in_specs=[pl.BlockSpec((block, part.shape[1]), lambda j, s: (j, 0)) for part in coming]
            + specs
            + [anywhere()] * len(after),
            out_specs=[pl.BlockSpec((block, count), lambda j, s: (j, 0)) for count in widths],
        ),
        compiler_params=params(),
        cost_estimate=taking(weight),
        name="combine",
    )(where, *coming, *operands, *after)


def total_kernel(cut, counts, *refs):
    coming = [refs[: counts[0]], refs[counts[0] : sum(counts)]]
    out_ref = refs[-1]
    for chunk, start in enumerate((cut, 0)):
        kept_ref = refs[sum(counts) + chunk]
        here = slice(start, start + kept_ref.shape[2])
        total = kept_ref[0]
        for parts in coming:
            total = total + (parts[0][:, here] if len(parts) == 1 else parts[chunk][...]).astype(f32)
        out_ref[0, :, here] = total


def total_grad(a, b, kept, cut):
    units = a[0].shape[0]
    model = sum(part.shape[1] for part in a)
    block = rows_of(units)
    return pl.pallas_call(
        functools.partial(total_kernel, cut, (len(a), len(b))),
        out_shape=jax.ShapeDtypeStruct((1, units, model), f32),
        grid=(units // block,),
        in_specs=[pl.BlockSpec((block, part.shape[1]), lambda j: (j, 0)) for part in (*a, *b)]
        + [
            pl.BlockSpec((1, block, part.shape[2]), functools.partial(lambda last, j: (last, j, 0), part.shape[0] - 1))
            for part in kept
        ],
        out_specs=pl.BlockSpec((1, block, model), lambda j: (0, j, 0)),
        compiler_params=params(),
        cost_estimate=taking(2),
        name="total_grad",
    )(*a, *b, *kept)


def back_kernel(table, model, cut, counts, places, choices, parts, guard, summed, where_ref, *refs):
    keys = [key for choice in choices for key in choice]
    used = sum(counts)
    late = blocks_of(refs[: counts[0]], places[0])
    early = blocks_of(refs[counts[0] : used], places[1])
    number = len(late)
    own_ref, first_ref, rest_ref = refs[used : used + 3]
    weight_refs, used = {}, used + 3
    for key, count in zip(keys, parts):
        weight_refs[key] = refs[used : used + count]
        used += count
    before_ref = refs[used] if summed else None
    outs, sums_ref = refs[-3:-1], refs[-1]
    tokens = late[0].shape[0]
    units = own_ref.shape[1]
    me = where_ref[table["me"]]
    start = late[0].shape[1] - LANES
    eight = lax.broadcasted_iota(jnp.int32, (8, LANES), 1)
    onehot = jnp.where(eight == model % LANES + me, 1.0, 0.0).astype(bf16)
    shards = {key: where_ref[table[("shard",) + key]] for key in keys}
    slots = {key: where_ref[table[("slot",) + key]] for key in keys}
    sums_ref[...] = before_ref[...] if summed else jnp.zeros(sums_ref.shape, f32)

    def whole_weight(key):
        got = weight_refs[key]
        return got[0][...] if len(got) == 1 else jnp.concatenate([got[1][...], got[0][...]], axis=1)

    def work():
        stack, here_valid, here_slot = [], [], []
        for choice in choices:
            weight, valid, slot = whole_weight(choice[0]), shards[choice[0]] >= 0, slots[choice[0]]
            for key in choice[1:]:
                weight = jnp.where(valid, weight, whole_weight(key))
                slot = jnp.where(valid, slot, slots[key])
                valid = jnp.logical_or(valid, shards[key] >= 0)
            stack.append(weight)
            here_valid.append(valid)
            here_slot.append(slot)
        weight = jnp.concatenate(stack, axis=0) if len(stack) > 1 else stack[0]
        for pair in range(0, number, 2):
            both = jnp.concatenate(
                [
                    jnp.concatenate([early[k][...], late[k][:, : model - cut]], axis=1)
                    for k in (pair, pair + 1)
                ],
                axis=0,
            )
            product = dot(weight, both, NT)
            for place in (pair, pair + 1):
                near = place < number // 2
                block = product[:, (place - pair) * tokens : (place - pair + 1) * tokens]
                gate = dot(onehot, late[place][:, start:], NT)[0:1]
                here = pl.ds(place_of(place % (number // 2), number // 2, me, tokens), tokens)
                wide = pl.ds(place_of(place, number // 2, me, tokens), tokens)
                gated = (block * gate).astype(bf16)
                total = jnp.zeros((1, tokens), f32)
                for index, (valid, slot) in enumerate(zip(here_valid, here_slot)):
                    some = slice(index * units, (index + 1) * units)
                    outs[0 if near else 1][index, :, here] = gated[some]
                    if near:
                        hidden = own_ref[slot, :, here].astype(f32)
                    else:
                        hidden = jnp.where(
                            slot == 0,
                            first_ref[0, :, here].astype(f32),
                            rest_ref[jnp.maximum(slot - 1, 0), :, here].astype(f32),
                        )
                    part = jnp.sum(hidden * block[some], axis=0, keepdims=True)
                    total = total + jnp.where(valid, part, 0.0)
                sums_ref[0:1, wide] += total

    if guard:
        pl.when(functools.reduce(jnp.logical_or, [shards[key] >= 0 for key in keys]))(work)
    else:
        work()


def back_part(table, where, late, early, own, first, rest, choices, got, before, guard, after, model):
    units, slots = own.shape[1:]
    arrays, places = zip(late, early)
    counts = [len(part) for part in arrays]
    cut = arrays[1][0].shape[-1]
    keys = [key for choice in choices for key in choice]
    weights = [got[key] for key in keys]
    flat = [part for weight in weights for part in weight]
    half = jax.ShapeDtypeStruct((len(choices), units, slots), bf16)
    summed = before is not None
    operands = [*arrays[0], *arrays[1], own, first, rest, *flat] + ([before] if summed else [])
    outs = [half, half, jax.ShapeDtypeStruct((8, 2 * slots), f32)]
    parts = [len(weight) for weight in weights]
    return pl.pallas_call(
        functools.partial(
            back_kernel, table, model, cut, counts, places, choices, parts, guard, summed
        ),
        out_shape=outs,
        in_specs=[scalars()] + [whole()] * len(operands) + [anywhere()] * len(after),
        out_specs=[whole()] * len(outs),
        compiler_params=params(),
        cost_estimate=taking(6),
        name="back_part",
    )(where, *operands, *after)


def join_kernel(table, choices, where_ref, *refs):
    out_ref, turned, sem = refs[-3:]
    slots, width = turned.shape[1:]
    row = lax.broadcasted_iota(jnp.int32, (slots, slots), 0)
    column = lax.broadcasted_iota(jnp.int32, (slots, slots), 1)
    unit = jnp.where(row == column, 1.0, 0.0).astype(bf16)
    low = where_ref[table["x"]] == 0
    copies = []
    pairs = [
        (refs[2 * group][place], refs[2 * group + 1][place])
        for group in range((len(refs) - 3) // 2)
        for place in range(refs[2 * group].shape[0])
    ]
    for place, (choice, (mine, theirs)) in enumerate(zip(choices, pairs)):
        index = where_ref[table[("shard",) + choice[0]]]
        for key in choice[1:]:
            index = jnp.where(index >= 0, index, where_ref[table[("shard",) + key]])
        both = jnp.concatenate([jnp.where(low, mine, theirs), jnp.where(low, theirs, mine)], axis=0)
        turned[place] = dot(unit, both, NT).astype(bf16)
        here = pl.ds(pl.multiple_of(jnp.maximum(index, 0) * width, LANES), width)
        copy = pltpu.make_async_copy(turned.at[place], out_ref.at[:, here], sem.at[place])
        copies.append((index, copy))
        pl.when(index >= 0)(copy.start)
    for index, copy in copies:
        pl.when(index >= 0)(copy.wait)


def join_hidden(table, where, choices, halves, slots, hidden):
    units = halves[0].shape[1]
    return pl.pallas_call(
        functools.partial(join_kernel, table, choices),
        out_shape=jax.ShapeDtypeStruct((slots, hidden), bf16),
        in_specs=[scalars()] + [whole()] * len(halves),
        out_specs=anywhere(),
        scratch_shapes=[
            pltpu.VMEM((len(choices), slots, 2 * units), bf16),
            pltpu.SemaphoreType.DMA((len(choices),)),
        ],
        compiler_params=params(),
        cost_estimate=taking(2),
        name="join_hidden",
    )(where, *halves)


def logits_kernel(gates_ref, ids_ref, grads_ref, out_ref):
    gates, ids, grads = gates_ref[...], ids_ref[...], grads_ref[...]
    picked = jnp.zeros_like(gates)
    for expert in range(grads.shape[0]):
        picked = picked + jnp.where(ids == expert, grads[expert : expert + 1, :], 0.0)
    out_ref[...] = gates * (picked - jnp.sum(gates * picked, axis=0, keepdims=True))


def logits_grad(gates, ids, grads):
    return pl.pallas_call(
        logits_kernel,
        out_shape=jax.ShapeDtypeStruct(gates.shape, f32),
        in_specs=[whole()] * 3,
        out_specs=whole(),
        compiler_params=params(),
        cost_estimate=taking(1),
        name="logits_grad",
    )(gates, ids, grads)


def per_device_full(grad_out, top_logits, expert_ids, saved_hidden, w_down):
    experts = lax.axis_size("exp")
    groups = lax.axis_size("ctx")
    depth = groups // 2
    tokens, model = grad_out.shape
    slots, hidden = saved_hidden.shape[2:]
    width = pl.cdiv(model + experts, LANES) * LANES
    cut = width // LANES // 2 * LANES

    table, brought, uses = device_scalars(depth, experts)
    where = table.row(lax.axis_index("ctx"), lax.axis_index("exp"))

    def swap(value, x, exp):
        if not exp:
            return lax.ppermute(value, "ctx", [(i, i ^ x) for i in range(groups)])
        if not x:
            return lax.ppermute(value, "exp", [(i, i ^ exp) for i in range(experts)])
        pairs = [(c * experts + e, (c ^ x) * experts + (e ^ exp)) for c in range(groups) for e in range(experts)]
        return lax.ppermute(value, ("ctx", "exp"), pairs)

    def swap_z(value, name, senders=range(depth)):
        first = "AB".index(name)
        pairs = []
        for low in range(first, depth - 1, 2):
            for z, other in ((low, low + 1), (low + 1, low)):
                pairs += [(2 * z + x, 2 * other + x) for x in range(2) if z in senders]
        return lax.ppermute(value, "ctx", pairs)

    got = {(0, "own"): [w_down[0]]}
    for name in "BA":
        got[1, name] = [swap_z(w_down[0], name)]

    late, early, gates = make_rows(grad_out, top_logits, expert_ids, width, cut)
    highs = list(range(2, experts, 2))

    def sides(mine):
        return [mine, swap(mine, 0, 1)]

    late_x = swap(late, 1, 0)
    late_near = [late] + [swap(late, 0, high) for high in highs]
    own, other_first, other_rest = split_hidden(
        table, where, saved_hidden[0, 0], depth, w_down.shape[1], [late]
    )
    other_first = swap(other_first, 1, 0)
    (late_x,) = hold((late_x,), late_near[1:])
    late_mine = late_near + [late_x] + [swap(late_x, 0, high) for high in highs]
    (early,) = hold((early,), [late_x, other_first])
    early_x = swap(early, 1, 0)
    late_rows = sides(pack(late_mine, [early_x]))
    late_rows = (late_rows, [(side, place) for place in range(experts) for side in range(2)])
    early_rows = sides(pack([early, early_x], []))
    places = [(0, 0), (1, 0)]
    for block, base in ((early, 0), (early_x, 1)):
        if base:
            places += [(0, 1), (1, 1)]
        for high in highs:
            places += [(len(early_rows), None), (len(early_rows) + 1, None)]
            early_rows += sides(swap(block, 0, high))
    early_rows = (early_rows, places)
    other_rest = swap(other_rest, 1, 0)

    for name, value in zip("BA", hold([got[1, "B"][0], got[1, "A"][0]], [], FIRST_WEIGHT)):
        got[1, name] = [value]
    chunks = ((late_rows, cut, model - cut), (early_rows, 0, cut))
    after = [early_rows[0][1]]
    first = []
    for rows, start, columns in chunks:
        value = first_sums(
            table, where, rows, late_rows, own, other_first, got[1, "B"][0], model, start, columns, after
        )
        if first:
            (value,) = hold([value], got[2, "A"], NEXT_WEIGHT)
        got.setdefault((2, "A"), []).append(swap_z(value, "A"))
        first.append(
            products(
                table, where, rows, late_rows, own, other_first, 0, model, columns, "first_kept", [value], True
            )
        )
        after = [first[0]]
    marker = value
    got[2, "B"] = [swap_z(got[1, "A"][0], "B")]
    (other_rest,) = hold([other_rest], [], HIDDEN_WEIGHT)

    halves, all_choices, weights_of = [], [], {}
    only_first = max(uses[3, "B"]) <= 0

    def backprop(choices, before, guard, after):
        mine, theirs, sums = back_part(
            table, where, late_rows, early_rows, own, other_first, other_rest, choices,
            {**got, **weights_of}, before, guard, after, model,
        )
        halves.extend([mine, swap(theirs, 1, 0)])
        all_choices.extend(choices)
        return sums

    def forward(turn, name, after):
        coming = got[turn - 1, "B" if name == "A" else "A"]
        coming[:] = hold(coming, after, PASS_WEIGHT)
        others = [z for z in range(depth) if uses[turn, name][z] < 0]
        weights_of[turn, name] = [swap_z(coming[0], name, others)]

    def pass_on(turn, name, after, chunk=None, waited=(), weight=1):
        coming = got[turn - 1, "B" if name == "A" else "A"]
        used = uses[turn, name]
        senders = range(depth)
        if turn == depth - 1 and min(used) < 0 and name == "A" and len(coming) == 1:
            senders = [z for z in range(depth) if used[z] >= 0]
            if chunk is None:
                forward(turn, name, [])
            if set(senders) <= {0, depth - 1}:
                coming = []
        parts, start = (first, rest), cut
        if chunk is not None:
            coming, parts, start = coming[chunk:][:1], (first[chunk:][:1], rest[chunk:][:1]), 0
        values = list(combine(table, where, coming, *parts, turn, name, used, start, after, False, weight))
        if waited:
            values = list(hold(values, list(waited), WAITED_WEIGHT))
        got.setdefault((turn, name), []).extend(swap_z(value, name, senders) for value in values)
        return values[-1]

    def choices_of(turn):
        both = any(b[turn, "A"] >= 0 and b[turn, "B"] >= 0 for b in brought)
        return [[(turn, "A")], [(turn, "B")]] if both else [[(turn, "A"), (turn, "B")]]

    rest = []

    def other_products(chunk, after):
        rows, _, columns = chunks[chunk]
        rest.append(
            products(table, where, rows, late_rows, own, other_rest, 1, model, columns, "rest_kept", after)
        )
        return rest[chunk]

    apart = max(uses[3, "B"]) <= 0 and depth == 4
    if apart:
        marker = pass_on(3, "B", [marker], 0)
        for chunk in range(2):
            marker = other_products(chunk, [marker])
            marker = pass_on(3, "A", [marker], chunk)
        forward(3, "A", [marker, first[1]])
        marker = pass_on(3, "B", [marker], 1)
    else:
        marker = other_products(1, [other_products(0, [marker])])
        marker = pass_on(3, "A", [marker])
        for chunk in range(2):
            marker = pass_on(3, "B", [marker], chunk)
    sums = backprop([[(0, "own")], [(1, "A")], [(1, "B")]], None, False, got[2, "A"][:1])
    sooner = halves[1::2]
    for turn in range(2, depth):
        choices = choices_of(turn)
        if turn > 2:
            waited = [array for key in ((turn, "A"), (turn, "B")) for array in weights_of.get(key, [])]
            if apart and turn + 1 == depth:
                pass_on(depth, "B", [sums], 0, (), ENTER_WEIGHT)
                pass_on(depth, "B", [sums], 1, [*waited, *sooner], LEAVE_WEIGHT)
                marker = pass_on(depth, "A", [sums], weight=LAST_WEIGHT)
            else:
                pass_on(turn + 1, "B", [sums, *sooner, *waited])
                marker = pass_on(turn + 1, "A", [sums])
        sums = backprop(choices, sums, len(choices) == 1, [marker])
    slot_grad = sums[0:1, :slots] + swap(sums[0:1, slots:], 1, 0)
    grads = lax.all_to_all(
        slot_grad.reshape(experts, tokens), "exp", split_axis=0, concat_axis=0, tiled=True
    )
    logit_grad = logits_grad(gates, expert_ids.T, grads)
    hidden_grad = join_hidden(table, where, all_choices, halves, slots, hidden)
    weight_grad = total_grad(got[depth, "A"], got[depth, "B"], rest, cut)
    return (logit_grad.T, hidden_grad[None, None], weight_grad)


def routing_tables(expert_ids, count_experts, capacity):
    columns = jnp.arange(count_experts, dtype=jnp.int32)
    matches = expert_ids[:, :, None] == columns[None, None, :]
    per_token = jnp.sum(matches.astype(jnp.int32), axis=1)
    rank_table = jnp.cumsum(per_token, axis=0) - per_token
    slot_iota = jnp.arange(capacity, dtype=jnp.int32)
    select = (per_token.T[:, None, :] == 1) & (rank_table.T[:, None, :] == slot_iota[None, :, None])
    return (matches.astype(jnp.float32), select)


def per_device_routed(grad_out, top_logits, expert_ids, saved_hidden, w_down):
    count_experts = lax.axis_size("exp")
    slot_count = saved_hidden.shape[2]
    capacity = slot_count // count_experts
    model_width = grad_out.shape[1]
    onehot, select = routing_tables(expert_ids, count_experts, capacity)
    select_wide = select.astype(jnp.float32)
    gate_probs = jax.nn.softmax(top_logits, axis=-1)
    gate_sent = gate_probs.astype(jnp.bfloat16)
    gate_by_expert = jnp.sum(onehot * gate_sent.astype(jnp.float32)[:, :, None], axis=1)
    send_rows = jnp.einsum(
        "ect,td->ecd", select.astype(jnp.bfloat16), grad_out, preferred_element_type=jnp.float32
    ).astype(jnp.bfloat16)
    send_gate = jnp.sum(select_wide * gate_by_expert.T[:, None, :], axis=2).astype(jnp.bfloat16)
    hidden = saved_hidden[0, 0]
    rows_in, gate_in = (
        lax.all_to_all(send_rows, "exp", split_axis=0, concat_axis=0, tiled=True),
        lax.all_to_all(send_gate, "exp", split_axis=0, concat_axis=0, tiled=True),
    )
    flat_rows = rows_in.reshape(slot_count, model_width)
    backprop = lax.dot_general(
        flat_rows,
        lax.all_gather(w_down[0], "ctx", axis=0, tiled=True),
        (((1,), (1,)), ((), ())),
        preferred_element_type=jnp.float32,
    )
    flat_gate = gate_in.reshape(slot_count, 1).astype(jnp.float32)
    hidden_grad = (flat_gate * backprop).astype(jnp.bfloat16)
    slot_grad = jnp.sum(hidden.astype(jnp.float32) * backprop, axis=1)
    scaled = (flat_gate * flat_rows.astype(jnp.float32)).astype(jnp.bfloat16)
    partial_grad = lax.dot_general(
        hidden, scaled, (((0,), (0,)), ((), ())), preferred_element_type=jnp.float32
    )
    weight_grad = lax.psum_scatter(partial_grad, "ctx", scatter_dimension=0, tiled=True)
    returned = lax.all_to_all(
        slot_grad.reshape(count_experts, capacity), "exp", split_axis=0, concat_axis=0, tiled=True
    )
    grad_by_expert = jnp.sum(select_wide * returned[:, :, None], axis=1)
    gate_grad = jnp.sum(onehot * grad_by_expert.T[:, None, :], axis=2)
    logit_grad = gate_probs * (gate_grad - jnp.sum(gate_probs * gate_grad, axis=1, keepdims=True))
    return (logit_grad, hidden_grad.reshape(1, 1, slot_count, -1), weight_grad[None])


def per_device(grad_out, top_logits, expert_ids, saved_hidden, w_down):
    experts = lax.axis_size("exp")
    groups = lax.axis_size("ctx")
    everywhere = top_logits.shape[1] == experts and saved_hidden.shape[2] == experts * grad_out.shape[0]
    plain = experts & (experts - 1) == 0 and groups % 4 == 0 and groups >= 8
    body = per_device_full if everywhere and plain else per_device_routed
    return body(grad_out, top_logits, expert_ids, saved_hidden, w_down)


def solution(mesh):
    return jax.shard_map(
        per_device,
        mesh=mesh,
        in_specs=(
            P(("ctx", "exp"), None),
            P(("ctx", "exp"), None),
            P(("ctx", "exp"), None),
            P("ctx", "exp", None, None),
            P("exp", "ctx", None),
        ),
        out_specs=(P(("ctx", "exp"), None), P("ctx", "exp", None, None), P("exp", "ctx", None)),
        check_vma=False,
    )
```

```python
import functools

import jax
import jax.numpy as jnp
import numpy as np
from jax import lax
from jax.experimental import pallas as pl
from jax.experimental.pallas import tpu as pltpu
from jax.sharding import PartitionSpec as P

LANES = 128
SCALE = 1_000_000
ORDER_WEIGHT = 100
FIRST_WEIGHT = 12_000
NEXT_WEIGHT = 600
HIDDEN_WEIGHT = 5_000
PASS_WEIGHT = 1
WAITED_WEIGHT = 210
ENTER_WEIGHT = 575
LEAVE_WEIGHT = 5_300
LAST_WEIGHT = 90
NT = (((1,), (1,)), ((), ()))
NN = (((1,), (0,)), ((), ()))
f32 = jnp.float32
bf16 = jnp.bfloat16


def dot(a, b, dims):
    return lax.dot_general(a, b, dims, preferred_element_type=f32)


def anywhere():
    return pl.BlockSpec(memory_space=pl.ANY)


def whole():
    return pl.BlockSpec(memory_space=pltpu.VMEM)


def scalars():
    return pl.BlockSpec(memory_space=pltpu.SMEM)


def params(mib=24):
    return pltpu.CompilerParams(vmem_limit_bytes=mib * 1024 * 1024)


def taking(microseconds):
    return pl.CostEstimate(flops=int(microseconds * SCALE), bytes_accessed=int(microseconds * 3e6), transcendentals=0)


def chain_plan(depth):
    products, weights = [], []
    for z in range(depth):
        uses = []
        for turn in range(2, depth + 1):
            if z < depth - 1 and turn >= z + 2:
                uses.append((turn, "AB"[z % 2], depth + 1 + z - turn))
            if z > 0 and turn >= depth - z + 1:
                uses.append((turn, "BA"[z % 2], z + turn - depth - 1))
        products.append(sorted(uses) + [(depth + 1, "own", z)])
        brought = {}
        for turn in range(1, depth):
            for name in "AB":
                index = z + turn if (name == "A") == (z % 2 == 0) else z - turn
                brought[turn, name] = index if 0 <= index < depth else -1
        weights.append(brought)
    return products, weights


class Scalars:
    def __init__(self):
        self.columns = []
        self.names = {}

    def add(self, name, values):
        self.names[name] = len(self.columns)
        self.columns.append(values)

    def __getitem__(self, name):
        return self.names[name]

    def row(self, place, me):
        return jnp.asarray(np.stack(self.columns, axis=-1).astype(np.int32))[place, me]


def device_scalars(depth, experts):
    products, weights = chain_plan(depth)
    table = Scalars()
    along = np.arange(2 * depth)[:, None] + np.zeros((1, experts), np.int32)

    def by_z(values):
        return np.asarray(values)[along // 2]

    table.add("x", along % 2)
    table.add("me", np.zeros_like(along) + np.arange(experts)[None, :])
    table.add(("shard", 0, "own"), along // 2)
    slot_of = [{use[2]: slot for slot, use in enumerate(products[z])} for z in range(depth)]
    for part in range(depth):
        table.add(("slot of", part), by_z([slot_of[z][part] for z in range(depth)]))
    table.add(("slot", 0, "own"), by_z([slot_of[z][z] for z in range(depth)]))
    for turn in range(1, depth):
        for name in "AB":
            shard = [weights[z][turn, name] for z in range(depth)]
            table.add(("shard", turn, name), by_z(shard))
            table.add(("slot", turn, name), by_z([slot_of[z].get(k, 0) for z, k in enumerate(shard)]))
    uses = {}
    for turn in range(2, depth + 1):
        for name in "AB":
            slots = [-1] * depth
            for z in range(depth):
                for slot, use in enumerate(products[z]):
                    if use[:2] == (turn, name):
                        slots[z] = slot
            uses[turn, name] = slots
            table.add(("use", turn, name), by_z(slots))
            limit = max(depth - 3, 0)
            table.add(("block", turn, name), by_z([min(max(slot - 1, 0), limit) for slot in slots]))
    return table, weights, uses


def rows_kernel(cut, grad_hbm, logits_hbm, ids_hbm, late_ref, early_ref, gates_ref, *scratch):
    grad_ref, logits_ref, ids_ref, sems = scratch
    model, tokens = grad_ref.shape
    copies = [
        pltpu.make_async_copy(source, target, sems.at[place])
        for place, (source, target) in enumerate(
            ((grad_hbm, grad_ref), (logits_hbm, logits_ref), (ids_hbm, ids_ref))
        )
    ]
    for copy in copies:
        copy.start()
    for copy in copies:
        copy.wait()
    count = logits_ref.shape[0]
    width = cut + late_ref.shape[1]
    logits = logits_ref[...]
    powers = jnp.exp(logits - jnp.max(logits, axis=0, keepdims=True))
    gates = powers / jnp.sum(powers, axis=0, keepdims=True)
    gates_ref[...] = gates
    sent = gates.astype(bf16).astype(f32)
    ids = ids_ref[...]
    row = lax.broadcasted_iota(jnp.int32, (width - model, tokens), 0)
    extra = jnp.zeros((width - model, tokens), f32)
    for expert in range(count):
        chosen = jnp.sum(jnp.where(ids == expert, sent, 0.0), axis=0, keepdims=True)
        extra = extra + jnp.where(row == expert, chosen, 0.0)
    for start in range(0, width, LANES):
        stop = start + LANES
        if stop <= model:
            block = grad_ref[start:stop, :].astype(f32)
        elif start >= model:
            block = extra[start - model : stop - model, :]
        else:
            block = jnp.concatenate(
                [grad_ref[start:model, :].astype(f32), extra[: stop - model, :]], axis=0
            )
        turned = block.T.astype(bf16)
        if start < cut:
            early_ref[:, start:stop] = turned
        else:
            late_ref[:, start - cut : stop - cut] = turned


def make_rows(grad_out, top_logits, expert_ids, width, cut):
    tokens, model = grad_out.shape
    count = top_logits.shape[1]
    return pl.pallas_call(
        functools.partial(rows_kernel, cut),
        out_shape=(
            jax.ShapeDtypeStruct((tokens, width - cut), bf16),
            jax.ShapeDtypeStruct((tokens, cut), bf16),
            jax.ShapeDtypeStruct((count, tokens), f32),
        ),
        in_specs=[pl.BlockSpec(memory_space=pltpu.HBM)] * 3,
        out_specs=(whole(),) * 3,
        scratch_shapes=[
            pltpu.VMEM((model, tokens), bf16),
            pltpu.VMEM((count, tokens), f32),
            pltpu.VMEM((count, tokens), jnp.int32),
            pltpu.SemaphoreType.DMA((3,)),
        ],
        compiler_params=params(58),
        cost_estimate=taking(2),
        name="make_rows",
    )(grad_out.T, top_logits.T, expert_ids.T)


def pack_kernel(*refs):
    out_ref, sems = refs[-2:]
    copies = []
    for place in range(out_ref.shape[0]):
        copies.append(pltpu.make_async_copy(refs[place], out_ref.at[place], sems.at[place]))
        copies[-1].start()
    for copy in copies:
        copy.wait()


def pack(values, after):
    number = len(values)
    return pl.pallas_call(
        pack_kernel,
        out_shape=jax.ShapeDtypeStruct((number, *values[0].shape), values[0].dtype),
        in_specs=[anywhere()] * (number + len(after)),
        out_specs=anywhere(),
        scratch_shapes=[pltpu.SemaphoreType.DMA((number,))],
        compiler_params=params(),
        cost_estimate=taking(1),
        name="pack_rows",
    )(*values, *after)


def blocks_of(refs, places):
    return [refs[array] if place is None else refs[array].at[place] for array, place in places]


def hold_kernel(*refs):
    del refs


def hold(values, after, weight=0):
    return pl.pallas_call(
        hold_kernel,
        out_shape=tuple(jax.ShapeDtypeStruct(value.shape, value.dtype) for value in values),
        in_specs=[anywhere()] * (len(values) + len(after)),
        out_specs=(anywhere(),) * len(values),
        input_output_aliases={place: place for place in range(len(values))},
        compiler_params=params(),
        cost_estimate=taking(weight),
        name="hold",
    )(*values, *after)


def split_kernel(table, where_ref, hidden_ref, *refs):
    own_ref, first_ref, rest_ref = refs[-3:]
    parts, units, _ = own_ref.shape
    row = lax.broadcasted_iota(jnp.int32, (2 * units, 2 * units), 0)
    column = lax.broadcasted_iota(jnp.int32, (2 * units, 2 * units), 1)
    unit = jnp.where(row == column, 1.0, 0.0).astype(bf16)
    low = where_ref[table["x"]] == 0
    for part in range(parts):
        block = hidden_ref[:, part * 2 * units : (part + 1) * 2 * units]
        turned = dot(unit, block, NT).astype(bf16)
        slot = where_ref[table["slot of", part]]
        other = jnp.where(low, turned[units:], turned[:units])
        own_ref[slot] = jnp.where(low, turned[:units], turned[units:])

        @pl.when(slot == 0)
        def _():
            first_ref[0] = other

        @pl.when(slot != 0)
        def _():
            rest_ref[slot - 1] = other


def split_hidden(table, where, hidden, parts, units, after):
    slots = hidden.shape[0]
    return pl.pallas_call(
        functools.partial(split_kernel, table),
        out_shape=tuple(
            jax.ShapeDtypeStruct((count, units, slots), bf16) for count in (parts, 1, parts - 1)
        ),
        in_specs=[scalars(), whole()] + [anywhere()] * len(after),
        out_specs=(whole(),) * 3,
        compiler_params=params(),
        cost_estimate=taking(2),
        name="split_hidden",
    )(where, hidden, *after)


def place_of(place, count, me, tokens):
    start = (place // count) * count * tokens + ((place % count) ^ me) * tokens
    return pl.multiple_of(start, tokens)


def scale_rows(table, model, where_ref, rows, gated, scaled):
    tokens = rows[0].shape[0]
    me = where_ref[table["me"]]
    lane = lax.broadcasted_iota(jnp.int32, (tokens, LANES), 1)
    for place, block in enumerate(rows):
        here = pl.ds(place_of(place, len(rows) // 2, me, tokens), tokens)
        tile = gated[place][:, gated[place].shape[1] - LANES :]
        picked = jnp.where(lane == model % LANES + me, tile.astype(f32), 0.0)
        gate = jnp.sum(picked, axis=1, keepdims=True)
        scaled[here, :] = (block[:, : scaled.shape[1]].astype(f32) * gate).astype(bf16)


def products_kernel(table, model, counts, places, shards, skip, where_it_runs, where_ref, *refs):
    used = sum(counts)
    rows = blocks_of(refs[: counts[0]], places[0])
    gated = blocks_of(refs[counts[0] : used], places[1])
    own_ref, other_ref = refs[used : used + 2]
    kept_ref, scaled, total_ref, sem = refs[-4:]
    units, slots = own_ref.shape[1:]

    def stacked(ref, offset):
        parts = [ref[offset + shard] for shard in range(shards)]
        return jnp.concatenate(parts, axis=0) if len(parts) > 1 else parts[0]

    def work():
        scale_rows(table, model, where_ref, rows, gated, scaled)
        total = dot(stacked(own_ref, skip), scaled[:slots, :], NN)
        total = total + dot(stacked(other_ref, 0), scaled[slots:, :], NN)
        for shard in range(shards):
            total_ref[shard] = total[shard * units : (shard + 1) * units]
        copy = pltpu.make_async_copy(total_ref, kept_ref, sem)
        copy.start()
        copy.wait()

    at_end = where_ref[table["use", 2, "A"]] == 0
    if where_it_runs == "ends":
        pl.when(at_end)(work)
    elif where_it_runs == "middle":
        pl.when(jnp.logical_not(at_end))(work)
    else:
        work()


def products(
    table, where, rows, gated, own, other, skip, model, width, name, after, where_it_runs="all", before=None
):
    arrays, places = zip(rows, gated)
    counts = [len(part) for part in arrays]
    shards, units, slots = other.shape
    kept = jax.ShapeDtypeStruct((shards, units, width), f32)
    operands = [*arrays[0], *arrays[1], own, other]
    extra = ([] if before is None else [before]) + list(after)
    return pl.pallas_call(
        functools.partial(products_kernel, table, model, counts, places, shards, skip, where_it_runs),
        out_shape=kept,
        in_specs=[scalars()] + [whole()] * len(operands) + [anywhere()] * len(extra),
        out_specs=anywhere(),
        scratch_shapes=[
            pltpu.VMEM((2 * slots, width), bf16),
            pltpu.VMEM(kept.shape, f32),
            pltpu.SemaphoreType.DMA,
        ],
        input_output_aliases={} if before is None else {1 + len(operands): 0},
        compiler_params=params(),
        cost_estimate=taking(1),
        name=name,
    )(where, *operands, *extra)


def first_kernel(table, model, counts, places, start, where_ref, *refs):
    used = sum(counts)
    rows = blocks_of(refs[: counts[0]], places[0])
    gated = blocks_of(refs[counts[0] : used], places[1])
    own_ref, other_ref, coming_ref = refs[used : used + 3]
    out_ref, scaled = refs[-2:]
    slots = own_ref.shape[2]
    ends = where_ref[table["use", 2, "A"]] == 0

    @pl.when(ends)
    def _():
        scale_rows(table, model, where_ref, rows, gated, scaled)
        total = dot(own_ref[0], scaled[:slots, :], NN)
        out_ref[...] = (total + dot(other_ref[0], scaled[slots:, :], NN)).astype(bf16)

    @pl.when(jnp.logical_not(ends))
    def _():
        out_ref[...] = coming_ref[:, start : start + out_ref.shape[1]]


def first_sums(table, where, rows, gated, own, other, coming, model, start, width, after):
    arrays, places = zip(rows, gated)
    counts = [len(part) for part in arrays]
    units, slots = own.shape[1:]
    return pl.pallas_call(
        functools.partial(first_kernel, table, model, counts, places, start),
        out_shape=jax.ShapeDtypeStruct((units, width), bf16),
        in_specs=[scalars()] + [whole()] * (sum(counts) + 3) + [anywhere()] * len(after),
        out_specs=whole(),
        scratch_shapes=[pltpu.VMEM((2 * slots, width), bf16)],
        compiler_params=params(),
        cost_estimate=taking(1),
        name="first_sums",
    )(where, *arrays[0], *arrays[1], own, other, coming, *after)


def rows_of(units):
    return units // 2 if units % 32 == 0 else units


def column_parts(arrays, cut):
    return [(0, arrays[0])] if len(arrays) == 1 else [(cut, arrays[0]), (0, arrays[1])]


def combine_kernel(table, key, cut, counts, sides, where_ref, *refs):
    slot = where_ref[table[key]]
    coming = refs[: counts[0]]
    outs = refs[len(refs) - counts[2] :]
    model = sum(ref.shape[1] for ref in outs)
    spans = [(cut, model), (0, cut)] if cut else [(0, model)]
    for chunk, (start, stop) in enumerate(spans):
        if counts[0] == 0:
            total = jnp.zeros((outs[0].shape[0], stop - start), f32)
        elif counts[0] == 1:
            total = coming[0][:, start:stop].astype(f32)
        else:
            total = coming[chunk][...].astype(f32)
        for number, side in enumerate(sides):
            flag = slot == 0 if side == "first" else slot > 0
            total = total + jnp.where(flag, refs[counts[0] + len(spans) * number + chunk][0], 0.0)
        total = total.astype(bf16)
        if counts[2] == 1:
            outs[0][:, start:stop] = total
        else:
            outs[chunk][...] = total


def combine(table, where, coming, first, rest, turn, name, used, cut, after, chunked=False, weight=1):
    units = first[0].shape[1]
    model = sum(part.shape[2] for part in first)
    block = rows_of(units)
    column = table["block", turn, name]
    sides, operands, specs = [], [], []
    if any(slot == 0 for slot in used):
        sides.append("first")
        operands += first
        specs += [pl.BlockSpec((1, block, part.shape[2]), lambda j, s: (0, j, 0)) for part in first]
    if any(slot > 0 for slot in used):
        sides.append("rest")
        operands += rest
        specs += [pl.BlockSpec((1, block, part.shape[2]), lambda j, s: (s[column], j, 0)) for part in rest]
    widths = [model - cut, cut] if chunked else [model]
    return pl.pallas_call(
        functools.partial(
            combine_kernel, table, ("use", turn, name), cut, (len(coming), len(operands), len(widths)), sides
        ),
        out_shape=[jax.ShapeDtypeStruct((units, count), bf16) for count in widths],
        grid_spec=pltpu.PrefetchScalarGridSpec(
            num_scalar_prefetch=1,
            grid=(units // block,),
            in_specs=[pl.BlockSpec((block, part.shape[1]), lambda j, s: (j, 0)) for part in coming]
            + specs
            + [anywhere()] * len(after),
            out_specs=[pl.BlockSpec((block, count), lambda j, s: (j, 0)) for count in widths],
        ),
        compiler_params=params(),
        cost_estimate=taking(weight),
        name="combine",
    )(where, *coming, *operands, *after)


def total_kernel(cut, counts, *refs):
    coming = [refs[: counts[0]], refs[counts[0] : sum(counts)]]
    out_ref = refs[-1]
    for chunk, start in enumerate((cut, 0)):
        kept_ref = refs[sum(counts) + chunk]
        here = slice(start, start + kept_ref.shape[2])
        total = kept_ref[0]
        for parts in coming:
            total = total + (parts[0][:, here] if len(parts) == 1 else parts[chunk][...]).astype(f32)
        out_ref[0, :, here] = total


def total_grad(a, b, kept, cut):
    units = a[0].shape[0]
    model = sum(part.shape[1] for part in a)
    block = rows_of(units)
    return pl.pallas_call(
        functools.partial(total_kernel, cut, (len(a), len(b))),
        out_shape=jax.ShapeDtypeStruct((1, units, model), f32),
        grid=(units // block,),
        in_specs=[pl.BlockSpec((block, part.shape[1]), lambda j: (j, 0)) for part in (*a, *b)]
        + [
            pl.BlockSpec((1, block, part.shape[2]), functools.partial(lambda last, j: (last, j, 0), part.shape[0] - 1))
            for part in kept
        ],
        out_specs=pl.BlockSpec((1, block, model), lambda j: (0, j, 0)),
        compiler_params=params(),
        cost_estimate=taking(2),
        name="total_grad",
    )(*a, *b, *kept)


def back_kernel(table, model, cut, counts, places, choices, parts, guard, summed, where_ref, *refs):
    keys = [key for choice in choices for key in choice]
    used = sum(counts)
    late = blocks_of(refs[: counts[0]], places[0])
    early = blocks_of(refs[counts[0] : used], places[1])
    number = len(late)
    own_ref, first_ref, rest_ref = refs[used : used + 3]
    weight_refs, used = {}, used + 3
    for key, count in zip(keys, parts):
        weight_refs[key] = refs[used : used + count]
        used += count
    before_ref = refs[used] if summed else None
    outs, sums_ref = refs[-3:-1], refs[-1]
    tokens = late[0].shape[0]
    units = own_ref.shape[1]
    me = where_ref[table["me"]]
    start = late[0].shape[1] - LANES
    eight = lax.broadcasted_iota(jnp.int32, (8, LANES), 1)
    onehot = jnp.where(eight == model % LANES + me, 1.0, 0.0).astype(bf16)
    shards = {key: where_ref[table[("shard",) + key]] for key in keys}
    slots = {key: where_ref[table[("slot",) + key]] for key in keys}
    sums_ref[...] = before_ref[...] if summed else jnp.zeros(sums_ref.shape, f32)

    def whole_weight(key):
        got = weight_refs[key]
        return got[0][...] if len(got) == 1 else jnp.concatenate([got[1][...], got[0][...]], axis=1)

    def work():
        stack, here_valid, here_slot = [], [], []
        for choice in choices:
            weight, valid, slot = whole_weight(choice[0]), shards[choice[0]] >= 0, slots[choice[0]]
            for key in choice[1:]:
                weight = jnp.where(valid, weight, whole_weight(key))
                slot = jnp.where(valid, slot, slots[key])
                valid = jnp.logical_or(valid, shards[key] >= 0)
            stack.append(weight)
            here_valid.append(valid)
            here_slot.append(slot)
        weight = jnp.concatenate(stack, axis=0) if len(stack) > 1 else stack[0]
        for pair in range(0, number, 2):
            both = jnp.concatenate(
                [
                    jnp.concatenate([early[k][...], late[k][:, : model - cut]], axis=1)
                    for k in (pair, pair + 1)
                ],
                axis=0,
            )
            product = dot(weight, both, NT)
            for place in (pair, pair + 1):
                near = place < number // 2
                block = product[:, (place - pair) * tokens : (place - pair + 1) * tokens]
                gate = dot(onehot, late[place][:, start:], NT)[0:1]
                here = pl.ds(place_of(place % (number // 2), number // 2, me, tokens), tokens)
                wide = pl.ds(place_of(place, number // 2, me, tokens), tokens)
                gated = (block * gate).astype(bf16)
                total = jnp.zeros((1, tokens), f32)
                for index, (valid, slot) in enumerate(zip(here_valid, here_slot)):
                    some = slice(index * units, (index + 1) * units)
                    outs[0 if near else 1][index, :, here] = gated[some]
                    if near:
                        hidden = own_ref[slot, :, here].astype(f32)
                    else:
                        hidden = jnp.where(
                            slot == 0,
                            first_ref[0, :, here].astype(f32),
                            rest_ref[jnp.maximum(slot - 1, 0), :, here].astype(f32),
                        )
                    part = jnp.sum(hidden * block[some], axis=0, keepdims=True)
                    total = total + jnp.where(valid, part, 0.0)
                sums_ref[0:1, wide] += total

    if guard:
        pl.when(functools.reduce(jnp.logical_or, [shards[key] >= 0 for key in keys]))(work)
    else:
        work()


def back_part(table, where, late, early, own, first, rest, choices, got, before, guard, after, model):
    units, slots = own.shape[1:]
    arrays, places = zip(late, early)
    counts = [len(part) for part in arrays]
    cut = arrays[1][0].shape[-1]
    keys = [key for choice in choices for key in choice]
    weights = [got[key] for key in keys]
    flat = [part for weight in weights for part in weight]
    half = jax.ShapeDtypeStruct((len(choices), units, slots), bf16)
    summed = before is not None
    operands = [*arrays[0], *arrays[1], own, first, rest, *flat] + ([before] if summed else [])
    outs = [half, half, jax.ShapeDtypeStruct((8, 2 * slots), f32)]
    parts = [len(weight) for weight in weights]
    return pl.pallas_call(
        functools.partial(
            back_kernel, table, model, cut, counts, places, choices, parts, guard, summed
        ),
        out_shape=outs,
        in_specs=[scalars()] + [whole()] * len(operands) + [anywhere()] * len(after),
        out_specs=[whole()] * len(outs),
        compiler_params=params(),
        cost_estimate=taking(6),
        name="back_part",
    )(where, *operands, *after)


def join_kernel(table, choices, where_ref, *refs):
    out_ref, turned, sem = refs[-3:]
    slots, width = turned.shape[1:]
    row = lax.broadcasted_iota(jnp.int32, (slots, slots), 0)
    column = lax.broadcasted_iota(jnp.int32, (slots, slots), 1)
    unit = jnp.where(row == column, 1.0, 0.0).astype(bf16)
    low = where_ref[table["x"]] == 0
    copies = []
    pairs = [
        (refs[2 * group][place], refs[2 * group + 1][place])
        for group in range((len(refs) - 3) // 2)
        for place in range(refs[2 * group].shape[0])
    ]
    for place, (choice, (mine, theirs)) in enumerate(zip(choices, pairs)):
        index = where_ref[table[("shard",) + choice[0]]]
        for key in choice[1:]:
            index = jnp.where(index >= 0, index, where_ref[table[("shard",) + key]])
        both = jnp.concatenate([jnp.where(low, mine, theirs), jnp.where(low, theirs, mine)], axis=0)
        turned[place] = dot(unit, both, NT).astype(bf16)
        here = pl.ds(pl.multiple_of(jnp.maximum(index, 0) * width, LANES), width)
        copy = pltpu.make_async_copy(turned.at[place], out_ref.at[:, here], sem.at[place])
        copies.append((index, copy))
        pl.when(index >= 0)(copy.start)
    for index, copy in copies:
        pl.when(index >= 0)(copy.wait)


def join_hidden(table, where, choices, halves, slots, hidden):
    units = halves[0].shape[1]
    return pl.pallas_call(
        functools.partial(join_kernel, table, choices),
        out_shape=jax.ShapeDtypeStruct((slots, hidden), bf16),
        in_specs=[scalars()] + [whole()] * len(halves),
        out_specs=anywhere(),
        scratch_shapes=[
            pltpu.VMEM((len(choices), slots, 2 * units), bf16),
            pltpu.SemaphoreType.DMA((len(choices),)),
        ],
        compiler_params=params(),
        cost_estimate=taking(2),
        name="join_hidden",
    )(where, *halves)


def logits_kernel(gates_ref, ids_ref, grads_ref, out_ref):
    gates, ids, grads = gates_ref[...], ids_ref[...], grads_ref[...]
    picked = jnp.zeros_like(gates)
    for expert in range(grads.shape[0]):
        picked = picked + jnp.where(ids == expert, grads[expert : expert + 1, :], 0.0)
    out_ref[...] = gates * (picked - jnp.sum(gates * picked, axis=0, keepdims=True))


def logits_grad(gates, ids, grads):
    return pl.pallas_call(
        logits_kernel,
        out_shape=jax.ShapeDtypeStruct(gates.shape, f32),
        in_specs=[whole()] * 3,
        out_specs=whole(),
        compiler_params=params(),
        cost_estimate=taking(1),
        name="logits_grad",
    )(gates, ids, grads)


def per_device_full(grad_out, top_logits, expert_ids, saved_hidden, w_down):
    experts = lax.axis_size("exp")
    groups = lax.axis_size("ctx")
    depth = groups // 2
    tokens, model = grad_out.shape
    slots, hidden = saved_hidden.shape[2:]
    width = pl.cdiv(model + experts, LANES) * LANES
    cut = width // LANES // 2 * LANES

    table, brought, uses = device_scalars(depth, experts)
    where = table.row(lax.axis_index("ctx"), lax.axis_index("exp"))

    def swap(value, x, exp):
        if not exp:
            return lax.ppermute(value, "ctx", [(i, i ^ x) for i in range(groups)])
        if not x:
            return lax.ppermute(value, "exp", [(i, i ^ exp) for i in range(experts)])
        pairs = [(c * experts + e, (c ^ x) * experts + (e ^ exp)) for c in range(groups) for e in range(experts)]
        return lax.ppermute(value, ("ctx", "exp"), pairs)

    def swap_z(value, name, senders=range(depth)):
        first = "AB".index(name)
        pairs = []
        for low in range(first, depth - 1, 2):
            for z, other in ((low, low + 1), (low + 1, low)):
                pairs += [(2 * z + x, 2 * other + x) for x in range(2) if z in senders]
        return lax.ppermute(value, "ctx", pairs)

    got = {(0, "own"): [w_down[0]]}
    for name in "BA":
        got[1, name] = [swap_z(w_down[0], name)]

    late, early, gates = make_rows(grad_out, top_logits, expert_ids, width, cut)
    highs = list(range(2, experts, 2))

    def sides(mine):
        return [mine, swap(mine, 0, 1)]

    late_x = swap(late, 1, 0)
    late_near = [late] + [swap(late, 0, high) for high in highs]
    own, other_first, other_rest = split_hidden(
        table, where, saved_hidden[0, 0], depth, w_down.shape[1], [late]
    )
    other_first = swap(other_first, 1, 0)
    (late_x,) = hold((late_x,), [], ORDER_WEIGHT)
    (late_x,) = hold((late_x,), late_near[1:])
    late_mine = late_near + [late_x] + [swap(late_x, 0, high) for high in highs]
    (early,) = hold((early,), [late_x, other_first])
    early_x = swap(early, 1, 0)
    late_rows = sides(pack(late_mine, [early_x]))
    late_rows = (late_rows, [(side, place) for place in range(experts) for side in range(2)])
    early_rows = sides(pack([early, early_x], []))
    early_far = [[swap(block, 0, high) for high in highs] for block in (early, early_x)]
    other_rest = swap(other_rest, 1, 0)

    got[1, "A"] = list(hold(got[1, "A"], [], ORDER_WEIGHT))
    got[1, "B"] = list(hold(got[1, "B"], got[1, "A"], FIRST_WEIGHT))
    chunks, first = [], []

    def first_chunk(rows, start, columns, after, before):
        chunks.append((rows, start, columns))
        value = first_sums(
            table, where, rows, late_rows, own, other_first, got[1, "B"][0], model, start, columns, after
        )
        if before:
            (value,) = hold([value], before, NEXT_WEIGHT)
        got.setdefault((2, "A"), []).append(swap_z(value, "A"))
        first.append(
            products(
                table, where, rows, late_rows, own, other_first, 0, model, columns, "first_kept", [value], "middle"
            )
        )
        return value

    first_chunk(late_rows, cut, model - cut, [early_rows[1]], [])
    places = []
    for base, blocks in enumerate(early_far):
        places += [(0, base), (1, base)]
        for block in hold(blocks, first):
            places += [(len(early_rows), None), (len(early_rows) + 1, None)]
            mine, theirs = sides(block)
            early_rows += [mine, theirs if base else hold([theirs], [], ORDER_WEIGHT)[0]]
    early_rows = (early_rows, places)
    marker = first_chunk(early_rows, 0, cut, [first[0]], got[2, "A"])
    got[2, "B"] = [swap_z(got[1, "A"][0], "B")]
    (other_rest,) = hold([other_rest], [], HIDDEN_WEIGHT)

    halves, all_choices, weights_of = [], [], {}
    only_first = max(uses[3, "B"]) <= 0

    def backprop(choices, before, guard, after):
        mine, theirs, sums = back_part(
            table, where, late_rows, early_rows, own, other_first, other_rest, choices,
            {**got, **weights_of}, before, guard, after, model,
        )
        halves.extend([mine, swap(theirs, 1, 0)])
        all_choices.extend(choices)
        return sums

    def forward(turn, name, after):
        coming = got[turn - 1, "B" if name == "A" else "A"]
        coming[:] = hold(coming, after, PASS_WEIGHT)
        others = [z for z in range(depth) if uses[turn, name][z] < 0]
        weights_of[turn, name] = [swap_z(coming[0], name, others)]

    def pass_on(turn, name, after, chunk=None, waited=(), weight=1):
        coming = got[turn - 1, "B" if name == "A" else "A"]
        used = uses[turn, name]
        senders = range(depth)
        if turn == depth - 1 and min(used) < 0 and name == "A" and len(coming) == 1:
            senders = [z for z in range(depth) if used[z] >= 0]
            if chunk is None:
                forward(turn, name, [])
            if set(senders) <= {0, depth - 1}:
                coming = []
        parts, start = (first, rest), cut
        if chunk is not None:
            coming, parts, start = coming[chunk:][:1], (first[chunk:][:1], rest[chunk:][:1]), 0
        values = list(combine(table, where, coming, *parts, turn, name, used, start, after, False, weight))
        if waited:
            values = list(hold(values, list(waited), WAITED_WEIGHT))
        got.setdefault((turn, name), []).extend(swap_z(value, name, senders) for value in values)
        return values[-1]

    def choices_of(turn):
        both = any(b[turn, "A"] >= 0 and b[turn, "B"] >= 0 for b in brought)
        return [[(turn, "A")], [(turn, "B")]] if both else [[(turn, "A"), (turn, "B")]]

    rest = []

    def other_products(chunk, after, *where_it_runs):
        rows, _, columns = chunks[chunk]
        return products(
            table, where, rows, late_rows, own, other_rest, 1, model, columns, "rest_kept", after, *where_it_runs
        )

    apart = max(uses[3, "B"]) <= 0 and depth == 4
    if apart:
        marker = pass_on(3, "B", [marker], 0)
        rest.append(other_products(0, [marker]))
        marker = pass_on(3, "A", rest, 0)
        forward(3, "A", [marker])
        rest.append(other_products(1, got[2, "B"], "ends"))
        marker = pass_on(3, "A", rest, 1)
        marker = pass_on(3, "B", [marker], 1)
        rest[1] = other_products(1, [marker], "middle", rest[1])
        marker = rest[1]
    else:
        rest.append(other_products(0, [marker]))
        rest.append(other_products(1, rest))
        marker = pass_on(3, "A", rest)
        for chunk in range(2):
            marker = pass_on(3, "B", [marker], chunk)
    sums = backprop([[(0, "own")], [(1, "A")], [(1, "B")]], None, False, got[2, "A"][:1])
    sooner = halves[1::2]
    for turn in range(2, depth):
        choices = choices_of(turn)
        if turn > 2:
            waited = [array for key in ((turn, "A"), (turn, "B")) for array in weights_of.get(key, [])]
            if apart and turn + 1 == depth:
                pass_on(depth, "B", [sums], 0, (), ENTER_WEIGHT)
                pass_on(depth, "B", [sums], 1, [*waited, *sooner], LEAVE_WEIGHT)
                marker = pass_on(depth, "A", [sums], weight=LAST_WEIGHT)
            else:
                pass_on(turn + 1, "B", [sums, *sooner, *waited])
                marker = pass_on(turn + 1, "A", [sums])
        sums = backprop(choices, sums, len(choices) == 1, [marker])
    slot_grad = sums[0:1, :slots] + swap(sums[0:1, slots:], 1, 0)
    grads = lax.all_to_all(
        slot_grad.reshape(experts, tokens), "exp", split_axis=0, concat_axis=0, tiled=True
    )
    logit_grad = logits_grad(gates, expert_ids.T, grads)
    hidden_grad = join_hidden(table, where, all_choices, halves, slots, hidden)
    weight_grad = total_grad(got[depth, "A"], got[depth, "B"], rest, cut)
    return (logit_grad.T, hidden_grad[None, None], weight_grad)


def routing_tables(expert_ids, count_experts, capacity):
    columns = jnp.arange(count_experts, dtype=jnp.int32)
    matches = expert_ids[:, :, None] == columns[None, None, :]
    per_token = jnp.sum(matches.astype(jnp.int32), axis=1)
    rank_table = jnp.cumsum(per_token, axis=0) - per_token
    slot_iota = jnp.arange(capacity, dtype=jnp.int32)
    select = (per_token.T[:, None, :] == 1) & (rank_table.T[:, None, :] == slot_iota[None, :, None])
    return (matches.astype(jnp.float32), select)


def per_device_routed(grad_out, top_logits, expert_ids, saved_hidden, w_down):
    count_experts = lax.axis_size("exp")
    slot_count = saved_hidden.shape[2]
    capacity = slot_count // count_experts
    model_width = grad_out.shape[1]
    onehot, select = routing_tables(expert_ids, count_experts, capacity)
    select_wide = select.astype(jnp.float32)
    gate_probs = jax.nn.softmax(top_logits, axis=-1)
    gate_sent = gate_probs.astype(jnp.bfloat16)
    gate_by_expert = jnp.sum(onehot * gate_sent.astype(jnp.float32)[:, :, None], axis=1)
    send_rows = jnp.einsum(
        "ect,td->ecd", select.astype(jnp.bfloat16), grad_out, preferred_element_type=jnp.float32
    ).astype(jnp.bfloat16)
    send_gate = jnp.sum(select_wide * gate_by_expert.T[:, None, :], axis=2).astype(jnp.bfloat16)
    hidden = saved_hidden[0, 0]
    rows_in, gate_in = (
        lax.all_to_all(send_rows, "exp", split_axis=0, concat_axis=0, tiled=True),
        lax.all_to_all(send_gate, "exp", split_axis=0, concat_axis=0, tiled=True),
    )
    flat_rows = rows_in.reshape(slot_count, model_width)
    backprop = lax.dot_general(
        flat_rows,
        lax.all_gather(w_down[0], "ctx", axis=0, tiled=True),
        (((1,), (1,)), ((), ())),
        preferred_element_type=jnp.float32,
    )
    flat_gate = gate_in.reshape(slot_count, 1).astype(jnp.float32)
    hidden_grad = (flat_gate * backprop).astype(jnp.bfloat16)
    slot_grad = jnp.sum(hidden.astype(jnp.float32) * backprop, axis=1)
    scaled = (flat_gate * flat_rows.astype(jnp.float32)).astype(jnp.bfloat16)
    partial_grad = lax.dot_general(
        hidden, scaled, (((0,), (0,)), ((), ())), preferred_element_type=jnp.float32
    )
    weight_grad = lax.psum_scatter(partial_grad, "ctx", scatter_dimension=0, tiled=True)
    returned = lax.all_to_all(
        slot_grad.reshape(count_experts, capacity), "exp", split_axis=0, concat_axis=0, tiled=True
    )
    grad_by_expert = jnp.sum(select_wide * returned[:, :, None], axis=1)
    gate_grad = jnp.sum(onehot * grad_by_expert.T[:, None, :], axis=2)
    logit_grad = gate_probs * (gate_grad - jnp.sum(gate_probs * gate_grad, axis=1, keepdims=True))
    return (logit_grad, hidden_grad.reshape(1, 1, slot_count, -1), weight_grad[None])


def per_device(grad_out, top_logits, expert_ids, saved_hidden, w_down):
    experts = lax.axis_size("exp")
    groups = lax.axis_size("ctx")
    everywhere = top_logits.shape[1] == experts and saved_hidden.shape[2] == experts * grad_out.shape[0]
    plain = experts & (experts - 1) == 0 and groups % 4 == 0 and groups >= 8
    body = per_device_full if everywhere and plain else per_device_routed
    return body(grad_out, top_logits, expert_ids, saved_hidden, w_down)


def solution(mesh):
    return jax.shard_map(
        per_device,
        mesh=mesh,
        in_specs=(
            P(("ctx", "exp"), None),
            P(("ctx", "exp"), None),
            P(("ctx", "exp"), None),
            P("ctx", "exp", None, None),
            P("exp", "ctx", None),
        ),
        out_specs=(P(("ctx", "exp"), None), P("ctx", "exp", None, None), P("exp", "ctx", None)),
        check_vma=False,
    )
```

```python
import functools

import jax
import jax.numpy as jnp
import numpy as np
from jax import lax
from jax.experimental import pallas as pl
from jax.experimental.pallas import tpu as pltpu
from jax.sharding import PartitionSpec as P

LANES = 128
SCALE = 1_000_000
ORDER_WEIGHT = 100
FIRST_WEIGHT = 12_000
NEXT_WEIGHT = 600
HIDDEN_WEIGHT = 5_000
PASS_WEIGHT = 1
WAITED_WEIGHT = 210
ENTER_WEIGHT = 575
LEAVE_WEIGHT = 5_300
LAST_WEIGHT = 90
NT = (((1,), (1,)), ((), ()))
NN = (((1,), (0,)), ((), ()))
f32 = jnp.float32
bf16 = jnp.bfloat16


def dot(a, b, dims):
    return lax.dot_general(a, b, dims, preferred_element_type=f32)


def anywhere():
    return pl.BlockSpec(memory_space=pl.ANY)


def whole():
    return pl.BlockSpec(memory_space=pltpu.VMEM)


def scalars():
    return pl.BlockSpec(memory_space=pltpu.SMEM)


def params(mib=24):
    return pltpu.CompilerParams(vmem_limit_bytes=mib * 1024 * 1024)


def taking(microseconds):
    return pl.CostEstimate(flops=int(microseconds * SCALE), bytes_accessed=int(microseconds * 3e6), transcendentals=0)


def chain_plan(depth):
    products, weights = [], []
    for z in range(depth):
        uses = []
        for turn in range(2, depth + 1):
            if z < depth - 1 and turn >= z + 2:
                uses.append((turn, "AB"[z % 2], depth + 1 + z - turn))
            if z > 0 and turn >= depth - z + 1:
                uses.append((turn, "BA"[z % 2], z + turn - depth - 1))
        products.append(sorted(uses) + [(depth + 1, "own", z)])
        brought = {}
        for turn in range(1, depth):
            for name in "AB":
                index = z + turn if (name == "A") == (z % 2 == 0) else z - turn
                brought[turn, name] = index if 0 <= index < depth else -1
        weights.append(brought)
    return products, weights


class Scalars:
    def __init__(self):
        self.columns = []
        self.names = {}

    def add(self, name, values):
        self.names[name] = len(self.columns)
        self.columns.append(values)

    def __getitem__(self, name):
        return self.names[name]

    def row(self, place, me):
        return jnp.asarray(np.stack(self.columns, axis=-1).astype(np.int32))[place, me]


def device_scalars(depth, experts):
    products, weights = chain_plan(depth)
    table = Scalars()
    along = np.arange(2 * depth)[:, None] + np.zeros((1, experts), np.int32)

    def by_z(values):
        return np.asarray(values)[along // 2]

    table.add("x", along % 2)
    table.add("me", np.zeros_like(along) + np.arange(experts)[None, :])
    table.add(("shard", 0, "own"), along // 2)
    slot_of = [{use[2]: slot for slot, use in enumerate(products[z])} for z in range(depth)]
    for part in range(depth):
        table.add(("slot of", part), by_z([slot_of[z][part] for z in range(depth)]))
    table.add(("slot", 0, "own"), by_z([slot_of[z][z] for z in range(depth)]))
    for turn in range(1, depth):
        for name in "AB":
            shard = [weights[z][turn, name] for z in range(depth)]
            table.add(("shard", turn, name), by_z(shard))
            table.add(("slot", turn, name), by_z([slot_of[z].get(k, 0) for z, k in enumerate(shard)]))
    uses = {}
    for turn in range(2, depth + 1):
        for name in "AB":
            slots = [-1] * depth
            for z in range(depth):
                for slot, use in enumerate(products[z]):
                    if use[:2] == (turn, name):
                        slots[z] = slot
            uses[turn, name] = slots
            table.add(("use", turn, name), by_z(slots))
            limit = max(depth - 3, 0)
            table.add(("block", turn, name), by_z([min(max(slot - 1, 0), limit) for slot in slots]))
    return table, weights, uses


def rows_kernel(cut, grad_hbm, logits_hbm, ids_hbm, late_ref, early_ref, gates_ref, *scratch):
    grad_ref, logits_ref, ids_ref, sems = scratch
    model, tokens = grad_ref.shape
    copies = [
        pltpu.make_async_copy(source, target, sems.at[place])
        for place, (source, target) in enumerate(
            ((grad_hbm, grad_ref), (logits_hbm, logits_ref), (ids_hbm, ids_ref))
        )
    ]
    for copy in copies:
        copy.start()
    for copy in copies:
        copy.wait()
    count = logits_ref.shape[0]
    width = cut + late_ref.shape[1]
    logits = logits_ref[...]
    powers = jnp.exp(logits - jnp.max(logits, axis=0, keepdims=True))
    gates = powers / jnp.sum(powers, axis=0, keepdims=True)
    gates_ref[...] = gates
    sent = gates.astype(bf16).astype(f32)
    ids = ids_ref[...]
    row = lax.broadcasted_iota(jnp.int32, (width - model, tokens), 0)
    extra = jnp.zeros((width - model, tokens), f32)
    for expert in range(count):
        chosen = jnp.sum(jnp.where(ids == expert, sent, 0.0), axis=0, keepdims=True)
        extra = extra + jnp.where(row == expert, chosen, 0.0)
    for start in range(0, width, LANES):
        stop = start + LANES
        if stop <= model:
            block = grad_ref[start:stop, :].astype(f32)
        elif start >= model:
            block = extra[start - model : stop - model, :]
        else:
            block = jnp.concatenate(
                [grad_ref[start:model, :].astype(f32), extra[: stop - model, :]], axis=0
            )
        turned = block.T.astype(bf16)
        if start < cut:
            early_ref[:, start:stop] = turned
        else:
            late_ref[:, start - cut : stop - cut] = turned


def make_rows(grad_out, top_logits, expert_ids, width, cut):
    tokens, model = grad_out.shape
    count = top_logits.shape[1]
    return pl.pallas_call(
        functools.partial(rows_kernel, cut),
        out_shape=(
            jax.ShapeDtypeStruct((tokens, width - cut), bf16),
            jax.ShapeDtypeStruct((tokens, cut), bf16),
            jax.ShapeDtypeStruct((count, tokens), f32),
        ),
        in_specs=[pl.BlockSpec(memory_space=pltpu.HBM)] * 3,
        out_specs=(whole(),) * 3,
        scratch_shapes=[
            pltpu.VMEM((model, tokens), bf16),
            pltpu.VMEM((count, tokens), f32),
            pltpu.VMEM((count, tokens), jnp.int32),
            pltpu.SemaphoreType.DMA((3,)),
        ],
        compiler_params=params(58),
        cost_estimate=taking(2),
        name="make_rows",
    )(grad_out.T, top_logits.T, expert_ids.T)


def pack_kernel(*refs):
    out_ref, sems = refs[-2:]
    copies = []
    for place in range(out_ref.shape[0]):
        copies.append(pltpu.make_async_copy(refs[place], out_ref.at[place], sems.at[place]))
        copies[-1].start()
    for copy in copies:
        copy.wait()


def pack(values, after):
    number = len(values)
    return pl.pallas_call(
        pack_kernel,
        out_shape=jax.ShapeDtypeStruct((number, *values[0].shape), values[0].dtype),
        in_specs=[anywhere()] * (number + len(after)),
        out_specs=anywhere(),
        scratch_shapes=[pltpu.SemaphoreType.DMA((number,))],
        compiler_params=params(),
        cost_estimate=taking(1),
        name="pack_rows",
    )(*values, *after)


def blocks_of(refs, places):
    return [refs[array] if place is None else refs[array].at[place] for array, place in places]


def hold_kernel(*refs):
    del refs


def hold(values, after, weight=0):
    return pl.pallas_call(
        hold_kernel,
        out_shape=tuple(jax.ShapeDtypeStruct(value.shape, value.dtype) for value in values),
        in_specs=[anywhere()] * (len(values) + len(after)),
        out_specs=(anywhere(),) * len(values),
        input_output_aliases={place: place for place in range(len(values))},
        compiler_params=params(),
        cost_estimate=taking(weight),
        name="hold",
    )(*values, *after)


def split_kernel(table, where_ref, hidden_ref, *refs):
    own_ref, first_ref, rest_ref = refs[-3:]
    parts, units, _ = own_ref.shape
    row = lax.broadcasted_iota(jnp.int32, (2 * units, 2 * units), 0)
    column = lax.broadcasted_iota(jnp.int32, (2 * units, 2 * units), 1)
    unit = jnp.where(row == column, 1.0, 0.0).astype(bf16)
    low = where_ref[table["x"]] == 0
    for part in range(parts):
        block = hidden_ref[:, part * 2 * units : (part + 1) * 2 * units]
        turned = dot(unit, block, NT).astype(bf16)
        slot = where_ref[table["slot of", part]]
        other = jnp.where(low, turned[units:], turned[:units])
        own_ref[slot] = jnp.where(low, turned[:units], turned[units:])

        @pl.when(slot == 0)
        def _():
            first_ref[0] = other

        @pl.when(slot != 0)
        def _():
            rest_ref[slot - 1] = other


def split_hidden(table, where, hidden, parts, units, after):
    slots = hidden.shape[0]
    return pl.pallas_call(
        functools.partial(split_kernel, table),
        out_shape=tuple(
            jax.ShapeDtypeStruct((count, units, slots), bf16) for count in (parts, 1, parts - 1)
        ),
        in_specs=[scalars(), whole()] + [anywhere()] * len(after),
        out_specs=(whole(),) * 3,
        compiler_params=params(),
        cost_estimate=taking(2),
        name="split_hidden",
    )(where, hidden, *after)


def place_of(place, count, me, tokens):
    start = (place // count) * count * tokens + ((place % count) ^ me) * tokens
    return pl.multiple_of(start, tokens)


def scale_rows(table, model, where_ref, rows, gated, scaled):
    tokens = rows[0].shape[0]
    me = where_ref[table["me"]]
    lane = lax.broadcasted_iota(jnp.int32, (tokens, LANES), 1)
    for place, block in enumerate(rows):
        here = pl.ds(place_of(place, len(rows) // 2, me, tokens), tokens)
        tile = gated[place][:, gated[place].shape[1] - LANES :]
        picked = jnp.where(lane == model % LANES + me, tile.astype(f32), 0.0)
        gate = jnp.sum(picked, axis=1, keepdims=True)
        scaled[here, :] = (block[:, : scaled.shape[1]].astype(f32) * gate).astype(bf16)


def products_kernel(table, model, counts, places, shards, skip, where_it_runs, where_ref, *refs):
    used = sum(counts)
    rows = blocks_of(refs[: counts[0]], places[0])
    gated = blocks_of(refs[counts[0] : used], places[1])
    own_ref, other_ref = refs[used : used + 2]
    kept_ref, scaled, total_ref, sem = refs[-4:]
    units, slots = own_ref.shape[1:]

    def stacked(ref, offset):
        parts = [ref[offset + shard] for shard in range(shards)]
        return jnp.concatenate(parts, axis=0) if len(parts) > 1 else parts[0]

    def work():
        scale_rows(table, model, where_ref, rows, gated, scaled)
        total = dot(stacked(own_ref, skip), scaled[:slots, :], NN)
        total = total + dot(stacked(other_ref, 0), scaled[slots:, :], NN)
        for shard in range(shards):
            total_ref[shard] = total[shard * units : (shard + 1) * units]
        copy = pltpu.make_async_copy(total_ref, kept_ref, sem)
        copy.start()
        copy.wait()

    at_end = where_ref[table["use", 2, "A"]] == 0
    if where_it_runs == "ends":
        pl.when(at_end)(work)
    elif where_it_runs == "middle":
        pl.when(jnp.logical_not(at_end))(work)
    else:
        work()


def products(
    table, where, rows, gated, own, other, skip, model, width, name, after, where_it_runs="all", before=None
):
    arrays, places = zip(rows, gated)
    counts = [len(part) for part in arrays]
    shards, units, slots = other.shape
    kept = jax.ShapeDtypeStruct((shards, units, width), f32)
    operands = [*arrays[0], *arrays[1], own, other]
    extra = ([] if before is None else [before]) + list(after)
    return pl.pallas_call(
        functools.partial(products_kernel, table, model, counts, places, shards, skip, where_it_runs),
        out_shape=kept,
        in_specs=[scalars()] + [whole()] * len(operands) + [anywhere()] * len(extra),
        out_specs=anywhere(),
        scratch_shapes=[
            pltpu.VMEM((2 * slots, width), bf16),
            pltpu.VMEM(kept.shape, f32),
            pltpu.SemaphoreType.DMA,
        ],
        input_output_aliases={} if before is None else {1 + len(operands): 0},
        compiler_params=params(),
        cost_estimate=taking(1),
        name=name,
    )(where, *operands, *extra)


def first_kernel(table, model, counts, places, start, where_ref, *refs):
    used = sum(counts)
    rows = blocks_of(refs[: counts[0]], places[0])
    gated = blocks_of(refs[counts[0] : used], places[1])
    own_ref, other_ref, coming_ref = refs[used : used + 3]
    out_ref, scaled = refs[-2:]
    slots = own_ref.shape[2]
    ends = where_ref[table["use", 2, "A"]] == 0

    @pl.when(ends)
    def _():
        scale_rows(table, model, where_ref, rows, gated, scaled)
        total = dot(own_ref[0], scaled[:slots, :], NN)
        out_ref[...] = (total + dot(other_ref[0], scaled[slots:, :], NN)).astype(bf16)

    @pl.when(jnp.logical_not(ends))
    def _():
        out_ref[...] = coming_ref[:, start : start + out_ref.shape[1]]


def first_sums(table, where, rows, gated, own, other, coming, model, start, width, after):
    arrays, places = zip(rows, gated)
    counts = [len(part) for part in arrays]
    units, slots = own.shape[1:]
    return pl.pallas_call(
        functools.partial(first_kernel, table, model, counts, places, start),
        out_shape=jax.ShapeDtypeStruct((units, width), bf16),
        in_specs=[scalars()] + [whole()] * (sum(counts) + 3) + [anywhere()] * len(after),
        out_specs=whole(),
        scratch_shapes=[pltpu.VMEM((2 * slots, width), bf16)],
        compiler_params=params(),
        cost_estimate=taking(1),
        name="first_sums",
    )(where, *arrays[0], *arrays[1], own, other, coming, *after)


def rows_of(units):
    return units // 2 if units % 32 == 0 else units


def column_parts(arrays, cut):
    return [(0, arrays[0])] if len(arrays) == 1 else [(cut, arrays[0]), (0, arrays[1])]


def combine_kernel(table, key, cut, counts, sides, where_ref, *refs):
    slot = where_ref[table[key]]
    coming = refs[: counts[0]]
    outs = refs[len(refs) - counts[2] :]
    model = sum(ref.shape[1] for ref in outs)
    spans = [(cut, model), (0, cut)] if cut else [(0, model)]
    for chunk, (start, stop) in enumerate(spans):
        if counts[0] == 0:
            total = jnp.zeros((outs[0].shape[0], stop - start), f32)
        elif counts[0] == 1:
            total = coming[0][:, start:stop].astype(f32)
        else:
            total = coming[chunk][...].astype(f32)
        for number, side in enumerate(sides):
            flag = slot == 0 if side == "first" else slot > 0
            total = total + jnp.where(flag, refs[counts[0] + len(spans) * number + chunk][0], 0.0)
        total = total.astype(bf16)
        if counts[2] == 1:
            outs[0][:, start:stop] = total
        else:
            outs[chunk][...] = total


def combine(table, where, coming, first, rest, turn, name, used, cut, after, chunked=False, weight=1):
    units = first[0].shape[1]
    model = sum(part.shape[2] for part in first)
    block = rows_of(units)
    column = table["block", turn, name]
    sides, operands, specs = [], [], []
    if any(slot == 0 for slot in used):
        sides.append("first")
        operands += first
        specs += [pl.BlockSpec((1, block, part.shape[2]), lambda j, s: (0, j, 0)) for part in first]
    if any(slot > 0 for slot in used):
        sides.append("rest")
        operands += rest
        specs += [pl.BlockSpec((1, block, part.shape[2]), lambda j, s: (s[column], j, 0)) for part in rest]
    widths = [model - cut, cut] if chunked else [model]
    return pl.pallas_call(
        functools.partial(
            combine_kernel, table, ("use", turn, name), cut, (len(coming), len(operands), len(widths)), sides
        ),
        out_shape=[jax.ShapeDtypeStruct((units, count), bf16) for count in widths],
        grid_spec=pltpu.PrefetchScalarGridSpec(
            num_scalar_prefetch=1,
            grid=(units // block,),
            in_specs=[pl.BlockSpec((block, part.shape[1]), lambda j, s: (j, 0)) for part in coming]
            + specs
            + [anywhere()] * len(after),
            out_specs=[pl.BlockSpec((block, count), lambda j, s: (j, 0)) for count in widths],
        ),
        compiler_params=params(),
        cost_estimate=taking(weight),
        name="combine",
    )(where, *coming, *operands, *after)


def total_kernel(cut, counts, *refs):
    coming = [refs[: counts[0]], refs[counts[0] : sum(counts)]]
    out_ref = refs[-1]
    for chunk, start in enumerate((cut, 0)):
        kept_ref = refs[sum(counts) + chunk]
        here = slice(start, start + kept_ref.shape[2])
        total = kept_ref[0]
        for parts in coming:
            total = total + (parts[0][:, here] if len(parts) == 1 else parts[chunk][...]).astype(f32)
        out_ref[0, :, here] = total


def total_grad(a, b, kept, cut):
    units = a[0].shape[0]
    model = sum(part.shape[1] for part in a)
    block = rows_of(units)
    return pl.pallas_call(
        functools.partial(total_kernel, cut, (len(a), len(b))),
        out_shape=jax.ShapeDtypeStruct((1, units, model), f32),
        grid=(units // block,),
        in_specs=[pl.BlockSpec((block, part.shape[1]), lambda j: (j, 0)) for part in (*a, *b)]
        + [
            pl.BlockSpec((1, block, part.shape[2]), functools.partial(lambda last, j: (last, j, 0), part.shape[0] - 1))
            for part in kept
        ],
        out_specs=pl.BlockSpec((1, block, model), lambda j: (0, j, 0)),
        compiler_params=params(),
        cost_estimate=taking(2),
        name="total_grad",
    )(*a, *b, *kept)


def back_kernel(table, model, cut, counts, places, choices, parts, guard, summed, where_ref, *refs):
    keys = [key for choice in choices for key in choice]
    used = sum(counts)
    late = blocks_of(refs[: counts[0]], places[0])
    early = blocks_of(refs[counts[0] : used], places[1])
    number = len(late)
    own_ref, first_ref, rest_ref = refs[used : used + 3]
    weight_refs, used = {}, used + 3
    for key, count in zip(keys, parts):
        weight_refs[key] = refs[used : used + count]
        used += count
    before_ref = refs[used] if summed else None
    outs, sums_ref = refs[-3:-1], refs[-1]
    tokens = late[0].shape[0]
    units = own_ref.shape[1]
    me = where_ref[table["me"]]
    start = late[0].shape[1] - LANES
    eight = lax.broadcasted_iota(jnp.int32, (8, LANES), 1)
    onehot = jnp.where(eight == model % LANES + me, 1.0, 0.0).astype(bf16)
    shards = {key: where_ref[table[("shard",) + key]] for key in keys}
    slots = {key: where_ref[table[("slot",) + key]] for key in keys}
    sums_ref[...] = before_ref[...] if summed else jnp.zeros(sums_ref.shape, f32)

    def whole_weight(key):
        got = weight_refs[key]
        return got[0][...] if len(got) == 1 else jnp.concatenate([got[1][...], got[0][...]], axis=1)

    def work():
        stack, here_valid, here_slot = [], [], []
        for choice in choices:
            weight, valid, slot = whole_weight(choice[0]), shards[choice[0]] >= 0, slots[choice[0]]
            for key in choice[1:]:
                weight = jnp.where(valid, weight, whole_weight(key))
                slot = jnp.where(valid, slot, slots[key])
                valid = jnp.logical_or(valid, shards[key] >= 0)
            stack.append(weight)
            here_valid.append(valid)
            here_slot.append(slot)
        weight = jnp.concatenate(stack, axis=0) if len(stack) > 1 else stack[0]
        for pair in range(0, number, 2):
            both = jnp.concatenate(
                [
                    jnp.concatenate([early[k][...], late[k][:, : model - cut]], axis=1)
                    for k in (pair, pair + 1)
                ],
                axis=0,
            )
            product = dot(weight, both, NT)
            for place in (pair, pair + 1):
                near = place < number // 2
                block = product[:, (place - pair) * tokens : (place - pair + 1) * tokens]
                gate = dot(onehot, late[place][:, start:], NT)[0:1]
                here = pl.ds(place_of(place % (number // 2), number // 2, me, tokens), tokens)
                wide = pl.ds(place_of(place, number // 2, me, tokens), tokens)
                gated = (block * gate).astype(bf16)
                total = jnp.zeros((1, tokens), f32)
                for index, (valid, slot) in enumerate(zip(here_valid, here_slot)):
                    some = slice(index * units, (index + 1) * units)
                    outs[0 if near else 1][index, :, here] = gated[some]
                    if near:
                        hidden = own_ref[slot, :, here].astype(f32)
                    else:
                        hidden = jnp.where(
                            slot == 0,
                            first_ref[0, :, here].astype(f32),
                            rest_ref[jnp.maximum(slot - 1, 0), :, here].astype(f32),
                        )
                    part = jnp.sum(hidden * block[some], axis=0, keepdims=True)
                    total = total + jnp.where(valid, part, 0.0)
                sums_ref[0:1, wide] += total

    if guard:
        pl.when(functools.reduce(jnp.logical_or, [shards[key] >= 0 for key in keys]))(work)
    else:
        work()


def back_part(table, where, late, early, own, first, rest, choices, got, before, guard, after, model):
    units, slots = own.shape[1:]
    arrays, places = zip(late, early)
    counts = [len(part) for part in arrays]
    cut = arrays[1][0].shape[-1]
    keys = [key for choice in choices for key in choice]
    weights = [got[key] for key in keys]
    flat = [part for weight in weights for part in weight]
    half = jax.ShapeDtypeStruct((len(choices), units, slots), bf16)
    summed = before is not None
    operands = [*arrays[0], *arrays[1], own, first, rest, *flat] + ([before] if summed else [])
    outs = [half, half, jax.ShapeDtypeStruct((8, 2 * slots), f32)]
    parts = [len(weight) for weight in weights]
    return pl.pallas_call(
        functools.partial(
            back_kernel, table, model, cut, counts, places, choices, parts, guard, summed
        ),
        out_shape=outs,
        in_specs=[scalars()] + [whole()] * len(operands) + [anywhere()] * len(after),
        out_specs=[whole()] * len(outs),
        compiler_params=params(),
        cost_estimate=taking(6),
        name="back_part",
    )(where, *operands, *after)


def join_kernel(table, choices, where_ref, *refs):
    out_ref, turned, sem = refs[-3:]
    slots, width = turned.shape[1:]
    row = lax.broadcasted_iota(jnp.int32, (slots, slots), 0)
    column = lax.broadcasted_iota(jnp.int32, (slots, slots), 1)
    unit = jnp.where(row == column, 1.0, 0.0).astype(bf16)
    low = where_ref[table["x"]] == 0
    copies = []
    pairs = [
        (refs[2 * group][place], refs[2 * group + 1][place])
        for group in range((len(refs) - 3) // 2)
        for place in range(refs[2 * group].shape[0])
    ]
    for place, (choice, (mine, theirs)) in enumerate(zip(choices, pairs)):
        index = where_ref[table[("shard",) + choice[0]]]
        for key in choice[1:]:
            index = jnp.where(index >= 0, index, where_ref[table[("shard",) + key]])
        both = jnp.concatenate([jnp.where(low, mine, theirs), jnp.where(low, theirs, mine)], axis=0)
        turned[place] = dot(unit, both, NT).astype(bf16)
        here = pl.ds(pl.multiple_of(jnp.maximum(index, 0) * width, LANES), width)
        copy = pltpu.make_async_copy(turned.at[place], out_ref.at[:, here], sem.at[place])
        copies.append((index, copy))
        pl.when(index >= 0)(copy.start)
    for index, copy in copies:
        pl.when(index >= 0)(copy.wait)


def join_hidden(table, where, choices, halves, slots, hidden):
    units = halves[0].shape[1]
    return pl.pallas_call(
        functools.partial(join_kernel, table, choices),
        out_shape=jax.ShapeDtypeStruct((slots, hidden), bf16),
        in_specs=[scalars()] + [whole()] * len(halves),
        out_specs=anywhere(),
        scratch_shapes=[
            pltpu.VMEM((len(choices), slots, 2 * units), bf16),
            pltpu.SemaphoreType.DMA((len(choices),)),
        ],
        compiler_params=params(),
        cost_estimate=taking(2),
        name="join_hidden",
    )(where, *halves)


def logits_kernel(gates_ref, ids_ref, grads_ref, out_ref):
    gates, ids, grads = gates_ref[...], ids_ref[...], grads_ref[...]
    picked = jnp.zeros_like(gates)
    for expert in range(grads.shape[0]):
        picked = picked + jnp.where(ids == expert, grads[expert : expert + 1, :], 0.0)
    out_ref[...] = gates * (picked - jnp.sum(gates * picked, axis=0, keepdims=True))


def logits_grad(gates, ids, grads):
    return pl.pallas_call(
        logits_kernel,
        out_shape=jax.ShapeDtypeStruct(gates.shape, f32),
        in_specs=[whole()] * 3,
        out_specs=whole(),
        compiler_params=params(),
        cost_estimate=taking(1),
        name="logits_grad",
    )(gates, ids, grads)


def per_device_full(grad_out, top_logits, expert_ids, saved_hidden, w_down):
    experts = lax.axis_size("exp")
    groups = lax.axis_size("ctx")
    depth = groups // 2
    tokens, model = grad_out.shape
    slots, hidden = saved_hidden.shape[2:]
    width = pl.cdiv(model + experts, LANES) * LANES
    cut = width // LANES // 2 * LANES

    table, brought, uses = device_scalars(depth, experts)
    where = table.row(lax.axis_index("ctx"), lax.axis_index("exp"))

    def swap(value, x, exp):
        if not exp:
            return lax.ppermute(value, "ctx", [(i, i ^ x) for i in range(groups)])
        if not x:
            return lax.ppermute(value, "exp", [(i, i ^ exp) for i in range(experts)])
        pairs = [(c * experts + e, (c ^ x) * experts + (e ^ exp)) for c in range(groups) for e in range(experts)]
        return lax.ppermute(value, ("ctx", "exp"), pairs)

    def swap_z(value, name, senders=range(depth)):
        first = "AB".index(name)
        pairs = []
        for low in range(first, depth - 1, 2):
            for z, other in ((low, low + 1), (low + 1, low)):
                pairs += [(2 * z + x, 2 * other + x) for x in range(2) if z in senders]
        return lax.ppermute(value, "ctx", pairs)

    got = {(0, "own"): [w_down[0]]}
    for name in "BA":
        got[1, name] = [swap_z(w_down[0], name)]

    late, early, gates = make_rows(grad_out, top_logits, expert_ids, width, cut)
    highs = list(range(2, experts, 2))

    def sides(mine):
        return [mine, swap(mine, 0, 1)]

    late_x = swap(late, 1, 0)
    late_near = [late] + [swap(late, 0, high) for high in highs]
    own, other_first, other_rest = split_hidden(
        table, where, saved_hidden[0, 0], depth, w_down.shape[1], [late]
    )
    other_first = swap(other_first, 1, 0)
    (late_x,) = hold((late_x,), [], ORDER_WEIGHT)
    (late_x,) = hold((late_x,), late_near[1:])
    late_mine = late_near + [late_x] + [swap(late_x, 0, high) for high in highs]
    (early,) = hold((early,), [late_x, other_first])
    early_x = swap(early, 1, 0)
    late_rows = sides(pack(late_mine, [early_x]))
    late_rows = (late_rows, [(side, place) for place in range(experts) for side in range(2)])
    early_rows = sides(pack([early, early_x], []))
    early_far = [[swap(block, 0, high) for high in highs] for block in (early, early_x)]
    other_rest = swap(other_rest, 1, 0)

    got[1, "A"] = list(hold(got[1, "A"], [], ORDER_WEIGHT))
    got[1, "B"] = list(hold(got[1, "B"], got[1, "A"], FIRST_WEIGHT))
    chunks, first = [], []

    def first_chunk(rows, start, columns, after, before):
        chunks.append((rows, start, columns))
        value = first_sums(
            table, where, rows, late_rows, own, other_first, got[1, "B"][0], model, start, columns, after
        )
        if before:
            (value,) = hold([value], before, NEXT_WEIGHT)
        got.setdefault((2, "A"), []).append(swap_z(value, "A"))
        first.append(
            products(
                table, where, rows, late_rows, own, other_first, 0, model, columns, "first_kept", [value], "middle"
            )
        )
        return value

    first_chunk(late_rows, cut, model - cut, [early_rows[1]], [])
    places = []
    for base, blocks in enumerate(early_far):
        places += [(0, base), (1, base)]
        for block in hold(blocks, first):
            places += [(len(early_rows), None), (len(early_rows) + 1, None)]
            mine, theirs = sides(block)
            early_rows += [mine, theirs if base else hold([theirs], [], ORDER_WEIGHT)[0]]
    early_rows = (early_rows, places)
    marker = first_chunk(early_rows, 0, cut, [first[0]], got[2, "A"])
    got[2, "B"] = [swap_z(got[1, "A"][0], "B")]
    (other_rest,) = hold([other_rest], [], HIDDEN_WEIGHT)

    halves, all_choices, weights_of = [], [], {}
    only_first = max(uses[3, "B"]) <= 0

    def backprop(choices, before, guard, after):
        mine, theirs, sums = back_part(
            table, where, late_rows, early_rows, own, other_first, other_rest, choices,
            {**got, **weights_of}, before, guard, after, model,
        )
        halves.extend([mine, swap(theirs, 1, 0)])
        all_choices.extend(choices)
        return sums

    def forward(turn, name, after):
        coming = got[turn - 1, "B" if name == "A" else "A"]
        coming[:] = hold(coming, after, PASS_WEIGHT)
        others = [z for z in range(depth) if uses[turn, name][z] < 0]
        weights_of[turn, name] = [swap_z(coming[0], name, others)]

    def pass_on(turn, name, after, chunk=None, waited=(), weight=1):
        coming = got[turn - 1, "B" if name == "A" else "A"]
        used = uses[turn, name]
        senders = range(depth)
        if turn == depth - 1 and min(used) < 0 and name == "A" and len(coming) == 1:
            senders = [z for z in range(depth) if used[z] >= 0]
            if chunk is None:
                forward(turn, name, [])
            if set(senders) <= {0, depth - 1}:
                coming = []
        parts, start = (first, rest), cut
        if chunk is not None:
            coming, parts, start = coming[chunk:][:1], (first[chunk:][:1], rest[chunk:][:1]), 0
        values = list(combine(table, where, coming, *parts, turn, name, used, start, after, False, weight))
        if waited:
            values = list(hold(values, list(waited), WAITED_WEIGHT))
        got.setdefault((turn, name), []).extend(swap_z(value, name, senders) for value in values)
        return values[-1]

    def choices_of(turn):
        both = any(b[turn, "A"] >= 0 and b[turn, "B"] >= 0 for b in brought)
        return [[(turn, "A")], [(turn, "B")]] if both else [[(turn, "A"), (turn, "B")]]

    rest = []

    def other_products(chunk, after, *where_it_runs):
        rows, _, columns = chunks[chunk]
        return products(
            table, where, rows, late_rows, own, other_rest, 1, model, columns, "rest_kept", after, *where_it_runs
        )

    apart = max(uses[3, "B"]) <= 0 and depth == 4
    if apart:
        marker = pass_on(3, "B", [marker], 0)
        rest.append(other_products(0, [marker]))
        marker = pass_on(3, "A", rest, 0)
        forward(3, "A", [marker, first[1]])
        rest.append(other_products(1, got[2, "B"], "ends"))
        marker = pass_on(3, "A", rest, 1)
        marker = pass_on(3, "B", [marker], 1)
        rest[1] = other_products(1, [marker], "middle", rest[1])
        marker = rest[1]
    else:
        rest.append(other_products(0, [marker]))
        rest.append(other_products(1, rest))
        marker = pass_on(3, "A", rest)
        for chunk in range(2):
            marker = pass_on(3, "B", [marker], chunk)
    sums = backprop([[(0, "own")], [(1, "A")], [(1, "B")]], None, False, got[2, "A"][:1])
    sooner = halves[1::2]
    for turn in range(2, depth):
        choices = choices_of(turn)
        if turn > 2:
            waited = [array for key in ((turn, "A"), (turn, "B")) for array in weights_of.get(key, [])]
            if apart and turn + 1 == depth:
                pass_on(depth, "B", [sums], 0, (), ENTER_WEIGHT)
                pass_on(depth, "B", [sums], 1, [*waited, *sooner], LEAVE_WEIGHT)
                marker = pass_on(depth, "A", [sums], weight=LAST_WEIGHT)
            else:
                pass_on(turn + 1, "B", [sums, *sooner, *waited])
                marker = pass_on(turn + 1, "A", [sums])
        sums = backprop(choices, sums, len(choices) == 1, [marker])
    slot_grad = sums[0:1, :slots] + swap(sums[0:1, slots:], 1, 0)
    grads = lax.all_to_all(
        slot_grad.reshape(experts, tokens), "exp", split_axis=0, concat_axis=0, tiled=True
    )
    logit_grad = logits_grad(gates, expert_ids.T, grads)
    hidden_grad = join_hidden(table, where, all_choices, halves, slots, hidden)
    weight_grad = total_grad(got[depth, "A"], got[depth, "B"], rest, cut)
    return (logit_grad.T, hidden_grad[None, None], weight_grad)


def routing_tables(expert_ids, count_experts, capacity):
    columns = jnp.arange(count_experts, dtype=jnp.int32)
    matches = expert_ids[:, :, None] == columns[None, None, :]
    per_token = jnp.sum(matches.astype(jnp.int32), axis=1)
    rank_table = jnp.cumsum(per_token, axis=0) - per_token
    slot_iota = jnp.arange(capacity, dtype=jnp.int32)
    select = (per_token.T[:, None, :] == 1) & (rank_table.T[:, None, :] == slot_iota[None, :, None])
    return (matches.astype(jnp.float32), select)


def per_device_routed(grad_out, top_logits, expert_ids, saved_hidden, w_down):
    count_experts = lax.axis_size("exp")
    slot_count = saved_hidden.shape[2]
    capacity = slot_count // count_experts
    model_width = grad_out.shape[1]
    onehot, select = routing_tables(expert_ids, count_experts, capacity)
    select_wide = select.astype(jnp.float32)
    gate_probs = jax.nn.softmax(top_logits, axis=-1)
    gate_sent = gate_probs.astype(jnp.bfloat16)
    gate_by_expert = jnp.sum(onehot * gate_sent.astype(jnp.float32)[:, :, None], axis=1)
    send_rows = jnp.einsum(
        "ect,td->ecd", select.astype(jnp.bfloat16), grad_out, preferred_element_type=jnp.float32
    ).astype(jnp.bfloat16)
    send_gate = jnp.sum(select_wide * gate_by_expert.T[:, None, :], axis=2).astype(jnp.bfloat16)
    hidden = saved_hidden[0, 0]
    rows_in, gate_in = (
        lax.all_to_all(send_rows, "exp", split_axis=0, concat_axis=0, tiled=True),
        lax.all_to_all(send_gate, "exp", split_axis=0, concat_axis=0, tiled=True),
    )
    flat_rows = rows_in.reshape(slot_count, model_width)
    backprop = lax.dot_general(
        flat_rows,
        lax.all_gather(w_down[0], "ctx", axis=0, tiled=True),
        (((1,), (1,)), ((), ())),
        preferred_element_type=jnp.float32,
    )
    flat_gate = gate_in.reshape(slot_count, 1).astype(jnp.float32)
    hidden_grad = (flat_gate * backprop).astype(jnp.bfloat16)
    slot_grad = jnp.sum(hidden.astype(jnp.float32) * backprop, axis=1)
    scaled = (flat_gate * flat_rows.astype(jnp.float32)).astype(jnp.bfloat16)
    partial_grad = lax.dot_general(
        hidden, scaled, (((0,), (0,)), ((), ())), preferred_element_type=jnp.float32
    )
    weight_grad = lax.psum_scatter(partial_grad, "ctx", scatter_dimension=0, tiled=True)
    returned = lax.all_to_all(
        slot_grad.reshape(count_experts, capacity), "exp", split_axis=0, concat_axis=0, tiled=True
    )
    grad_by_expert = jnp.sum(select_wide * returned[:, :, None], axis=1)
    gate_grad = jnp.sum(onehot * grad_by_expert.T[:, None, :], axis=2)
    logit_grad = gate_probs * (gate_grad - jnp.sum(gate_probs * gate_grad, axis=1, keepdims=True))
    return (logit_grad, hidden_grad.reshape(1, 1, slot_count, -1), weight_grad[None])


def per_device(grad_out, top_logits, expert_ids, saved_hidden, w_down):
    experts = lax.axis_size("exp")
    groups = lax.axis_size("ctx")
    everywhere = top_logits.shape[1] == experts and saved_hidden.shape[2] == experts * grad_out.shape[0]
    plain = experts & (experts - 1) == 0 and groups % 4 == 0 and groups >= 8
    body = per_device_full if everywhere and plain else per_device_routed
    return body(grad_out, top_logits, expert_ids, saved_hidden, w_down)


def solution(mesh):
    return jax.shard_map(
        per_device,
        mesh=mesh,
        in_specs=(
            P(("ctx", "exp"), None),
            P(("ctx", "exp"), None),
            P(("ctx", "exp"), None),
            P("ctx", "exp", None, None),
            P("exp", "ctx", None),
        ),
        out_specs=(P(("ctx", "exp"), None), P("ctx", "exp", None, None), P("exp", "ctx", None)),
        check_vma=False,
    )
```

```python
import functools

import jax
import jax.numpy as jnp
import numpy as np
from jax import lax
from jax.experimental import pallas as pl
from jax.experimental.pallas import tpu as pltpu
from jax.sharding import PartitionSpec as P

LANES = 128
SCALE = 1_000_000
ORDER_WEIGHT = 100
FIRST_WEIGHT = 12_000
NEXT_WEIGHT = 600
HIDDEN_WEIGHT = 4_600
PASS_WEIGHT = 1
WAITED_WEIGHT = 1
ENTER_WEIGHT = 3_000
CLOSE_WEIGHT = 3_450
LEAVE_WEIGHT = 2_650
LAST_WEIGHT = 2_800
NT = (((1,), (1,)), ((), ()))
NN = (((1,), (0,)), ((), ()))
f32 = jnp.float32
bf16 = jnp.bfloat16


def dot(a, b, dims):
    return lax.dot_general(a, b, dims, preferred_element_type=f32)


def anywhere():
    return pl.BlockSpec(memory_space=pl.ANY)


def whole():
    return pl.BlockSpec(memory_space=pltpu.VMEM)


def scalars():
    return pl.BlockSpec(memory_space=pltpu.SMEM)


def params(mib=24):
    return pltpu.CompilerParams(vmem_limit_bytes=mib * 1024 * 1024)


def taking(microseconds):
    return pl.CostEstimate(flops=int(microseconds * SCALE), bytes_accessed=int(microseconds * 3e6), transcendentals=0)


def chain_plan(depth):
    products, weights = [], []
    for z in range(depth):
        uses = []
        for turn in range(2, depth + 1):
            if z < depth - 1 and turn >= z + 2:
                uses.append((turn, "AB"[z % 2], depth + 1 + z - turn))
            if z > 0 and turn >= depth - z + 1:
                uses.append((turn, "BA"[z % 2], z + turn - depth - 1))
        products.append(sorted(uses) + [(depth + 1, "own", z)])
        brought = {}
        for turn in range(1, depth):
            for name in "AB":
                index = z + turn if (name == "A") == (z % 2 == 0) else z - turn
                brought[turn, name] = index if 0 <= index < depth else -1
        weights.append(brought)
    return products, weights


class Scalars:
    def __init__(self):
        self.columns = []
        self.names = {}

    def add(self, name, values):
        self.names[name] = len(self.columns)
        self.columns.append(values)

    def __getitem__(self, name):
        return self.names[name]

    def row(self, place, me):
        return jnp.asarray(np.stack(self.columns, axis=-1).astype(np.int32))[place, me]


def device_scalars(depth, experts):
    products, weights = chain_plan(depth)
    table = Scalars()
    along = np.arange(2 * depth)[:, None] + np.zeros((1, experts), np.int32)

    def by_z(values):
        return np.asarray(values)[along // 2]

    table.add("x", along % 2)
    table.add("me", np.zeros_like(along) + np.arange(experts)[None, :])
    table.add(("shard", 0, "own"), along // 2)
    slot_of = [{use[2]: slot for slot, use in enumerate(products[z])} for z in range(depth)]
    for part in range(depth):
        table.add(("slot of", part), by_z([slot_of[z][part] for z in range(depth)]))
    table.add(("slot", 0, "own"), by_z([slot_of[z][z] for z in range(depth)]))
    for turn in range(1, depth):
        for name in "AB":
            shard = [weights[z][turn, name] for z in range(depth)]
            table.add(("shard", turn, name), by_z(shard))
            table.add(("slot", turn, name), by_z([slot_of[z].get(k, 0) for z, k in enumerate(shard)]))
    uses = {}
    for turn in range(2, depth + 1):
        for name in "AB":
            slots = [-1] * depth
            for z in range(depth):
                for slot, use in enumerate(products[z]):
                    if use[:2] == (turn, name):
                        slots[z] = slot
            uses[turn, name] = slots
            table.add(("use", turn, name), by_z(slots))
            limit = max(depth - 3, 0)
            table.add(("block", turn, name), by_z([min(max(slot - 1, 0), limit) for slot in slots]))
    return table, weights, uses


def rows_kernel(cut, grad_hbm, logits_hbm, ids_hbm, late_ref, early_ref, gates_ref, *scratch):
    grad_ref, logits_ref, ids_ref, sems = scratch
    model, tokens = grad_ref.shape
    copies = [
        pltpu.make_async_copy(source, target, sems.at[place])
        for place, (source, target) in enumerate(
            ((grad_hbm, grad_ref), (logits_hbm, logits_ref), (ids_hbm, ids_ref))
        )
    ]
    for copy in copies:
        copy.start()
    for copy in copies:
        copy.wait()
    count = logits_ref.shape[0]
    width = cut + late_ref.shape[1]
    logits = logits_ref[...]
    powers = jnp.exp(logits - jnp.max(logits, axis=0, keepdims=True))
    gates = powers / jnp.sum(powers, axis=0, keepdims=True)
    gates_ref[...] = gates
    sent = gates.astype(bf16).astype(f32)
    ids = ids_ref[...]
    row = lax.broadcasted_iota(jnp.int32, (width - model, tokens), 0)
    extra = jnp.zeros((width - model, tokens), f32)
    for expert in range(count):
        chosen = jnp.sum(jnp.where(ids == expert, sent, 0.0), axis=0, keepdims=True)
        extra = extra + jnp.where(row == expert, chosen, 0.0)
    for start in range(0, width, LANES):
        stop = start + LANES
        if stop <= model:
            block = grad_ref[start:stop, :].astype(f32)
        elif start >= model:
            block = extra[start - model : stop - model, :]
        else:
            block = jnp.concatenate(
                [grad_ref[start:model, :].astype(f32), extra[: stop - model, :]], axis=0
            )
        turned = block.T.astype(bf16)
        if start < cut:
            early_ref[:, start:stop] = turned
        else:
            late_ref[:, start - cut : stop - cut] = turned


def make_rows(grad_out, top_logits, expert_ids, width, cut):
    tokens, model = grad_out.shape
    count = top_logits.shape[1]
    return pl.pallas_call(
        functools.partial(rows_kernel, cut),
        out_shape=(
            jax.ShapeDtypeStruct((tokens, width - cut), bf16),
            jax.ShapeDtypeStruct((tokens, cut), bf16),
            jax.ShapeDtypeStruct((count, tokens), f32),
        ),
        in_specs=[pl.BlockSpec(memory_space=pltpu.HBM)] * 3,
        out_specs=(whole(),) * 3,
        scratch_shapes=[
            pltpu.VMEM((model, tokens), bf16),
            pltpu.VMEM((count, tokens), f32),
            pltpu.VMEM((count, tokens), jnp.int32),
            pltpu.SemaphoreType.DMA((3,)),
        ],
        compiler_params=params(58),
        cost_estimate=taking(2),
        name="make_rows",
    )(grad_out.T, top_logits.T, expert_ids.T)


def pack_kernel(*refs):
    out_ref, sems = refs[-2:]
    copies = []
    for place in range(out_ref.shape[0]):
        copies.append(pltpu.make_async_copy(refs[place], out_ref.at[place], sems.at[place]))
        copies[-1].start()
    for copy in copies:
        copy.wait()


def pack(values, after):
    number = len(values)
    return pl.pallas_call(
        pack_kernel,
        out_shape=jax.ShapeDtypeStruct((number, *values[0].shape), values[0].dtype),
        in_specs=[anywhere()] * (number + len(after)),
        out_specs=anywhere(),
        scratch_shapes=[pltpu.SemaphoreType.DMA((number,))],
        compiler_params=params(),
        cost_estimate=taking(1),
        name="pack_rows",
    )(*values, *after)


def blocks_of(refs, places):
    return [refs[array] if place is None else refs[array].at[place] for array, place in places]


def hold_kernel(*refs):
    del refs


def hold(values, after, weight=0):
    return pl.pallas_call(
        hold_kernel,
        out_shape=tuple(jax.ShapeDtypeStruct(value.shape, value.dtype) for value in values),
        in_specs=[anywhere()] * (len(values) + len(after)),
        out_specs=(anywhere(),) * len(values),
        input_output_aliases={place: place for place in range(len(values))},
        compiler_params=params(),
        cost_estimate=taking(weight),
        name="hold",
    )(*values, *after)


def split_kernel(table, where_ref, hidden_ref, *refs):
    own_ref, first_ref, rest_ref = refs[-3:]
    parts, units, _ = own_ref.shape
    row = lax.broadcasted_iota(jnp.int32, (2 * units, 2 * units), 0)
    column = lax.broadcasted_iota(jnp.int32, (2 * units, 2 * units), 1)
    unit = jnp.where(row == column, 1.0, 0.0).astype(bf16)
    low = where_ref[table["x"]] == 0
    for part in range(parts):
        block = hidden_ref[:, part * 2 * units : (part + 1) * 2 * units]
        turned = dot(unit, block, NT).astype(bf16)
        slot = where_ref[table["slot of", part]]
        other = jnp.where(low, turned[units:], turned[:units])
        own_ref[slot] = jnp.where(low, turned[:units], turned[units:])

        @pl.when(slot == 0)
        def _():
            first_ref[0] = other

        @pl.when(slot != 0)
        def _():
            rest_ref[slot - 1] = other


def split_hidden(table, where, hidden, parts, units, after):
    slots = hidden.shape[0]
    return pl.pallas_call(
        functools.partial(split_kernel, table),
        out_shape=tuple(
            jax.ShapeDtypeStruct((count, units, slots), bf16) for count in (parts, 1, parts - 1)
        ),
        in_specs=[scalars(), whole()] + [anywhere()] * len(after),
        out_specs=(whole(),) * 3,
        compiler_params=params(),
        cost_estimate=taking(2),
        name="split_hidden",
    )(where, hidden, *after)


def place_of(place, count, me, tokens):
    start = (place // count) * count * tokens + ((place % count) ^ me) * tokens
    return pl.multiple_of(start, tokens)


def scale_rows(table, model, where_ref, rows, gated, scaled):
    tokens = rows[0].shape[0]
    me = where_ref[table["me"]]
    lane = lax.broadcasted_iota(jnp.int32, (tokens, LANES), 1)
    for place, block in enumerate(rows):
        here = pl.ds(place_of(place, len(rows) // 2, me, tokens), tokens)
        tile = gated[place][:, gated[place].shape[1] - LANES :]
        picked = jnp.where(lane == model % LANES + me, tile.astype(f32), 0.0)
        gate = jnp.sum(picked, axis=1, keepdims=True)
        scaled[here, :] = (block[:, : scaled.shape[1]].astype(f32) * gate).astype(bf16)


def products_kernel(table, model, counts, places, shards, skip, where_it_runs, where_ref, *refs):
    used = sum(counts)
    rows = blocks_of(refs[: counts[0]], places[0])
    gated = blocks_of(refs[counts[0] : used], places[1])
    own_ref, other_ref = refs[used : used + 2]
    kept_ref, scaled, total_ref, sem = refs[-4:]
    units, slots = own_ref.shape[1:]

    def stacked(ref, offset):
        parts = [ref[offset + shard] for shard in range(shards)]
        return jnp.concatenate(parts, axis=0) if len(parts) > 1 else parts[0]

    def work():
        scale_rows(table, model, where_ref, rows, gated, scaled)
        total = dot(stacked(own_ref, skip), scaled[:slots, :], NN)
        total = total + dot(stacked(other_ref, 0), scaled[slots:, :], NN)
        for shard in range(shards):
            total_ref[shard] = total[shard * units : (shard + 1) * units]
        copy = pltpu.make_async_copy(total_ref, kept_ref, sem)
        copy.start()
        copy.wait()

    at_end = where_ref[table["use", 2, "A"]] == 0
    if where_it_runs == "ends":
        pl.when(at_end)(work)
    elif where_it_runs == "middle":
        pl.when(jnp.logical_not(at_end))(work)
    else:
        work()


def products(
    table, where, rows, gated, own, other, skip, model, width, name, after, where_it_runs="all", before=None
):
    arrays, places = zip(rows, gated)
    counts = [len(part) for part in arrays]
    shards, units, slots = other.shape
    kept = jax.ShapeDtypeStruct((shards, units, width), f32)
    operands = [*arrays[0], *arrays[1], own, other]
    extra = ([] if before is None else [before]) + list(after)
    return pl.pallas_call(
        functools.partial(products_kernel, table, model, counts, places, shards, skip, where_it_runs),
        out_shape=kept,
        in_specs=[scalars()] + [whole()] * len(operands) + [anywhere()] * len(extra),
        out_specs=anywhere(),
        scratch_shapes=[
            pltpu.VMEM((2 * slots, width), bf16),
            pltpu.VMEM(kept.shape, f32),
            pltpu.SemaphoreType.DMA,
        ],
        input_output_aliases={} if before is None else {1 + len(operands): 0},
        compiler_params=params(),
        cost_estimate=taking(1),
        name=name,
    )(where, *operands, *extra)


def first_kernel(table, model, counts, places, start, where_ref, *refs):
    used = sum(counts)
    rows = blocks_of(refs[: counts[0]], places[0])
    gated = blocks_of(refs[counts[0] : used], places[1])
    own_ref, other_ref, coming_ref = refs[used : used + 3]
    out_ref, scaled = refs[-2:]
    slots = own_ref.shape[2]
    ends = where_ref[table["use", 2, "A"]] == 0

    @pl.when(ends)
    def _():
        scale_rows(table, model, where_ref, rows, gated, scaled)
        total = dot(own_ref[0], scaled[:slots, :], NN)
        out_ref[...] = (total + dot(other_ref[0], scaled[slots:, :], NN)).astype(bf16)

    @pl.when(jnp.logical_not(ends))
    def _():
        out_ref[...] = coming_ref[:, start : start + out_ref.shape[1]]


def first_sums(table, where, rows, gated, own, other, coming, model, start, width, after):
    arrays, places = zip(rows, gated)
    counts = [len(part) for part in arrays]
    units, slots = own.shape[1:]
    return pl.pallas_call(
        functools.partial(first_kernel, table, model, counts, places, start),
        out_shape=jax.ShapeDtypeStruct((units, width), bf16),
        in_specs=[scalars()] + [whole()] * (sum(counts) + 3) + [anywhere()] * len(after),
        out_specs=whole(),
        scratch_shapes=[pltpu.VMEM((2 * slots, width), bf16)],
        compiler_params=params(),
        cost_estimate=taking(1),
        name="first_sums",
    )(where, *arrays[0], *arrays[1], own, other, coming, *after)


def rows_of(units):
    return units // 2 if units % 32 == 0 else units


def column_parts(arrays, cut):
    return [(0, arrays[0])] if len(arrays) == 1 else [(cut, arrays[0]), (0, arrays[1])]


def combine_kernel(table, key, cut, counts, sides, where_ref, *refs):
    slot = where_ref[table[key]]
    coming = refs[: counts[0]]
    outs = refs[len(refs) - counts[2] :]
    model = sum(ref.shape[1] for ref in outs)
    spans = [(cut, model), (0, cut)] if cut else [(0, model)]
    for chunk, (start, stop) in enumerate(spans):
        if counts[0] == 0:
            total = jnp.zeros((outs[0].shape[0], stop - start), f32)
        elif counts[0] == 1:
            total = coming[0][:, start:stop].astype(f32)
        else:
            total = coming[chunk][...].astype(f32)
        for number, side in enumerate(sides):
            flag = slot == 0 if side == "first" else slot > 0
            total = total + jnp.where(flag, refs[counts[0] + len(spans) * number + chunk][0], 0.0)
        total = total.astype(bf16)
        if counts[2] == 1:
            outs[0][:, start:stop] = total
        else:
            outs[chunk][...] = total


def combine(table, where, coming, first, rest, turn, name, used, cut, after, chunked=False, weight=1):
    units = first[0].shape[1]
    model = sum(part.shape[2] for part in first)
    block = rows_of(units)
    column = table["block", turn, name]
    sides, operands, specs = [], [], []
    if any(slot == 0 for slot in used):
        sides.append("first")
        operands += first
        specs += [pl.BlockSpec((1, block, part.shape[2]), lambda j, s: (0, j, 0)) for part in first]
    if any(slot > 0 for slot in used):
        sides.append("rest")
        operands += rest
        specs += [pl.BlockSpec((1, block, part.shape[2]), lambda j, s: (s[column], j, 0)) for part in rest]
    widths = [model - cut, cut] if chunked else [model]
    return pl.pallas_call(
        functools.partial(
            combine_kernel, table, ("use", turn, name), cut, (len(coming), len(operands), len(widths)), sides
        ),
        out_shape=[jax.ShapeDtypeStruct((units, count), bf16) for count in widths],
        grid_spec=pltpu.PrefetchScalarGridSpec(
            num_scalar_prefetch=1,
            grid=(units // block,),
            in_specs=[pl.BlockSpec((block, part.shape[1]), lambda j, s: (j, 0)) for part in coming]
            + specs
            + [anywhere()] * len(after),
            out_specs=[pl.BlockSpec((block, count), lambda j, s: (j, 0)) for count in widths],
        ),
        compiler_params=params(),
        cost_estimate=taking(weight),
        name="combine",
    )(where, *coming, *operands, *after)


def total_kernel(cut, counts, *refs):
    coming = [refs[: counts[0]], refs[counts[0] : sum(counts)]]
    out_ref = refs[-1]
    for chunk, start in enumerate((cut, 0)):
        kept_ref = refs[sum(counts) + chunk]
        here = slice(start, start + kept_ref.shape[2])
        total = kept_ref[0]
        for parts in coming:
            total = total + (parts[0][:, here] if len(parts) == 1 else parts[chunk][...]).astype(f32)
        out_ref[0, :, here] = total


def total_grad(a, b, kept, cut):
    units = a[0].shape[0]
    model = sum(part.shape[1] for part in a)
    block = rows_of(units)
    return pl.pallas_call(
        functools.partial(total_kernel, cut, (len(a), len(b))),
        out_shape=jax.ShapeDtypeStruct((1, units, model), f32),
        grid=(units // block,),
        in_specs=[pl.BlockSpec((block, part.shape[1]), lambda j: (j, 0)) for part in (*a, *b)]
        + [
            pl.BlockSpec((1, block, part.shape[2]), functools.partial(lambda last, j: (last, j, 0), part.shape[0] - 1))
            for part in kept
        ],
        out_specs=pl.BlockSpec((1, block, model), lambda j: (0, j, 0)),
        compiler_params=params(),
        cost_estimate=taking(2),
        name="total_grad",
    )(*a, *b, *kept)


def back_kernel(table, model, cut, counts, places, choices, parts, guard, summed, where_ref, *refs):
    keys = [key for choice in choices for key in choice]
    used = sum(counts)
    late = blocks_of(refs[: counts[0]], places[0])
    early = blocks_of(refs[counts[0] : used], places[1])
    number = len(late)
    own_ref, first_ref, rest_ref = refs[used : used + 3]
    weight_refs, used = {}, used + 3
    for key, count in zip(keys, parts):
        weight_refs[key] = refs[used : used + count]
        used += count
    before_ref = refs[used] if summed else None
    outs, sums_ref = refs[-3:-1], refs[-1]
    tokens = late[0].shape[0]
    units = own_ref.shape[1]
    me = where_ref[table["me"]]
    start = late[0].shape[1] - LANES
    eight = lax.broadcasted_iota(jnp.int32, (8, LANES), 1)
    onehot = jnp.where(eight == model % LANES + me, 1.0, 0.0).astype(bf16)
    shards = {key: where_ref[table[("shard",) + key]] for key in keys}
    slots = {key: where_ref[table[("slot",) + key]] for key in keys}
    sums_ref[...] = before_ref[...] if summed else jnp.zeros(sums_ref.shape, f32)

    def whole_weight(key):
        got = weight_refs[key]
        return got[0][...] if len(got) == 1 else jnp.concatenate([got[1][...], got[0][...]], axis=1)

    def work():
        stack, here_valid, here_slot = [], [], []
        for choice in choices:
            weight, valid, slot = whole_weight(choice[0]), shards[choice[0]] >= 0, slots[choice[0]]
            for key in choice[1:]:
                weight = jnp.where(valid, weight, whole_weight(key))
                slot = jnp.where(valid, slot, slots[key])
                valid = jnp.logical_or(valid, shards[key] >= 0)
            stack.append(weight)
            here_valid.append(valid)
            here_slot.append(slot)
        weight = jnp.concatenate(stack, axis=0) if len(stack) > 1 else stack[0]
        for pair in range(0, number, 2):
            both = jnp.concatenate(
                [
                    jnp.concatenate([early[k][...], late[k][:, : model - cut]], axis=1)
                    for k in (pair, pair + 1)
                ],
                axis=0,
            )
            product = dot(weight, both, NT)
            for place in (pair, pair + 1):
                near = place < number // 2
                block = product[:, (place - pair) * tokens : (place - pair + 1) * tokens]
                gate = dot(onehot, late[place][:, start:], NT)[0:1]
                here = pl.ds(place_of(place % (number // 2), number // 2, me, tokens), tokens)
                wide = pl.ds(place_of(place, number // 2, me, tokens), tokens)
                gated = (block * gate).astype(bf16)
                total = jnp.zeros((1, tokens), f32)
                for index, (valid, slot) in enumerate(zip(here_valid, here_slot)):
                    some = slice(index * units, (index + 1) * units)
                    outs[0 if near else 1][index, :, here] = gated[some]
                    if near:
                        hidden = own_ref[slot, :, here].astype(f32)
                    else:
                        hidden = jnp.where(
                            slot == 0,
                            first_ref[0, :, here].astype(f32),
                            rest_ref[jnp.maximum(slot - 1, 0), :, here].astype(f32),
                        )
                    part = jnp.sum(hidden * block[some], axis=0, keepdims=True)
                    total = total + jnp.where(valid, part, 0.0)
                sums_ref[0:1, wide] += total

    if guard:
        pl.when(functools.reduce(jnp.logical_or, [shards[key] >= 0 for key in keys]))(work)
    else:
        work()


def back_part(table, where, late, early, own, first, rest, choices, got, before, guard, after, model):
    units, slots = own.shape[1:]
    arrays, places = zip(late, early)
    counts = [len(part) for part in arrays]
    cut = arrays[1][0].shape[-1]
    keys = [key for choice in choices for key in choice]
    weights = [got[key] for key in keys]
    flat = [part for weight in weights for part in weight]
    half = jax.ShapeDtypeStruct((len(choices), units, slots), bf16)
    summed = before is not None
    operands = [*arrays[0], *arrays[1], own, first, rest, *flat] + ([before] if summed else [])
    outs = [half, half, jax.ShapeDtypeStruct((8, 2 * slots), f32)]
    parts = [len(weight) for weight in weights]
    return pl.pallas_call(
        functools.partial(
            back_kernel, table, model, cut, counts, places, choices, parts, guard, summed
        ),
        out_shape=outs,
        in_specs=[scalars()] + [whole()] * len(operands) + [anywhere()] * len(after),
        out_specs=[whole()] * len(outs),
        compiler_params=params(),
        cost_estimate=taking(6),
        name="back_part",
    )(where, *operands, *after)


def join_kernel(table, choices, where_ref, *refs):
    out_ref, turned, sem = refs[-3:]
    slots, width = turned.shape[1:]
    row = lax.broadcasted_iota(jnp.int32, (slots, slots), 0)
    column = lax.broadcasted_iota(jnp.int32, (slots, slots), 1)
    unit = jnp.where(row == column, 1.0, 0.0).astype(bf16)
    low = where_ref[table["x"]] == 0
    copies = []
    pairs = [
        (refs[2 * group][place], refs[2 * group + 1][place])
        for group in range((len(refs) - 3) // 2)
        for place in range(refs[2 * group].shape[0])
    ]
    for place, (choice, (mine, theirs)) in enumerate(zip(choices, pairs)):
        index = where_ref[table[("shard",) + choice[0]]]
        for key in choice[1:]:
            index = jnp.where(index >= 0, index, where_ref[table[("shard",) + key]])
        both = jnp.concatenate([jnp.where(low, mine, theirs), jnp.where(low, theirs, mine)], axis=0)
        turned[place] = dot(unit, both, NT).astype(bf16)
        here = pl.ds(pl.multiple_of(jnp.maximum(index, 0) * width, LANES), width)
        copy = pltpu.make_async_copy(turned.at[place], out_ref.at[:, here], sem.at[place])
        copies.append((index, copy))
        pl.when(index >= 0)(copy.start)
    for index, copy in copies:
        pl.when(index >= 0)(copy.wait)


def join_hidden(table, where, choices, halves, slots, hidden):
    units = halves[0].shape[1]
    return pl.pallas_call(
        functools.partial(join_kernel, table, choices),
        out_shape=jax.ShapeDtypeStruct((slots, hidden), bf16),
        in_specs=[scalars()] + [whole()] * len(halves),
        out_specs=anywhere(),
        scratch_shapes=[
            pltpu.VMEM((len(choices), slots, 2 * units), bf16),
            pltpu.SemaphoreType.DMA((len(choices),)),
        ],
        compiler_params=params(),
        cost_estimate=taking(2),
        name="join_hidden",
    )(where, *halves)


def logits_kernel(gates_ref, ids_ref, grads_ref, out_ref):
    gates, ids, grads = gates_ref[...], ids_ref[...], grads_ref[...]
    picked = jnp.zeros_like(gates)
    for expert in range(grads.shape[0]):
        picked = picked + jnp.where(ids == expert, grads[expert : expert + 1, :], 0.0)
    out_ref[...] = gates * (picked - jnp.sum(gates * picked, axis=0, keepdims=True))


def logits_grad(gates, ids, grads):
    return pl.pallas_call(
        logits_kernel,
        out_shape=jax.ShapeDtypeStruct(gates.shape, f32),
        in_specs=[whole()] * 3,
        out_specs=whole(),
        compiler_params=params(),
        cost_estimate=taking(1),
        name="logits_grad",
    )(gates, ids, grads)


def per_device_full(grad_out, top_logits, expert_ids, saved_hidden, w_down):
    experts = lax.axis_size("exp")
    groups = lax.axis_size("ctx")
    depth = groups // 2
    tokens, model = grad_out.shape
    slots, hidden = saved_hidden.shape[2:]
    width = pl.cdiv(model + experts, LANES) * LANES
    cut = width // LANES // 2 * LANES

    table, brought, uses = device_scalars(depth, experts)
    where = table.row(lax.axis_index("ctx"), lax.axis_index("exp"))

    def swap(value, x, exp):
        if not exp:
            return lax.ppermute(value, "ctx", [(i, i ^ x) for i in range(groups)])
        if not x:
            return lax.ppermute(value, "exp", [(i, i ^ exp) for i in range(experts)])
        pairs = [(c * experts + e, (c ^ x) * experts + (e ^ exp)) for c in range(groups) for e in range(experts)]
        return lax.ppermute(value, ("ctx", "exp"), pairs)

    def swap_z(value, name, senders=range(depth)):
        first = "AB".index(name)
        pairs = []
        for low in range(first, depth - 1, 2):
            for z, other in ((low, low + 1), (low + 1, low)):
                pairs += [(2 * z + x, 2 * other + x) for x in range(2) if z in senders]
        return lax.ppermute(value, "ctx", pairs)

    got = {(0, "own"): [w_down[0]]}
    for name in "BA":
        got[1, name] = [swap_z(w_down[0], name)]

    late, early, gates = make_rows(grad_out, top_logits, expert_ids, width, cut)
    highs = list(range(2, experts, 2))

    def sides(mine):
        return [mine, swap(mine, 0, 1)]

    late_x = swap(late, 1, 0)
    late_near = [late] + [swap(late, 0, high) for high in highs]
    own, other_first, other_rest = split_hidden(
        table, where, saved_hidden[0, 0], depth, w_down.shape[1], [late]
    )
    other_first = swap(other_first, 1, 0)
    (late_x,) = hold((late_x,), [], ORDER_WEIGHT)
    (late_x,) = hold((late_x,), late_near[1:])
    late_mine = late_near + [late_x] + [swap(late_x, 0, high) for high in highs]
    (early,) = hold((early,), [late_x, other_first])
    early_x = swap(early, 1, 0)
    late_rows = sides(pack(late_mine, [early_x]))
    late_rows = (late_rows, [(side, place) for place in range(experts) for side in range(2)])
    early_rows = sides(pack([early, early_x], []))
    early_far = [[swap(block, 0, high) for high in highs] for block in (early, early_x)]
    other_rest = swap(other_rest, 1, 0)

    got[1, "A"] = list(hold(got[1, "A"], [], ORDER_WEIGHT))
    got[1, "B"] = list(hold(got[1, "B"], got[1, "A"], FIRST_WEIGHT))
    chunks, first = [], []

    def first_chunk(rows, start, columns, after, before):
        chunks.append((rows, start, columns))
        value = first_sums(
            table, where, rows, late_rows, own, other_first, got[1, "B"][0], model, start, columns, after
        )
        if before:
            (value,) = hold([value], before, NEXT_WEIGHT)
        got.setdefault((2, "A"), []).append(swap_z(value, "A"))
        first.append(
            products(
                table, where, rows, late_rows, own, other_first, 0, model, columns, "first_kept", [value], "middle"
            )
        )
        return value

    first_chunk(late_rows, cut, model - cut, [early_rows[1]], [])
    places = []
    for base, blocks in enumerate(early_far):
        places += [(0, base), (1, base)]
        for block in hold(blocks, first):
            places += [(len(early_rows), None), (len(early_rows) + 1, None)]
            mine, theirs = sides(block)
            early_rows += [mine, theirs if base else hold([theirs], [], ORDER_WEIGHT)[0]]
    early_rows = (early_rows, places)
    marker = first_chunk(early_rows, 0, cut, [first[0]], got[2, "A"])
    got[2, "B"] = [swap_z(got[1, "A"][0], "B")]
    (other_rest,) = hold([other_rest], [], HIDDEN_WEIGHT)

    halves, all_choices, weights_of = [], [], {}
    only_first = max(uses[3, "B"]) <= 0

    def backprop(choices, before, guard, after):
        mine, theirs, sums = back_part(
            table, where, late_rows, early_rows, own, other_first, other_rest, choices,
            {**got, **weights_of}, before, guard, after, model,
        )
        halves.extend([mine, swap(theirs, 1, 0)])
        all_choices.extend(choices)
        return sums

    def forward(turn, name, after):
        coming = got[turn - 1, "B" if name == "A" else "A"]
        coming[:] = hold(coming, after, PASS_WEIGHT)
        others = [z for z in range(depth) if uses[turn, name][z] < 0]
        weights_of[turn, name] = [swap_z(coming[0], name, others)]

    def pass_on(turn, name, after, chunk=None, waited=(), weight=1):
        coming = got[turn - 1, "B" if name == "A" else "A"]
        used = uses[turn, name]
        senders = range(depth)
        if turn == depth - 1 and min(used) < 0 and name == "A" and len(coming) == 1:
            senders = [z for z in range(depth) if used[z] >= 0]
            if chunk is None:
                forward(turn, name, [])
            if set(senders) <= {0, depth - 1}:
                coming = []
        parts, start = (first, rest), cut
        if chunk is not None:
            coming, parts, start = coming[chunk:][:1], (first[chunk:][:1], rest[chunk:][:1]), 0
        values = list(combine(table, where, coming, *parts, turn, name, used, start, after, False, weight))
        if waited:
            values = list(hold(values, list(waited), WAITED_WEIGHT))
        got.setdefault((turn, name), []).extend(swap_z(value, name, senders) for value in values)
        return values[-1]

    def choices_of(turn):
        both = any(b[turn, "A"] >= 0 and b[turn, "B"] >= 0 for b in brought)
        return [[(turn, "A")], [(turn, "B")]] if both else [[(turn, "A"), (turn, "B")]]

    rest = []

    def other_products(chunk, after, *where_it_runs):
        rows, _, columns = chunks[chunk]
        return products(
            table, where, rows, late_rows, own, other_rest, 1, model, columns, "rest_kept", after, *where_it_runs
        )

    apart = max(uses[3, "B"]) <= 0 and depth == 4
    if apart:
        marker = pass_on(3, "B", [marker], 0)
        rest.append(other_products(0, [marker]))
        marker = pass_on(3, "A", rest, 0)
        forward(3, "A", [marker, first[1]])
        rest.append(other_products(1, got[2, "B"], "ends"))
        marker = pass_on(3, "A", rest, 1)
        marker = pass_on(3, "B", [marker], 1)
        rest[1] = other_products(1, [marker], "middle", rest[1])
        marker = rest[1]
    else:
        rest.append(other_products(0, [marker]))
        rest.append(other_products(1, rest))
        marker = pass_on(3, "A", rest)
        for chunk in range(2):
            marker = pass_on(3, "B", [marker], chunk)
    sums = backprop([[(0, "own")], [(1, "A")], [(1, "B")]], None, False, got[2, "A"][:1])
    sooner = halves[1::2]
    for turn in range(2, depth):
        choices = choices_of(turn)
        if turn > 2:
            waited = [array for key in ((turn, "A"), (turn, "B")) for array in weights_of.get(key, [])]
            if apart and turn + 1 == depth:
                pass_on(depth, "B", [], 0)
                pass_on(depth, "B", [], 1, sooner, LEAVE_WEIGHT)
                marker = pass_on(depth, "A", [sums], weight=LAST_WEIGHT)
                sums = backprop(choices_of(turn - 1), sums, True, [marker])
            else:
                pass_on(turn + 1, "B", [sums, *sooner, *waited])
                marker = pass_on(turn + 1, "A", [sums])
        if not apart or turn > 2:
            sums = backprop(choices, sums, len(choices) == 1, [marker])
    slot_grad = sums[0:1, :slots] + swap(sums[0:1, slots:], 1, 0)
    grads = lax.all_to_all(
        slot_grad.reshape(experts, tokens), "exp", split_axis=0, concat_axis=0, tiled=True
    )
    logit_grad = logits_grad(gates, expert_ids.T, grads)
    hidden_grad = join_hidden(table, where, all_choices, halves, slots, hidden)
    if apart:
        entered = list(hold(got[depth, "B"][:1], [hidden_grad], ENTER_WEIGHT))
        got[depth, "B"] = entered + list(hold(got[depth, "B"][1:], entered, CLOSE_WEIGHT))
    weight_grad = total_grad(got[depth, "A"], got[depth, "B"], rest, cut)
    return (logit_grad.T, hidden_grad[None, None], weight_grad)


def routing_tables(expert_ids, count_experts, capacity):
    columns = jnp.arange(count_experts, dtype=jnp.int32)
    matches = expert_ids[:, :, None] == columns[None, None, :]
    per_token = jnp.sum(matches.astype(jnp.int32), axis=1)
    rank_table = jnp.cumsum(per_token, axis=0) - per_token
    slot_iota = jnp.arange(capacity, dtype=jnp.int32)
    select = (per_token.T[:, None, :] == 1) & (rank_table.T[:, None, :] == slot_iota[None, :, None])
    return (matches.astype(jnp.float32), select)


def per_device_routed(grad_out, top_logits, expert_ids, saved_hidden, w_down):
    count_experts = lax.axis_size("exp")
    slot_count = saved_hidden.shape[2]
    capacity = slot_count // count_experts
    model_width = grad_out.shape[1]
    onehot, select = routing_tables(expert_ids, count_experts, capacity)
    select_wide = select.astype(jnp.float32)
    gate_probs = jax.nn.softmax(top_logits, axis=-1)
    gate_sent = gate_probs.astype(jnp.bfloat16)
    gate_by_expert = jnp.sum(onehot * gate_sent.astype(jnp.float32)[:, :, None], axis=1)
    send_rows = jnp.einsum(
        "ect,td->ecd", select.astype(jnp.bfloat16), grad_out, preferred_element_type=jnp.float32
    ).astype(jnp.bfloat16)
    send_gate = jnp.sum(select_wide * gate_by_expert.T[:, None, :], axis=2).astype(jnp.bfloat16)
    hidden = saved_hidden[0, 0]
    rows_in, gate_in = (
        lax.all_to_all(send_rows, "exp", split_axis=0, concat_axis=0, tiled=True),
        lax.all_to_all(send_gate, "exp", split_axis=0, concat_axis=0, tiled=True),
    )
    flat_rows = rows_in.reshape(slot_count, model_width)
    backprop = lax.dot_general(
        flat_rows,
        lax.all_gather(w_down[0], "ctx", axis=0, tiled=True),
        (((1,), (1,)), ((), ())),
        preferred_element_type=jnp.float32,
    )
    flat_gate = gate_in.reshape(slot_count, 1).astype(jnp.float32)
    hidden_grad = (flat_gate * backprop).astype(jnp.bfloat16)
    slot_grad = jnp.sum(hidden.astype(jnp.float32) * backprop, axis=1)
    scaled = (flat_gate * flat_rows.astype(jnp.float32)).astype(jnp.bfloat16)
    partial_grad = lax.dot_general(
        hidden, scaled, (((0,), (0,)), ((), ())), preferred_element_type=jnp.float32
    )
    weight_grad = lax.psum_scatter(partial_grad, "ctx", scatter_dimension=0, tiled=True)
    returned = lax.all_to_all(
        slot_grad.reshape(count_experts, capacity), "exp", split_axis=0, concat_axis=0, tiled=True
    )
    grad_by_expert = jnp.sum(select_wide * returned[:, :, None], axis=1)
    gate_grad = jnp.sum(onehot * grad_by_expert.T[:, None, :], axis=2)
    logit_grad = gate_probs * (gate_grad - jnp.sum(gate_probs * gate_grad, axis=1, keepdims=True))
    return (logit_grad, hidden_grad.reshape(1, 1, slot_count, -1), weight_grad[None])


def per_device(grad_out, top_logits, expert_ids, saved_hidden, w_down):
    experts = lax.axis_size("exp")
    groups = lax.axis_size("ctx")
    everywhere = top_logits.shape[1] == experts and saved_hidden.shape[2] == experts * grad_out.shape[0]
    plain = experts & (experts - 1) == 0 and groups % 4 == 0 and groups >= 8
    body = per_device_full if everywhere and plain else per_device_routed
    return body(grad_out, top_logits, expert_ids, saved_hidden, w_down)


def solution(mesh):
    return jax.shard_map(
        per_device,
        mesh=mesh,
        in_specs=(
            P(("ctx", "exp"), None),
            P(("ctx", "exp"), None),
            P(("ctx", "exp"), None),
            P("ctx", "exp", None, None),
            P("exp", "ctx", None),
        ),
        out_specs=(P(("ctx", "exp"), None), P("ctx", "exp", None, None), P("exp", "ctx", None)),
        check_vma=False,
    )
```

```python
import functools

import jax
import jax.numpy as jnp
import numpy as np
from jax import lax
from jax.experimental import pallas as pl
from jax.experimental.pallas import tpu as pltpu
from jax.sharding import PartitionSpec as P

LANES = 128
SCALE = 1_000_000
ORDER_WEIGHT = 100
FIRST_WEIGHT = 12_000
NEXT_WEIGHT = 600
HIDDEN_WEIGHT = 4_600
PASS_WEIGHT = 1
WAITED_WEIGHT = 1
ENTER_WEIGHT = 3_000
CLOSE_WEIGHT = 3_450
LEAVE_WEIGHT = 2_650
LAST_WEIGHT = 2_800
NT = (((1,), (1,)), ((), ()))
NN = (((1,), (0,)), ((), ()))
f32 = jnp.float32
bf16 = jnp.bfloat16


def dot(a, b, dims):
    return lax.dot_general(a, b, dims, preferred_element_type=f32)


def anywhere():
    return pl.BlockSpec(memory_space=pl.ANY)


def whole():
    return pl.BlockSpec(memory_space=pltpu.VMEM)


def scalars():
    return pl.BlockSpec(memory_space=pltpu.SMEM)


def params(mib=24):
    return pltpu.CompilerParams(vmem_limit_bytes=mib * 1024 * 1024)


def taking(microseconds):
    return pl.CostEstimate(flops=int(microseconds * SCALE), bytes_accessed=int(microseconds * 3e6), transcendentals=0)


def chain_plan(depth):
    products, weights = [], []
    for z in range(depth):
        uses = []
        for turn in range(2, depth + 1):
            if z < depth - 1 and turn >= z + 2:
                uses.append((turn, "AB"[z % 2], depth + 1 + z - turn))
            if z > 0 and turn >= depth - z + 1:
                uses.append((turn, "BA"[z % 2], z + turn - depth - 1))
        products.append(sorted(uses) + [(depth + 1, "own", z)])
        brought = {}
        for turn in range(1, depth):
            for name in "AB":
                index = z + turn if (name == "A") == (z % 2 == 0) else z - turn
                brought[turn, name] = index if 0 <= index < depth else -1
        weights.append(brought)
    return products, weights


class Scalars:
    def __init__(self):
        self.columns = []
        self.names = {}

    def add(self, name, values):
        self.names[name] = len(self.columns)
        self.columns.append(values)

    def __getitem__(self, name):
        return self.names[name]

    def row(self, place, me):
        return jnp.asarray(np.stack(self.columns, axis=-1).astype(np.int32))[place, me]


def device_scalars(depth, experts):
    products, weights = chain_plan(depth)
    table = Scalars()
    along = np.arange(2 * depth)[:, None] + np.zeros((1, experts), np.int32)

    def by_z(values):
        return np.asarray(values)[along // 2]

    table.add("x", along % 2)
    table.add("me", np.zeros_like(along) + np.arange(experts)[None, :])
    table.add(("shard", 0, "own"), along // 2)
    slot_of = [{use[2]: slot for slot, use in enumerate(products[z])} for z in range(depth)]
    for part in range(depth):
        table.add(("slot of", part), by_z([slot_of[z][part] for z in range(depth)]))
    table.add(("slot", 0, "own"), by_z([slot_of[z][z] for z in range(depth)]))
    for turn in range(1, depth):
        for name in "AB":
            shard = [weights[z][turn, name] for z in range(depth)]
            table.add(("shard", turn, name), by_z(shard))
            table.add(("slot", turn, name), by_z([slot_of[z].get(k, 0) for z, k in enumerate(shard)]))
    uses = {}
    for turn in range(2, depth + 1):
        for name in "AB":
            slots = [-1] * depth
            for z in range(depth):
                for slot, use in enumerate(products[z]):
                    if use[:2] == (turn, name):
                        slots[z] = slot
            uses[turn, name] = slots
            table.add(("use", turn, name), by_z(slots))
            limit = max(depth - 3, 0)
            table.add(("block", turn, name), by_z([min(max(slot - 1, 0), limit) for slot in slots]))
    return table, weights, uses


def rows_kernel(cut, grad_hbm, logits_hbm, ids_hbm, late_ref, early_ref, gates_ref, *scratch):
    grad_ref, logits_ref, ids_ref, sems = scratch
    model, tokens = grad_ref.shape
    copies = [
        pltpu.make_async_copy(source, target, sems.at[place])
        for place, (source, target) in enumerate(
            ((grad_hbm, grad_ref), (logits_hbm, logits_ref), (ids_hbm, ids_ref))
        )
    ]
    for copy in copies:
        copy.start()
    for copy in copies:
        copy.wait()
    count = logits_ref.shape[0]
    width = cut + late_ref.shape[1]
    logits = logits_ref[...]
    powers = jnp.exp(logits - jnp.max(logits, axis=0, keepdims=True))
    gates = powers / jnp.sum(powers, axis=0, keepdims=True)
    gates_ref[...] = gates
    sent = gates.astype(bf16).astype(f32)
    ids = ids_ref[...]
    row = lax.broadcasted_iota(jnp.int32, (width - model, tokens), 0)
    extra = jnp.zeros((width - model, tokens), f32)
    for expert in range(count):
        chosen = jnp.sum(jnp.where(ids == expert, sent, 0.0), axis=0, keepdims=True)
        extra = extra + jnp.where(row == expert, chosen, 0.0)
    for start in range(0, width, LANES):
        stop = start + LANES
        if stop <= model:
            block = grad_ref[start:stop, :].astype(f32)
        elif start >= model:
            block = extra[start - model : stop - model, :]
        else:
            block = jnp.concatenate(
                [grad_ref[start:model, :].astype(f32), extra[: stop - model, :]], axis=0
            )
        turned = block.T.astype(bf16)
        if start < cut:
            early_ref[:, start:stop] = turned
        else:
            late_ref[:, start - cut : stop - cut] = turned


def make_rows(grad_out, top_logits, expert_ids, width, cut):
    tokens, model = grad_out.shape
    count = top_logits.shape[1]
    return pl.pallas_call(
        functools.partial(rows_kernel, cut),
        out_shape=(
            jax.ShapeDtypeStruct((tokens, width - cut), bf16),
            jax.ShapeDtypeStruct((tokens, cut), bf16),
            jax.ShapeDtypeStruct((count, tokens), f32),
        ),
        in_specs=[pl.BlockSpec(memory_space=pltpu.HBM)] * 3,
        out_specs=(whole(),) * 3,
        scratch_shapes=[
            pltpu.VMEM((model, tokens), bf16),
            pltpu.VMEM((count, tokens), f32),
            pltpu.VMEM((count, tokens), jnp.int32),
            pltpu.SemaphoreType.DMA((3,)),
        ],
        compiler_params=params(58),
        cost_estimate=taking(2),
        name="make_rows",
    )(grad_out.T, top_logits.T, expert_ids.T)


def pack_kernel(*refs):
    out_ref, sems = refs[-2:]
    copies = []
    for place in range(out_ref.shape[0]):
        copies.append(pltpu.make_async_copy(refs[place], out_ref.at[place], sems.at[place]))
        copies[-1].start()
    for copy in copies:
        copy.wait()


def pack(values, after):
    number = len(values)
    return pl.pallas_call(
        pack_kernel,
        out_shape=jax.ShapeDtypeStruct((number, *values[0].shape), values[0].dtype),
        in_specs=[anywhere()] * (number + len(after)),
        out_specs=anywhere(),
        scratch_shapes=[pltpu.SemaphoreType.DMA((number,))],
        compiler_params=params(),
        cost_estimate=taking(1),
        name="pack_rows",
    )(*values, *after)


def blocks_of(refs, places):
    return [refs[array] if place is None else refs[array].at[place] for array, place in places]


def hold_kernel(*refs):
    del refs


def hold(values, after, weight=0):
    return pl.pallas_call(
        hold_kernel,
        out_shape=tuple(jax.ShapeDtypeStruct(value.shape, value.dtype) for value in values),
        in_specs=[anywhere()] * (len(values) + len(after)),
        out_specs=(anywhere(),) * len(values),
        input_output_aliases={place: place for place in range(len(values))},
        compiler_params=params(),
        cost_estimate=taking(weight),
        name="hold",
    )(*values, *after)


def split_kernel(table, where_ref, hidden_ref, *refs):
    own_ref, first_ref, rest_ref = refs[-3:]
    parts, units, _ = own_ref.shape
    row = lax.broadcasted_iota(jnp.int32, (2 * units, 2 * units), 0)
    column = lax.broadcasted_iota(jnp.int32, (2 * units, 2 * units), 1)
    unit = jnp.where(row == column, 1.0, 0.0).astype(bf16)
    low = where_ref[table["x"]] == 0
    for part in range(parts):
        block = hidden_ref[:, part * 2 * units : (part + 1) * 2 * units]
        turned = dot(unit, block, NT).astype(bf16)
        slot = where_ref[table["slot of", part]]
        other = jnp.where(low, turned[units:], turned[:units])
        own_ref[slot] = jnp.where(low, turned[:units], turned[units:])

        @pl.when(slot == 0)
        def _():
            first_ref[0] = other

        @pl.when(slot != 0)
        def _():
            rest_ref[slot - 1] = other


def split_hidden(table, where, hidden, parts, units, after):
    slots = hidden.shape[0]
    return pl.pallas_call(
        functools.partial(split_kernel, table),
        out_shape=tuple(
            jax.ShapeDtypeStruct((count, units, slots), bf16) for count in (parts, 1, parts - 1)
        ),
        in_specs=[scalars(), whole()] + [anywhere()] * len(after),
        out_specs=(whole(),) * 3,
        compiler_params=params(),
        cost_estimate=taking(2),
        name="split_hidden",
    )(where, hidden, *after)


def place_of(place, count, me, tokens):
    start = (place // count) * count * tokens + ((place % count) ^ me) * tokens
    return pl.multiple_of(start, tokens)


def scale_rows(table, model, where_ref, rows, gated, scaled):
    tokens = rows[0].shape[0]
    me = where_ref[table["me"]]
    lane = lax.broadcasted_iota(jnp.int32, (tokens, LANES), 1)
    for place, block in enumerate(rows):
        here = pl.ds(place_of(place, len(rows) // 2, me, tokens), tokens)
        tile = gated[place][:, gated[place].shape[1] - LANES :]
        picked = jnp.where(lane == model % LANES + me, tile.astype(f32), 0.0)
        gate = jnp.sum(picked, axis=1, keepdims=True)
        scaled[here, :] = (block[:, : scaled.shape[1]].astype(f32) * gate).astype(bf16)


def products_kernel(table, model, counts, places, shards, skip, where_it_runs, where_ref, *refs):
    used = sum(counts)
    rows = blocks_of(refs[: counts[0]], places[0])
    gated = blocks_of(refs[counts[0] : used], places[1])
    own_ref, other_ref = refs[used : used + 2]
    kept_ref, scaled, total_ref, sem = refs[-4:]
    units, slots = own_ref.shape[1:]

    def stacked(ref, offset):
        parts = [ref[offset + shard] for shard in range(shards)]
        return jnp.concatenate(parts, axis=0) if len(parts) > 1 else parts[0]

    def work():
        scale_rows(table, model, where_ref, rows, gated, scaled)
        total = dot(stacked(own_ref, skip), scaled[:slots, :], NN)
        total = total + dot(stacked(other_ref, 0), scaled[slots:, :], NN)
        for shard in range(shards):
            total_ref[shard] = total[shard * units : (shard + 1) * units]
        copy = pltpu.make_async_copy(total_ref, kept_ref, sem)
        copy.start()
        copy.wait()

    at_end = where_ref[table["use", 2, "A"]] == 0
    if where_it_runs == "ends":
        pl.when(at_end)(work)
    elif where_it_runs == "middle":
        pl.when(jnp.logical_not(at_end))(work)
    else:
        work()


def products(
    table, where, rows, gated, own, other, skip, model, width, name, after, where_it_runs="all", before=None
):
    arrays, places = zip(rows, gated)
    counts = [len(part) for part in arrays]
    shards, units, slots = other.shape
    kept = jax.ShapeDtypeStruct((shards, units, width), f32)
    operands = [*arrays[0], *arrays[1], own, other]
    extra = ([] if before is None else [before]) + list(after)
    return pl.pallas_call(
        functools.partial(products_kernel, table, model, counts, places, shards, skip, where_it_runs),
        out_shape=kept,
        in_specs=[scalars()] + [whole()] * len(operands) + [anywhere()] * len(extra),
        out_specs=anywhere(),
        scratch_shapes=[
            pltpu.VMEM((2 * slots, width), bf16),
            pltpu.VMEM(kept.shape, f32),
            pltpu.SemaphoreType.DMA,
        ],
        input_output_aliases={} if before is None else {1 + len(operands): 0},
        compiler_params=params(),
        cost_estimate=taking(1),
        name=name,
    )(where, *operands, *extra)


def first_kernel(table, model, counts, places, start, where_ref, *refs):
    used = sum(counts)
    rows = blocks_of(refs[: counts[0]], places[0])
    gated = blocks_of(refs[counts[0] : used], places[1])
    own_ref, other_ref, coming_ref = refs[used : used + 3]
    out_ref, scaled = refs[-2:]
    slots = own_ref.shape[2]
    ends = where_ref[table["use", 2, "A"]] == 0

    @pl.when(ends)
    def _():
        scale_rows(table, model, where_ref, rows, gated, scaled)
        total = dot(own_ref[0], scaled[:slots, :], NN)
        out_ref[...] = (total + dot(other_ref[0], scaled[slots:, :], NN)).astype(bf16)

    @pl.when(jnp.logical_not(ends))
    def _():
        out_ref[...] = coming_ref[:, start : start + out_ref.shape[1]]


def first_sums(table, where, rows, gated, own, other, coming, model, start, width, after):
    arrays, places = zip(rows, gated)
    counts = [len(part) for part in arrays]
    units, slots = own.shape[1:]
    return pl.pallas_call(
        functools.partial(first_kernel, table, model, counts, places, start),
        out_shape=jax.ShapeDtypeStruct((units, width), bf16),
        in_specs=[scalars()] + [whole()] * (sum(counts) + 3) + [anywhere()] * len(after),
        out_specs=whole(),
        scratch_shapes=[pltpu.VMEM((2 * slots, width), bf16)],
        compiler_params=params(),
        cost_estimate=taking(1),
        name="first_sums",
    )(where, *arrays[0], *arrays[1], own, other, coming, *after)


def rows_of(units):
    return units // 2 if units % 32 == 0 else units


def column_parts(arrays, cut):
    return [(0, arrays[0])] if len(arrays) == 1 else [(cut, arrays[0]), (0, arrays[1])]


def combine_kernel(table, key, cut, counts, sides, where_ref, *refs):
    slot = where_ref[table[key]]
    coming = refs[: counts[0]]
    outs = refs[len(refs) - counts[2] :]
    model = sum(ref.shape[1] for ref in outs)
    spans = [(cut, model), (0, cut)] if cut else [(0, model)]
    for chunk, (start, stop) in enumerate(spans):
        if counts[0] == 0:
            total = jnp.zeros((outs[0].shape[0], stop - start), f32)
        elif counts[0] == 1:
            total = coming[0][:, start:stop].astype(f32)
        else:
            total = coming[chunk][...].astype(f32)
        for number, side in enumerate(sides):
            flag = slot == 0 if side == "first" else slot > 0
            total = total + jnp.where(flag, refs[counts[0] + len(spans) * number + chunk][0], 0.0)
        total = total.astype(bf16)
        if counts[2] == 1:
            outs[0][:, start:stop] = total
        else:
            outs[chunk][...] = total


def combine(table, where, coming, first, rest, turn, name, used, cut, after, chunked=False, weight=1):
    units = first[0].shape[1]
    model = sum(part.shape[2] for part in first)
    block = rows_of(units)
    column = table["block", turn, name]
    sides, operands, specs = [], [], []
    if any(slot == 0 for slot in used):
        sides.append("first")
        operands += first
        specs += [pl.BlockSpec((1, block, part.shape[2]), lambda j, s: (0, j, 0)) for part in first]
    if any(slot > 0 for slot in used):
        sides.append("rest")
        operands += rest
        specs += [pl.BlockSpec((1, block, part.shape[2]), lambda j, s: (s[column], j, 0)) for part in rest]
    widths = [model - cut, cut] if chunked else [model]
    return pl.pallas_call(
        functools.partial(
            combine_kernel, table, ("use", turn, name), cut, (len(coming), len(operands), len(widths)), sides
        ),
        out_shape=[jax.ShapeDtypeStruct((units, count), bf16) for count in widths],
        grid_spec=pltpu.PrefetchScalarGridSpec(
            num_scalar_prefetch=1,
            grid=(units // block,),
            in_specs=[pl.BlockSpec((block, part.shape[1]), lambda j, s: (j, 0)) for part in coming]
            + specs
            + [anywhere()] * len(after),
            out_specs=[pl.BlockSpec((block, count), lambda j, s: (j, 0)) for count in widths],
        ),
        compiler_params=params(),
        cost_estimate=taking(weight),
        name="combine",
    )(where, *coming, *operands, *after)


def total_kernel(cut, counts, *refs):
    coming = [refs[: counts[0]], refs[counts[0] : sum(counts)]]
    out_ref = refs[-1]
    for chunk, start in enumerate((cut, 0)):
        kept_ref = refs[sum(counts) + chunk]
        here = slice(start, start + kept_ref.shape[2])
        total = kept_ref[0]
        for parts in coming:
            total = total + (parts[0][:, here] if len(parts) == 1 else parts[chunk][...]).astype(f32)
        out_ref[0, :, here] = total


def total_grad(a, b, kept, cut):
    units = a[0].shape[0]
    model = sum(part.shape[1] for part in a)
    block = rows_of(units)
    return pl.pallas_call(
        functools.partial(total_kernel, cut, (len(a), len(b))),
        out_shape=jax.ShapeDtypeStruct((1, units, model), f32),
        grid=(units // block,),
        in_specs=[pl.BlockSpec((block, part.shape[1]), lambda j: (j, 0)) for part in (*a, *b)]
        + [
            pl.BlockSpec((1, block, part.shape[2]), functools.partial(lambda last, j: (last, j, 0), part.shape[0] - 1))
            for part in kept
        ],
        out_specs=pl.BlockSpec((1, block, model), lambda j: (0, j, 0)),
        compiler_params=params(),
        cost_estimate=taking(2),
        name="total_grad",
    )(*a, *b, *kept)


def back_kernel(table, model, cut, counts, places, choices, parts, guard, summed, where_ref, *refs):
    keys = [key for choice in choices for key in choice]
    used = sum(counts)
    late = blocks_of(refs[: counts[0]], places[0])
    early = blocks_of(refs[counts[0] : used], places[1])
    number = len(late)
    own_ref, first_ref, rest_ref = refs[used : used + 3]
    weight_refs, used = {}, used + 3
    for key, count in zip(keys, parts):
        weight_refs[key] = refs[used : used + count]
        used += count
    before_ref = refs[used] if summed else None
    outs, sums_ref = refs[-3:-1], refs[-1]
    tokens = late[0].shape[0]
    units = own_ref.shape[1]
    me = where_ref[table["me"]]
    start = late[0].shape[1] - LANES
    eight = lax.broadcasted_iota(jnp.int32, (8, LANES), 1)
    onehot = jnp.where(eight == model % LANES + me, 1.0, 0.0).astype(bf16)
    shards = {key: where_ref[table[("shard",) + key]] for key in keys}
    slots = {key: where_ref[table[("slot",) + key]] for key in keys}
    sums_ref[...] = before_ref[...] if summed else jnp.zeros(sums_ref.shape, f32)

    def whole_weight(key):
        got = weight_refs[key]
        return got[0][...] if len(got) == 1 else jnp.concatenate([got[1][...], got[0][...]], axis=1)

    def work():
        stack, here_valid, here_slot = [], [], []
        for choice in choices:
            weight, valid, slot = whole_weight(choice[0]), shards[choice[0]] >= 0, slots[choice[0]]
            for key in choice[1:]:
                weight = jnp.where(valid, weight, whole_weight(key))
                slot = jnp.where(valid, slot, slots[key])
                valid = jnp.logical_or(valid, shards[key] >= 0)
            stack.append(weight)
            here_valid.append(valid)
            here_slot.append(slot)
        weight = jnp.concatenate(stack, axis=0) if len(stack) > 1 else stack[0]
        for pair in range(0, number, 2):
            both = jnp.concatenate(
                [
                    jnp.concatenate([early[k][...], late[k][:, : model - cut]], axis=1)
                    for k in (pair, pair + 1)
                ],
                axis=0,
            )
            product = dot(weight, both, NT)
            for place in (pair, pair + 1):
                near = place < number // 2
                block = product[:, (place - pair) * tokens : (place - pair + 1) * tokens]
                gate = dot(onehot, late[place][:, start:], NT)[0:1]
                here = pl.ds(place_of(place % (number // 2), number // 2, me, tokens), tokens)
                wide = pl.ds(place_of(place, number // 2, me, tokens), tokens)
                gated = (block * gate).astype(bf16)
                total = jnp.zeros((1, tokens), f32)
                for index, (valid, slot) in enumerate(zip(here_valid, here_slot)):
                    some = slice(index * units, (index + 1) * units)
                    outs[0 if near else 1][index, :, here] = gated[some]
                    if near:
                        hidden = own_ref[slot, :, here].astype(f32)
                    else:
                        hidden = jnp.where(
                            slot == 0,
                            first_ref[0, :, here].astype(f32),
                            rest_ref[jnp.maximum(slot - 1, 0), :, here].astype(f32),
                        )
                    part = jnp.sum(hidden * block[some], axis=0, keepdims=True)
                    total = total + jnp.where(valid, part, 0.0)
                sums_ref[0:1, wide] += total

    if guard:
        pl.when(functools.reduce(jnp.logical_or, [shards[key] >= 0 for key in keys]))(work)
    else:
        work()


def back_part(table, where, late, early, own, first, rest, choices, got, before, guard, after, model):
    units, slots = own.shape[1:]
    arrays, places = zip(late, early)
    counts = [len(part) for part in arrays]
    cut = arrays[1][0].shape[-1]
    keys = [key for choice in choices for key in choice]
    weights = [got[key] for key in keys]
    flat = [part for weight in weights for part in weight]
    half = jax.ShapeDtypeStruct((len(choices), units, slots), bf16)
    summed = before is not None
    operands = [*arrays[0], *arrays[1], own, first, rest, *flat] + ([before] if summed else [])
    outs = [half, half, jax.ShapeDtypeStruct((8, 2 * slots), f32)]
    parts = [len(weight) for weight in weights]
    return pl.pallas_call(
        functools.partial(
            back_kernel, table, model, cut, counts, places, choices, parts, guard, summed
        ),
        out_shape=outs,
        in_specs=[scalars()] + [whole()] * len(operands) + [anywhere()] * len(after),
        out_specs=[whole()] * len(outs),
        compiler_params=params(),
        cost_estimate=taking(6),
        name="back_part",
    )(where, *operands, *after)


def join_kernel(table, choices, where_ref, *refs):
    out_ref, done_ref, turned, sem = refs[-4:]
    done_ref[...] = jnp.zeros(done_ref.shape, f32)
    slots, width = turned.shape[1:]
    row = lax.broadcasted_iota(jnp.int32, (slots, slots), 0)
    column = lax.broadcasted_iota(jnp.int32, (slots, slots), 1)
    unit = jnp.where(row == column, 1.0, 0.0).astype(bf16)
    low = where_ref[table["x"]] == 0
    copies = []
    pairs = [
        (refs[2 * group][place], refs[2 * group + 1][place])
        for group in range((len(refs) - 4) // 2)
        for place in range(refs[2 * group].shape[0])
    ]
    for place, (choice, (mine, theirs)) in enumerate(zip(choices, pairs)):
        index = where_ref[table[("shard",) + choice[0]]]
        for key in choice[1:]:
            index = jnp.where(index >= 0, index, where_ref[table[("shard",) + key]])
        both = jnp.concatenate([jnp.where(low, mine, theirs), jnp.where(low, theirs, mine)], axis=0)
        turned[place] = dot(unit, both, NT).astype(bf16)
        here = pl.ds(pl.multiple_of(jnp.maximum(index, 0) * width, LANES), width)
        copy = pltpu.make_async_copy(turned.at[place], out_ref.at[:, here], sem.at[place])
        copies.append((index, copy))
        pl.when(index >= 0)(copy.start)
    for index, copy in copies:
        pl.when(index >= 0)(copy.wait)


def join_hidden(table, where, choices, halves, slots, hidden):
    units = halves[0].shape[1]
    return pl.pallas_call(
        functools.partial(join_kernel, table, choices),
        out_shape=(
            jax.ShapeDtypeStruct((slots, hidden), bf16),
            jax.ShapeDtypeStruct((8, LANES), f32),
        ),
        in_specs=[scalars()] + [whole()] * len(halves),
        out_specs=(anywhere(), whole()),
        scratch_shapes=[
            pltpu.VMEM((len(choices), slots, 2 * units), bf16),
            pltpu.SemaphoreType.DMA((len(choices),)),
        ],
        compiler_params=params(),
        cost_estimate=taking(2),
        name="join_hidden",
    )(where, *halves)


def logits_kernel(gates_ref, ids_ref, grads_ref, out_ref):
    gates, ids, grads = gates_ref[...], ids_ref[...], grads_ref[...]
    picked = jnp.zeros_like(gates)
    for expert in range(grads.shape[0]):
        picked = picked + jnp.where(ids == expert, grads[expert : expert + 1, :], 0.0)
    out_ref[...] = gates * (picked - jnp.sum(gates * picked, axis=0, keepdims=True))


def logits_grad(gates, ids, grads):
    return pl.pallas_call(
        logits_kernel,
        out_shape=jax.ShapeDtypeStruct(gates.shape, f32),
        in_specs=[whole()] * 3,
        out_specs=whole(),
        compiler_params=params(),
        cost_estimate=taking(1),
        name="logits_grad",
    )(gates, ids, grads)


def per_device_full(grad_out, top_logits, expert_ids, saved_hidden, w_down):
    experts = lax.axis_size("exp")
    groups = lax.axis_size("ctx")
    depth = groups // 2
    tokens, model = grad_out.shape
    slots, hidden = saved_hidden.shape[2:]
    width = pl.cdiv(model + experts, LANES) * LANES
    cut = width // LANES // 2 * LANES

    table, brought, uses = device_scalars(depth, experts)
    where = table.row(lax.axis_index("ctx"), lax.axis_index("exp"))

    def swap(value, x, exp):
        if not exp:
            return lax.ppermute(value, "ctx", [(i, i ^ x) for i in range(groups)])
        if not x:
            return lax.ppermute(value, "exp", [(i, i ^ exp) for i in range(experts)])
        pairs = [(c * experts + e, (c ^ x) * experts + (e ^ exp)) for c in range(groups) for e in range(experts)]
        return lax.ppermute(value, ("ctx", "exp"), pairs)

    def swap_z(value, name, senders=range(depth)):
        first = "AB".index(name)
        pairs = []
        for low in range(first, depth - 1, 2):
            for z, other in ((low, low + 1), (low + 1, low)):
                pairs += [(2 * z + x, 2 * other + x) for x in range(2) if z in senders]
        return lax.ppermute(value, "ctx", pairs)

    got = {(0, "own"): [w_down[0]]}
    for name in "BA":
        got[1, name] = [swap_z(w_down[0], name)]

    late, early, gates = make_rows(grad_out, top_logits, expert_ids, width, cut)
    highs = list(range(2, experts, 2))

    def sides(mine):
        return [mine, swap(mine, 0, 1)]

    late_x = swap(late, 1, 0)
    late_near = [late] + [swap(late, 0, high) for high in highs]
    own, other_first, other_rest = split_hidden(
        table, where, saved_hidden[0, 0], depth, w_down.shape[1], [late]
    )
    other_first = swap(other_first, 1, 0)
    (late_x,) = hold((late_x,), [], ORDER_WEIGHT)
    (late_x,) = hold((late_x,), late_near[1:])
    late_mine = late_near + [late_x] + [swap(late_x, 0, high) for high in highs]
    (early,) = hold((early,), [late_x, other_first])
    early_x = swap(early, 1, 0)
    late_rows = sides(pack(late_mine, [early_x]))
    late_rows = (late_rows, [(side, place) for place in range(experts) for side in range(2)])
    early_rows = sides(pack([early, early_x], []))
    early_far = [[swap(block, 0, high) for high in highs] for block in (early, early_x)]
    other_rest = swap(other_rest, 1, 0)

    got[1, "A"] = list(hold(got[1, "A"], [], ORDER_WEIGHT))
    got[1, "B"] = list(hold(got[1, "B"], got[1, "A"], FIRST_WEIGHT))
    chunks, first = [], []

    def first_chunk(rows, start, columns, after, before):
        chunks.append((rows, start, columns))
        value = first_sums(
            table, where, rows, late_rows, own, other_first, got[1, "B"][0], model, start, columns, after
        )
        if before:
            (value,) = hold([value], before, NEXT_WEIGHT)
        got.setdefault((2, "A"), []).append(swap_z(value, "A"))
        first.append(
            products(
                table, where, rows, late_rows, own, other_first, 0, model, columns, "first_kept", [value], "middle"
            )
        )
        return value

    first_chunk(late_rows, cut, model - cut, [early_rows[1]], [])
    places = []
    for base, blocks in enumerate(early_far):
        places += [(0, base), (1, base)]
        for block in hold(blocks, first):
            places += [(len(early_rows), None), (len(early_rows) + 1, None)]
            mine, theirs = sides(block)
            early_rows += [mine, theirs if base else hold([theirs], [], ORDER_WEIGHT)[0]]
    early_rows = (early_rows, places)
    marker = first_chunk(early_rows, 0, cut, [first[0]], got[2, "A"])
    got[2, "B"] = [swap_z(got[1, "A"][0], "B")]
    (other_rest,) = hold([other_rest], [], HIDDEN_WEIGHT)

    halves, all_choices, weights_of = [], [], {}
    only_first = max(uses[3, "B"]) <= 0

    def backprop(choices, before, guard, after):
        mine, theirs, sums = back_part(
            table, where, late_rows, early_rows, own, other_first, other_rest, choices,
            {**got, **weights_of}, before, guard, after, model,
        )
        halves.extend([mine, swap(theirs, 1, 0)])
        all_choices.extend(choices)
        return sums

    def forward(turn, name, after):
        coming = got[turn - 1, "B" if name == "A" else "A"]
        coming[:] = hold(coming, after, PASS_WEIGHT)
        others = [z for z in range(depth) if uses[turn, name][z] < 0]
        weights_of[turn, name] = [swap_z(coming[0], name, others)]

    def pass_on(turn, name, after, chunk=None, waited=(), weight=1):
        coming = got[turn - 1, "B" if name == "A" else "A"]
        used = uses[turn, name]
        senders = range(depth)
        if turn == depth - 1 and min(used) < 0 and name == "A" and len(coming) == 1:
            senders = [z for z in range(depth) if used[z] >= 0]
            if chunk is None:
                forward(turn, name, [])
            if set(senders) <= {0, depth - 1}:
                coming = []
        parts, start = (first, rest), cut
        if chunk is not None:
            coming, parts, start = coming[chunk:][:1], (first[chunk:][:1], rest[chunk:][:1]), 0
        values = list(combine(table, where, coming, *parts, turn, name, used, start, after, False, weight))
        if waited:
            values = list(hold(values, list(waited), WAITED_WEIGHT))
        got.setdefault((turn, name), []).extend(swap_z(value, name, senders) for value in values)
        return values[-1]

    def choices_of(turn):
        both = any(b[turn, "A"] >= 0 and b[turn, "B"] >= 0 for b in brought)
        return [[(turn, "A")], [(turn, "B")]] if both else [[(turn, "A"), (turn, "B")]]

    rest = []

    def other_products(chunk, after, *where_it_runs):
        rows, _, columns = chunks[chunk]
        return products(
            table, where, rows, late_rows, own, other_rest, 1, model, columns, "rest_kept", after, *where_it_runs
        )

    apart = max(uses[3, "B"]) <= 0 and depth == 4
    if apart:
        marker = pass_on(3, "B", [marker], 0)
        rest.append(other_products(0, [marker]))
        marker = pass_on(3, "A", rest, 0)
        forward(3, "A", [marker, first[1]])
        rest.append(other_products(1, got[2, "B"], "ends"))
        marker = pass_on(3, "A", rest, 1)
        marker = pass_on(3, "B", [marker], 1)
        rest[1] = other_products(1, [marker], "middle", rest[1])
        marker = rest[1]
    else:
        rest.append(other_products(0, [marker]))
        rest.append(other_products(1, rest))
        marker = pass_on(3, "A", rest)
        for chunk in range(2):
            marker = pass_on(3, "B", [marker], chunk)
    sums = backprop([[(0, "own")], [(1, "A")], [(1, "B")]], None, False, got[2, "A"][:1])
    sooner = halves[1::2]
    for turn in range(2, depth):
        choices = choices_of(turn)
        if turn > 2:
            waited = [array for key in ((turn, "A"), (turn, "B")) for array in weights_of.get(key, [])]
            if apart and turn + 1 == depth:
                pass_on(depth, "B", [], 0)
                pass_on(depth, "B", [], 1, sooner, LEAVE_WEIGHT)
                marker = pass_on(depth, "A", [sums], weight=LAST_WEIGHT)
                sums = backprop(choices_of(turn - 1), sums, True, [marker])
            else:
                pass_on(turn + 1, "B", [sums, *sooner, *waited])
                marker = pass_on(turn + 1, "A", [sums])
        if not apart or turn > 2:
            sums = backprop(choices, sums, len(choices) == 1, [marker])
    slot_grad = sums[0:1, :slots] + swap(sums[0:1, slots:], 1, 0)
    grads = lax.all_to_all(
        slot_grad.reshape(experts, tokens), "exp", split_axis=0, concat_axis=0, tiled=True
    )
    logit_grad = logits_grad(gates, expert_ids.T, grads)
    hidden_grad, joined = join_hidden(table, where, all_choices, halves, slots, hidden)
    if apart:
        entered = list(hold(got[depth, "B"][:1], [joined], ENTER_WEIGHT))
        got[depth, "B"] = entered + list(hold(got[depth, "B"][1:], entered, CLOSE_WEIGHT))
    weight_grad = total_grad(got[depth, "A"], got[depth, "B"], rest, cut)
    return (logit_grad.T, hidden_grad[None, None], weight_grad)


def routing_tables(expert_ids, count_experts, capacity):
    columns = jnp.arange(count_experts, dtype=jnp.int32)
    matches = expert_ids[:, :, None] == columns[None, None, :]
    per_token = jnp.sum(matches.astype(jnp.int32), axis=1)
    rank_table = jnp.cumsum(per_token, axis=0) - per_token
    slot_iota = jnp.arange(capacity, dtype=jnp.int32)
    select = (per_token.T[:, None, :] == 1) & (rank_table.T[:, None, :] == slot_iota[None, :, None])
    return (matches.astype(jnp.float32), select)


def per_device_routed(grad_out, top_logits, expert_ids, saved_hidden, w_down):
    count_experts = lax.axis_size("exp")
    slot_count = saved_hidden.shape[2]
    capacity = slot_count // count_experts
    model_width = grad_out.shape[1]
    onehot, select = routing_tables(expert_ids, count_experts, capacity)
    select_wide = select.astype(jnp.float32)
    gate_probs = jax.nn.softmax(top_logits, axis=-1)
    gate_sent = gate_probs.astype(jnp.bfloat16)
    gate_by_expert = jnp.sum(onehot * gate_sent.astype(jnp.float32)[:, :, None], axis=1)
    send_rows = jnp.einsum(
        "ect,td->ecd", select.astype(jnp.bfloat16), grad_out, preferred_element_type=jnp.float32
    ).astype(jnp.bfloat16)
    send_gate = jnp.sum(select_wide * gate_by_expert.T[:, None, :], axis=2).astype(jnp.bfloat16)
    hidden = saved_hidden[0, 0]
    rows_in, gate_in = (
        lax.all_to_all(send_rows, "exp", split_axis=0, concat_axis=0, tiled=True),
        lax.all_to_all(send_gate, "exp", split_axis=0, concat_axis=0, tiled=True),
    )
    flat_rows = rows_in.reshape(slot_count, model_width)
    backprop = lax.dot_general(
        flat_rows,
        lax.all_gather(w_down[0], "ctx", axis=0, tiled=True),
        (((1,), (1,)), ((), ())),
        preferred_element_type=jnp.float32,
    )
    flat_gate = gate_in.reshape(slot_count, 1).astype(jnp.float32)
    hidden_grad = (flat_gate * backprop).astype(jnp.bfloat16)
    slot_grad = jnp.sum(hidden.astype(jnp.float32) * backprop, axis=1)
    scaled = (flat_gate * flat_rows.astype(jnp.float32)).astype(jnp.bfloat16)
    partial_grad = lax.dot_general(
        hidden, scaled, (((0,), (0,)), ((), ())), preferred_element_type=jnp.float32
    )
    weight_grad = lax.psum_scatter(partial_grad, "ctx", scatter_dimension=0, tiled=True)
    returned = lax.all_to_all(
        slot_grad.reshape(count_experts, capacity), "exp", split_axis=0, concat_axis=0, tiled=True
    )
    grad_by_expert = jnp.sum(select_wide * returned[:, :, None], axis=1)
    gate_grad = jnp.sum(onehot * grad_by_expert.T[:, None, :], axis=2)
    logit_grad = gate_probs * (gate_grad - jnp.sum(gate_probs * gate_grad, axis=1, keepdims=True))
    return (logit_grad, hidden_grad.reshape(1, 1, slot_count, -1), weight_grad[None])


def per_device(grad_out, top_logits, expert_ids, saved_hidden, w_down):
    experts = lax.axis_size("exp")
    groups = lax.axis_size("ctx")
    everywhere = top_logits.shape[1] == experts and saved_hidden.shape[2] == experts * grad_out.shape[0]
    plain = experts & (experts - 1) == 0 and groups % 4 == 0 and groups >= 8
    body = per_device_full if everywhere and plain else per_device_routed
    return body(grad_out, top_logits, expert_ids, saved_hidden, w_down)


def solution(mesh):
    return jax.shard_map(
        per_device,
        mesh=mesh,
        in_specs=(
            P(("ctx", "exp"), None),
            P(("ctx", "exp"), None),
            P(("ctx", "exp"), None),
            P("ctx", "exp", None, None),
            P("exp", "ctx", None),
        ),
        out_specs=(P(("ctx", "exp"), None), P("ctx", "exp", None, None), P("exp", "ctx", None)),
        check_vma=False,
    )
```

```python
import functools

import jax
import jax.numpy as jnp
import numpy as np
from jax import lax
from jax.experimental import pallas as pl
from jax.experimental.pallas import tpu as pltpu
from jax.sharding import PartitionSpec as P

LANES = 128
SCALE = 1_000_000
SPLIT_MIB = 52
ORDER_WEIGHT = 100
FIRST_WEIGHT = 12_000
NEXT_WEIGHT = 600
HIDDEN_WEIGHT = 4_600
PASS_WEIGHT = 1
WAITED_WEIGHT = 1
ENTER_WEIGHT = 3_000
CLOSE_WEIGHT = 3_450
LEAVE_WEIGHT = 2_650
LAST_WEIGHT = 2_800
NT = (((1,), (1,)), ((), ()))
NN = (((1,), (0,)), ((), ()))
f32 = jnp.float32
bf16 = jnp.bfloat16


def dot(a, b, dims):
    return lax.dot_general(a, b, dims, preferred_element_type=f32)


def anywhere():
    return pl.BlockSpec(memory_space=pl.ANY)


def whole():
    return pl.BlockSpec(memory_space=pltpu.VMEM)


def scalars():
    return pl.BlockSpec(memory_space=pltpu.SMEM)


def params(mib=24):
    return pltpu.CompilerParams(vmem_limit_bytes=mib * 1024 * 1024)


def taking(microseconds):
    return pl.CostEstimate(flops=int(microseconds * SCALE), bytes_accessed=int(microseconds * 3e6), transcendentals=0)


def chain_plan(depth):
    products, weights = [], []
    for z in range(depth):
        uses = []
        for turn in range(2, depth + 1):
            if z < depth - 1 and turn >= z + 2:
                uses.append((turn, "AB"[z % 2], depth + 1 + z - turn))
            if z > 0 and turn >= depth - z + 1:
                uses.append((turn, "BA"[z % 2], z + turn - depth - 1))
        products.append(sorted(uses) + [(depth + 1, "own", z)])
        brought = {}
        for turn in range(1, depth):
            for name in "AB":
                index = z + turn if (name == "A") == (z % 2 == 0) else z - turn
                brought[turn, name] = index if 0 <= index < depth else -1
        weights.append(brought)
    return products, weights


class Scalars:
    def __init__(self):
        self.columns = []
        self.names = {}

    def add(self, name, values):
        self.names[name] = len(self.columns)
        self.columns.append(values)

    def __getitem__(self, name):
        return self.names[name]

    def row(self, place, me):
        return jnp.asarray(np.stack(self.columns, axis=-1).astype(np.int32))[place, me]


def device_scalars(depth, experts):
    products, weights = chain_plan(depth)
    table = Scalars()
    along = np.arange(2 * depth)[:, None] + np.zeros((1, experts), np.int32)

    def by_z(values):
        return np.asarray(values)[along // 2]

    table.add("x", along % 2)
    table.add("me", np.zeros_like(along) + np.arange(experts)[None, :])
    table.add(("shard", 0, "own"), along // 2)
    slot_of = [{use[2]: slot for slot, use in enumerate(products[z])} for z in range(depth)]
    for part in range(depth):
        table.add(("slot of", part), by_z([slot_of[z][part] for z in range(depth)]))
    table.add(("slot", 0, "own"), by_z([slot_of[z][z] for z in range(depth)]))
    for turn in range(1, depth):
        for name in "AB":
            shard = [weights[z][turn, name] for z in range(depth)]
            table.add(("shard", turn, name), by_z(shard))
            table.add(("slot", turn, name), by_z([slot_of[z].get(k, 0) for z, k in enumerate(shard)]))
    uses = {}
    for turn in range(2, depth + 1):
        for name in "AB":
            slots = [-1] * depth
            for z in range(depth):
                for slot, use in enumerate(products[z]):
                    if use[:2] == (turn, name):
                        slots[z] = slot
            uses[turn, name] = slots
            table.add(("use", turn, name), by_z(slots))
            limit = max(depth - 3, 0)
            table.add(("block", turn, name), by_z([min(max(slot - 1, 0), limit) for slot in slots]))
    return table, weights, uses


def rows_kernel(cut, grad_hbm, logits_hbm, ids_hbm, late_ref, early_ref, gates_ref, *scratch):
    grad_ref, logits_ref, ids_ref, sems = scratch
    model, tokens = grad_ref.shape
    bounds = list(range(cut, model, 4 * LANES)) + list(range(0, cut, 4 * LANES))
    copies = [
        pltpu.make_async_copy(source, target, sems.at[place])
        for place, (source, target) in enumerate(((logits_hbm, logits_ref), (ids_hbm, ids_ref)))
    ]
    pieces = {}
    for place, start in enumerate(bounds):
        here = slice(start, min(start + 4 * LANES, model if start >= cut else cut))
        pieces[start] = pltpu.make_async_copy(grad_hbm.at[here, :], grad_ref.at[here, :], sems.at[2 + place])
    for copy in [*pieces.values(), *copies]:
        copy.start()
    for copy in copies:
        copy.wait()
    count = logits_ref.shape[0]
    width = cut + late_ref.shape[1]
    logits = logits_ref[...]
    powers = jnp.exp(logits - jnp.max(logits, axis=0, keepdims=True))
    gates = powers / jnp.sum(powers, axis=0, keepdims=True)
    gates_ref[...] = gates
    sent = gates.astype(bf16).astype(f32)
    ids = ids_ref[...]
    row = lax.broadcasted_iota(jnp.int32, (width - model, tokens), 0)
    extra = jnp.zeros((width - model, tokens), f32)
    for expert in range(count):
        chosen = jnp.sum(jnp.where(ids == expert, sent, 0.0), axis=0, keepdims=True)
        extra = extra + jnp.where(row == expert, chosen, 0.0)
    for start in [*range(cut, width, LANES), *range(0, cut, LANES)]:
        stop = start + LANES
        if start in pieces:
            pieces[start].wait()
        if stop <= model:
            block = grad_ref[start:stop, :].astype(f32)
        elif start >= model:
            block = extra[start - model : stop - model, :]
        else:
            block = jnp.concatenate(
                [grad_ref[start:model, :].astype(f32), extra[: stop - model, :]], axis=0
            )
        turned = block.T.astype(bf16)
        if start < cut:
            early_ref[:, start:stop] = turned
        else:
            late_ref[:, start - cut : stop - cut] = turned


def make_rows(grad_out, top_logits, expert_ids, width, cut):
    tokens, model = grad_out.shape
    count = top_logits.shape[1]
    return pl.pallas_call(
        functools.partial(rows_kernel, cut),
        out_shape=(
            jax.ShapeDtypeStruct((tokens, width - cut), bf16),
            jax.ShapeDtypeStruct((tokens, cut), bf16),
            jax.ShapeDtypeStruct((count, tokens), f32),
        ),
        in_specs=[pl.BlockSpec(memory_space=pltpu.HBM)] * 3,
        out_specs=(whole(),) * 3,
        scratch_shapes=[
            pltpu.VMEM((model, tokens), bf16),
            pltpu.VMEM((count, tokens), f32),
            pltpu.VMEM((count, tokens), jnp.int32),
            pltpu.SemaphoreType.DMA((2 + pl.cdiv(cut, 4 * LANES) + pl.cdiv(model - cut, 4 * LANES),)),
        ],
        compiler_params=params(58),
        cost_estimate=taking(2),
        name="make_rows",
    )(grad_out.T, top_logits.T, expert_ids.T)


def pack_kernel(*refs):
    out_ref, sems = refs[-2:]
    copies = []
    for place in range(out_ref.shape[0]):
        copies.append(pltpu.make_async_copy(refs[place], out_ref.at[place], sems.at[place]))
        copies[-1].start()
    for copy in copies:
        copy.wait()


def pack(values, after):
    number = len(values)
    return pl.pallas_call(
        pack_kernel,
        out_shape=jax.ShapeDtypeStruct((number, *values[0].shape), values[0].dtype),
        in_specs=[anywhere()] * (number + len(after)),
        out_specs=anywhere(),
        scratch_shapes=[pltpu.SemaphoreType.DMA((number,))],
        compiler_params=params(),
        cost_estimate=taking(1),
        name="pack_rows",
    )(*values, *after)


def blocks_of(refs, places):
    return [refs[array] if place is None else refs[array].at[place] for array, place in places]


def hold_kernel(*refs):
    del refs


def hold(values, after, weight=0):
    return pl.pallas_call(
        hold_kernel,
        out_shape=tuple(jax.ShapeDtypeStruct(value.shape, value.dtype) for value in values),
        in_specs=[anywhere()] * (len(values) + len(after)),
        out_specs=(anywhere(),) * len(values),
        input_output_aliases={place: place for place in range(len(values))},
        compiler_params=params(),
        cost_estimate=taking(weight),
        name="hold",
    )(*values, *after)


def split_kernel(table, where_ref, hidden_ref, *refs):
    own_ref, first_ref, rest_ref, held, sems = refs[-5:]
    parts, units, _ = own_ref.shape
    copies = []
    for part in range(parts):
        here = slice(part * 2 * units, (part + 1) * 2 * units)
        copies.append(pltpu.make_async_copy(hidden_ref.at[:, here], held.at[:, here], sems.at[part]))
        copies[-1].start()
    row = lax.broadcasted_iota(jnp.int32, (2 * units, 2 * units), 0)
    column = lax.broadcasted_iota(jnp.int32, (2 * units, 2 * units), 1)
    unit = jnp.where(row == column, 1.0, 0.0).astype(bf16)
    low = where_ref[table["x"]] == 0
    for part in range(parts):
        copies[part].wait()
        block = held[:, part * 2 * units : (part + 1) * 2 * units]
        turned = dot(unit, block, NT).astype(bf16)
        slot = where_ref[table["slot of", part]]
        other = jnp.where(low, turned[units:], turned[:units])
        own_ref[slot] = jnp.where(low, turned[:units], turned[units:])

        @pl.when(slot == 0)
        def _():
            first_ref[0] = other

        @pl.when(slot != 0)
        def _():
            rest_ref[slot - 1] = other


def split_hidden(table, where, hidden, parts, units, after):
    slots = hidden.shape[0]
    return pl.pallas_call(
        functools.partial(split_kernel, table),
        out_shape=tuple(
            jax.ShapeDtypeStruct((count, units, slots), bf16) for count in (parts, 1, parts - 1)
        ),
        in_specs=[scalars()] + [anywhere()] * (1 + len(after)),
        out_specs=(whole(),) * 3,
        scratch_shapes=[pltpu.VMEM(hidden.shape, bf16), pltpu.SemaphoreType.DMA((parts,))],
        compiler_params=params(SPLIT_MIB),
        cost_estimate=taking(2),
        name="split_hidden",
    )(where, hidden, *after)


def place_of(place, count, me, tokens):
    start = (place // count) * count * tokens + ((place % count) ^ me) * tokens
    return pl.multiple_of(start, tokens)


def scale_rows(table, model, where_ref, rows, gated, scaled):
    tokens = rows[0].shape[0]
    me = where_ref[table["me"]]
    lane = lax.broadcasted_iota(jnp.int32, (tokens, LANES), 1)
    for place, block in enumerate(rows):
        here = pl.ds(place_of(place, len(rows) // 2, me, tokens), tokens)
        tile = gated[place][:, gated[place].shape[1] - LANES :]
        picked = jnp.where(lane == model % LANES + me, tile.astype(f32), 0.0)
        gate = jnp.sum(picked, axis=1, keepdims=True)
        scaled[here, :] = (block[:, : scaled.shape[1]].astype(f32) * gate).astype(bf16)


def products_kernel(table, model, counts, places, shards, skip, where_it_runs, where_ref, *refs):
    used = sum(counts)
    rows = blocks_of(refs[: counts[0]], places[0])
    gated = blocks_of(refs[counts[0] : used], places[1])
    own_ref, other_ref = refs[used : used + 2]
    kept_ref, scaled, total_ref, sem = refs[-4:]
    units, slots = own_ref.shape[1:]

    def stacked(ref, offset):
        parts = [ref[offset + shard] for shard in range(shards)]
        return jnp.concatenate(parts, axis=0) if len(parts) > 1 else parts[0]

    def work():
        scale_rows(table, model, where_ref, rows, gated, scaled)
        total = dot(stacked(own_ref, skip), scaled[:slots, :], NN)
        total = total + dot(stacked(other_ref, 0), scaled[slots:, :], NN)
        for shard in range(shards):
            total_ref[shard] = total[shard * units : (shard + 1) * units]
        copy = pltpu.make_async_copy(total_ref, kept_ref, sem)
        copy.start()
        copy.wait()

    at_end = where_ref[table["use", 2, "A"]] == 0
    if where_it_runs == "ends":
        pl.when(at_end)(work)
    elif where_it_runs == "middle":
        pl.when(jnp.logical_not(at_end))(work)
    else:
        work()


def products(
    table, where, rows, gated, own, other, skip, model, width, name, after, where_it_runs="all", before=None
):
    arrays, places = zip(rows, gated)
    counts = [len(part) for part in arrays]
    shards, units, slots = other.shape
    kept = jax.ShapeDtypeStruct((shards, units, width), f32)
    operands = [*arrays[0], *arrays[1], own, other]
    extra = ([] if before is None else [before]) + list(after)
    return pl.pallas_call(
        functools.partial(products_kernel, table, model, counts, places, shards, skip, where_it_runs),
        out_shape=kept,
        in_specs=[scalars()] + [whole()] * len(operands) + [anywhere()] * len(extra),
        out_specs=anywhere(),
        scratch_shapes=[
            pltpu.VMEM((2 * slots, width), bf16),
            pltpu.VMEM(kept.shape, f32),
            pltpu.SemaphoreType.DMA,
        ],
        input_output_aliases={} if before is None else {1 + len(operands): 0},
        compiler_params=params(),
        cost_estimate=taking(1),
        name=name,
    )(where, *operands, *extra)


def first_kernel(table, model, counts, places, start, where_ref, *refs):
    used = sum(counts)
    rows = blocks_of(refs[: counts[0]], places[0])
    gated = blocks_of(refs[counts[0] : used], places[1])
    own_ref, other_ref, coming_ref = refs[used : used + 3]
    out_ref, scaled = refs[-2:]
    slots = own_ref.shape[2]
    ends = where_ref[table["use", 2, "A"]] == 0

    @pl.when(ends)
    def _():
        scale_rows(table, model, where_ref, rows, gated, scaled)
        total = dot(own_ref[0], scaled[:slots, :], NN)
        out_ref[...] = (total + dot(other_ref[0], scaled[slots:, :], NN)).astype(bf16)

    @pl.when(jnp.logical_not(ends))
    def _():
        out_ref[...] = coming_ref[:, start : start + out_ref.shape[1]]


def first_sums(table, where, rows, gated, own, other, coming, model, start, width, after):
    arrays, places = zip(rows, gated)
    counts = [len(part) for part in arrays]
    units, slots = own.shape[1:]
    return pl.pallas_call(
        functools.partial(first_kernel, table, model, counts, places, start),
        out_shape=jax.ShapeDtypeStruct((units, width), bf16),
        in_specs=[scalars()] + [whole()] * (sum(counts) + 3) + [anywhere()] * len(after),
        out_specs=whole(),
        scratch_shapes=[pltpu.VMEM((2 * slots, width), bf16)],
        compiler_params=params(),
        cost_estimate=taking(1),
        name="first_sums",
    )(where, *arrays[0], *arrays[1], own, other, coming, *after)


def rows_of(units):
    return units // 2 if units % 32 == 0 else units


def column_parts(arrays, cut):
    return [(0, arrays[0])] if len(arrays) == 1 else [(cut, arrays[0]), (0, arrays[1])]


def combine_kernel(table, key, cut, counts, sides, where_ref, *refs):
    slot = where_ref[table[key]]
    coming = refs[: counts[0]]
    outs = refs[len(refs) - counts[2] :]
    model = sum(ref.shape[1] for ref in outs)
    spans = [(cut, model), (0, cut)] if cut else [(0, model)]
    for chunk, (start, stop) in enumerate(spans):
        if counts[0] == 0:
            total = jnp.zeros((outs[0].shape[0], stop - start), f32)
        elif counts[0] == 1:
            total = coming[0][:, start:stop].astype(f32)
        else:
            total = coming[chunk][...].astype(f32)
        for number, side in enumerate(sides):
            flag = slot == 0 if side == "first" else slot > 0
            total = total + jnp.where(flag, refs[counts[0] + len(spans) * number + chunk][0], 0.0)
        total = total.astype(bf16)
        if counts[2] == 1:
            outs[0][:, start:stop] = total
        else:
            outs[chunk][...] = total


def combine(table, where, coming, first, rest, turn, name, used, cut, after, chunked=False, weight=1):
    units = first[0].shape[1]
    model = sum(part.shape[2] for part in first)
    block = rows_of(units)
    column = table["block", turn, name]
    sides, operands, specs = [], [], []
    if any(slot == 0 for slot in used):
        sides.append("first")
        operands += first
        specs += [pl.BlockSpec((1, block, part.shape[2]), lambda j, s: (0, j, 0)) for part in first]
    if any(slot > 0 for slot in used):
        sides.append("rest")
        operands += rest
        specs += [pl.BlockSpec((1, block, part.shape[2]), lambda j, s: (s[column], j, 0)) for part in rest]
    widths = [model - cut, cut] if chunked else [model]
    return pl.pallas_call(
        functools.partial(
            combine_kernel, table, ("use", turn, name), cut, (len(coming), len(operands), len(widths)), sides
        ),
        out_shape=[jax.ShapeDtypeStruct((units, count), bf16) for count in widths],
        grid_spec=pltpu.PrefetchScalarGridSpec(
            num_scalar_prefetch=1,
            grid=(units // block,),
            in_specs=[pl.BlockSpec((block, part.shape[1]), lambda j, s: (j, 0)) for part in coming]
            + specs
            + [anywhere()] * len(after),
            out_specs=[pl.BlockSpec((block, count), lambda j, s: (j, 0)) for count in widths],
        ),
        compiler_params=params(),
        cost_estimate=taking(weight),
        name="combine",
    )(where, *coming, *operands, *after)


def total_kernel(cut, counts, *refs):
    coming = [refs[: counts[0]], refs[counts[0] : sum(counts)]]
    out_ref = refs[-1]
    for chunk, start in enumerate((cut, 0)):
        kept_ref = refs[sum(counts) + chunk]
        here = slice(start, start + kept_ref.shape[2])
        total = kept_ref[0]
        for parts in coming:
            total = total + (parts[0][:, here] if len(parts) == 1 else parts[chunk][...]).astype(f32)
        out_ref[0, :, here] = total


def total_grad(a, b, kept, cut):
    units = a[0].shape[0]
    model = sum(part.shape[1] for part in a)
    block = rows_of(units)
    return pl.pallas_call(
        functools.partial(total_kernel, cut, (len(a), len(b))),
        out_shape=jax.ShapeDtypeStruct((1, units, model), f32),
        grid=(units // block,),
        in_specs=[pl.BlockSpec((block, part.shape[1]), lambda j: (j, 0)) for part in (*a, *b)]
        + [
            pl.BlockSpec((1, block, part.shape[2]), functools.partial(lambda last, j: (last, j, 0), part.shape[0] - 1))
            for part in kept
        ],
        out_specs=pl.BlockSpec((1, block, model), lambda j: (0, j, 0)),
        compiler_params=params(),
        cost_estimate=taking(2),
        name="total_grad",
    )(*a, *b, *kept)


def back_kernel(table, model, cut, counts, places, choices, parts, guard, summed, where_ref, *refs):
    keys = [key for choice in choices for key in choice]
    used = sum(counts)
    late = blocks_of(refs[: counts[0]], places[0])
    early = blocks_of(refs[counts[0] : used], places[1])
    number = len(late)
    own_ref, first_ref, rest_ref = refs[used : used + 3]
    weight_refs, used = {}, used + 3
    for key, count in zip(keys, parts):
        weight_refs[key] = refs[used : used + count]
        used += count
    before_ref = refs[used] if summed else None
    outs, sums_ref = refs[-3:-1], refs[-1]
    tokens = late[0].shape[0]
    units = own_ref.shape[1]
    me = where_ref[table["me"]]
    start = late[0].shape[1] - LANES
    eight = lax.broadcasted_iota(jnp.int32, (8, LANES), 1)
    onehot = jnp.where(eight == model % LANES + me, 1.0, 0.0).astype(bf16)
    shards = {key: where_ref[table[("shard",) + key]] for key in keys}
    slots = {key: where_ref[table[("slot",) + key]] for key in keys}
    sums_ref[...] = before_ref[...] if summed else jnp.zeros(sums_ref.shape, f32)

    def whole_weight(key):
        got = weight_refs[key]
        return got[0][...] if len(got) == 1 else jnp.concatenate([got[1][...], got[0][...]], axis=1)

    def work():
        stack, here_valid, here_slot = [], [], []
        for choice in choices:
            weight, valid, slot = whole_weight(choice[0]), shards[choice[0]] >= 0, slots[choice[0]]
            for key in choice[1:]:
                weight = jnp.where(valid, weight, whole_weight(key))
                slot = jnp.where(valid, slot, slots[key])
                valid = jnp.logical_or(valid, shards[key] >= 0)
            stack.append(weight)
            here_valid.append(valid)
            here_slot.append(slot)
        weight = jnp.concatenate(stack, axis=0) if len(stack) > 1 else stack[0]
        for pair in range(0, number, 2):
            both = jnp.concatenate(
                [
                    jnp.concatenate([early[k][...], late[k][:, : model - cut]], axis=1)
                    for k in (pair, pair + 1)
                ],
                axis=0,
            )
            product = dot(weight, both, NT)
            for place in (pair, pair + 1):
                near = place < number // 2
                block = product[:, (place - pair) * tokens : (place - pair + 1) * tokens]
                gate = dot(onehot, late[place][:, start:], NT)[0:1]
                here = pl.ds(place_of(place % (number // 2), number // 2, me, tokens), tokens)
                wide = pl.ds(place_of(place, number // 2, me, tokens), tokens)
                gated = (block * gate).astype(bf16)
                total = jnp.zeros((1, tokens), f32)
                for index, (valid, slot) in enumerate(zip(here_valid, here_slot)):
                    some = slice(index * units, (index + 1) * units)
                    outs[0 if near else 1][index, :, here] = gated[some]
                    if near:
                        hidden = own_ref[slot, :, here].astype(f32)
                    else:
                        hidden = jnp.where(
                            slot == 0,
                            first_ref[0, :, here].astype(f32),
                            rest_ref[jnp.maximum(slot - 1, 0), :, here].astype(f32),
                        )
                    part = jnp.sum(hidden * block[some], axis=0, keepdims=True)
                    total = total + jnp.where(valid, part, 0.0)
                sums_ref[0:1, wide] += total

    if guard:
        pl.when(functools.reduce(jnp.logical_or, [shards[key] >= 0 for key in keys]))(work)
    else:
        work()


def back_part(table, where, late, early, own, first, rest, choices, got, before, guard, after, model):
    units, slots = own.shape[1:]
    arrays, places = zip(late, early)
    counts = [len(part) for part in arrays]
    cut = arrays[1][0].shape[-1]
    keys = [key for choice in choices for key in choice]
    weights = [got[key] for key in keys]
    flat = [part for weight in weights for part in weight]
    half = jax.ShapeDtypeStruct((len(choices), units, slots), bf16)
    summed = before is not None
    operands = [*arrays[0], *arrays[1], own, first, rest, *flat] + ([before] if summed else [])
    outs = [half, half, jax.ShapeDtypeStruct((8, 2 * slots), f32)]
    parts = [len(weight) for weight in weights]
    return pl.pallas_call(
        functools.partial(
            back_kernel, table, model, cut, counts, places, choices, parts, guard, summed
        ),
        out_shape=outs,
        in_specs=[scalars()] + [whole()] * len(operands) + [anywhere()] * len(after),
        out_specs=[whole()] * len(outs),
        compiler_params=params(),
        cost_estimate=taking(6),
        name="back_part",
    )(where, *operands, *after)


def join_kernel(table, choices, where_ref, *refs):
    out_ref, done_ref, turned, sem = refs[-4:]
    done_ref[...] = jnp.zeros(done_ref.shape, f32)
    slots, width = turned.shape[1:]
    row = lax.broadcasted_iota(jnp.int32, (slots, slots), 0)
    column = lax.broadcasted_iota(jnp.int32, (slots, slots), 1)
    unit = jnp.where(row == column, 1.0, 0.0).astype(bf16)
    low = where_ref[table["x"]] == 0
    copies = []
    pairs = [
        (refs[2 * group][place], refs[2 * group + 1][place])
        for group in range((len(refs) - 4) // 2)
        for place in range(refs[2 * group].shape[0])
    ]
    for place, (choice, (mine, theirs)) in enumerate(zip(choices, pairs)):
        index = where_ref[table[("shard",) + choice[0]]]
        for key in choice[1:]:
            index = jnp.where(index >= 0, index, where_ref[table[("shard",) + key]])
        both = jnp.concatenate([jnp.where(low, mine, theirs), jnp.where(low, theirs, mine)], axis=0)
        turned[place] = dot(unit, both, NT).astype(bf16)
        here = pl.ds(pl.multiple_of(jnp.maximum(index, 0) * width, LANES), width)
        copy = pltpu.make_async_copy(turned.at[place], out_ref.at[:, here], sem.at[place])
        copies.append((index, copy))
        pl.when(index >= 0)(copy.start)
    for index, copy in copies:
        pl.when(index >= 0)(copy.wait)


def join_hidden(table, where, choices, halves, slots, hidden):
    units = halves[0].shape[1]
    return pl.pallas_call(
        functools.partial(join_kernel, table, choices),
        out_shape=(
            jax.ShapeDtypeStruct((slots, hidden), bf16),
            jax.ShapeDtypeStruct((8, LANES), f32),
        ),
        in_specs=[scalars()] + [whole()] * len(halves),
        out_specs=(anywhere(), whole()),
        scratch_shapes=[
            pltpu.VMEM((len(choices), slots, 2 * units), bf16),
            pltpu.SemaphoreType.DMA((len(choices),)),
        ],
        compiler_params=params(),
        cost_estimate=taking(2),
        name="join_hidden",
    )(where, *halves)


def logits_kernel(gates_ref, ids_ref, grads_ref, out_ref):
    gates, ids, grads = gates_ref[...], ids_ref[...], grads_ref[...]
    picked = jnp.zeros_like(gates)
    for expert in range(grads.shape[0]):
        picked = picked + jnp.where(ids == expert, grads[expert : expert + 1, :], 0.0)
    out_ref[...] = gates * (picked - jnp.sum(gates * picked, axis=0, keepdims=True))


def logits_grad(gates, ids, grads):
    return pl.pallas_call(
        logits_kernel,
        out_shape=jax.ShapeDtypeStruct(gates.shape, f32),
        in_specs=[whole()] * 3,
        out_specs=whole(),
        compiler_params=params(),
        cost_estimate=taking(1),
        name="logits_grad",
    )(gates, ids, grads)


def per_device_full(grad_out, top_logits, expert_ids, saved_hidden, w_down):
    experts = lax.axis_size("exp")
    groups = lax.axis_size("ctx")
    depth = groups // 2
    tokens, model = grad_out.shape
    slots, hidden = saved_hidden.shape[2:]
    width = pl.cdiv(model + experts, LANES) * LANES
    cut = width // LANES // 2 * LANES

    table, brought, uses = device_scalars(depth, experts)
    where = table.row(lax.axis_index("ctx"), lax.axis_index("exp"))

    def swap(value, x, exp):
        if not exp:
            return lax.ppermute(value, "ctx", [(i, i ^ x) for i in range(groups)])
        if not x:
            return lax.ppermute(value, "exp", [(i, i ^ exp) for i in range(experts)])
        pairs = [(c * experts + e, (c ^ x) * experts + (e ^ exp)) for c in range(groups) for e in range(experts)]
        return lax.ppermute(value, ("ctx", "exp"), pairs)

    def swap_z(value, name, senders=range(depth)):
        first = "AB".index(name)
        pairs = []
        for low in range(first, depth - 1, 2):
            for z, other in ((low, low + 1), (low + 1, low)):
                pairs += [(2 * z + x, 2 * other + x) for x in range(2) if z in senders]
        return lax.ppermute(value, "ctx", pairs)

    got = {(0, "own"): [w_down[0]]}
    for name in "BA":
        got[1, name] = [swap_z(w_down[0], name)]

    late, early, gates = make_rows(grad_out, top_logits, expert_ids, width, cut)
    highs = list(range(2, experts, 2))

    def sides(mine):
        return [mine, swap(mine, 0, 1)]

    late_x = swap(late, 1, 0)
    late_near = [late] + [swap(late, 0, high) for high in highs]
    own, other_first, other_rest = split_hidden(
        table, where, saved_hidden[0, 0], depth, w_down.shape[1], [late]
    )
    other_first = swap(other_first, 1, 0)
    (late_x,) = hold((late_x,), [], ORDER_WEIGHT)
    (late_x,) = hold((late_x,), late_near[1:])
    late_mine = late_near + [late_x] + [swap(late_x, 0, high) for high in highs]
    (early,) = hold((early,), [late_x, other_first])
    early_x = swap(early, 1, 0)
    late_rows = sides(pack(late_mine, [early_x]))
    late_rows = (late_rows, [(side, place) for place in range(experts) for side in range(2)])
    early_rows = sides(pack([early, early_x], []))
    early_far = [[swap(block, 0, high) for high in highs] for block in (early, early_x)]
    other_rest = swap(other_rest, 1, 0)

    got[1, "A"] = list(hold(got[1, "A"], [], ORDER_WEIGHT))
    got[1, "B"] = list(hold(got[1, "B"], got[1, "A"], FIRST_WEIGHT))
    chunks, first = [], []

    def first_chunk(rows, start, columns, after, before):
        chunks.append((rows, start, columns))
        value = first_sums(
            table, where, rows, late_rows, own, other_first, got[1, "B"][0], model, start, columns, after
        )
        if before:
            (value,) = hold([value], before, NEXT_WEIGHT)
        got.setdefault((2, "A"), []).append(swap_z(value, "A"))
        first.append(
            products(
                table, where, rows, late_rows, own, other_first, 0, model, columns, "first_kept", [value], "middle"
            )
        )
        return value

    first_chunk(late_rows, cut, model - cut, [early_rows[1]], [])
    places = []
    for base, blocks in enumerate(early_far):
        places += [(0, base), (1, base)]
        for block in hold(blocks, first):
            places += [(len(early_rows), None), (len(early_rows) + 1, None)]
            mine, theirs = sides(block)
            early_rows += [mine, theirs if base else hold([theirs], [], ORDER_WEIGHT)[0]]
    early_rows = (early_rows, places)
    marker = first_chunk(early_rows, 0, cut, [first[0]], got[2, "A"])
    got[2, "B"] = [swap_z(got[1, "A"][0], "B")]
    (other_rest,) = hold([other_rest], [], HIDDEN_WEIGHT)

    halves, all_choices, weights_of = [], [], {}
    only_first = max(uses[3, "B"]) <= 0

    def backprop(choices, before, guard, after):
        mine, theirs, sums = back_part(
            table, where, late_rows, early_rows, own, other_first, other_rest, choices,
            {**got, **weights_of}, before, guard, after, model,
        )
        halves.extend([mine, swap(theirs, 1, 0)])
        all_choices.extend(choices)
        return sums

    def forward(turn, name, after):
        coming = got[turn - 1, "B" if name == "A" else "A"]
        coming[:] = hold(coming, after, PASS_WEIGHT)
        others = [z for z in range(depth) if uses[turn, name][z] < 0]
        weights_of[turn, name] = [swap_z(coming[0], name, others)]

    def pass_on(turn, name, after, chunk=None, waited=(), weight=1):
        coming = got[turn - 1, "B" if name == "A" else "A"]
        used = uses[turn, name]
        senders = range(depth)
        if turn == depth - 1 and min(used) < 0 and name == "A" and len(coming) == 1:
            senders = [z for z in range(depth) if used[z] >= 0]
            if chunk is None:
                forward(turn, name, [])
            if set(senders) <= {0, depth - 1}:
                coming = []
        parts, start = (first, rest), cut
        if chunk is not None:
            coming, parts, start = coming[chunk:][:1], (first[chunk:][:1], rest[chunk:][:1]), 0
        values = list(combine(table, where, coming, *parts, turn, name, used, start, after, False, weight))
        if waited:
            values = list(hold(values, list(waited), WAITED_WEIGHT))
        got.setdefault((turn, name), []).extend(swap_z(value, name, senders) for value in values)
        return values[-1]

    def choices_of(turn):
        both = any(b[turn, "A"] >= 0 and b[turn, "B"] >= 0 for b in brought)
        return [[(turn, "A")], [(turn, "B")]] if both else [[(turn, "A"), (turn, "B")]]

    rest = []

    def other_products(chunk, after, *where_it_runs):
        rows, _, columns = chunks[chunk]
        return products(
            table, where, rows, late_rows, own, other_rest, 1, model, columns, "rest_kept", after, *where_it_runs
        )

    apart = max(uses[3, "B"]) <= 0 and depth == 4
    if apart:
        marker = pass_on(3, "B", [marker], 0)
        rest.append(other_products(0, [marker]))
        marker = pass_on(3, "A", rest, 0)
        forward(3, "A", [marker, first[1]])
        rest.append(other_products(1, got[2, "B"], "ends"))
        marker = pass_on(3, "A", rest, 1)
        marker = pass_on(3, "B", [marker], 1)
        rest[1] = other_products(1, [marker], "middle", rest[1])
        marker = rest[1]
    else:
        rest.append(other_products(0, [marker]))
        rest.append(other_products(1, rest))
        marker = pass_on(3, "A", rest)
        for chunk in range(2):
            marker = pass_on(3, "B", [marker], chunk)
    sums = backprop([[(0, "own")], [(1, "A")], [(1, "B")]], None, False, got[2, "A"][:1])
    sooner = halves[1::2]
    for turn in range(2, depth):
        choices = choices_of(turn)
        if turn > 2:
            waited = [array for key in ((turn, "A"), (turn, "B")) for array in weights_of.get(key, [])]
            if apart and turn + 1 == depth:
                pass_on(depth, "B", [], 0)
                pass_on(depth, "B", [], 1, sooner, LEAVE_WEIGHT)
                marker = pass_on(depth, "A", [sums], weight=LAST_WEIGHT)
                sums = backprop(choices_of(turn - 1), sums, True, [marker])
            else:
                pass_on(turn + 1, "B", [sums, *sooner, *waited])
                marker = pass_on(turn + 1, "A", [sums])
        if not apart or turn > 2:
            sums = backprop(choices, sums, len(choices) == 1, [marker])
    slot_grad = sums[0:1, :slots] + swap(sums[0:1, slots:], 1, 0)
    grads = lax.all_to_all(
        slot_grad.reshape(experts, tokens), "exp", split_axis=0, concat_axis=0, tiled=True
    )
    logit_grad = logits_grad(gates, expert_ids.T, grads)
    hidden_grad, joined = join_hidden(table, where, all_choices, halves, slots, hidden)
    if apart:
        entered = list(hold(got[depth, "B"][:1], [joined], ENTER_WEIGHT))
        got[depth, "B"] = entered + list(hold(got[depth, "B"][1:], entered, CLOSE_WEIGHT))
    weight_grad = total_grad(got[depth, "A"], got[depth, "B"], rest, cut)
    return (logit_grad.T, hidden_grad[None, None], weight_grad)


def routing_tables(expert_ids, count_experts, capacity):
    columns = jnp.arange(count_experts, dtype=jnp.int32)
    matches = expert_ids[:, :, None] == columns[None, None, :]
    per_token = jnp.sum(matches.astype(jnp.int32), axis=1)
    rank_table = jnp.cumsum(per_token, axis=0) - per_token
    slot_iota = jnp.arange(capacity, dtype=jnp.int32)
    select = (per_token.T[:, None, :] == 1) & (rank_table.T[:, None, :] == slot_iota[None, :, None])
    return (matches.astype(jnp.float32), select)


def per_device_routed(grad_out, top_logits, expert_ids, saved_hidden, w_down):
    count_experts = lax.axis_size("exp")
    slot_count = saved_hidden.shape[2]
    capacity = slot_count // count_experts
    model_width = grad_out.shape[1]
    onehot, select = routing_tables(expert_ids, count_experts, capacity)
    select_wide = select.astype(jnp.float32)
    gate_probs = jax.nn.softmax(top_logits, axis=-1)
    gate_sent = gate_probs.astype(jnp.bfloat16)
    gate_by_expert = jnp.sum(onehot * gate_sent.astype(jnp.float32)[:, :, None], axis=1)
    send_rows = jnp.einsum(
        "ect,td->ecd", select.astype(jnp.bfloat16), grad_out, preferred_element_type=jnp.float32
    ).astype(jnp.bfloat16)
    send_gate = jnp.sum(select_wide * gate_by_expert.T[:, None, :], axis=2).astype(jnp.bfloat16)
    hidden = saved_hidden[0, 0]
    rows_in, gate_in = (
        lax.all_to_all(send_rows, "exp", split_axis=0, concat_axis=0, tiled=True),
        lax.all_to_all(send_gate, "exp", split_axis=0, concat_axis=0, tiled=True),
    )
    flat_rows = rows_in.reshape(slot_count, model_width)
    backprop = lax.dot_general(
        flat_rows,
        lax.all_gather(w_down[0], "ctx", axis=0, tiled=True),
        (((1,), (1,)), ((), ())),
        preferred_element_type=jnp.float32,
    )
    flat_gate = gate_in.reshape(slot_count, 1).astype(jnp.float32)
    hidden_grad = (flat_gate * backprop).astype(jnp.bfloat16)
    slot_grad = jnp.sum(hidden.astype(jnp.float32) * backprop, axis=1)
    scaled = (flat_gate * flat_rows.astype(jnp.float32)).astype(jnp.bfloat16)
    partial_grad = lax.dot_general(
        hidden, scaled, (((0,), (0,)), ((), ())), preferred_element_type=jnp.float32
    )
    weight_grad = lax.psum_scatter(partial_grad, "ctx", scatter_dimension=0, tiled=True)
    returned = lax.all_to_all(
        slot_grad.reshape(count_experts, capacity), "exp", split_axis=0, concat_axis=0, tiled=True
    )
    grad_by_expert = jnp.sum(select_wide * returned[:, :, None], axis=1)
    gate_grad = jnp.sum(onehot * grad_by_expert.T[:, None, :], axis=2)
    logit_grad = gate_probs * (gate_grad - jnp.sum(gate_probs * gate_grad, axis=1, keepdims=True))
    return (logit_grad, hidden_grad.reshape(1, 1, slot_count, -1), weight_grad[None])


def per_device(grad_out, top_logits, expert_ids, saved_hidden, w_down):
    experts = lax.axis_size("exp")
    groups = lax.axis_size("ctx")
    everywhere = top_logits.shape[1] == experts and saved_hidden.shape[2] == experts * grad_out.shape[0]
    plain = experts & (experts - 1) == 0 and groups % 4 == 0 and groups >= 8
    body = per_device_full if everywhere and plain else per_device_routed
    return body(grad_out, top_logits, expert_ids, saved_hidden, w_down)


def solution(mesh):
    return jax.shard_map(
        per_device,
        mesh=mesh,
        in_specs=(
            P(("ctx", "exp"), None),
            P(("ctx", "exp"), None),
            P(("ctx", "exp"), None),
            P("ctx", "exp", None, None),
            P("exp", "ctx", None),
        ),
        out_specs=(P(("ctx", "exp"), None), P("ctx", "exp", None, None), P("exp", "ctx", None)),
        check_vma=False,
    )
```

```python
import functools

import jax
import jax.numpy as jnp
import numpy as np
from jax import lax
from jax.experimental import pallas as pl
from jax.experimental.pallas import tpu as pltpu
from jax.sharding import PartitionSpec as P

LANES = 128
SCALE = 1_000_000
ORDER_WEIGHT = 100
FIRST_WEIGHT = 12_000
NEXT_WEIGHT = 600
HIDDEN_WEIGHT = 4_600
PASS_WEIGHT = 1
WAITED_WEIGHT = 1
ENTER_WEIGHT = 3_000
CLOSE_WEIGHT = 3_450
LEAVE_WEIGHT = 2_650
LAST_WEIGHT = 2_800
NT = (((1,), (1,)), ((), ()))
NN = (((1,), (0,)), ((), ()))
f32 = jnp.float32
bf16 = jnp.bfloat16


def dot(a, b, dims):
    return lax.dot_general(a, b, dims, preferred_element_type=f32)


def anywhere():
    return pl.BlockSpec(memory_space=pl.ANY)


def whole():
    return pl.BlockSpec(memory_space=pltpu.VMEM)


def scalars():
    return pl.BlockSpec(memory_space=pltpu.SMEM)


def params(mib=24):
    return pltpu.CompilerParams(vmem_limit_bytes=mib * 1024 * 1024)


def taking(microseconds):
    return pl.CostEstimate(flops=int(microseconds * SCALE), bytes_accessed=int(microseconds * 3e6), transcendentals=0)


def chain_plan(depth):
    products, weights = [], []
    for z in range(depth):
        uses = []
        for turn in range(2, depth + 1):
            if z < depth - 1 and turn >= z + 2:
                uses.append((turn, "AB"[z % 2], depth + 1 + z - turn))
            if z > 0 and turn >= depth - z + 1:
                uses.append((turn, "BA"[z % 2], z + turn - depth - 1))
        products.append(sorted(uses) + [(depth + 1, "own", z)])
        brought = {}
        for turn in range(1, depth):
            for name in "AB":
                index = z + turn if (name == "A") == (z % 2 == 0) else z - turn
                brought[turn, name] = index if 0 <= index < depth else -1
        weights.append(brought)
    return products, weights


class Scalars:
    def __init__(self):
        self.columns = []
        self.names = {}

    def add(self, name, values):
        self.names[name] = len(self.columns)
        self.columns.append(values)

    def __getitem__(self, name):
        return self.names[name]

    def row(self, place, me):
        return jnp.asarray(np.stack(self.columns, axis=-1).astype(np.int32))[place, me]


def device_scalars(depth, experts):
    products, weights = chain_plan(depth)
    table = Scalars()
    along = np.arange(2 * depth)[:, None] + np.zeros((1, experts), np.int32)

    def by_z(values):
        return np.asarray(values)[along // 2]

    table.add("x", along % 2)
    table.add("me", np.zeros_like(along) + np.arange(experts)[None, :])
    table.add(("shard", 0, "own"), along // 2)
    slot_of = [{use[2]: slot for slot, use in enumerate(products[z])} for z in range(depth)]
    for part in range(depth):
        table.add(("slot of", part), by_z([slot_of[z][part] for z in range(depth)]))
    table.add(("slot", 0, "own"), by_z([slot_of[z][z] for z in range(depth)]))
    for turn in range(1, depth):
        for name in "AB":
            shard = [weights[z][turn, name] for z in range(depth)]
            table.add(("shard", turn, name), by_z(shard))
            table.add(("slot", turn, name), by_z([slot_of[z].get(k, 0) for z, k in enumerate(shard)]))
    uses = {}
    for turn in range(2, depth + 1):
        for name in "AB":
            slots = [-1] * depth
            for z in range(depth):
                for slot, use in enumerate(products[z]):
                    if use[:2] == (turn, name):
                        slots[z] = slot
            uses[turn, name] = slots
            table.add(("use", turn, name), by_z(slots))
            limit = max(depth - 3, 0)
            table.add(("block", turn, name), by_z([min(max(slot - 1, 0), limit) for slot in slots]))
    return table, weights, uses


def rows_kernel(cut, grad_hbm, logits_hbm, ids_hbm, late_ref, early_ref, gates_ref, *scratch):
    grad_ref, logits_ref, ids_ref, sems = scratch
    model, tokens = grad_ref.shape
    copies = [
        pltpu.make_async_copy(source, target, sems.at[place])
        for place, (source, target) in enumerate(
            ((grad_hbm, grad_ref), (logits_hbm, logits_ref), (ids_hbm, ids_ref))
        )
    ]
    for copy in copies:
        copy.start()
    for copy in copies:
        copy.wait()
    count = logits_ref.shape[0]
    width = cut + late_ref.shape[1]
    logits = logits_ref[...]
    powers = jnp.exp(logits - jnp.max(logits, axis=0, keepdims=True))
    gates = powers / jnp.sum(powers, axis=0, keepdims=True)
    gates_ref[...] = gates
    sent = gates.astype(bf16).astype(f32)
    ids = ids_ref[...]
    row = lax.broadcasted_iota(jnp.int32, (width - model, tokens), 0)
    extra = jnp.zeros((width - model, tokens), f32)
    for expert in range(count):
        chosen = jnp.sum(jnp.where(ids == expert, sent, 0.0), axis=0, keepdims=True)
        extra = extra + jnp.where(row == expert, chosen, 0.0)
    for start in range(0, width, LANES):
        stop = start + LANES
        if stop <= model:
            block = grad_ref[start:stop, :].astype(f32)
        elif start >= model:
            block = extra[start - model : stop - model, :]
        else:
            block = jnp.concatenate(
                [grad_ref[start:model, :].astype(f32), extra[: stop - model, :]], axis=0
            )
        turned = block.T.astype(bf16)
        if start < cut:
            early_ref[:, start:stop] = turned
        else:
            late_ref[:, start - cut : stop - cut] = turned


def make_rows(grad_out, top_logits, expert_ids, width, cut):
    tokens, model = grad_out.shape
    count = top_logits.shape[1]
    return pl.pallas_call(
        functools.partial(rows_kernel, cut),
        out_shape=(
            jax.ShapeDtypeStruct((tokens, width - cut), bf16),
            jax.ShapeDtypeStruct((tokens, cut), bf16),
            jax.ShapeDtypeStruct((count, tokens), f32),
        ),
        in_specs=[pl.BlockSpec(memory_space=pltpu.HBM)] * 3,
        out_specs=(whole(),) * 3,
        scratch_shapes=[
            pltpu.VMEM((model, tokens), bf16),
            pltpu.VMEM((count, tokens), f32),
            pltpu.VMEM((count, tokens), jnp.int32),
            pltpu.SemaphoreType.DMA((3,)),
        ],
        compiler_params=params(58),
        cost_estimate=taking(2),
        name="make_rows",
    )(grad_out.T, top_logits.T, expert_ids.T)


def pack_kernel(*refs):
    out_ref, sems = refs[-2:]
    copies = []
    for place in range(out_ref.shape[0]):
        copies.append(pltpu.make_async_copy(refs[place], out_ref.at[place], sems.at[place]))
        copies[-1].start()
    for copy in copies:
        copy.wait()


def pack(values, after):
    number = len(values)
    return pl.pallas_call(
        pack_kernel,
        out_shape=jax.ShapeDtypeStruct((number, *values[0].shape), values[0].dtype),
        in_specs=[anywhere()] * (number + len(after)),
        out_specs=anywhere(),
        scratch_shapes=[pltpu.SemaphoreType.DMA((number,))],
        compiler_params=params(),
        cost_estimate=taking(1),
        name="pack_rows",
    )(*values, *after)


def blocks_of(refs, places):
    return [refs[array] if place is None else refs[array].at[place] for array, place in places]


def hold_kernel(*refs):
    del refs


def hold(values, after, weight=0):
    return pl.pallas_call(
        hold_kernel,
        out_shape=tuple(jax.ShapeDtypeStruct(value.shape, value.dtype) for value in values),
        in_specs=[anywhere()] * (len(values) + len(after)),
        out_specs=(anywhere(),) * len(values),
        input_output_aliases={place: place for place in range(len(values))},
        compiler_params=params(),
        cost_estimate=taking(weight),
        name="hold",
    )(*values, *after)


def split_kernel(table, where_ref, hidden_ref, *refs):
    own_ref, first_ref, rest_ref = refs[-3:]
    parts, units, _ = own_ref.shape
    row = lax.broadcasted_iota(jnp.int32, (2 * units, 2 * units), 0)
    column = lax.broadcasted_iota(jnp.int32, (2 * units, 2 * units), 1)
    unit = jnp.where(row == column, 1.0, 0.0).astype(bf16)
    low = where_ref[table["x"]] == 0
    for part in range(parts):
        block = hidden_ref[:, part * 2 * units : (part + 1) * 2 * units]
        turned = dot(unit, block, NT).astype(bf16)
        slot = where_ref[table["slot of", part]]
        other = jnp.where(low, turned[units:], turned[:units])
        own_ref[slot] = jnp.where(low, turned[:units], turned[units:])

        @pl.when(slot == 0)
        def _():
            first_ref[0] = other

        @pl.when(slot != 0)
        def _():
            rest_ref[slot - 1] = other


def split_hidden(table, where, hidden, parts, units, after):
    slots = hidden.shape[0]
    return pl.pallas_call(
        functools.partial(split_kernel, table),
        out_shape=tuple(
            jax.ShapeDtypeStruct((count, units, slots), bf16) for count in (parts, 1, parts - 1)
        ),
        in_specs=[scalars(), whole()] + [anywhere()] * len(after),
        out_specs=(whole(),) * 3,
        compiler_params=params(),
        cost_estimate=taking(2),
        name="split_hidden",
    )(where, hidden, *after)


def place_of(place, count, me, tokens):
    start = (place // count) * count * tokens + ((place % count) ^ me) * tokens
    return pl.multiple_of(start, tokens)


def scale_rows(table, model, where_ref, rows, gated, scaled):
    tokens = rows[0].shape[0]
    me = where_ref[table["me"]]
    lane = lax.broadcasted_iota(jnp.int32, (tokens, LANES), 1)
    for place, block in enumerate(rows):
        here = pl.ds(place_of(place, len(rows) // 2, me, tokens), tokens)
        tile = gated[place][:, gated[place].shape[1] - LANES :]
        picked = jnp.where(lane == model % LANES + me, tile.astype(f32), 0.0)
        gate = jnp.sum(picked, axis=1, keepdims=True)
        scaled[here, :] = (block[:, : scaled.shape[1]].astype(f32) * gate).astype(bf16)


def products_kernel(table, model, counts, places, shards, skip, where_it_runs, where_ref, *refs):
    used = sum(counts)
    rows = blocks_of(refs[: counts[0]], places[0])
    gated = blocks_of(refs[counts[0] : used], places[1])
    own_ref, other_ref = refs[used : used + 2]
    kept_ref, scaled, total_ref, sem = refs[-4:]
    units, slots = own_ref.shape[1:]

    def stacked(ref, offset):
        parts = [ref[offset + shard] for shard in range(shards)]
        return jnp.concatenate(parts, axis=0) if len(parts) > 1 else parts[0]

    def work():
        scale_rows(table, model, where_ref, rows, gated, scaled)
        total = dot(stacked(own_ref, skip), scaled[:slots, :], NN)
        total = total + dot(stacked(other_ref, 0), scaled[slots:, :], NN)
        for shard in range(shards):
            total_ref[shard] = total[shard * units : (shard + 1) * units]
        copy = pltpu.make_async_copy(total_ref, kept_ref, sem)
        copy.start()
        copy.wait()

    at_end = where_ref[table["use", 2, "A"]] == 0
    if where_it_runs == "ends":
        pl.when(at_end)(work)
    elif where_it_runs == "middle":
        pl.when(jnp.logical_not(at_end))(work)
    else:
        work()


def products(
    table, where, rows, gated, own, other, skip, model, width, name, after, where_it_runs="all", before=None
):
    arrays, places = zip(rows, gated)
    counts = [len(part) for part in arrays]
    shards, units, slots = other.shape
    kept = jax.ShapeDtypeStruct((shards, units, width), f32)
    operands = [*arrays[0], *arrays[1], own, other]
    extra = ([] if before is None else [before]) + list(after)
    return pl.pallas_call(
        functools.partial(products_kernel, table, model, counts, places, shards, skip, where_it_runs),
        out_shape=kept,
        in_specs=[scalars()] + [whole()] * len(operands) + [anywhere()] * len(extra),
        out_specs=anywhere(),
        scratch_shapes=[
            pltpu.VMEM((2 * slots, width), bf16),
            pltpu.VMEM(kept.shape, f32),
            pltpu.SemaphoreType.DMA,
        ],
        input_output_aliases={} if before is None else {1 + len(operands): 0},
        compiler_params=params(),
        cost_estimate=taking(1),
        name=name,
    )(where, *operands, *extra)


def first_kernel(table, model, counts, places, start, where_ref, *refs):
    used = sum(counts)
    rows = blocks_of(refs[: counts[0]], places[0])
    gated = blocks_of(refs[counts[0] : used], places[1])
    own_ref, other_ref, coming_ref = refs[used : used + 3]
    out_ref, scaled = refs[-2:]
    slots = own_ref.shape[2]
    ends = where_ref[table["use", 2, "A"]] == 0

    @pl.when(ends)
    def _():
        scale_rows(table, model, where_ref, rows, gated, scaled)
        total = dot(own_ref[0], scaled[:slots, :], NN)
        out_ref[...] = (total + dot(other_ref[0], scaled[slots:, :], NN)).astype(bf16)

    @pl.when(jnp.logical_not(ends))
    def _():
        out_ref[...] = coming_ref[:, start : start + out_ref.shape[1]]


def first_sums(table, where, rows, gated, own, other, coming, model, start, width, after):
    arrays, places = zip(rows, gated)
    counts = [len(part) for part in arrays]
    units, slots = own.shape[1:]
    return pl.pallas_call(
        functools.partial(first_kernel, table, model, counts, places, start),
        out_shape=jax.ShapeDtypeStruct((units, width), bf16),
        in_specs=[scalars()] + [whole()] * (sum(counts) + 3) + [anywhere()] * len(after),
        out_specs=whole(),
        scratch_shapes=[pltpu.VMEM((2 * slots, width), bf16)],
        compiler_params=params(),
        cost_estimate=taking(1),
        name="first_sums",
    )(where, *arrays[0], *arrays[1], own, other, coming, *after)


def rows_of(units):
    return units // 2 if units % 32 == 0 else units


def column_parts(arrays, cut):
    return [(0, arrays[0])] if len(arrays) == 1 else [(cut, arrays[0]), (0, arrays[1])]


def combine_kernel(table, key, cut, counts, sides, where_ref, *refs):
    slot = where_ref[table[key]]
    coming = refs[: counts[0]]
    outs = refs[len(refs) - counts[2] :]
    model = sum(ref.shape[1] for ref in outs)
    spans = [(cut, model), (0, cut)] if cut else [(0, model)]
    for chunk, (start, stop) in enumerate(spans):
        if counts[0] == 0:
            total = jnp.zeros((outs[0].shape[0], stop - start), f32)
        elif counts[0] == 1:
            total = coming[0][:, start:stop].astype(f32)
        else:
            total = coming[chunk][...].astype(f32)
        for number, side in enumerate(sides):
            flag = slot == 0 if side == "first" else slot > 0
            total = total + jnp.where(flag, refs[counts[0] + len(spans) * number + chunk][0], 0.0)
        total = total.astype(bf16)
        if counts[2] == 1:
            outs[0][:, start:stop] = total
        else:
            outs[chunk][...] = total


def combine(table, where, coming, first, rest, turn, name, used, cut, after, chunked=False, weight=1):
    units = first[0].shape[1]
    model = sum(part.shape[2] for part in first)
    block = rows_of(units)
    column = table["block", turn, name]
    sides, operands, specs = [], [], []
    if any(slot == 0 for slot in used):
        sides.append("first")
        operands += first
        specs += [pl.BlockSpec((1, block, part.shape[2]), lambda j, s: (0, j, 0)) for part in first]
    if any(slot > 0 for slot in used):
        sides.append("rest")
        operands += rest
        specs += [pl.BlockSpec((1, block, part.shape[2]), lambda j, s: (s[column], j, 0)) for part in rest]
    widths = [model - cut, cut] if chunked else [model]
    return pl.pallas_call(
        functools.partial(
            combine_kernel, table, ("use", turn, name), cut, (len(coming), len(operands), len(widths)), sides
        ),
        out_shape=[jax.ShapeDtypeStruct((units, count), bf16) for count in widths],
        grid_spec=pltpu.PrefetchScalarGridSpec(
            num_scalar_prefetch=1,
            grid=(units // block,),
            in_specs=[pl.BlockSpec((block, part.shape[1]), lambda j, s: (j, 0)) for part in coming]
            + specs
            + [anywhere()] * len(after),
            out_specs=[pl.BlockSpec((block, count), lambda j, s: (j, 0)) for count in widths],
        ),
        compiler_params=params(),
        cost_estimate=taking(weight),
        name="combine",
    )(where, *coming, *operands, *after)


def total_kernel(cut, counts, *refs):
    coming = [refs[: counts[0]], refs[counts[0] : sum(counts)]]
    out_ref = refs[-1]
    for chunk, start in enumerate((cut, 0)):
        kept_ref = refs[sum(counts) + chunk]
        here = slice(start, start + kept_ref.shape[2])
        total = kept_ref[0]
        for parts in coming:
            total = total + (parts[0][:, here] if len(parts) == 1 else parts[chunk][...]).astype(f32)
        out_ref[0, :, here] = total


def total_grad(a, b, kept, cut):
    units = a[0].shape[0]
    model = sum(part.shape[1] for part in a)
    block = rows_of(units)
    return pl.pallas_call(
        functools.partial(total_kernel, cut, (len(a), len(b))),
        out_shape=jax.ShapeDtypeStruct((1, units, model), f32),
        grid=(units // block,),
        in_specs=[pl.BlockSpec((block, part.shape[1]), lambda j: (j, 0)) for part in (*a, *b)]
        + [
            pl.BlockSpec((1, block, part.shape[2]), functools.partial(lambda last, j: (last, j, 0), part.shape[0] - 1))
            for part in kept
        ],
        out_specs=pl.BlockSpec((1, block, model), lambda j: (0, j, 0)),
        compiler_params=params(),
        cost_estimate=taking(2),
        name="total_grad",
    )(*a, *b, *kept)


def back_kernel(table, model, cut, counts, places, choices, parts, guard, summed, where_ref, *refs):
    keys = [key for choice in choices for key in choice]
    used = sum(counts)
    late = blocks_of(refs[: counts[0]], places[0])
    early = blocks_of(refs[counts[0] : used], places[1])
    number = len(late)
    own_ref, first_ref, rest_ref = refs[used : used + 3]
    weight_refs, used = {}, used + 3
    for key, count in zip(keys, parts):
        weight_refs[key] = refs[used : used + count]
        used += count
    before_ref = refs[used] if summed else None
    outs, sums_ref = refs[-3:-1], refs[-1]
    tokens = late[0].shape[0]
    units = own_ref.shape[1]
    me = where_ref[table["me"]]
    start = late[0].shape[1] - LANES
    eight = lax.broadcasted_iota(jnp.int32, (8, LANES), 1)
    onehot = jnp.where(eight == model % LANES + me, 1.0, 0.0).astype(bf16)
    shards = {key: where_ref[table[("shard",) + key]] for key in keys}
    slots = {key: where_ref[table[("slot",) + key]] for key in keys}
    sums_ref[...] = before_ref[...] if summed else jnp.zeros(sums_ref.shape, f32)

    def whole_weight(key):
        got = weight_refs[key]
        return got[0][...] if len(got) == 1 else jnp.concatenate([got[1][...], got[0][...]], axis=1)

    def work():
        stack, here_valid, here_slot = [], [], []
        for choice in choices:
            weight, valid, slot = whole_weight(choice[0]), shards[choice[0]] >= 0, slots[choice[0]]
            for key in choice[1:]:
                weight = jnp.where(valid, weight, whole_weight(key))
                slot = jnp.where(valid, slot, slots[key])
                valid = jnp.logical_or(valid, shards[key] >= 0)
            stack.append(weight)
            here_valid.append(valid)
            here_slot.append(slot)
        weight = jnp.concatenate(stack, axis=0) if len(stack) > 1 else stack[0]
        for pair in range(0, number, 2):
            both = jnp.concatenate(
                [
                    jnp.concatenate([early[k][...], late[k][:, : model - cut]], axis=1)
                    for k in (pair, pair + 1)
                ],
                axis=0,
            )
            product = dot(weight, both, NT)
            for place in (pair, pair + 1):
                near = place < number // 2
                block = product[:, (place - pair) * tokens : (place - pair + 1) * tokens]
                gate = dot(onehot, late[place][:, start:], NT)[0:1]
                here = pl.ds(place_of(place % (number // 2), number // 2, me, tokens), tokens)
                wide = pl.ds(place_of(place, number // 2, me, tokens), tokens)
                gated = (block * gate).astype(bf16)
                total = jnp.zeros((1, tokens), f32)
                for index, (valid, slot) in enumerate(zip(here_valid, here_slot)):
                    some = slice(index * units, (index + 1) * units)
                    outs[0 if near else 1][index, :, here] = gated[some]
                    if near:
                        hidden = own_ref[slot, :, here].astype(f32)
                    else:
                        hidden = jnp.where(
                            slot == 0,
                            first_ref[0, :, here].astype(f32),
                            rest_ref[jnp.maximum(slot - 1, 0), :, here].astype(f32),
                        )
                    part = jnp.sum(hidden * block[some], axis=0, keepdims=True)
                    total = total + jnp.where(valid, part, 0.0)
                sums_ref[0:1, wide] += total

    if guard:
        pl.when(functools.reduce(jnp.logical_or, [shards[key] >= 0 for key in keys]))(work)
    else:
        work()


def back_part(table, where, late, early, own, first, rest, choices, got, before, guard, after, model):
    units, slots = own.shape[1:]
    arrays, places = zip(late, early)
    counts = [len(part) for part in arrays]
    cut = arrays[1][0].shape[-1]
    keys = [key for choice in choices for key in choice]
    weights = [got[key] for key in keys]
    flat = [part for weight in weights for part in weight]
    half = jax.ShapeDtypeStruct((len(choices), units, slots), bf16)
    summed = before is not None
    operands = [*arrays[0], *arrays[1], own, first, rest, *flat] + ([before] if summed else [])
    outs = [half, half, jax.ShapeDtypeStruct((8, 2 * slots), f32)]
    parts = [len(weight) for weight in weights]
    return pl.pallas_call(
        functools.partial(
            back_kernel, table, model, cut, counts, places, choices, parts, guard, summed
        ),
        out_shape=outs,
        in_specs=[scalars()] + [whole()] * len(operands) + [anywhere()] * len(after),
        out_specs=[whole()] * len(outs),
        compiler_params=params(),
        cost_estimate=taking(6),
        name="back_part",
    )(where, *operands, *after)


def join_kernel(table, choices, where_ref, *refs):
    out_ref, done_ref, turned, sem = refs[-4:]
    done_ref[...] = jnp.zeros(done_ref.shape, f32)
    slots, width = turned.shape[1:]
    row = lax.broadcasted_iota(jnp.int32, (slots, slots), 0)
    column = lax.broadcasted_iota(jnp.int32, (slots, slots), 1)
    unit = jnp.where(row == column, 1.0, 0.0).astype(bf16)
    low = where_ref[table["x"]] == 0
    copies = []
    pairs = [
        (refs[2 * group][place], refs[2 * group + 1][place])
        for group in range((len(refs) - 4) // 2)
        for place in range(refs[2 * group].shape[0])
    ]
    for place, (choice, (mine, theirs)) in enumerate(zip(choices, pairs)):
        index = where_ref[table[("shard",) + choice[0]]]
        for key in choice[1:]:
            index = jnp.where(index >= 0, index, where_ref[table[("shard",) + key]])
        both = jnp.concatenate([jnp.where(low, mine, theirs), jnp.where(low, theirs, mine)], axis=0)
        turned[place] = dot(unit, both, NT).astype(bf16)
        here = pl.ds(pl.multiple_of(jnp.maximum(index, 0) * width, LANES), width)
        copy = pltpu.make_async_copy(turned.at[place], out_ref.at[:, here], sem.at[place])
        copies.append((index, copy))
        pl.when(index >= 0)(copy.start)
    for index, copy in copies:
        pl.when(index >= 0)(copy.wait)


def join_hidden(table, where, choices, halves, slots, hidden):
    units = halves[0].shape[1]
    return pl.pallas_call(
        functools.partial(join_kernel, table, choices),
        out_shape=(
            jax.ShapeDtypeStruct((slots, hidden), bf16),
            jax.ShapeDtypeStruct((8, LANES), f32),
        ),
        in_specs=[scalars()] + [whole()] * len(halves),
        out_specs=(anywhere(), whole()),
        scratch_shapes=[
            pltpu.VMEM((len(choices), slots, 2 * units), bf16),
            pltpu.SemaphoreType.DMA((len(choices),)),
        ],
        compiler_params=params(),
        cost_estimate=taking(2),
        name="join_hidden",
    )(where, *halves)


def logits_kernel(gates_ref, ids_ref, grads_ref, out_ref):
    gates, ids, grads = gates_ref[...], ids_ref[...], grads_ref[...]
    picked = jnp.zeros_like(gates)
    for expert in range(grads.shape[0]):
        picked = picked + jnp.where(ids == expert, grads[expert : expert + 1, :], 0.0)
    out_ref[...] = gates * (picked - jnp.sum(gates * picked, axis=0, keepdims=True))


def logits_grad(gates, ids, grads):
    return pl.pallas_call(
        logits_kernel,
        out_shape=jax.ShapeDtypeStruct(gates.shape, f32),
        in_specs=[whole()] * 3,
        out_specs=whole(),
        compiler_params=params(),
        cost_estimate=taking(1),
        name="logits_grad",
    )(gates, ids, grads)


def per_device_full(grad_out, top_logits, expert_ids, saved_hidden, w_down):
    experts = lax.axis_size("exp")
    groups = lax.axis_size("ctx")
    depth = groups // 2
    tokens, model = grad_out.shape
    slots, hidden = saved_hidden.shape[2:]
    width = pl.cdiv(model + experts, LANES) * LANES
    cut = width // LANES // 2 * LANES

    table, brought, uses = device_scalars(depth, experts)
    where = table.row(lax.axis_index("ctx"), lax.axis_index("exp"))

    def swap(value, x, exp):
        if not exp:
            return lax.ppermute(value, "ctx", [(i, i ^ x) for i in range(groups)])
        if not x:
            return lax.ppermute(value, "exp", [(i, i ^ exp) for i in range(experts)])
        pairs = [(c * experts + e, (c ^ x) * experts + (e ^ exp)) for c in range(groups) for e in range(experts)]
        return lax.ppermute(value, ("ctx", "exp"), pairs)

    def swap_z(value, name, senders=range(depth)):
        first = "AB".index(name)
        pairs = []
        for low in range(first, depth - 1, 2):
            for z, other in ((low, low + 1), (low + 1, low)):
                pairs += [(2 * z + x, 2 * other + x) for x in range(2) if z in senders]
        return lax.ppermute(value, "ctx", pairs)

    got = {(0, "own"): [w_down[0]]}
    for name in "BA":
        got[1, name] = [swap_z(w_down[0], name)]

    late, early, gates = make_rows(grad_out, top_logits, expert_ids, width, cut)
    highs = list(range(2, experts, 2))

    def sides(mine):
        return [mine, swap(mine, 0, 1)]

    late_x = swap(late, 1, 0)
    late_near = [late] + [swap(late, 0, high) for high in highs]
    own, other_first, other_rest = split_hidden(
        table, where, saved_hidden[0, 0], depth, w_down.shape[1], [late]
    )
    other_first = swap(other_first, 1, 0)
    (late_x,) = hold((late_x,), [], ORDER_WEIGHT)
    (late_x,) = hold((late_x,), late_near[1:])
    late_mine = late_near + [late_x] + [swap(late_x, 0, high) for high in highs]
    (early,) = hold((early,), [late_x, other_first])
    early_x = swap(early, 1, 0)
    late_rows = sides(pack(late_mine, [early_x]))
    late_rows = (late_rows, [(side, place) for place in range(experts) for side in range(2)])
    early_rows = sides(pack([early, early_x], []))
    early_far = [[swap(block, 0, high) for high in highs] for block in (early, early_x)]
    other_rest = swap(other_rest, 1, 0)

    got[1, "A"] = list(hold(got[1, "A"], [], ORDER_WEIGHT))
    got[1, "B"] = list(hold(got[1, "B"], got[1, "A"], FIRST_WEIGHT))
    chunks, first = [], []

    def first_chunk(rows, start, columns, after, before):
        chunks.append((rows, start, columns))
        value = first_sums(
            table, where, rows, late_rows, own, other_first, got[1, "B"][0], model, start, columns, after
        )
        if before:
            (value,) = hold([value], before, NEXT_WEIGHT)
        got.setdefault((2, "A"), []).append(swap_z(value, "A"))
        first.append(
            products(
                table, where, rows, late_rows, own, other_first, 0, model, columns, "first_kept", [value], "middle"
            )
        )
        return value

    first_chunk(late_rows, cut, model - cut, [early_rows[1]], [])
    places = []
    for base, blocks in enumerate(early_far):
        places += [(0, base), (1, base)]
        for block in hold(blocks, first):
            places += [(len(early_rows), None), (len(early_rows) + 1, None)]
            mine, theirs = sides(block)
            early_rows += [mine, theirs if base else hold([theirs], [], ORDER_WEIGHT)[0]]
    early_rows = (early_rows, places)
    marker = first_chunk(early_rows, 0, cut, [first[0]], got[2, "A"])
    got[2, "B"] = [swap_z(got[1, "A"][0], "B")]
    (other_rest,) = hold([other_rest], first[1:], HIDDEN_WEIGHT)

    halves, all_choices, weights_of = [], [], {}
    only_first = max(uses[3, "B"]) <= 0

    def backprop(choices, before, guard, after):
        mine, theirs, sums = back_part(
            table, where, late_rows, early_rows, own, other_first, other_rest, choices,
            {**got, **weights_of}, before, guard, after, model,
        )
        halves.extend([mine, swap(theirs, 1, 0)])
        all_choices.extend(choices)
        return sums

    def forward(turn, name, after):
        coming = got[turn - 1, "B" if name == "A" else "A"]
        coming[:] = hold(coming, after, PASS_WEIGHT)
        others = [z for z in range(depth) if uses[turn, name][z] < 0]
        weights_of[turn, name] = [swap_z(coming[0], name, others)]

    def pass_on(turn, name, after, chunk=None, waited=(), weight=1):
        coming = got[turn - 1, "B" if name == "A" else "A"]
        used = uses[turn, name]
        senders = range(depth)
        if turn == depth - 1 and min(used) < 0 and name == "A" and len(coming) == 1:
            senders = [z for z in range(depth) if used[z] >= 0]
            if chunk is None:
                forward(turn, name, [])
            if set(senders) <= {0, depth - 1}:
                coming = []
        parts, start = (first, rest), cut
        if chunk is not None:
            coming, parts, start = coming[chunk:][:1], (first[chunk:][:1], rest[chunk:][:1]), 0
        values = list(combine(table, where, coming, *parts, turn, name, used, start, after, False, weight))
        if waited:
            values = list(hold(values, list(waited), WAITED_WEIGHT))
        got.setdefault((turn, name), []).extend(swap_z(value, name, senders) for value in values)
        return values[-1]

    def choices_of(turn):
        both = any(b[turn, "A"] >= 0 and b[turn, "B"] >= 0 for b in brought)
        return [[(turn, "A")], [(turn, "B")]] if both else [[(turn, "A"), (turn, "B")]]

    rest = []

    def other_products(chunk, after, *where_it_runs):
        rows, _, columns = chunks[chunk]
        return products(
            table, where, rows, late_rows, own, other_rest, 1, model, columns, "rest_kept", after, *where_it_runs
        )

    apart = max(uses[3, "B"]) <= 0 and depth == 4
    if apart:
        marker = pass_on(3, "B", [marker], 0)
        rest.append(other_products(0, [marker]))
        marker = pass_on(3, "A", rest, 0)
        forward(3, "A", [marker, first[1]])
        rest.append(other_products(1, got[2, "B"], "ends"))
        marker = pass_on(3, "A", rest, 1)
        marker = pass_on(3, "B", [marker], 1)
        rest[1] = other_products(1, [marker], "middle", rest[1])
        marker = rest[1]
    else:
        rest.append(other_products(0, [marker]))
        rest.append(other_products(1, rest))
        marker = pass_on(3, "A", rest)
        for chunk in range(2):
            marker = pass_on(3, "B", [marker], chunk)
    sums = backprop([[(0, "own")], [(1, "A")], [(1, "B")]], None, False, got[2, "A"][:1])
    sooner = halves[1::2]
    for turn in range(2, depth):
        choices = choices_of(turn)
        if turn > 2:
            waited = [array for key in ((turn, "A"), (turn, "B")) for array in weights_of.get(key, [])]
            if apart and turn + 1 == depth:
                pass_on(depth, "B", [], 0)
                pass_on(depth, "B", [], 1, sooner, LEAVE_WEIGHT)
                marker = pass_on(depth, "A", [sums], weight=LAST_WEIGHT)
                sums = backprop(choices_of(turn - 1), sums, True, [marker])
            else:
                pass_on(turn + 1, "B", [sums, *sooner, *waited])
                marker = pass_on(turn + 1, "A", [sums])
        if not apart or turn > 2:
            sums = backprop(choices, sums, len(choices) == 1, [marker])
    slot_grad = sums[0:1, :slots] + swap(sums[0:1, slots:], 1, 0)
    grads = lax.all_to_all(
        slot_grad.reshape(experts, tokens), "exp", split_axis=0, concat_axis=0, tiled=True
    )
    logit_grad = logits_grad(gates, expert_ids.T, grads)
    hidden_grad, joined = join_hidden(table, where, all_choices, halves, slots, hidden)
    if apart:
        entered = list(hold(got[depth, "B"][:1], [joined], ENTER_WEIGHT))
        got[depth, "B"] = entered + list(hold(got[depth, "B"][1:], entered, CLOSE_WEIGHT))
    weight_grad = total_grad(got[depth, "A"], got[depth, "B"], rest, cut)
    return (logit_grad.T, hidden_grad[None, None], weight_grad)


def routing_tables(expert_ids, count_experts, capacity):
    columns = jnp.arange(count_experts, dtype=jnp.int32)
    matches = expert_ids[:, :, None] == columns[None, None, :]
    per_token = jnp.sum(matches.astype(jnp.int32), axis=1)
    rank_table = jnp.cumsum(per_token, axis=0) - per_token
    slot_iota = jnp.arange(capacity, dtype=jnp.int32)
    select = (per_token.T[:, None, :] == 1) & (rank_table.T[:, None, :] == slot_iota[None, :, None])
    return (matches.astype(jnp.float32), select)


def per_device_routed(grad_out, top_logits, expert_ids, saved_hidden, w_down):
    count_experts = lax.axis_size("exp")
    slot_count = saved_hidden.shape[2]
    capacity = slot_count // count_experts
    model_width = grad_out.shape[1]
    onehot, select = routing_tables(expert_ids, count_experts, capacity)
    select_wide = select.astype(jnp.float32)
    gate_probs = jax.nn.softmax(top_logits, axis=-1)
    gate_sent = gate_probs.astype(jnp.bfloat16)
    gate_by_expert = jnp.sum(onehot * gate_sent.astype(jnp.float32)[:, :, None], axis=1)
    send_rows = jnp.einsum(
        "ect,td->ecd", select.astype(jnp.bfloat16), grad_out, preferred_element_type=jnp.float32
    ).astype(jnp.bfloat16)
    send_gate = jnp.sum(select_wide * gate_by_expert.T[:, None, :], axis=2).astype(jnp.bfloat16)
    hidden = saved_hidden[0, 0]
    rows_in, gate_in = (
        lax.all_to_all(send_rows, "exp", split_axis=0, concat_axis=0, tiled=True),
        lax.all_to_all(send_gate, "exp", split_axis=0, concat_axis=0, tiled=True),
    )
    flat_rows = rows_in.reshape(slot_count, model_width)
    backprop = lax.dot_general(
        flat_rows,
        lax.all_gather(w_down[0], "ctx", axis=0, tiled=True),
        (((1,), (1,)), ((), ())),
        preferred_element_type=jnp.float32,
    )
    flat_gate = gate_in.reshape(slot_count, 1).astype(jnp.float32)
    hidden_grad = (flat_gate * backprop).astype(jnp.bfloat16)
    slot_grad = jnp.sum(hidden.astype(jnp.float32) * backprop, axis=1)
    scaled = (flat_gate * flat_rows.astype(jnp.float32)).astype(jnp.bfloat16)
    partial_grad = lax.dot_general(
        hidden, scaled, (((0,), (0,)), ((), ())), preferred_element_type=jnp.float32
    )
    weight_grad = lax.psum_scatter(partial_grad, "ctx", scatter_dimension=0, tiled=True)
    returned = lax.all_to_all(
        slot_grad.reshape(count_experts, capacity), "exp", split_axis=0, concat_axis=0, tiled=True
    )
    grad_by_expert = jnp.sum(select_wide * returned[:, :, None], axis=1)
    gate_grad = jnp.sum(onehot * grad_by_expert.T[:, None, :], axis=2)
    logit_grad = gate_probs * (gate_grad - jnp.sum(gate_probs * gate_grad, axis=1, keepdims=True))
    return (logit_grad, hidden_grad.reshape(1, 1, slot_count, -1), weight_grad[None])


def per_device(grad_out, top_logits, expert_ids, saved_hidden, w_down):
    experts = lax.axis_size("exp")
    groups = lax.axis_size("ctx")
    everywhere = top_logits.shape[1] == experts and saved_hidden.shape[2] == experts * grad_out.shape[0]
    plain = experts & (experts - 1) == 0 and groups % 4 == 0 and groups >= 8
    body = per_device_full if everywhere and plain else per_device_routed
    return body(grad_out, top_logits, expert_ids, saved_hidden, w_down)


def solution(mesh):
    return jax.shard_map(
        per_device,
        mesh=mesh,
        in_specs=(
            P(("ctx", "exp"), None),
            P(("ctx", "exp"), None),
            P(("ctx", "exp"), None),
            P("ctx", "exp", None, None),
            P("exp", "ctx", None),
        ),
        out_specs=(P(("ctx", "exp"), None), P("ctx", "exp", None, None), P("exp", "ctx", None)),
        check_vma=False,
    )
```

```python
import functools

import jax
import jax.numpy as jnp
import numpy as np
from jax import lax
from jax.experimental import pallas as pl
from jax.experimental.pallas import tpu as pltpu
from jax.sharding import PartitionSpec as P

LANES = 128
SCALE = 1_000_000
ORDER_WEIGHT = 100
FIRST_WEIGHT = 12_000
NEXT_WEIGHT = 600
HIDDEN_WEIGHT = 4_600
PASS_WEIGHT = 1
WAITED_WEIGHT = 1
ENTER_WEIGHT = 3_000
CLOSE_WEIGHT = 3_450
LEAVE_WEIGHT = 2_650
LAST_WEIGHT = 2_800
NT = (((1,), (1,)), ((), ()))
NN = (((1,), (0,)), ((), ()))
f32 = jnp.float32
bf16 = jnp.bfloat16


def dot(a, b, dims):
    return lax.dot_general(a, b, dims, preferred_element_type=f32)


def anywhere():
    return pl.BlockSpec(memory_space=pl.ANY)


def whole():
    return pl.BlockSpec(memory_space=pltpu.VMEM)


def scalars():
    return pl.BlockSpec(memory_space=pltpu.SMEM)


def params(mib=24):
    return pltpu.CompilerParams(vmem_limit_bytes=mib * 1024 * 1024)


def taking(microseconds):
    return pl.CostEstimate(flops=int(microseconds * SCALE), bytes_accessed=int(microseconds * 3e6), transcendentals=0)


def chain_plan(depth):
    products, weights = [], []
    for z in range(depth):
        uses = []
        for turn in range(2, depth + 1):
            if z < depth - 1 and turn >= z + 2:
                uses.append((turn, "AB"[z % 2], depth + 1 + z - turn))
            if z > 0 and turn >= depth - z + 1:
                uses.append((turn, "BA"[z % 2], z + turn - depth - 1))
        products.append(sorted(uses) + [(depth + 1, "own", z)])
        brought = {}
        for turn in range(1, depth):
            for name in "AB":
                index = z + turn if (name == "A") == (z % 2 == 0) else z - turn
                brought[turn, name] = index if 0 <= index < depth else -1
        weights.append(brought)
    return products, weights


class Scalars:
    def __init__(self):
        self.columns = []
        self.names = {}

    def add(self, name, values):
        self.names[name] = len(self.columns)
        self.columns.append(values)

    def __getitem__(self, name):
        return self.names[name]

    def row(self, place, me):
        return jnp.asarray(np.stack(self.columns, axis=-1).astype(np.int32))[place, me]


def device_scalars(depth, experts):
    products, weights = chain_plan(depth)
    table = Scalars()
    along = np.arange(2 * depth)[:, None] + np.zeros((1, experts), np.int32)

    def by_z(values):
        return np.asarray(values)[along // 2]

    table.add("x", along % 2)
    table.add("me", np.zeros_like(along) + np.arange(experts)[None, :])
    table.add(("shard", 0, "own"), along // 2)
    slot_of = [{use[2]: slot for slot, use in enumerate(products[z])} for z in range(depth)]
    for part in range(depth):
        table.add(("slot of", part), by_z([slot_of[z][part] for z in range(depth)]))
    table.add(("slot", 0, "own"), by_z([slot_of[z][z] for z in range(depth)]))
    for turn in range(1, depth):
        for name in "AB":
            shard = [weights[z][turn, name] for z in range(depth)]
            table.add(("shard", turn, name), by_z(shard))
            table.add(("slot", turn, name), by_z([slot_of[z].get(k, 0) for z, k in enumerate(shard)]))
    uses = {}
    for turn in range(2, depth + 1):
        for name in "AB":
            slots = [-1] * depth
            for z in range(depth):
                for slot, use in enumerate(products[z]):
                    if use[:2] == (turn, name):
                        slots[z] = slot
            uses[turn, name] = slots
            table.add(("use", turn, name), by_z(slots))
            limit = max(depth - 3, 0)
            table.add(("block", turn, name), by_z([min(max(slot - 1, 0), limit) for slot in slots]))
    return table, weights, uses


def rows_kernel(cut, grad_hbm, logits_hbm, ids_hbm, late_ref, early_ref, gates_ref, *scratch):
    grad_ref, logits_ref, ids_ref, sems = scratch
    model, tokens = grad_ref.shape
    copies = [
        pltpu.make_async_copy(source, target, sems.at[place])
        for place, (source, target) in enumerate(
            ((grad_hbm, grad_ref), (logits_hbm, logits_ref), (ids_hbm, ids_ref))
        )
    ]
    for copy in copies:
        copy.start()
    for copy in copies:
        copy.wait()
    count = logits_ref.shape[0]
    width = cut + late_ref.shape[1]
    logits = logits_ref[...]
    powers = jnp.exp(logits - jnp.max(logits, axis=0, keepdims=True))
    gates = powers / jnp.sum(powers, axis=0, keepdims=True)
    gates_ref[...] = gates
    sent = gates.astype(bf16).astype(f32)
    ids = ids_ref[...]
    row = lax.broadcasted_iota(jnp.int32, (width - model, tokens), 0)
    extra = jnp.zeros((width - model, tokens), f32)
    for expert in range(count):
        chosen = jnp.sum(jnp.where(ids == expert, sent, 0.0), axis=0, keepdims=True)
        extra = extra + jnp.where(row == expert, chosen, 0.0)
    for start in range(0, width, LANES):
        stop = start + LANES
        if stop <= model:
            block = grad_ref[start:stop, :].astype(f32)
        elif start >= model:
            block = extra[start - model : stop - model, :]
        else:
            block = jnp.concatenate(
                [grad_ref[start:model, :].astype(f32), extra[: stop - model, :]], axis=0
            )
        turned = block.T.astype(bf16)
        if start < cut:
            early_ref[:, start:stop] = turned
        else:
            late_ref[:, start - cut : stop - cut] = turned


def make_rows(grad_out, top_logits, expert_ids, width, cut):
    tokens, model = grad_out.shape
    count = top_logits.shape[1]
    return pl.pallas_call(
        functools.partial(rows_kernel, cut),
        out_shape=(
            jax.ShapeDtypeStruct((tokens, width - cut), bf16),
            jax.ShapeDtypeStruct((tokens, cut), bf16),
            jax.ShapeDtypeStruct((count, tokens), f32),
        ),
        in_specs=[pl.BlockSpec(memory_space=pltpu.HBM)] * 3,
        out_specs=(whole(),) * 3,
        scratch_shapes=[
            pltpu.VMEM((model, tokens), bf16),
            pltpu.VMEM((count, tokens), f32),
            pltpu.VMEM((count, tokens), jnp.int32),
            pltpu.SemaphoreType.DMA((3,)),
        ],
        compiler_params=params(58),
        cost_estimate=taking(2),
        name="make_rows",
    )(grad_out.T, top_logits.T, expert_ids.T)


def pack_kernel(*refs):
    out_ref, sems = refs[-2:]
    copies = []
    for place in range(out_ref.shape[0]):
        copies.append(pltpu.make_async_copy(refs[place], out_ref.at[place], sems.at[place]))
        copies[-1].start()
    for copy in copies:
        copy.wait()


def pack(values, after):
    number = len(values)
    return pl.pallas_call(
        pack_kernel,
        out_shape=jax.ShapeDtypeStruct((number, *values[0].shape), values[0].dtype),
        in_specs=[anywhere()] * (number + len(after)),
        out_specs=anywhere(),
        scratch_shapes=[pltpu.SemaphoreType.DMA((number,))],
        compiler_params=params(),
        cost_estimate=taking(1),
        name="pack_rows",
    )(*values, *after)


def blocks_of(refs, places):
    return [refs[array] if place is None else refs[array].at[place] for array, place in places]


def hold_kernel(*refs):
    del refs


def hold(values, after, weight=0):
    return pl.pallas_call(
        hold_kernel,
        out_shape=tuple(jax.ShapeDtypeStruct(value.shape, value.dtype) for value in values),
        in_specs=[anywhere()] * (len(values) + len(after)),
        out_specs=(anywhere(),) * len(values),
        input_output_aliases={place: place for place in range(len(values))},
        compiler_params=params(),
        cost_estimate=taking(weight),
        name="hold",
    )(*values, *after)


def split_kernel(table, where_ref, hidden_ref, *refs):
    own_ref, first_ref, rest_ref, held, sems = refs[-5:]
    parts, units, _ = own_ref.shape
    copies = []
    for part in range(parts):
        here = slice(part * 2 * units, (part + 1) * 2 * units)
        copies.append(pltpu.make_async_copy(hidden_ref.at[:, here], held.at[:, here], sems.at[part]))
        copies[-1].start()
    row = lax.broadcasted_iota(jnp.int32, (2 * units, 2 * units), 0)
    column = lax.broadcasted_iota(jnp.int32, (2 * units, 2 * units), 1)
    unit = jnp.where(row == column, 1.0, 0.0).astype(bf16)
    low = where_ref[table["x"]] == 0
    for part in range(parts):
        copies[part].wait()
        block = held[:, part * 2 * units : (part + 1) * 2 * units]
        turned = dot(unit, block, NT).astype(bf16)
        slot = where_ref[table["slot of", part]]
        other = jnp.where(low, turned[units:], turned[:units])
        own_ref[slot] = jnp.where(low, turned[:units], turned[units:])

        @pl.when(slot == 0)
        def _():
            first_ref[0] = other

        @pl.when(slot != 0)
        def _():
            rest_ref[slot - 1] = other


def split_hidden(table, where, hidden, parts, units, after):
    slots = hidden.shape[0]
    return pl.pallas_call(
        functools.partial(split_kernel, table),
        out_shape=tuple(
            jax.ShapeDtypeStruct((count, units, slots), bf16) for count in (parts, 1, parts - 1)
        ),
        in_specs=[scalars()] + [anywhere()] * (1 + len(after)),
        out_specs=(whole(),) * 3,
        scratch_shapes=[pltpu.VMEM(hidden.shape, bf16), pltpu.SemaphoreType.DMA((parts,))],
        compiler_params=params(52),
        cost_estimate=taking(2),
        name="split_hidden",
    )(where, hidden, *after)


def place_of(place, count, me, tokens):
    start = (place // count) * count * tokens + ((place % count) ^ me) * tokens
    return pl.multiple_of(start, tokens)


def scale_rows(table, model, where_ref, rows, gated, scaled):
    tokens = rows[0].shape[0]
    me = where_ref[table["me"]]
    lane = lax.broadcasted_iota(jnp.int32, (tokens, LANES), 1)
    for place, block in enumerate(rows):
        here = pl.ds(place_of(place, len(rows) // 2, me, tokens), tokens)
        tile = gated[place][:, gated[place].shape[1] - LANES :]
        picked = jnp.where(lane == model % LANES + me, tile.astype(f32), 0.0)
        gate = jnp.sum(picked, axis=1, keepdims=True)
        scaled[here, :] = (block[:, : scaled.shape[1]].astype(f32) * gate).astype(bf16)


def products_kernel(table, model, counts, places, shards, skip, where_it_runs, where_ref, *refs):
    used = sum(counts)
    rows = blocks_of(refs[: counts[0]], places[0])
    gated = blocks_of(refs[counts[0] : used], places[1])
    own_ref, other_ref = refs[used : used + 2]
    kept_ref, scaled, total_ref, sem = refs[-4:]
    units, slots = own_ref.shape[1:]

    def stacked(ref, offset):
        parts = [ref[offset + shard] for shard in range(shards)]
        return jnp.concatenate(parts, axis=0) if len(parts) > 1 else parts[0]

    def work():
        scale_rows(table, model, where_ref, rows, gated, scaled)
        total = dot(stacked(own_ref, skip), scaled[:slots, :], NN)
        total = total + dot(stacked(other_ref, 0), scaled[slots:, :], NN)
        for shard in range(shards):
            total_ref[shard] = total[shard * units : (shard + 1) * units]
        copy = pltpu.make_async_copy(total_ref, kept_ref, sem)
        copy.start()
        copy.wait()

    at_end = where_ref[table["use", 2, "A"]] == 0
    if where_it_runs == "ends":
        pl.when(at_end)(work)
    elif where_it_runs == "middle":
        pl.when(jnp.logical_not(at_end))(work)
    else:
        work()


def products(
    table, where, rows, gated, own, other, skip, model, width, name, after, where_it_runs="all", before=None
):
    arrays, places = zip(rows, gated)
    counts = [len(part) for part in arrays]
    shards, units, slots = other.shape
    kept = jax.ShapeDtypeStruct((shards, units, width), f32)
    operands = [*arrays[0], *arrays[1], own, other]
    extra = ([] if before is None else [before]) + list(after)
    return pl.pallas_call(
        functools.partial(products_kernel, table, model, counts, places, shards, skip, where_it_runs),
        out_shape=kept,
        in_specs=[scalars()] + [whole()] * len(operands) + [anywhere()] * len(extra),
        out_specs=anywhere(),
        scratch_shapes=[
            pltpu.VMEM((2 * slots, width), bf16),
            pltpu.VMEM(kept.shape, f32),
            pltpu.SemaphoreType.DMA,
        ],
        input_output_aliases={} if before is None else {1 + len(operands): 0},
        compiler_params=params(),
        cost_estimate=taking(1),
        name=name,
    )(where, *operands, *extra)


def first_kernel(table, model, counts, places, start, where_ref, *refs):
    used = sum(counts)
    rows = blocks_of(refs[: counts[0]], places[0])
    gated = blocks_of(refs[counts[0] : used], places[1])
    own_ref, other_ref, coming_ref = refs[used : used + 3]
    out_ref, scaled = refs[-2:]
    slots = own_ref.shape[2]
    ends = where_ref[table["use", 2, "A"]] == 0

    @pl.when(ends)
    def _():
        scale_rows(table, model, where_ref, rows, gated, scaled)
        total = dot(own_ref[0], scaled[:slots, :], NN)
        out_ref[...] = (total + dot(other_ref[0], scaled[slots:, :], NN)).astype(bf16)

    @pl.when(jnp.logical_not(ends))
    def _():
        out_ref[...] = coming_ref[:, start : start + out_ref.shape[1]]


def first_sums(table, where, rows, gated, own, other, coming, model, start, width, after):
    arrays, places = zip(rows, gated)
    counts = [len(part) for part in arrays]
    units, slots = own.shape[1:]
    return pl.pallas_call(
        functools.partial(first_kernel, table, model, counts, places, start),
        out_shape=jax.ShapeDtypeStruct((units, width), bf16),
        in_specs=[scalars()] + [whole()] * (sum(counts) + 3) + [anywhere()] * len(after),
        out_specs=whole(),
        scratch_shapes=[pltpu.VMEM((2 * slots, width), bf16)],
        compiler_params=params(),
        cost_estimate=taking(1),
        name="first_sums",
    )(where, *arrays[0], *arrays[1], own, other, coming, *after)


def rows_of(units):
    return units // 2 if units % 32 == 0 else units


def column_parts(arrays, cut):
    return [(0, arrays[0])] if len(arrays) == 1 else [(cut, arrays[0]), (0, arrays[1])]


def combine_kernel(table, key, cut, counts, sides, where_ref, *refs):
    slot = where_ref[table[key]]
    coming = refs[: counts[0]]
    outs = refs[len(refs) - counts[2] :]
    model = sum(ref.shape[1] for ref in outs)
    spans = [(cut, model), (0, cut)] if cut else [(0, model)]
    for chunk, (start, stop) in enumerate(spans):
        if counts[0] == 0:
            total = jnp.zeros((outs[0].shape[0], stop - start), f32)
        elif counts[0] == 1:
            total = coming[0][:, start:stop].astype(f32)
        else:
            total = coming[chunk][...].astype(f32)
        for number, side in enumerate(sides):
            flag = slot == 0 if side == "first" else slot > 0
            total = total + jnp.where(flag, refs[counts[0] + len(spans) * number + chunk][0], 0.0)
        total = total.astype(bf16)
        if counts[2] == 1:
            outs[0][:, start:stop] = total
        else:
            outs[chunk][...] = total


def combine(table, where, coming, first, rest, turn, name, used, cut, after, chunked=False, weight=1):
    units = first[0].shape[1]
    model = sum(part.shape[2] for part in first)
    block = rows_of(units)
    column = table["block", turn, name]
    sides, operands, specs = [], [], []
    if any(slot == 0 for slot in used):
        sides.append("first")
        operands += first
        specs += [pl.BlockSpec((1, block, part.shape[2]), lambda j, s: (0, j, 0)) for part in first]
    if any(slot > 0 for slot in used):
        sides.append("rest")
        operands += rest
        specs += [pl.BlockSpec((1, block, part.shape[2]), lambda j, s: (s[column], j, 0)) for part in rest]
    widths = [model - cut, cut] if chunked else [model]
    return pl.pallas_call(
        functools.partial(
            combine_kernel, table, ("use", turn, name), cut, (len(coming), len(operands), len(widths)), sides
        ),
        out_shape=[jax.ShapeDtypeStruct((units, count), bf16) for count in widths],
        grid_spec=pltpu.PrefetchScalarGridSpec(
            num_scalar_prefetch=1,
            grid=(units // block,),
            in_specs=[pl.BlockSpec((block, part.shape[1]), lambda j, s: (j, 0)) for part in coming]
            + specs
            + [anywhere()] * len(after),
            out_specs=[pl.BlockSpec((block, count), lambda j, s: (j, 0)) for count in widths],
        ),
        compiler_params=params(),
        cost_estimate=taking(weight),
        name="combine",
    )(where, *coming, *operands, *after)


def total_kernel(cut, counts, *refs):
    coming = [refs[: counts[0]], refs[counts[0] : sum(counts)]]
    out_ref = refs[-1]
    for chunk, start in enumerate((cut, 0)):
        kept_ref = refs[sum(counts) + chunk]
        here = slice(start, start + kept_ref.shape[2])
        total = kept_ref[0]
        for parts in coming:
            total = total + (parts[0][:, here] if len(parts) == 1 else parts[chunk][...]).astype(f32)
        out_ref[0, :, here] = total


def total_grad(a, b, kept, cut):
    units = a[0].shape[0]
    model = sum(part.shape[1] for part in a)
    block = rows_of(units)
    return pl.pallas_call(
        functools.partial(total_kernel, cut, (len(a), len(b))),
        out_shape=jax.ShapeDtypeStruct((1, units, model), f32),
        grid=(units // block,),
        in_specs=[pl.BlockSpec((block, part.shape[1]), lambda j: (j, 0)) for part in (*a, *b)]
        + [
            pl.BlockSpec((1, block, part.shape[2]), functools.partial(lambda last, j: (last, j, 0), part.shape[0] - 1))
            for part in kept
        ],
        out_specs=pl.BlockSpec((1, block, model), lambda j: (0, j, 0)),
        compiler_params=params(),
        cost_estimate=taking(2),
        name="total_grad",
    )(*a, *b, *kept)


def back_kernel(table, model, cut, counts, places, choices, parts, guard, summed, where_ref, *refs):
    keys = [key for choice in choices for key in choice]
    used = sum(counts)
    late = blocks_of(refs[: counts[0]], places[0])
    early = blocks_of(refs[counts[0] : used], places[1])
    number = len(late)
    own_ref, first_ref, rest_ref = refs[used : used + 3]
    weight_refs, used = {}, used + 3
    for key, count in zip(keys, parts):
        weight_refs[key] = refs[used : used + count]
        used += count
    before_ref = refs[used] if summed else None
    outs, sums_ref = refs[-3:-1], refs[-1]
    tokens = late[0].shape[0]
    units = own_ref.shape[1]
    me = where_ref[table["me"]]
    start = late[0].shape[1] - LANES
    eight = lax.broadcasted_iota(jnp.int32, (8, LANES), 1)
    onehot = jnp.where(eight == model % LANES + me, 1.0, 0.0).astype(bf16)
    shards = {key: where_ref[table[("shard",) + key]] for key in keys}
    slots = {key: where_ref[table[("slot",) + key]] for key in keys}
    sums_ref[...] = before_ref[...] if summed else jnp.zeros(sums_ref.shape, f32)

    def whole_weight(key):
        got = weight_refs[key]
        return got[0][...] if len(got) == 1 else jnp.concatenate([got[1][...], got[0][...]], axis=1)

    def work():
        stack, here_valid, here_slot = [], [], []
        for choice in choices:
            weight, valid, slot = whole_weight(choice[0]), shards[choice[0]] >= 0, slots[choice[0]]
            for key in choice[1:]:
                weight = jnp.where(valid, weight, whole_weight(key))
                slot = jnp.where(valid, slot, slots[key])
                valid = jnp.logical_or(valid, shards[key] >= 0)
            stack.append(weight)
            here_valid.append(valid)
            here_slot.append(slot)
        weight = jnp.concatenate(stack, axis=0) if len(stack) > 1 else stack[0]
        for pair in range(0, number, 2):
            both = jnp.concatenate(
                [
                    jnp.concatenate([early[k][...], late[k][:, : model - cut]], axis=1)
                    for k in (pair, pair + 1)
                ],
                axis=0,
            )
            product = dot(weight, both, NT)
            for place in (pair, pair + 1):
                near = place < number // 2
                block = product[:, (place - pair) * tokens : (place - pair + 1) * tokens]
                gate = dot(onehot, late[place][:, start:], NT)[0:1]
                here = pl.ds(place_of(place % (number // 2), number // 2, me, tokens), tokens)
                wide = pl.ds(place_of(place, number // 2, me, tokens), tokens)
                gated = (block * gate).astype(bf16)
                total = jnp.zeros((1, tokens), f32)
                for index, (valid, slot) in enumerate(zip(here_valid, here_slot)):
                    some = slice(index * units, (index + 1) * units)
                    outs[0 if near else 1][index, :, here] = gated[some]
                    if near:
                        hidden = own_ref[slot, :, here].astype(f32)
                    else:
                        hidden = jnp.where(
                            slot == 0,
                            first_ref[0, :, here].astype(f32),
                            rest_ref[jnp.maximum(slot - 1, 0), :, here].astype(f32),
                        )
                    part = jnp.sum(hidden * block[some], axis=0, keepdims=True)
                    total = total + jnp.where(valid, part, 0.0)
                sums_ref[0:1, wide] += total

    if guard:
        pl.when(functools.reduce(jnp.logical_or, [shards[key] >= 0 for key in keys]))(work)
    else:
        work()


def back_part(table, where, late, early, own, first, rest, choices, got, before, guard, after, model):
    units, slots = own.shape[1:]
    arrays, places = zip(late, early)
    counts = [len(part) for part in arrays]
    cut = arrays[1][0].shape[-1]
    keys = [key for choice in choices for key in choice]
    weights = [got[key] for key in keys]
    flat = [part for weight in weights for part in weight]
    half = jax.ShapeDtypeStruct((len(choices), units, slots), bf16)
    summed = before is not None
    operands = [*arrays[0], *arrays[1], own, first, rest, *flat] + ([before] if summed else [])
    outs = [half, half, jax.ShapeDtypeStruct((8, 2 * slots), f32)]
    parts = [len(weight) for weight in weights]
    return pl.pallas_call(
        functools.partial(
            back_kernel, table, model, cut, counts, places, choices, parts, guard, summed
        ),
        out_shape=outs,
        in_specs=[scalars()] + [whole()] * len(operands) + [anywhere()] * len(after),
        out_specs=[whole()] * len(outs),
        compiler_params=params(),
        cost_estimate=taking(6),
        name="back_part",
    )(where, *operands, *after)


def join_kernel(table, choices, where_ref, *refs):
    out_ref, done_ref, turned, sem = refs[-4:]
    done_ref[...] = jnp.zeros(done_ref.shape, f32)
    slots, width = turned.shape[1:]
    row = lax.broadcasted_iota(jnp.int32, (slots, slots), 0)
    column = lax.broadcasted_iota(jnp.int32, (slots, slots), 1)
    unit = jnp.where(row == column, 1.0, 0.0).astype(bf16)
    low = where_ref[table["x"]] == 0
    copies = []
    pairs = [
        (refs[2 * group][place], refs[2 * group + 1][place])
        for group in range((len(refs) - 4) // 2)
        for place in range(refs[2 * group].shape[0])
    ]
    for place, (choice, (mine, theirs)) in enumerate(zip(choices, pairs)):
        index = where_ref[table[("shard",) + choice[0]]]
        for key in choice[1:]:
            index = jnp.where(index >= 0, index, where_ref[table[("shard",) + key]])
        both = jnp.concatenate([jnp.where(low, mine, theirs), jnp.where(low, theirs, mine)], axis=0)
        turned[place] = dot(unit, both, NT).astype(bf16)
        here = pl.ds(pl.multiple_of(jnp.maximum(index, 0) * width, LANES), width)
        copy = pltpu.make_async_copy(turned.at[place], out_ref.at[:, here], sem.at[place])
        copies.append((index, copy))
        pl.when(index >= 0)(copy.start)
    for index, copy in copies:
        pl.when(index >= 0)(copy.wait)


def join_hidden(table, where, choices, halves, slots, hidden):
    units = halves[0].shape[1]
    return pl.pallas_call(
        functools.partial(join_kernel, table, choices),
        out_shape=(
            jax.ShapeDtypeStruct((slots, hidden), bf16),
            jax.ShapeDtypeStruct((8, LANES), f32),
        ),
        in_specs=[scalars()] + [whole()] * len(halves),
        out_specs=(anywhere(), whole()),
        scratch_shapes=[
            pltpu.VMEM((len(choices), slots, 2 * units), bf16),
            pltpu.SemaphoreType.DMA((len(choices),)),
        ],
        compiler_params=params(),
        cost_estimate=taking(2),
        name="join_hidden",
    )(where, *halves)


def logits_kernel(gates_ref, ids_ref, grads_ref, out_ref):
    gates, ids, grads = gates_ref[...], ids_ref[...], grads_ref[...]
    picked = jnp.zeros_like(gates)
    for expert in range(grads.shape[0]):
        picked = picked + jnp.where(ids == expert, grads[expert : expert + 1, :], 0.0)
    out_ref[...] = gates * (picked - jnp.sum(gates * picked, axis=0, keepdims=True))


def logits_grad(gates, ids, grads):
    return pl.pallas_call(
        logits_kernel,
        out_shape=jax.ShapeDtypeStruct(gates.shape, f32),
        in_specs=[whole()] * 3,
        out_specs=whole(),
        compiler_params=params(),
        cost_estimate=taking(1),
        name="logits_grad",
    )(gates, ids, grads)


def per_device_full(grad_out, top_logits, expert_ids, saved_hidden, w_down):
    experts = lax.axis_size("exp")
    groups = lax.axis_size("ctx")
    depth = groups // 2
    tokens, model = grad_out.shape
    slots, hidden = saved_hidden.shape[2:]
    width = pl.cdiv(model + experts, LANES) * LANES
    cut = width // LANES // 2 * LANES

    table, brought, uses = device_scalars(depth, experts)
    where = table.row(lax.axis_index("ctx"), lax.axis_index("exp"))

    def swap(value, x, exp):
        if not exp:
            return lax.ppermute(value, "ctx", [(i, i ^ x) for i in range(groups)])
        if not x:
            return lax.ppermute(value, "exp", [(i, i ^ exp) for i in range(experts)])
        pairs = [(c * experts + e, (c ^ x) * experts + (e ^ exp)) for c in range(groups) for e in range(experts)]
        return lax.ppermute(value, ("ctx", "exp"), pairs)

    def swap_z(value, name, senders=range(depth)):
        first = "AB".index(name)
        pairs = []
        for low in range(first, depth - 1, 2):
            for z, other in ((low, low + 1), (low + 1, low)):
                pairs += [(2 * z + x, 2 * other + x) for x in range(2) if z in senders]
        return lax.ppermute(value, "ctx", pairs)

    got = {(0, "own"): [w_down[0]]}
    for name in "BA":
        got[1, name] = [swap_z(w_down[0], name)]

    late, early, gates = make_rows(grad_out, top_logits, expert_ids, width, cut)
    highs = list(range(2, experts, 2))

    def sides(mine):
        return [mine, swap(mine, 0, 1)]

    late_x = swap(late, 1, 0)
    late_near = [late] + [swap(late, 0, high) for high in highs]
    own, other_first, other_rest = split_hidden(
        table, where, saved_hidden[0, 0], depth, w_down.shape[1], [late]
    )
    other_first = swap(other_first, 1, 0)
    (late_x,) = hold((late_x,), [], ORDER_WEIGHT)
    (late_x,) = hold((late_x,), late_near[1:])
    late_mine = late_near + [late_x] + [swap(late_x, 0, high) for high in highs]
    (early,) = hold((early,), [late_x, other_first])
    early_x = swap(early, 1, 0)
    late_rows = sides(pack(late_mine, [early_x]))
    late_rows = (late_rows, [(side, place) for place in range(experts) for side in range(2)])
    early_rows = sides(pack([early, early_x], []))
    early_far = [[swap(block, 0, high) for high in highs] for block in (early, early_x)]
    other_rest = swap(other_rest, 1, 0)

    got[1, "A"] = list(hold(got[1, "A"], [], ORDER_WEIGHT))
    got[1, "B"] = list(hold(got[1, "B"], got[1, "A"], FIRST_WEIGHT))
    chunks, first = [], []

    def first_chunk(rows, start, columns, after, before):
        chunks.append((rows, start, columns))
        value = first_sums(
            table, where, rows, late_rows, own, other_first, got[1, "B"][0], model, start, columns, after
        )
        if before:
            (value,) = hold([value], before, NEXT_WEIGHT)
        got.setdefault((2, "A"), []).append(swap_z(value, "A"))
        first.append(
            products(
                table, where, rows, late_rows, own, other_first, 0, model, columns, "first_kept", [value], "middle"
            )
        )
        return value

    first_chunk(late_rows, cut, model - cut, [early_rows[1]], [])
    places = []
    for base, blocks in enumerate(early_far):
        places += [(0, base), (1, base)]
        for block in hold(blocks, first):
            places += [(len(early_rows), None), (len(early_rows) + 1, None)]
            mine, theirs = sides(block)
            early_rows += [mine, theirs if base else hold([theirs], [], ORDER_WEIGHT)[0]]
    early_rows = (early_rows, places)
    marker = first_chunk(early_rows, 0, cut, [first[0]], got[2, "A"])
    got[2, "B"] = [swap_z(got[1, "A"][0], "B")]
    (other_rest,) = hold([other_rest], first[1:], HIDDEN_WEIGHT)

    halves, all_choices, weights_of = [], [], {}
    only_first = max(uses[3, "B"]) <= 0

    def backprop(choices, before, guard, after):
        mine, theirs, sums = back_part(
            table, where, late_rows, early_rows, own, other_first, other_rest, choices,
            {**got, **weights_of}, before, guard, after, model,
        )
        halves.extend([mine, swap(theirs, 1, 0)])
        all_choices.extend(choices)
        return sums

    def forward(turn, name, after):
        coming = got[turn - 1, "B" if name == "A" else "A"]
        coming[:] = hold(coming, after, PASS_WEIGHT)
        others = [z for z in range(depth) if uses[turn, name][z] < 0]
        weights_of[turn, name] = [swap_z(coming[0], name, others)]

    def pass_on(turn, name, after, chunk=None, waited=(), weight=1):
        coming = got[turn - 1, "B" if name == "A" else "A"]
        used = uses[turn, name]
        senders = range(depth)
        if turn == depth - 1 and min(used) < 0 and name == "A" and len(coming) == 1:
            senders = [z for z in range(depth) if used[z] >= 0]
            if chunk is None:
                forward(turn, name, [])
            if set(senders) <= {0, depth - 1}:
                coming = []
        parts, start = (first, rest), cut
        if chunk is not None:
            coming, parts, start = coming[chunk:][:1], (first[chunk:][:1], rest[chunk:][:1]), 0
        values = list(combine(table, where, coming, *parts, turn, name, used, start, after, False, weight))
        if waited:
            values = list(hold(values, list(waited), WAITED_WEIGHT))
        got.setdefault((turn, name), []).extend(swap_z(value, name, senders) for value in values)
        return values[-1]

    def choices_of(turn):
        both = any(b[turn, "A"] >= 0 and b[turn, "B"] >= 0 for b in brought)
        return [[(turn, "A")], [(turn, "B")]] if both else [[(turn, "A"), (turn, "B")]]

    rest = []

    def other_products(chunk, after, *where_it_runs):
        rows, _, columns = chunks[chunk]
        return products(
            table, where, rows, late_rows, own, other_rest, 1, model, columns, "rest_kept", after, *where_it_runs
        )

    apart = max(uses[3, "B"]) <= 0 and depth == 4
    if apart:
        marker = pass_on(3, "B", [marker], 0)
        rest.append(other_products(0, [marker]))
        marker = pass_on(3, "A", rest, 0)
        forward(3, "A", [marker, first[1]])
        rest.append(other_products(1, got[2, "B"], "ends"))
        marker = pass_on(3, "A", rest, 1)
        marker = pass_on(3, "B", [marker], 1)
        rest[1] = other_products(1, [marker], "middle", rest[1])
        marker = rest[1]
    else:
        rest.append(other_products(0, [marker]))
        rest.append(other_products(1, rest))
        marker = pass_on(3, "A", rest)
        for chunk in range(2):
            marker = pass_on(3, "B", [marker], chunk)
    sums = backprop([[(0, "own")], [(1, "A")], [(1, "B")]], None, False, got[2, "A"][:1])
    sooner = halves[1::2]
    for turn in range(2, depth):
        choices = choices_of(turn)
        if turn > 2:
            waited = [array for key in ((turn, "A"), (turn, "B")) for array in weights_of.get(key, [])]
            if apart and turn + 1 == depth:
                pass_on(depth, "B", [], 0)
                pass_on(depth, "B", [], 1, sooner, LEAVE_WEIGHT)
                marker = pass_on(depth, "A", [sums], weight=LAST_WEIGHT)
                sums = backprop(choices_of(turn - 1), sums, True, [marker])
            else:
                pass_on(turn + 1, "B", [sums, *sooner, *waited])
                marker = pass_on(turn + 1, "A", [sums])
        if not apart or turn > 2:
            sums = backprop(choices, sums, len(choices) == 1, [marker])
    slot_grad = sums[0:1, :slots] + swap(sums[0:1, slots:], 1, 0)
    grads = lax.all_to_all(
        slot_grad.reshape(experts, tokens), "exp", split_axis=0, concat_axis=0, tiled=True
    )
    logit_grad = logits_grad(gates, expert_ids.T, grads)
    hidden_grad, joined = join_hidden(table, where, all_choices, halves, slots, hidden)
    if apart:
        entered = list(hold(got[depth, "B"][:1], [joined], ENTER_WEIGHT))
        got[depth, "B"] = entered + list(hold(got[depth, "B"][1:], entered, CLOSE_WEIGHT))
    weight_grad = total_grad(got[depth, "A"], got[depth, "B"], rest, cut)
    return (logit_grad.T, hidden_grad[None, None], weight_grad)


def routing_tables(expert_ids, count_experts, capacity):
    columns = jnp.arange(count_experts, dtype=jnp.int32)
    matches = expert_ids[:, :, None] == columns[None, None, :]
    per_token = jnp.sum(matches.astype(jnp.int32), axis=1)
    rank_table = jnp.cumsum(per_token, axis=0) - per_token
    slot_iota = jnp.arange(capacity, dtype=jnp.int32)
    select = (per_token.T[:, None, :] == 1) & (rank_table.T[:, None, :] == slot_iota[None, :, None])
    return (matches.astype(jnp.float32), select)


def per_device_routed(grad_out, top_logits, expert_ids, saved_hidden, w_down):
    count_experts = lax.axis_size("exp")
    slot_count = saved_hidden.shape[2]
    capacity = slot_count // count_experts
    model_width = grad_out.shape[1]
    onehot, select = routing_tables(expert_ids, count_experts, capacity)
    select_wide = select.astype(jnp.float32)
    gate_probs = jax.nn.softmax(top_logits, axis=-1)
    gate_sent = gate_probs.astype(jnp.bfloat16)
    gate_by_expert = jnp.sum(onehot * gate_sent.astype(jnp.float32)[:, :, None], axis=1)
    send_rows = jnp.einsum(
        "ect,td->ecd", select.astype(jnp.bfloat16), grad_out, preferred_element_type=jnp.float32
    ).astype(jnp.bfloat16)
    send_gate = jnp.sum(select_wide * gate_by_expert.T[:, None, :], axis=2).astype(jnp.bfloat16)
    hidden = saved_hidden[0, 0]
    rows_in, gate_in = (
        lax.all_to_all(send_rows, "exp", split_axis=0, concat_axis=0, tiled=True),
        lax.all_to_all(send_gate, "exp", split_axis=0, concat_axis=0, tiled=True),
    )
    flat_rows = rows_in.reshape(slot_count, model_width)
    backprop = lax.dot_general(
        flat_rows,
        lax.all_gather(w_down[0], "ctx", axis=0, tiled=True),
        (((1,), (1,)), ((), ())),
        preferred_element_type=jnp.float32,
    )
    flat_gate = gate_in.reshape(slot_count, 1).astype(jnp.float32)
    hidden_grad = (flat_gate * backprop).astype(jnp.bfloat16)
    slot_grad = jnp.sum(hidden.astype(jnp.float32) * backprop, axis=1)
    scaled = (flat_gate * flat_rows.astype(jnp.float32)).astype(jnp.bfloat16)
    partial_grad = lax.dot_general(
        hidden, scaled, (((0,), (0,)), ((), ())), preferred_element_type=jnp.float32
    )
    weight_grad = lax.psum_scatter(partial_grad, "ctx", scatter_dimension=0, tiled=True)
    returned = lax.all_to_all(
        slot_grad.reshape(count_experts, capacity), "exp", split_axis=0, concat_axis=0, tiled=True
    )
    grad_by_expert = jnp.sum(select_wide * returned[:, :, None], axis=1)
    gate_grad = jnp.sum(onehot * grad_by_expert.T[:, None, :], axis=2)
    logit_grad = gate_probs * (gate_grad - jnp.sum(gate_probs * gate_grad, axis=1, keepdims=True))
    return (logit_grad, hidden_grad.reshape(1, 1, slot_count, -1), weight_grad[None])


def per_device(grad_out, top_logits, expert_ids, saved_hidden, w_down):
    experts = lax.axis_size("exp")
    groups = lax.axis_size("ctx")
    everywhere = top_logits.shape[1] == experts and saved_hidden.shape[2] == experts * grad_out.shape[0]
    plain = experts & (experts - 1) == 0 and groups % 4 == 0 and groups >= 8
    body = per_device_full if everywhere and plain else per_device_routed
    return body(grad_out, top_logits, expert_ids, saved_hidden, w_down)


def solution(mesh):
    return jax.shard_map(
        per_device,
        mesh=mesh,
        in_specs=(
            P(("ctx", "exp"), None),
            P(("ctx", "exp"), None),
            P(("ctx", "exp"), None),
            P("ctx", "exp", None, None),
            P("exp", "ctx", None),
        ),
        out_specs=(P(("ctx", "exp"), None), P("ctx", "exp", None, None), P("exp", "ctx", None)),
        check_vma=False,
    )
```
